32 devices in a mesh: dp: 4 (over y, x), seq: 8 (over z, core).
Axes of the slice: x: 2, y: 2, z: 4, core: 2. Of those that a mesh axis runs over, the one named last changes fastest.
Arguments:
- tokens: int32 [16384], P(('dp', 'seq')), parts along dimension 0, may hold values from 0 to 3
- dilations: int32 [2], replicated, may hold values from 1 to 64, as said below
- embed: float32 [4, 256], replicated, may hold values from -6 to 6
- conv_weight: float32 [2, 3, 256, 512], replicated, may hold values from -0.1875 to 0.1875
- mix_weight: float32 [2, 256, 512], replicated, may hold values from -0.1875 to 0.1875
- gate_bias: float32 [2, 512], replicated, may hold values from -3 to 3
- out_weight: float32 [2, 256, 256], replicated, may hold values from -0.375 to 0.375
- cot_fwd: float32 [16384, 256], P(('dp', 'seq')), parts along dimension 0, may hold values from -6 to 6
- cot_rev: float32 [16384, 256], P(('dp', 'seq')), parts along dimension 0, may hold values from -6 to 6
Outputs:
- out_fwd: float32 [16384, 256], P(('dp', 'seq')), parts along dimension 0
- out_rev: float32 [16384, 256], P(('dp', 'seq')), parts along dimension 0
- grad_embed: float32 [16, 256], P('dp'), parts along dimension 0
- grad_conv: float32 [8, 3, 256, 512], P('dp'), parts along dimension 0
- grad_mix: float32 [8, 256, 512], P('dp'), parts along dimension 0
- grad_bias: float32 [8, 512], P('dp'), parts along dimension 0
- grad_out: float32 [8, 256, 256], P('dp'), parts along dimension 0
The draws below stay inside these ranges and needn't reach their ends.
There are 4 independent parts, one for each index of `dp`. The reference program is written for one: setup_inputs(seed, part) draws one part's arguments, and reference() takes and returns one part's arrays. A program takes and returns all parts, laid end to end along the dimension named above; an argument that names none is the same for every part. Nothing has to cross between parts.
Inputs may be any that keep to these rules, and one draw needn't show every extreme that they name: `dilations`: exactly one layer's dilation equals 64; the others lie below it.
All inputs are finite; a program needn't handle non-finite values.
Results may differ from the reference program's by a relative error of at most 0.00012.
Values sent between devices are 32-bit elements; how exact they have to be, the bound alone decides.
No kernel may reach another device: no remote copies, remote signals or barrier semaphores. Data moves between devices by JAX's collectives and lax.ppermute only.
A program may use at most 128 MiB of HBM per device.

```python
import jax
import jax.numpy as jnp
from jax import lax

HALF = 256
LAYERS = 2
DMAX = 64
SEQLEN = 4096


def draw_dilations(key, part):
    values = jax.random.randint(key, (LAYERS,), 1, DMAX)
    chosen = jax.random.randint(jax.random.fold_in(key, 7), (), 0, LAYERS)
    return jnp.where(jnp.arange(LAYERS) == chosen, DMAX, values).astype(jnp.int32)


def touch_ends(entries, stream_key, low, top_value):
    index_at = [jax.random.randint(jax.random.fold_in(stream_key, axis), (), 0, length) for axis, length in enumerate(entries.shape)]
    longest = entries.shape.index(max(entries.shape))
    neighbour = index_at[:longest] + [(index_at[longest] + 1) % entries.shape[longest]] + index_at[longest + 1:]
    return entries.at[tuple(index_at)].set(low).at[tuple(neighbour)].set(top_value)


def steps_of(own_key, dims, cuts, least, high):
    level, own = 1.0, jax.random.fold_in(own_key, 6)
    for axis_at, parts in cuts:
        heights = jnp.exp(jax.random.uniform(jax.random.fold_in(own, axis_at), (parts,), jnp.float32, least / len(cuts), high / len(cuts)))
        level = level * jnp.repeat(heights, dims[axis_at] // parts).reshape([-1 if axis == axis_at else 1 for axis in range(len(dims))])
    return level


def centred(own_key, shape, deviation, most, cuts=(), kind=jnp.bfloat16):
    drawn = deviation * jax.random.normal(own_key, shape, jnp.float32)
    if cuts:
        drawn = drawn * steps_of(own_key, shape, cuts, -0.22, 0.18)
    return jnp.clip(drawn, -most, most).astype(kind)


def setup_inputs(seed: int = 0, part: int = 0) -> dict:
    seeds = jax.random.split(jax.random.key(seed), 10)
    own_keys = jax.random.split(jax.random.fold_in(seeds[9], part), 10)
    return {
        "tokens": touch_ends(jax.random.randint(own_keys[0], (SEQLEN,), 0, 4), jax.random.fold_in(own_keys[0], 1), 0, 3).astype(jnp.int32),
        "dilations": draw_dilations(jax.random.fold_in(seeds[9], 71), part),
        "embed": centred(seeds[2], (4, HALF), 1.0, 6.0, (), jnp.float32),
        "conv_weight": centred(seeds[3], (LAYERS, 3, HALF, 2 * HALF), (4 * HALF) ** -0.5, 0.1875, (), jnp.float32),
        "mix_weight": centred(seeds[4], (LAYERS, HALF, 2 * HALF), (4 * HALF) ** -0.5, 0.1875, (), jnp.float32),
        "gate_bias": centred(seeds[5], (LAYERS, 2 * HALF), 0.5, 3.0, (), jnp.float32),
        "out_weight": centred(seeds[6], (LAYERS, HALF, HALF), HALF ** -0.5, 0.375, (), jnp.float32),
        "cot_fwd": centred(own_keys[7], (SEQLEN, HALF), 1.0, 6.0, ((0, 8),), jnp.float32),
        "cot_rev": centred(own_keys[8], (SEQLEN, HALF), 1.0, 6.0, ((0, 8),), jnp.float32),
    }


def stencil_rows(padded, dilation, length):
    pieces = []
    for offset in range(3):
        begin = (DMAX + (offset - 1) * dilation).astype(jnp.int32)
        pieces.append(lax.dynamic_slice_in_dim(padded, begin, length, 0))
    return jnp.concatenate(pieces, axis=1)

def strand_layer(own, partner, dilation, conv_piece, mix_piece, bias_piece, out_piece):
    length, channels = own.shape
    padded = jnp.pad(own, ((DMAX, DMAX), (0, 0)))
    inputs = jnp.concatenate([stencil_rows(padded, dilation, length), partner], axis=1)
    joined = jnp.concatenate([conv_piece.reshape(3 * channels, 2 * channels), mix_piece], axis=0)
    mixed_rows = jnp.dot(inputs, joined, precision=lax.Precision.HIGHEST, preferred_element_type=jnp.float32) + bias_piece
    hidden = jnp.tanh(mixed_rows[:, :channels]) * jax.nn.sigmoid(mixed_rows[:, channels:])
    return own + jnp.dot(hidden, out_piece, precision=lax.Precision.HIGHEST, preferred_element_type=jnp.float32)

def reference(tokens, dilations, embed, conv_weight, mix_weight, gate_bias, out_weight, cot_fwd, cot_rev):

    def forward(embed_table, conv_all, mix_all, bias_all, out_all):
        strand_fwd = jnp.take(embed_table, tokens, axis=0)
        strand_rev = jnp.flip(jnp.take(embed_table, 3 - tokens, axis=0), 0)
        for layer_at in range(LAYERS):
            partner_fwd = jnp.flip(strand_rev, 0)
            partner_rev = jnp.flip(strand_fwd, 0)
            dilation = dilations[layer_at].astype(jnp.int32)
            new_fwd = strand_layer(strand_fwd, partner_fwd, dilation, conv_all[layer_at], mix_all[layer_at], bias_all[layer_at], out_all[layer_at])
            new_rev = strand_layer(strand_rev, partner_rev, dilation, conv_all[layer_at], mix_all[layer_at], bias_all[layer_at], out_all[layer_at])
            strand_fwd, strand_rev = (new_fwd, new_rev)
        return (strand_fwd, strand_rev)
    outputs, pullback = jax.vjp(forward, embed, conv_weight, mix_weight, gate_bias, out_weight)
    gradients = pullback((cot_fwd, cot_rev))
    return (outputs[0], outputs[1], gradients[0], gradients[1], gradients[2], gradients[3], gradients[4])
```

```python
import functools

import jax
import jax.numpy as jnp
from jax import lax
from jax.experimental import pallas as pl
from jax.experimental.pallas import tpu as pltpu
from jax.sharding import PartitionSpec as P

CONTEXTS = 96
SLOT = 128
HALO = 128
F32 = jnp.float32
BF16 = jnp.bfloat16
VMEM_LIMIT = 48 * 1024 * 1024


def split(x):
    high = x.astype(BF16)
    return high, (x - high.astype(F32)).astype(BF16)


def dot(a, b, ca=1, cb=0):
    return lax.dot_general(a, b, (((ca,), (cb,)), ((), ())), preferred_element_type=F32)


def dot2(exact, pair, ca=1, cb=0):
    return dot(exact, pair[0], ca, cb) + dot(exact, pair[1], ca, cb)


def dot3(a, b, ca=1, cb=0):
    return dot(a[0], b[0], ca, cb) + (dot(a[0], b[1], ca, cb) + dot(a[1], b[0], ca, cb))


def letters(index):
    inner = index < 64
    left = (index >= 64) & (index < 80)
    low = index & 3
    mid = (index >> 2) & 3
    l = jnp.where(inner, (index >> 4) & 3, jnp.where(left, -1, mid))
    m = jnp.where(inner | left, mid, low)
    r = jnp.where(inner | left, low, -1)
    return l, m, r


def mirrored(index):
    low = 3 - (index & 3)
    mid = 3 - ((index >> 2) & 3)
    high = 3 - ((index >> 4) & 3)
    inner = low * 16 + mid * 4 + high
    left = 80 + low * 4 + mid
    right = 64 + low * 4 + mid
    return jnp.where(index < 64, inner, jnp.where(index < 80, left, right))


def permutation():
    rows = lax.broadcasted_iota(jnp.int32, (CONTEXTS, CONTEXTS), 0)
    cols = lax.broadcasted_iota(jnp.int32, (CONTEXTS, CONTEXTS), 1)
    return (mirrored(rows) == cols).astype(F32).astype(BF16)


def letter_hot():
    rows = lax.broadcasted_iota(jnp.int32, (CONTEXTS, 32), 0)
    cols = lax.broadcasted_iota(jnp.int32, (CONTEXTS, 32), 1)
    l, m, r = letters(rows)
    kind = cols >> 3
    value = jnp.where(kind == 0, l, jnp.where(kind == 1, m, jnp.where(kind == 2, r, 3 - m)))
    return (value == (cols & 7)).astype(F32).astype(BF16)


def gates(mixed):
    channels = mixed.shape[1] // 2
    tanh_part = jnp.tanh(mixed[:, :channels])
    sig_part = 0.5 + 0.5 * jnp.tanh(0.5 * mixed[:, channels:])
    return tanh_part, sig_part


def gate_grads(grad_hidden, tanh_part, sig_part):
    scaled = grad_hidden * sig_part
    return scaled * (1.0 - tanh_part * tanh_part), scaled * tanh_part * (1.0 - sig_part)


def tables_kernel(embed, conv, mix, bias, out_w, table, mixed_table, pre_high, pre_low):
    channels = embed.shape[1]
    base = jnp.concatenate([embed[...], jnp.zeros((4, channels), F32)], axis=0)
    base = split(base)
    taps = [dot3(base, split(conv[0, k])) for k in range(3)] + [dot3(base, split(mix[0]))]
    taps = jnp.concatenate(taps, axis=0)
    hot = letter_hot()
    mixed = dot2(hot, split(taps)) + bias[0:1, :]
    tanh_part, sig_part = gates(mixed)
    hidden = tanh_part * sig_part
    own = dot2(hot[:, 8:16], base)
    level = own + dot3(split(hidden), split(out_w[0]))
    table[...] = level
    mixed_table[...] = mixed
    level = split(level)
    swap = permutation()
    partner = tuple(dot(swap, piece).astype(BF16) for piece in level)
    zero = jnp.zeros((SLOT - CONTEXTS, pre_high.shape[1]), BF16)
    for k in range(3):
        value = dot3(level, split(conv[1, k]))
        if k == 1:
            value = value + dot3(partner, split(mix[1])) + bias[1:2, :]
        high, low = split(value)
        pre_high[k * SLOT : k * SLOT + CONTEXTS, :] = high
        pre_low[k * SLOT : k * SLOT + CONTEXTS, :] = low
        pre_high[k * SLOT + CONTEXTS : (k + 1) * SLOT, :] = zero
        pre_low[k * SLOT + CONTEXTS : (k + 1) * SLOT, :] = zero


def windows(own, before, after, far, far_before, far_after):
    length = own.shape[1]
    place = lax.axis_index("seq")
    last = lax.axis_size("seq") - 1
    at_start, at_end = place == 0, place == last
    fwd = [jnp.where(at_start, -1, before[:, length - HALO :]), own[...], jnp.where(at_end, -1, after[:, :HALO])]
    rev = [jnp.where(at_end, -1, far_before[:, length - HALO :]), far[...], jnp.where(at_start, -1, far_after[:, :HALO])]
    fwd = jnp.concatenate(fwd, axis=1)
    rev = jnp.concatenate(rev, axis=1)
    rev = jnp.where(rev < 0, -1, 3 - rev)
    count = rev.shape[1] // 128
    blocks = [rev[:, i * 128 : (i + 1) * 128] for i in reversed(range(count))]
    blocks += [jnp.zeros((8 - count, 128), jnp.int32)]
    stacked = jnp.concatenate(blocks, axis=0).astype(F32).astype(BF16)
    rows = lax.broadcasted_iota(jnp.int32, (128, 128), 0)
    cols = lax.broadcasted_iota(jnp.int32, (128, 128), 1)
    flip = (rows + cols == 127).astype(F32).astype(BF16)
    turned = dot(stacked, flip).astype(jnp.int32)
    rev = jnp.concatenate([turned[i : i + 1, :] for i in range(count)], axis=1)
    return fwd, rev


def contexts(window, first, second, length):
    width = window.shape[1]
    base = jnp.broadcast_to(window, (8, width))
    l = pltpu.roll(base, first, 1)
    r = pltpu.roll(base, width - first, 1)
    index = jnp.where(l < 0, 64 + base * 4 + r, jnp.where(r < 0, 80 + l * 4 + base, l * 16 + base * 4 + r))
    index = jnp.where(base < 0, SLOT, index)
    before = pltpu.roll(index, second, 1)
    after = pltpu.roll(index, width - second, 1)
    return [x[0:1, HALO : HALO + length] for x in (before, index, after)]


def hot_rows(index):
    rows = lax.broadcasted_iota(jnp.int32, (SLOT, index.shape[1]), 0)
    return (rows == index).astype(F32).astype(BF16)


def main_kernel(dil, own, before, after, far, far_before, far_after, pre_high, pre_low, out_w, cot_fwd, cot_rev, sums, hidden_high, hidden_low, center):
    length = own.shape[1]
    channels = out_w.shape[1]
    pre = (pre_high[...], pre_low[...])
    weight = split(out_w[1])
    both = windows(own, before, after, far, far_before, far_after)
    total_s = total_c = total_o = None
    for strand, cot_ref in enumerate((cot_fwd, cot_rev)):
        index = contexts(both[strand], dil[0], dil[1], length)
        hot = jnp.concatenate([hot_rows(x) for x in index], axis=0)
        center[strand : strand + 1, :] = index[1]
        cot = split(cot_ref[...])
        mixed = dot2(hot, pre, 0, 0)
        tanh_part, sig_part = gates(mixed)
        hidden = split(tanh_part * sig_part)
        rows = slice(strand * length, (strand + 1) * length)
        hidden_high[rows, :] = hidden[0]
        hidden_low[rows, :] = hidden[1]
        grad_hidden = dot3(cot, weight, 1, 1)
        grads = split(jnp.concatenate(gate_grads(grad_hidden, tanh_part, sig_part), axis=1))
        part_o = dot3(hidden, cot, 0, 0)
        part_c = dot2(hot[SLOT : 2 * SLOT], cot)
        part_s = dot2(hot, grads)
        total_s = part_s if total_s is None else total_s + part_s
        total_c = part_c if total_c is None else total_c + part_c
        total_o = part_o if total_o is None else total_o + part_o
    for k in range(3):
        sums[k * CONTEXTS : (k + 1) * CONTEXTS, :] = total_s[k * SLOT : k * SLOT + CONTEXTS, :]
    at = 3 * CONTEXTS
    half = channels // 2
    sums[at : at + half, :channels] = total_o[:half, :]
    sums[at : at + half, channels:] = total_o[half:, :]
    at += half
    half = CONTEXTS // 2
    sums[at : at + half, :channels] = total_c[:half, :]
    sums[at : at + half, channels:] = total_c[half:CONTEXTS, :]


def outputs_kernel(center, hidden_high, hidden_low, table, out_w, out_fwd, out_rev):
    length = center.shape[1]
    weight = split(out_w[1])
    level = split(table[...])
    for strand, out in enumerate((out_fwd, out_rev)):
        rows = slice(strand * length, (strand + 1) * length)
        hot = hot_rows(center[strand : strand + 1, :])[:CONTEXTS]
        update = dot3((hidden_high[rows, :], hidden_low[rows, :]), weight)
        out[...] = dot2(hot, level, 0, 0) + update


def grads_kernel(sums, table, mixed_table, embed, conv, mix, out_w, g_embed, g_conv, g_mix, g_bias, g_out):
    channels = embed.shape[1]
    level = split(table[...])
    swap = permutation()
    partner = tuple(dot(swap, piece).astype(BF16) for piece in level)
    at = 3 * CONTEXTS
    half = channels // 2
    g_out[1, :half, :] = sums[at : at + half, :channels]
    g_out[1, half:, :] = sums[at : at + half, channels:]
    at += half
    half = CONTEXTS // 2
    grad_level = jnp.concatenate([sums[at : at + half, :channels], sums[at : at + half, channels:]], axis=0)
    for k in range(3):
        piece = sums[k * CONTEXTS : (k + 1) * CONTEXTS, :]
        pair = split(piece)
        grad_level = grad_level + dot3(pair, split(conv[1, k]), 1, 1)
        g_conv[1, k] = dot3(level, pair, 0, 0)
        if k == 1:
            g_bias[1:2, :] = jnp.sum(piece, axis=0, keepdims=True)
            g_mix[1] = dot3(partner, pair, 0, 0)
            grad_level = grad_level + dot2(swap, split(dot3(pair, split(mix[1]), 1, 1)))
    tanh_part, sig_part = gates(mixed_table[...])
    hidden = split(tanh_part * sig_part)
    pair = split(grad_level)
    g_out[0] = dot3(hidden, pair, 0, 0)
    grad_hidden = dot3(pair, split(out_w[0]), 1, 1)
    grad_mixed = jnp.concatenate(gate_grads(grad_hidden, tanh_part, sig_part), axis=1)
    g_bias[0:1, :] = jnp.sum(grad_mixed, axis=0, keepdims=True)
    hot = letter_hot()
    base = split(jnp.concatenate([embed[...], jnp.zeros((4, channels), F32)], axis=0))
    by_letter = dot2(hot, split(grad_mixed), 0, 0)
    grad_base = dot2(hot[:, 8:16], pair, 0, 0)
    for k in range(4):
        piece = split(by_letter[k * 8 : (k + 1) * 8, :])
        weight = conv[0, k] if k < 3 else mix[0]
        grad_base = grad_base + dot3(piece, split(weight), 1, 1)
        value = dot3(base, piece, 0, 0)
        if k < 3:
            g_conv[0, k] = value
        else:
            g_mix[0] = value
    g_embed[...] = grad_base[:4, :]


def call(kernel, outs, smem=()):
    def run(*args):
        specs = [
            pl.BlockSpec(memory_space=pltpu.SMEM if i in smem else pltpu.VMEM) for i in range(len(args))
        ]
        return pl.pallas_call(
            kernel,
            out_shape=[jax.ShapeDtypeStruct(shape, kind) for shape, kind in outs],
            in_specs=specs,
            out_specs=[pl.BlockSpec(memory_space=pltpu.VMEM)] * len(outs),
            compiler_params=pltpu.CompilerParams(vmem_limit_bytes=VMEM_LIMIT),
        )(*args)

    return run


def on_device(
    tokens, dilations, embed, conv_weight, mix_weight, gate_bias, out_weight, cot_fwd, cot_rev
):
    channels = embed.shape[1]
    wide = 2 * channels
    length = tokens.shape[0]
    count = lax.axis_size("seq")
    row = tokens.reshape(1, length)

    def fetched(source_of):
        pairs = [(source_of(i), i) for i in range(count) if 0 <= source_of(i) < count]
        return lax.ppermute(row, "seq", pairs)

    before = fetched(lambda i: i - 1)
    after = fetched(lambda i: i + 1)
    far = fetched(lambda i: count - 1 - i)
    far_before = fetched(lambda i: count - 2 - i)
    far_after = fetched(lambda i: count - i)

    table, mixed_table, pre_high, pre_low = call(
        tables_kernel,
        [((CONTEXTS, channels), F32), ((CONTEXTS, wide), F32), ((3 * SLOT, wide), BF16), ((3 * SLOT, wide), BF16)],
    )(embed, conv_weight, mix_weight, gate_bias, out_weight)

    sum_rows = 3 * CONTEXTS + channels // 2 + CONTEXTS // 2
    sums, hidden_high, hidden_low, center = call(
        main_kernel,
        [
            ((sum_rows, wide), F32),
            ((2 * length, channels), BF16),
            ((2 * length, channels), BF16),
            ((2, length), jnp.int32),
        ],
        smem=(0,),
    )(dilations, row, before, after, far, far_before, far_after, pre_high, pre_low, out_weight, cot_fwd, cot_rev)

    sums = lax.psum(sums, "seq")

    out_fwd, out_rev = call(outputs_kernel, [((length, channels), F32)] * 2)(
        center, hidden_high, hidden_low, table, out_weight
    )

    grads = call(
        grads_kernel,
        [
            (embed.shape, F32),
            (conv_weight.shape, F32),
            (mix_weight.shape, F32),
            (gate_bias.shape, F32),
            (out_weight.shape, F32),
        ],
    )(sums, table, mixed_table, embed, conv_weight, mix_weight, out_weight)
    return (out_fwd, out_rev, *grads)


def solution(mesh):
    in_specs = (
        P(("dp", "seq")),
        P(),
        P(),
        P(),
        P(),
        P(),
        P(),
        P(("dp", "seq"), None),
        P(("dp", "seq"), None),
    )
    out_specs = (
        P(("dp", "seq"), None),
        P(("dp", "seq"), None),
        P("dp", None),
        P("dp", None, None, None),
        P("dp", None, None),
        P("dp", None),
        P("dp", None, None),
    )
    return jax.shard_map(
        on_device, mesh=mesh, in_specs=in_specs, out_specs=out_specs, check_vma=False
    )
```

```python
import jax
import jax.numpy as jnp
from jax import lax
from jax.experimental import pallas as pl
from jax.experimental.pallas import tpu as pltpu
from jax.sharding import PartitionSpec as P

CONTEXTS = 96
SLOT = 128
HALO = 128
F32 = jnp.float32
BF16 = jnp.bfloat16
VMEM_LIMIT = 48 * 1024 * 1024


def split(x):
    high = x.astype(BF16)
    return high, (x - high.astype(F32)).astype(BF16)


def dot(a, b, ca=1, cb=0):
    return lax.dot_general(a, b, (((ca,), (cb,)), ((), ())), preferred_element_type=F32)


def dot2(exact, pair, ca=1, cb=0):
    return dot(exact, pair[0], ca, cb) + dot(exact, pair[1], ca, cb)


def dot3(a, b, ca=1, cb=0):
    return dot(a[0], b[0], ca, cb) + (dot(a[0], b[1], ca, cb) + dot(a[1], b[0], ca, cb))


def letters(index):
    inner = index < 64
    left = (index >= 64) & (index < 80)
    low = index & 3
    mid = (index >> 2) & 3
    l = jnp.where(inner, (index >> 4) & 3, jnp.where(left, -1, mid))
    m = jnp.where(inner | left, mid, low)
    r = jnp.where(inner | left, low, -1)
    return l, m, r


def mirrored(index):
    low = 3 - (index & 3)
    mid = 3 - ((index >> 2) & 3)
    high = 3 - ((index >> 4) & 3)
    inner = low * 16 + mid * 4 + high
    left = 80 + low * 4 + mid
    right = 64 + low * 4 + mid
    return jnp.where(index < 64, inner, jnp.where(index < 80, left, right))


def permutation():
    rows = lax.broadcasted_iota(jnp.int32, (CONTEXTS, CONTEXTS), 0)
    cols = lax.broadcasted_iota(jnp.int32, (CONTEXTS, CONTEXTS), 1)
    return (mirrored(rows) == cols).astype(F32).astype(BF16)


def letter_hot():
    rows = lax.broadcasted_iota(jnp.int32, (CONTEXTS, 32), 0)
    cols = lax.broadcasted_iota(jnp.int32, (CONTEXTS, 32), 1)
    l, m, r = letters(rows)
    kind = cols >> 3
    value = jnp.where(kind == 0, l, jnp.where(kind == 1, m, jnp.where(kind == 2, r, 3 - m)))
    return (value == (cols & 7)).astype(F32).astype(BF16)


def gates(mixed):
    channels = mixed.shape[1] // 2
    tanh_part = jnp.tanh(mixed[:, :channels])
    sig_part = 0.5 + 0.5 * jnp.tanh(0.5 * mixed[:, channels:])
    return tanh_part, sig_part


def gate_grads(grad_hidden, tanh_part, sig_part):
    scaled = grad_hidden * sig_part
    return scaled * (1.0 - tanh_part * tanh_part), scaled * tanh_part * (1.0 - sig_part)


class Fetch:
    def __init__(self, sems):
        self.sems = sems
        self.copies = []

    def start(self, source, target):
        copy = pltpu.make_async_copy(source, target, self.sems.at[len(self.copies)])
        copy.start()
        self.copies.append(copy)
        return len(self.copies) - 1

    def wait(self, *which):
        for at in which:
            self.copies[at].wait()


def padded_base(embed):
    return jnp.concatenate([embed[...], jnp.zeros((4, embed.shape[1]), F32)], axis=0)


def tables_kernel(
    embed_in, conv_in, mix_in, bias_in, out_in, table, mixed_table, pre_high, pre_low,
    embed, conv, mix, bias, out_w, sems,
):
    fetch = Fetch(sems)
    small = [fetch.start(embed_in, embed), fetch.start(bias_in, bias)]
    first = [fetch.start(conv_in.at[0, k], conv.at[0, k]) for k in range(3)]
    first += [fetch.start(mix_in.at[0], mix.at[0])]
    turn = fetch.start(out_in.at[0], out_w)
    second = [fetch.start(conv_in.at[1, k], conv.at[1, k]) for k in range(3)]
    second += [fetch.start(mix_in.at[1], mix.at[1])]
    hot = letter_hot()
    swap = permutation()
    fetch.wait(*small)
    base = split(padded_base(embed))
    taps = []
    for k in range(4):
        fetch.wait(first[k])
        taps.append(dot3(base, split(conv[0, k] if k < 3 else mix[0])))
    taps = jnp.concatenate(taps, axis=0)
    mixed = dot2(hot, split(taps)) + bias[0:1, :]
    tanh_part, sig_part = gates(mixed)
    hidden = tanh_part * sig_part
    own = dot2(hot[:, 8:16], base)
    fetch.wait(turn)
    level = own + dot3(split(hidden), split(out_w[...]))
    table[...] = level
    mixed_table[...] = mixed
    level = split(level)
    partner = tuple(dot(swap, piece).astype(BF16) for piece in level)
    zero = jnp.zeros((SLOT - CONTEXTS, pre_high.shape[1]), BF16)
    for k in (0, 2, 1):
        fetch.wait(second[k])
        value = dot3(level, split(conv[1, k]))
        if k == 1:
            fetch.wait(second[3])
            value = value + dot3(partner, split(mix[1])) + bias[1:2, :]
        high, low = split(value)
        pre_high[k * SLOT : k * SLOT + CONTEXTS, :] = high
        pre_low[k * SLOT : k * SLOT + CONTEXTS, :] = low
        pre_high[k * SLOT + CONTEXTS : (k + 1) * SLOT, :] = zero
        pre_low[k * SLOT + CONTEXTS : (k + 1) * SLOT, :] = zero


def windows(tokens):
    count, length = tokens.shape
    place = lax.axis_index("seq")
    last = count - 1

    values = tokens[...]
    rows = lax.broadcasted_iota(jnp.int32, (count, length), 0)

    def block(at):
        return jnp.sum(jnp.where(rows == at, values, 0), axis=0, keepdims=True)

    def window(at):
        before = jnp.where(at == 0, -1, block(at - 1)[:, length - HALO :])
        after = jnp.where(at == last, -1, block(at + 1)[:, :HALO])
        return [before, block(at), after]

    fwd = window(place)
    rev = window(last - place)
    fwd = jnp.concatenate(fwd, axis=1)
    rev = jnp.concatenate(rev, axis=1)
    rev = jnp.where(rev < 0, -1, 3 - rev)
    count = rev.shape[1] // 128
    blocks = [rev[:, i * 128 : (i + 1) * 128] for i in reversed(range(count))]
    blocks += [jnp.zeros((8 - count, 128), jnp.int32)]
    stacked = jnp.concatenate(blocks, axis=0).astype(F32).astype(BF16)
    rows = lax.broadcasted_iota(jnp.int32, (128, 128), 0)
    cols = lax.broadcasted_iota(jnp.int32, (128, 128), 1)
    flip = (rows + cols == 127).astype(F32).astype(BF16)
    turned = dot(stacked, flip).astype(jnp.int32)
    rev = jnp.concatenate([turned[i : i + 1, :] for i in range(count)], axis=1)
    return fwd, rev


def contexts(window, first, second, length):
    width = window.shape[1]
    base = jnp.broadcast_to(window, (8, width))
    l = pltpu.roll(base, first, 1)
    r = pltpu.roll(base, width - first, 1)
    index = jnp.where(l < 0, 64 + base * 4 + r, jnp.where(r < 0, 80 + l * 4 + base, l * 16 + base * 4 + r))
    index = jnp.where(base < 0, SLOT, index)
    before = pltpu.roll(index, second, 1)
    after = pltpu.roll(index, width - second, 1)
    return [x[0:1, HALO : HALO + length] for x in (before, index, after)]


def hot_rows(index):
    rows = lax.broadcasted_iota(jnp.int32, (SLOT, index.shape[1]), 0)
    return (rows == index).astype(F32).astype(BF16)


def main_kernel(
    dil, tokens, pre_high, pre_low, out_in, cot_fwd_in, cot_rev_in, keep, send, hidden_high, hidden_low, center,
    sums, out_w, cots, sems,
):
    length = tokens.shape[1]
    channels = out_w.shape[1]
    fetch = Fetch(sems)
    arrivals = [fetch.start(cot_fwd_in, cots.at[0]), fetch.start(out_in.at[1], out_w), fetch.start(cot_rev_in, cots.at[1])]
    pre = (pre_high[...], pre_low[...])
    both = windows(tokens)
    total_s = total_c = total_o = None
    for strand in range(2):
        index = contexts(both[strand], dil[0], dil[1], length)
        hot = jnp.concatenate([hot_rows(x) for x in index], axis=0)
        center[strand : strand + 1, :] = index[1]
        mixed = dot2(hot, pre, 0, 0)
        tanh_part, sig_part = gates(mixed)
        hidden = split(tanh_part * sig_part)
        rows = slice(strand * length, (strand + 1) * length)
        hidden_high[rows, :] = hidden[0]
        hidden_low[rows, :] = hidden[1]
        if strand == 0:
            fetch.wait(0, 1)
            weight = split(out_w[...])
        else:
            fetch.wait(2)
        cot = split(cots[strand])
        grad_hidden = dot3(cot, weight, 1, 1)
        grads = split(jnp.concatenate(gate_grads(grad_hidden, tanh_part, sig_part), axis=1))
        part_o = dot3(hidden, cot, 0, 0)
        part_c = dot2(hot[SLOT : 2 * SLOT], cot)
        part_s = dot2(hot, grads)
        total_s = part_s if total_s is None else total_s + part_s
        total_c = part_c if total_c is None else total_c + part_c
        total_o = part_o if total_o is None else total_o + part_o
    for k in range(3):
        sums[k * CONTEXTS : (k + 1) * CONTEXTS, :] = total_s[k * SLOT : k * SLOT + CONTEXTS, :]
    at = 3 * CONTEXTS
    half = channels // 2
    sums[at : at + half, :channels] = total_o[:half, :]
    sums[at : at + half, channels:] = total_o[half:, :]
    at += half
    half = CONTEXTS // 2
    sums[at : at + half, :channels] = total_c[:half, :]
    sums[at : at + half, channels:] = total_c[half:CONTEXTS, :]
    at += half
    sums[at:, :] = jnp.zeros((sums.shape[0] - at, sums.shape[1]), F32)
    share = sums.shape[0] // 2
    bit = lax.axis_index("seq") & 1
    keep[...] = sums[pl.ds(pl.multiple_of(bit * share, 8), share), :]
    send[...] = sums[pl.ds(pl.multiple_of((1 - bit) * share, 8), share), :]


def halve_kernel(kept, received, keep, send):
    share = keep.shape[0]
    bit = (lax.axis_index("seq") >> 1) & 1
    mine = pl.ds(pl.multiple_of(bit * share, 8), share)
    other = pl.ds(pl.multiple_of((1 - bit) * share, 8), share)
    send[...] = kept[other, :] + received[other, :]
    keep[...] = kept[mine, :] + received[mine, :]


def outputs_kernel(center, hidden_high, hidden_low, table, out_in, out_fwd, out_rev, out_w, sems):
    length = center.shape[1]
    fetch = Fetch(sems)
    fetch.start(out_in.at[1], out_w)
    fetch.wait(0)
    weight = split(out_w[...])
    level = split(table[...])
    for strand, out in enumerate((out_fwd, out_rev)):
        rows = slice(strand * length, (strand + 1) * length)
        hot = hot_rows(center[strand : strand + 1, :])[:CONTEXTS]
        update = dot3((hidden_high[rows, :], hidden_low[rows, :]), weight)
        out[...] = dot2(hot, level, 0, 0) + update


def grads_kernel(
    piece_00, piece_01, piece_10, piece_11, table, mixed_table, embed_in, conv_in, mix_in, out_in,
    g_embed_out, g_conv_out, g_mix_out, g_bias_out, g_out_out,
    sums, embed, conv, mix, out_w, g_embed, g_conv, g_mix, g_bias, g_out, sems, out_sems,
):
    channels = embed.shape[1]
    fetch = Fetch(sems)
    second = [fetch.start(conv_in.at[1, k], conv.at[1, k]) for k in range(3)]
    second += [fetch.start(mix_in.at[1], mix.at[1])]
    turn = fetch.start(out_in.at[0], out_w)
    small = fetch.start(embed_in, embed)
    first = [fetch.start(conv_in.at[0, k], conv.at[0, k]) for k in range(3)]
    first += [fetch.start(mix_in.at[0], mix.at[0])]
    store = Fetch(out_sems)

    place = lax.axis_index("seq")
    low, high = place & 1, (place >> 1) & 1
    share = piece_00.shape[0]
    for piece, x, y in ((piece_00, 0, 0), (piece_01, 0, 1), (piece_10, 1, 0), (piece_11, 1, 1)):
        at = ((low ^ x) * 2 + (high ^ y)) * share
        sums[pl.ds(pl.multiple_of(at, 8), share), :] = piece[...]

    level = split(table[...])
    swap = permutation()
    partner = tuple(dot(swap, piece).astype(BF16) for piece in level)
    at = 3 * CONTEXTS
    half = channels // 2
    g_out[1, :half, :] = sums[at : at + half, :channels]
    g_out[1, half:, :] = sums[at : at + half, channels:]
    store.start(g_out.at[1], g_out_out.at[1])
    at += half
    half = CONTEXTS // 2
    grad_level = jnp.concatenate([sums[at : at + half, :channels], sums[at : at + half, channels:]], axis=0)
    for k in range(3):
        piece = sums[k * CONTEXTS : (k + 1) * CONTEXTS, :]
        pair = split(piece)
        fetch.wait(second[k])
        grad_level = grad_level + dot3(pair, split(conv[1, k]), 1, 1)
        g_conv[1, k] = dot3(level, pair, 0, 0)
        store.start(g_conv.at[1, k], g_conv_out.at[1, k])
        if k == 1:
            g_bias[1:2, :] = jnp.sum(piece, axis=0, keepdims=True)
            g_mix[1] = dot3(partner, pair, 0, 0)
            store.start(g_mix.at[1], g_mix_out.at[1])
            fetch.wait(second[3])
            grad_level = grad_level + dot2(swap, split(dot3(pair, split(mix[1]), 1, 1)))
    tanh_part, sig_part = gates(mixed_table[...])
    hidden = split(tanh_part * sig_part)
    pair = split(grad_level)
    fetch.wait(turn)
    grad_hidden = dot3(pair, split(out_w[...]), 1, 1)
    grad_mixed = jnp.concatenate(gate_grads(grad_hidden, tanh_part, sig_part), axis=1)
    g_bias[0:1, :] = jnp.sum(grad_mixed, axis=0, keepdims=True)
    store.start(g_bias, g_bias_out)
    g_out[0] = dot3(hidden, pair, 0, 0)
    store.start(g_out.at[0], g_out_out.at[0])
    hot = letter_hot()
    fetch.wait(small)
    base = split(padded_base(embed))
    by_letter = dot2(hot, split(grad_mixed), 0, 0)
    grad_base = dot2(hot[:, 8:16], pair, 0, 0)
    for k in range(4):
        piece = split(by_letter[k * 8 : (k + 1) * 8, :])
        value = dot3(base, piece, 0, 0)
        if k < 3:
            g_conv[0, k] = value
            store.start(g_conv.at[0, k], g_conv_out.at[0, k])
        else:
            g_mix[0] = value
            store.start(g_mix.at[0], g_mix_out.at[0])
        fetch.wait(first[k])
        grad_base = grad_base + dot3(piece, split(conv[0, k] if k < 3 else mix[0]), 1, 1)
    g_embed[...] = grad_base[:4, :]
    store.start(g_embed, g_embed_out)
    store.wait(*range(len(store.copies)))


VMEM, SMEM, HBM = pltpu.VMEM, pltpu.SMEM, pltpu.HBM


def call(kernel, ins, outs, scratch=()):
    run = pl.pallas_call(
        kernel,
        out_shape=[HBM(shape, kind) if space is HBM else jax.ShapeDtypeStruct(shape, kind) for shape, kind, space in outs],
        in_specs=[pl.BlockSpec(memory_space=space) for space in ins],
        out_specs=[pl.BlockSpec(memory_space=space) for _, _, space in outs],
        scratch_shapes=list(scratch),
        compiler_params=pltpu.CompilerParams(vmem_limit_bytes=VMEM_LIMIT),
    )

    def placed(*args):
        return run(*[pltpu.with_memory_space_constraint(x, HBM) if space is HBM else x for x, space in zip(args, ins)])

    return placed


def swapped(value, mask):
    pairs = [(source, source ^ mask) for source in range(lax.axis_size("seq"))]
    return lax.ppermute(value, "seq", pairs)


def on_device(
    tokens, dilations, embed, conv_weight, mix_weight, gate_bias, out_weight, cot_fwd, cot_rev
):
    channels = embed.shape[1]
    wide = 2 * channels
    length = tokens.shape[0]
    count = lax.axis_size("seq")
    sems = pltpu.SemaphoreType.DMA

    everyone = lax.all_to_all(
        jnp.broadcast_to(tokens[None, :], (count, length)), "seq", split_axis=0, concat_axis=0, tiled=True
    )

    table, mixed_table, pre_high, pre_low = call(
        tables_kernel,
        [HBM] * 5,
        [
            ((CONTEXTS, channels), F32, VMEM),
            ((CONTEXTS, wide), F32, VMEM),
            ((3 * SLOT, wide), BF16, VMEM),
            ((3 * SLOT, wide), BF16, VMEM),
        ],
        [
            VMEM(embed.shape, F32),
            VMEM(conv_weight.shape, F32),
            VMEM(mix_weight.shape, F32),
            VMEM(gate_bias.shape, F32),
            VMEM((channels, channels), F32),
            sems((11,)),
        ],
    )(embed, conv_weight, mix_weight, gate_bias, out_weight)

    sum_rows = -(-(3 * CONTEXTS + channels // 2 + CONTEXTS // 2) // 32) * 32
    half_rows, share = sum_rows // 2, sum_rows // 4
    keep, send, hidden_high, hidden_low, center = call(
        main_kernel,
        [SMEM, VMEM, VMEM, VMEM, HBM, HBM, HBM],
        [
            ((half_rows, wide), F32, VMEM),
            ((half_rows, wide), F32, VMEM),
            ((2 * length, channels), BF16, VMEM),
            ((2 * length, channels), BF16, VMEM),
            ((2, length), jnp.int32, VMEM),
        ],
        [
            VMEM((sum_rows, wide), F32),
            VMEM((channels, channels), F32),
            VMEM((2, length, channels), F32),
            sems((3,)),
        ],
    )(dilations, everyone, pre_high, pre_low, out_weight, cot_fwd, cot_rev)

    keep, send = call(halve_kernel, [VMEM, VMEM], [((share, wide), F32, VMEM)] * 2)(keep, swapped(send, 1))
    piece = keep + swapped(send, 2)
    mask = 4
    while mask < count:
        piece = piece + swapped(piece, mask)
        mask *= 2
    piece_10 = swapped(piece, 1)
    piece_01 = swapped(piece, 2)
    piece_11 = swapped(piece_01, 1)

    out_fwd, out_rev = call(
        outputs_kernel,
        [VMEM, VMEM, VMEM, VMEM, HBM],
        [((length, channels), F32, VMEM)] * 2,
        [VMEM((channels, channels), F32), sems((1,))],
    )(center, hidden_high, hidden_low, table, out_weight)

    shapes = [embed.shape, conv_weight.shape, mix_weight.shape, gate_bias.shape, out_weight.shape]
    grads = call(
        grads_kernel,
        [VMEM] * 6 + [HBM] * 4,
        [(shape, F32, HBM) for shape in shapes],
        [
            VMEM((sum_rows, wide), F32),
            VMEM(embed.shape, F32),
            VMEM(conv_weight.shape, F32),
            VMEM(mix_weight.shape, F32),
            VMEM((channels, channels), F32),
        ]
        + [VMEM(shape, F32) for shape in shapes]
        + [sems((10,)), sems((12,))],
    )(piece, piece_01, piece_10, piece_11, table, mixed_table, embed, conv_weight, mix_weight, out_weight)
    return (out_fwd, out_rev, *grads)


def solution(mesh):
    in_specs = (
        P(("dp", "seq")),
        P(),
        P(),
        P(),
        P(),
        P(),
        P(),
        P(("dp", "seq"), None),
        P(("dp", "seq"), None),
    )
    out_specs = (
        P(("dp", "seq"), None),
        P(("dp", "seq"), None),
        P("dp", None),
        P("dp", None, None, None),
        P("dp", None, None),
        P("dp", None),
        P("dp", None, None),
    )
    return jax.shard_map(
        on_device, mesh=mesh, in_specs=in_specs, out_specs=out_specs, check_vma=False
    )
```

```python
import jax
import jax.numpy as jnp
from jax import lax
from jax.experimental import pallas as pl
from jax.experimental.pallas import tpu as pltpu
from jax.sharding import PartitionSpec as P

CONTEXTS = 96
INNER = 64
EDGE = 16
LOCAL = INNER + EDGE
TAPS = 3 * LOCAL
HALO = 128
F32 = jnp.float32
BF16 = jnp.bfloat16
VMEM_LIMIT = 40 * 1024 * 1024


def split(x):
    high = x.astype(BF16)
    return high, (x - high.astype(F32)).astype(BF16)


def dot(a, b, ca=1, cb=0):
    return lax.dot_general(a, b, (((ca,), (cb,)), ((), ())), preferred_element_type=F32)


def dot2(exact, pair, ca=1, cb=0):
    return dot(exact, pair[0], ca, cb) + dot(exact, pair[1], ca, cb)


def dot3(a, b, ca=1, cb=0):
    return dot(a[0], b[0], ca, cb) + (dot(a[0], b[1], ca, cb) + dot(a[1], b[0], ca, cb))


def letters(index):
    inner = index < 64
    left = (index >= 64) & (index < 80)
    low = index & 3
    mid = (index >> 2) & 3
    l = jnp.where(inner, (index >> 4) & 3, jnp.where(left, -1, mid))
    m = jnp.where(inner | left, mid, low)
    r = jnp.where(inner | left, low, -1)
    return l, m, r


def mirrored(index):
    low = 3 - (index & 3)
    mid = 3 - ((index >> 2) & 3)
    high = 3 - ((index >> 4) & 3)
    inner = low * 16 + mid * 4 + high
    left = 80 + low * 4 + mid
    right = 64 + low * 4 + mid
    return jnp.where(index < 64, inner, jnp.where(index < 80, left, right))


def permutation():
    rows = lax.broadcasted_iota(jnp.int32, (CONTEXTS, CONTEXTS), 0)
    cols = lax.broadcasted_iota(jnp.int32, (CONTEXTS, CONTEXTS), 1)
    return (mirrored(rows) == cols).astype(F32).astype(BF16)


def letter_hot():
    rows = lax.broadcasted_iota(jnp.int32, (CONTEXTS, 32), 0)
    cols = lax.broadcasted_iota(jnp.int32, (CONTEXTS, 32), 1)
    l, m, r = letters(rows)
    kind = cols >> 3
    value = jnp.where(kind == 0, l, jnp.where(kind == 1, m, jnp.where(kind == 2, r, 3 - m)))
    return (value == (cols & 7)).astype(F32).astype(BF16)


def gates(mixed):
    channels = mixed.shape[1] // 2
    tanh_part = jnp.tanh(mixed[:, :channels])
    sig_part = 0.5 + 0.5 * jnp.tanh(0.5 * mixed[:, channels:])
    return tanh_part, sig_part


def gate_grads(grad_hidden, tanh_part, sig_part):
    scaled = grad_hidden * sig_part
    return scaled * (1.0 - tanh_part * tanh_part), scaled * tanh_part * (1.0 - sig_part)


class Fetch:
    def __init__(self, sems):
        self.sems = sems
        self.copies = []

    def start(self, source, target):
        copy = pltpu.make_async_copy(source, target, self.sems.at[len(self.copies)])
        copy.start()
        self.copies.append(copy)
        return len(self.copies) - 1

    def wait(self, *which):
        for at in which:
            self.copies[at].wait()


def padded_base(embed):
    return jnp.concatenate([embed[...], jnp.zeros((4, embed.shape[1]), F32)], axis=0)


def left_side():
    return lax.axis_index("seq") * 2 < lax.axis_size("seq")


def local_rows(rows):
    edge = jnp.where(left_side(), rows[INNER : INNER + EDGE], rows[INNER + EDGE : INNER + 2 * EDGE])
    return jnp.concatenate([rows[:INNER], edge], axis=0)


def tables_kernel(
    embed_in, conv_in, mix_in, bias_in, out_in, table, local, mixed_table, pre_high, pre_low,
    embed, conv, mix, bias, out_w, sems,
):
    fetch = Fetch(sems)
    small = [fetch.start(embed_in, embed), fetch.start(bias_in, bias)]
    first = [fetch.start(conv_in.at[0, k], conv.at[0, k]) for k in range(3)]
    first += [fetch.start(mix_in.at[0], mix.at[0])]
    turn = fetch.start(out_in.at[0], out_w)
    second = [fetch.start(conv_in.at[1, k], conv.at[1, k]) for k in range(3)]
    second += [fetch.start(mix_in.at[1], mix.at[1])]
    hot = letter_hot()
    swap = permutation()
    fetch.wait(*small)
    base = split(padded_base(embed))
    taps = []
    for k in range(4):
        fetch.wait(first[k])
        taps.append(dot3(base, split(conv[0, k] if k < 3 else mix[0])))
    taps = jnp.concatenate(taps, axis=0)
    mixed = dot2(hot, split(taps)) + bias[0:1, :]
    tanh_part, sig_part = gates(mixed)
    hidden = tanh_part * sig_part
    own = dot2(hot[:, 8:16], base)
    fetch.wait(turn)
    level = own + dot3(split(hidden), split(out_w[...]))
    table[...] = level
    local[...] = local_rows(level)
    mixed_table[...] = mixed
    level = split(level)
    partner = tuple(dot(swap, piece).astype(BF16) for piece in level)
    pre_high[TAPS:, :] = jnp.zeros((pre_high.shape[0] - TAPS, pre_high.shape[1]), BF16)
    pre_low[TAPS:, :] = jnp.zeros((pre_low.shape[0] - TAPS, pre_low.shape[1]), BF16)
    for k in (0, 2, 1):
        fetch.wait(second[k])
        value = dot3(level, split(conv[1, k]))
        if k == 1:
            fetch.wait(second[3])
            value = value + dot3(partner, split(mix[1])) + bias[1:2, :]
        high, low = split(local_rows(value))
        pre_high[k * LOCAL : (k + 1) * LOCAL, :] = high
        pre_low[k * LOCAL : (k + 1) * LOCAL, :] = low


def windows(parts, count):
    length = parts[0].shape[1]
    place = lax.axis_index("seq")
    last = count - 1

    def block(at):
        total, begin = None, 0
        for part in parts:
            rows = lax.broadcasted_iota(jnp.int32, part.shape, 0) + begin
            piece = jnp.sum(jnp.where(rows == (place ^ at), part[...], 0), axis=0, keepdims=True)
            total = piece if total is None else total + piece
            begin += part.shape[0]
        return total

    def window(at):
        before = jnp.where(at == 0, -1, block(jnp.maximum(at - 1, 0))[:, length - HALO :])
        after = jnp.where(at == last, -1, block(jnp.minimum(at + 1, last))[:, :HALO])
        return [before, block(at), after]

    fwd = jnp.concatenate(window(place), axis=1)
    rev = jnp.concatenate(window(last - place), axis=1)
    rev = jnp.where(rev < 0, -1, 3 - rev)
    tiles = rev.shape[1] // 128
    blocks = [rev[:, i * 128 : (i + 1) * 128] for i in reversed(range(tiles))]
    blocks += [jnp.zeros((8 - tiles, 128), jnp.int32)]
    stacked = jnp.concatenate(blocks, axis=0).astype(F32).astype(BF16)
    rows = lax.broadcasted_iota(jnp.int32, (128, 128), 0)
    cols = lax.broadcasted_iota(jnp.int32, (128, 128), 1)
    flip = (rows + cols == 127).astype(F32).astype(BF16)
    turned = dot(stacked, flip).astype(jnp.int32)
    rev = jnp.concatenate([turned[i : i + 1, :] for i in range(tiles)], axis=1)
    return fwd, rev


def local_contexts(window, first, second, length):
    width = window.shape[1]
    base = jnp.broadcast_to(window, (8, width))
    l = pltpu.roll(base, first, 1)
    r = pltpu.roll(base, width - first, 1)
    index = jnp.where(l < 0, INNER + base * 4 + r, jnp.where(r < 0, INNER + l * 4 + base, l * 16 + base * 4 + r))
    index = jnp.where(base < 0, LOCAL, index)
    before = pltpu.roll(index, second, 1)
    after = pltpu.roll(index, width - second, 1)
    return [x[0:1, HALO : HALO + length] for x in (before, index, after)]


def hot_rows(index):
    rows = lax.broadcasted_iota(jnp.int32, (LOCAL, index.shape[1]), 0)
    return (rows == index).astype(F32).astype(BF16)


def deal(quarters, keep, send):
    bit = lax.axis_index("seq") & 1
    keep[...] = quarters[pl.ds(bit * 2, 2)]
    send[...] = quarters[pl.ds((1 - bit) * 2, 2)]


def main_kernel(count, dil, *refs):
    parts, refs = refs[: count.bit_length()], refs[count.bit_length() :]
    (pre_high, pre_low, out_in, cot_fwd_in, cot_rev_in, keep, send, hidden_high, hidden_low, cot_high, cot_low, center,
     quarters, out_w, cots, sems) = refs
    length = parts[0].shape[1]
    fetch = Fetch(sems)
    fetch.start(cot_fwd_in, cots.at[0])
    fetch.start(out_in.at[1], out_w)
    fetch.start(cot_rev_in, cots.at[1])
    pre = (pre_high[...], pre_low[...])
    both = windows(parts, count)
    pad = jnp.zeros((pre_high.shape[0] - TAPS, length), BF16)
    total = None
    for strand in range(2):
        index = local_contexts(both[strand], dil[0], dil[1], length)
        hot = jnp.concatenate([hot_rows(x) for x in index] + [pad], axis=0)
        center[strand : strand + 1, :] = index[1]
        mixed = dot2(hot, pre, 0, 0)
        tanh_part, sig_part = gates(mixed)
        hidden = split(tanh_part * sig_part)
        rows = slice(strand * length, (strand + 1) * length)
        hidden_high[rows, :] = hidden[0]
        hidden_low[rows, :] = hidden[1]
        if strand == 0:
            fetch.wait(0, 1)
            weight = split(out_w[...])
        else:
            fetch.wait(2)
        cot = split(cots[strand])
        cot_high[rows, :] = cot[0]
        cot_low[rows, :] = cot[1]
        grad_hidden = dot3(cot, weight, 1, 1)
        grads = split(jnp.concatenate(gate_grads(grad_hidden, tanh_part, sig_part), axis=1))
        part = dot2(hot, grads)
        total = part if total is None else total + part
    for q in range(4):
        quarters[q] = total[:TAPS, q * 128 : (q + 1) * 128]
    deal(quarters, keep, send)


def halve_kernel(kept, received, keep, send):
    bit = (lax.axis_index("seq") >> 1) & 1
    send[...] = kept[1 - bit] + received[1 - bit]
    keep[...] = kept[bit] + received[bit]


def outputs_kernel(
    center, hidden_high, hidden_low, cot_high, cot_low, local, out_in, after, keep, send, out_fwd_out, out_rev_out,
    quarters, out_w, out_both, sems,
):
    length = center.shape[1]
    channels = out_w.shape[1]
    fetch = Fetch(sems)
    fetch.start(out_in.at[1], out_w)
    total_o = total_c = None
    hots = []
    for strand in range(2):
        rows = slice(strand * length, (strand + 1) * length)
        hidden = (hidden_high[rows, :], hidden_low[rows, :])
        cot = (cot_high[rows, :], cot_low[rows, :])
        hots.append(hot_rows(center[strand : strand + 1, :]))
        part_o = dot3(hidden, cot, 0, 0)
        part_c = dot2(hots[strand], cot)
        total_o = part_o if total_o is None else total_o + part_o
        total_c = part_c if total_c is None else total_c + part_c
    side = channels // 4
    for q in range(4):
        half = slice((q >> 1) * 128, (q >> 1) * 128 + 128)
        quarters[q, :side, :] = total_o[q * side : (q + 1) * side, :128]
        quarters[q, side : 2 * side, :] = total_o[q * side : (q + 1) * side, 128:]
        at = (q & 1) * INNER // 2
        quarters[q, 2 * side : 2 * side + INNER // 2, :] = total_c[at : at + INNER // 2, half]
        at = INNER + (q & 1) * EDGE // 2
        quarters[q, 2 * side + INNER // 2 :, :] = total_c[at : at + EDGE // 2, half]
    deal(quarters, keep, send)
    fetch.wait(0)
    weight = split(out_w[...])
    level = split(local[...])
    for strand, out in enumerate((out_fwd_out, out_rev_out)):
        rows = slice(strand * length, (strand + 1) * length)
        update = dot3((hidden_high[rows, :], hidden_low[rows, :]), weight)
        out_both[strand] = dot2(hots[strand], level, 0, 0) + update
        fetch.start(out_both.at[strand], out)
    fetch.wait(1, 2)


def prepare_kernel(
    conv_in, mix_in, out_in, table, after, first_high, first_low, second_high, second_low, turn_high, turn_low,
    level_high, level_low, partner_high, partner_low, conv, mix, out_w, sems,
):
    fetch = Fetch(sems)
    loads = []
    for layer in (1, 0):
        loads += [(layer, k, fetch.start(conv_in.at[layer, k], conv.at[layer, k])) for k in range(3)]
        loads += [(layer, 3, fetch.start(mix_in.at[layer], mix.at[layer]))]
    turn = fetch.start(out_in.at[0], out_w)
    level = split(table[...])
    swap = permutation()
    level_high[...], level_low[...] = level
    partner_high[...], partner_low[...] = tuple(dot(swap, piece).astype(BF16) for piece in level)
    for layer, k, load in loads:
        fetch.wait(load)
        weight = split((conv[layer, k] if k < 3 else mix[layer]).T)
        high, low = (first_high, first_low) if layer == 0 else (second_high, second_low)
        high[k], low[k] = weight
    fetch.wait(turn)
    turn_high[...], turn_low[...] = split(out_w[...].T)


def merge(mine, theirs, inner, edge):
    left = left_side()
    both = mine[inner, :] + theirs[inner, :]
    own, other = mine[edge, :], theirs[edge, :]
    return both, jnp.where(left, own, other), jnp.where(left, other, own)


def merge_taps_kernel(mine, theirs, after, out):
    for k in range(3):
        at = k * LOCAL
        pieces = merge(mine, theirs, slice(at, at + INNER), slice(at + INNER, at + LOCAL))
        at = k * CONTEXTS
        out[at : at + INNER, :], out[at + INNER : at + LOCAL, :], out[at + LOCAL : at + CONTEXTS, :] = pieces


def merge_rest_kernel(mine, theirs, out):
    rows = mine.shape[0]
    inner = rows - EDGE // 2
    pieces = merge(mine, theirs, slice(0, inner), slice(inner, rows))
    out[:inner, :], out[inner:rows, :], out[rows:, :] = pieces


def gather_quarters(pieces, quarters):
    place = lax.axis_index("seq")
    low, high = place & 1, (place >> 1) & 1
    for piece, x, y in zip(pieces, (0, 0, 1, 1), (0, 1, 0, 1)):
        quarters[(low ^ x) * 2 + (high ^ y)] = piece[...]


def last_layer_kernel(
    piece_00, piece_01, piece_10, piece_11, level_high, level_low, partner_high, partner_low, second_high, second_low,
    g_conv_out, g_mix_out, g_bias, partial,
    quarters, g_conv, g_mix, out_sems,
):
    store = Fetch(out_sems)
    gather_quarters((piece_00, piece_01, piece_10, piece_11), quarters)
    level = (level_high[...], level_low[...])
    partner = (partner_high[...], partner_low[...])
    grad_level = None
    for k in range(3):
        piece = jnp.concatenate([quarters[q, k * CONTEXTS : (k + 1) * CONTEXTS, :] for q in range(4)], axis=1)
        pair = split(piece)
        g_conv[k] = dot3(level, pair, 0, 0)
        store.start(g_conv.at[k], g_conv_out.at[1, k])
        part = dot3(pair, (second_high[k], second_low[k]))
        grad_level = part if grad_level is None else grad_level + part
        if k == 1:
            g_bias[...] = jnp.sum(piece, axis=0, keepdims=True)
            g_mix[...] = dot3(partner, pair, 0, 0)
            store.start(g_mix, g_mix_out.at[1])
            grad_level = grad_level + dot2(permutation(), split(dot3(pair, (second_high[3], second_low[3]))))
    partial[...] = grad_level
    store.wait(*range(len(store.copies)))


def first_layer_kernel(
    piece_00, piece_01, piece_10, piece_11, partial, mixed_table, bias_row, embed, first_high, first_low, turn_high, turn_low,
    g_conv_in, g_mix_in, g_conv_out, g_mix_out, g_embed, g_bias, g_out_out,
    quarters, g_conv, g_mix, g_out, out_sems,
):
    channels = embed.shape[1]
    store = Fetch(out_sems)
    gather_quarters((piece_00, piece_01, piece_10, piece_11), quarters)
    side = channels // 4
    half = INNER // 2
    inner, left, right = [], [], []
    for h in range(2):
        lanes = slice(h * 128, (h + 1) * 128)
        for q in range(4):
            g_out[1, q * side : (q + 1) * side, lanes] = quarters[q, h * side : (h + 1) * side, :]
        at = 2 * side
        low, high = quarters[2 * h], quarters[2 * h + 1]
        pick = lambda begin, rows: jnp.concatenate([low[begin : begin + rows], high[begin : begin + rows]], axis=0)
        inner.append(pick(at, half))
        left.append(pick(at + half, EDGE // 2))
        right.append(pick(at + half + EDGE // 2, EDGE // 2))
    store.start(g_out.at[1], g_out_out.at[1])
    rest = jnp.concatenate([jnp.concatenate(x, axis=1) for x in (inner, left, right)], axis=0)
    grad_level = split(partial[...] + rest)
    tanh_part, sig_part = gates(mixed_table[...])
    hidden = split(tanh_part * sig_part)
    grad_hidden = dot3(grad_level, (turn_high[...], turn_low[...]))
    grad_mixed = jnp.concatenate(gate_grads(grad_hidden, tanh_part, sig_part), axis=1)
    hot = letter_hot()
    by_letter = dot2(hot, split(grad_mixed), 0, 0)
    base = split(padded_base(embed))
    stacked = jnp.concatenate([base[0].astype(F32), base[0].astype(F32), base[1].astype(F32)], axis=0).astype(BF16)
    pieces = []
    for k in range(4):
        piece = split(by_letter[k * 8 : (k + 1) * 8, :])
        pieces.append(piece)
        high, low = piece[0].astype(F32), piece[1].astype(F32)
        value = dot(stacked, jnp.concatenate([high, low, high], axis=0).astype(BF16), 0, 0)
        if k < 3:
            g_conv[k] = value
            store.start(g_conv.at[k], g_conv_out.at[0, k])
        else:
            g_mix[...] = value
            store.start(g_mix, g_mix_out.at[0])
    g_out[0] = dot3(hidden, grad_level, 0, 0)
    store.start(g_out.at[0], g_out_out.at[0])
    grad_base = dot2(hot[:, 8:16], grad_level, 0, 0)
    for k in range(4):
        grad_base = grad_base + dot3(pieces[k], (first_high[k], first_low[k]))
    g_embed[...] = grad_base[:4, :]
    g_bias[0:1, :] = jnp.sum(grad_mixed, axis=0, keepdims=True)
    g_bias[1:2, :] = bias_row[...]
    store.wait(*range(len(store.copies)))


VMEM, SMEM, HBM = pltpu.VMEM, pltpu.SMEM, pltpu.HBM


def call(kernel, ins, outs, scratch=(), aliases=None):
    run = pl.pallas_call(
        kernel,
        out_shape=[space(shape, kind) for shape, kind, space in outs],
        in_specs=[pl.BlockSpec(memory_space=space) for space in ins],
        out_specs=[pl.BlockSpec(memory_space=space) for _, _, space in outs],
        scratch_shapes=list(scratch),
        input_output_aliases=aliases or {},
        compiler_params=pltpu.CompilerParams(vmem_limit_bytes=VMEM_LIMIT),
    )

    def placed(*args):
        return run(*[pltpu.with_memory_space_constraint(x, HBM) if space is HBM else x for x, space in zip(args, ins)])

    return placed


def swapped(value, mask):
    pairs = [(source, source ^ mask) for source in range(lax.axis_size("seq"))]
    return lax.ppermute(value, "seq", pairs)


def crossed(piece, count, rest):
    mask = 4
    while mask < count // 2:
        piece = piece + swapped(piece, mask)
        mask *= 2
    return rest(piece, swapped(piece, mask))


def spread(piece):
    piece_10 = swapped(piece, 1)
    piece_01 = swapped(piece, 2)
    return piece, piece_01, piece_10, swapped(piece_01, 1)


def on_device(
    tokens, dilations, embed, conv_weight, mix_weight, gate_bias, out_weight, cot_fwd, cot_rev
):
    channels = embed.shape[1]
    wide = 2 * channels
    length = tokens.shape[0]
    count = lax.axis_size("seq")
    sems = pltpu.SemaphoreType.DMA

    known = tokens.reshape(1, length)
    parts = [known]
    mask = 1
    while mask < count:
        parts.append(swapped(known, mask))
        mask *= 2
        if mask < count:
            known = jnp.concatenate([known, parts[-1]], axis=0)

    deep = -(-TAPS // 128) * 128
    table, local, mixed_table, pre_high, pre_low = call(
        tables_kernel,
        [HBM] * 5,
        [
            ((CONTEXTS, channels), F32, VMEM),
            ((LOCAL, channels), F32, VMEM),
            ((CONTEXTS, wide), F32, VMEM),
            ((deep, wide), BF16, VMEM),
            ((deep, wide), BF16, VMEM),
        ],
        [
            VMEM(embed.shape, F32),
            VMEM(conv_weight.shape, F32),
            VMEM(mix_weight.shape, F32),
            VMEM(gate_bias.shape, F32),
            VMEM((channels, channels), F32),
            sems((11,)),
        ],
    )(embed, conv_weight, mix_weight, gate_bias, out_weight)

    keep_x, send_x, *hidden_cot, center = call(
        lambda *refs: main_kernel(count, *refs),
        [SMEM] + [VMEM] * (len(parts) + 2) + [HBM] * 3,
        [((2, TAPS, 128), F32, VMEM)] * 2
        + [((2 * length, channels), BF16, VMEM)] * 4
        + [((2, length), jnp.int32, VMEM)],
        [
            VMEM((4, TAPS, 128), F32),
            VMEM((channels, channels), F32),
            VMEM((2, length, channels), F32),
            sems((3,)),
        ],
    )(dilations, *parts, pre_high, pre_low, out_weight, cot_fwd, cot_rev)

    halve_x = call(halve_kernel, [VMEM] * 2, [((TAPS, 128), F32, VMEM)] * 2)
    keep_x, send_x = halve_x(keep_x, swapped(send_x, 1))

    rest_rows = channels // 2 + LOCAL // 2
    keep_y, send_y, out_fwd, out_rev = call(
        outputs_kernel,
        [VMEM] * 6 + [HBM, VMEM],
        [((2, rest_rows, 128), F32, VMEM)] * 2 + [((length, channels), F32, HBM)] * 2,
        [
            VMEM((4, rest_rows, 128), F32),
            VMEM((channels, channels), F32),
            VMEM((2, length, channels), F32),
            sems((3,)),
        ],
    )(center, *hidden_cot, local, out_weight, keep_x)
    halve_y = call(halve_kernel, [VMEM] * 2, [((rest_rows, 128), F32, VMEM)] * 2)
    keep_y, send_y = halve_y(keep_y, swapped(send_y, 1))

    first_high, first_low, second_high, second_low, turn_high, turn_low, *levels = call(
        prepare_kernel,
        [HBM] * 3 + [VMEM] * 2,
        [((4, wide, channels), BF16, VMEM)] * 4
        + [((channels, channels), BF16, VMEM)] * 2
        + [((CONTEXTS, channels), BF16, VMEM)] * 4,
        [
            VMEM(conv_weight.shape, F32),
            VMEM(mix_weight.shape, F32),
            VMEM((channels, channels), F32),
            sems((9,)),
        ],
    )(conv_weight, mix_weight, out_weight, table, keep_y)

    merge_x = call(merge_taps_kernel, [VMEM] * 3, [((3 * CONTEXTS, 128), F32, VMEM)])
    merge_y = call(merge_rest_kernel, [VMEM] * 2, [((rest_rows + EDGE // 2, 128), F32, VMEM)])
    piece_x = crossed(keep_x + swapped(send_x, 2), count, lambda a, b: merge_x(a, b, turn_low)[0])
    pieces_x = spread(piece_x)
    piece_y = crossed(keep_y + swapped(send_y, 2), count, lambda a, b: merge_y(a, b)[0])
    pieces_y = spread(piece_y)

    g_conv, g_mix, bias_row, partial = call(
        last_layer_kernel,
        [VMEM] * 10,
        [
            (conv_weight.shape, F32, HBM),
            (mix_weight.shape, F32, HBM),
            ((1, wide), F32, VMEM),
            ((CONTEXTS, channels), F32, VMEM),
        ],
        [
            VMEM((4, 3 * CONTEXTS, 128), F32),
            VMEM(conv_weight.shape[1:], F32),
            VMEM(mix_weight.shape[1:], F32),
            sems((4,)),
        ],
    )(*pieces_x, *levels, second_high, second_low)

    g_conv, g_mix, g_embed, g_bias, g_out = call(
        first_layer_kernel,
        [VMEM] * 12 + [HBM] * 2,
        [
            (conv_weight.shape, F32, HBM),
            (mix_weight.shape, F32, HBM),
            (embed.shape, F32, VMEM),
            (gate_bias.shape, F32, VMEM),
            (out_weight.shape, F32, HBM),
        ],
        [
            VMEM((4, rest_rows + EDGE // 2, 128), F32),
            VMEM(conv_weight.shape[1:], F32),
            VMEM(mix_weight.shape[1:], F32),
            VMEM(out_weight.shape, F32),
            sems((6,)),
        ],
        aliases={12: 0, 13: 1},
    )(*pieces_y, partial, mixed_table, bias_row, embed, first_high, first_low, turn_high, turn_low, g_conv, g_mix)
    return (out_fwd, out_rev, g_embed, g_conv, g_mix, g_bias, g_out)


def solution(mesh):
    in_specs = (
        P(("dp", "seq")),
        P(),
        P(),
        P(),
        P(),
        P(),
        P(),
        P(("dp", "seq"), None),
        P(("dp", "seq"), None),
    )
    out_specs = (
        P(("dp", "seq"), None),
        P(("dp", "seq"), None),
        P("dp", None),
        P("dp", None, None, None),
        P("dp", None, None),
        P("dp", None),
        P("dp", None, None),
    )
    return jax.shard_map(
        on_device, mesh=mesh, in_specs=in_specs, out_specs=out_specs, check_vma=False
    )
```

```python
import jax
import jax.numpy as jnp
from jax import lax
from jax.experimental import pallas as pl
from jax.experimental.pallas import tpu as pltpu
from jax.sharding import PartitionSpec as P

CONTEXTS = 96
INNER = 64
EDGE = 16
LOCAL = INNER + EDGE
TAPS = 3 * LOCAL
HALO = 128
F32 = jnp.float32
BF16 = jnp.bfloat16
VMEM_LIMIT = 40 * 1024 * 1024


def split(x):
    high = x.astype(BF16)
    return high, (x - high.astype(F32)).astype(BF16)


def dot(a, b, ca=1, cb=0):
    return lax.dot_general(a, b, (((ca,), (cb,)), ((), ())), preferred_element_type=F32)


def dot2(exact, pair, ca=1, cb=0):
    return dot(exact, pair[0], ca, cb) + dot(exact, pair[1], ca, cb)


def dot3(a, b, ca=1, cb=0):
    return dot(a[0], b[0], ca, cb) + (dot(a[0], b[1], ca, cb) + dot(a[1], b[0], ca, cb))


def letters(index):
    inner = index < 64
    left = (index >= 64) & (index < 80)
    low = index & 3
    mid = (index >> 2) & 3
    l = jnp.where(inner, (index >> 4) & 3, jnp.where(left, -1, mid))
    m = jnp.where(inner | left, mid, low)
    r = jnp.where(inner | left, low, -1)
    return l, m, r


def mirrored(index):
    low = 3 - (index & 3)
    mid = 3 - ((index >> 2) & 3)
    high = 3 - ((index >> 4) & 3)
    inner = low * 16 + mid * 4 + high
    left = 80 + low * 4 + mid
    right = 64 + low * 4 + mid
    return jnp.where(index < 64, inner, jnp.where(index < 80, left, right))


def permutation():
    rows = lax.broadcasted_iota(jnp.int32, (CONTEXTS, CONTEXTS), 0)
    cols = lax.broadcasted_iota(jnp.int32, (CONTEXTS, CONTEXTS), 1)
    return (mirrored(rows) == cols).astype(F32).astype(BF16)


def letter_hot():
    rows = lax.broadcasted_iota(jnp.int32, (CONTEXTS, 32), 0)
    cols = lax.broadcasted_iota(jnp.int32, (CONTEXTS, 32), 1)
    l, m, r = letters(rows)
    kind = cols >> 3
    value = jnp.where(kind == 0, l, jnp.where(kind == 1, m, jnp.where(kind == 2, r, 3 - m)))
    return (value == (cols & 7)).astype(F32).astype(BF16)


def gates(mixed):
    channels = mixed.shape[1] // 2
    tanh_part = jnp.tanh(mixed[:, :channels])
    sig_part = 0.5 + 0.5 * jnp.tanh(0.5 * mixed[:, channels:])
    return tanh_part, sig_part


def gate_grads(grad_hidden, tanh_part, sig_part):
    scaled = grad_hidden * sig_part
    return scaled * (1.0 - tanh_part * tanh_part), scaled * tanh_part * (1.0 - sig_part)


class Fetch:
    def __init__(self, sems):
        self.sems = sems
        self.copies = []

    def start(self, source, target):
        copy = pltpu.make_async_copy(source, target, self.sems.at[len(self.copies)])
        copy.start()
        self.copies.append(copy)
        return len(self.copies) - 1

    def wait(self, *which):
        for at in which:
            self.copies[at].wait()


def padded_base(embed):
    return jnp.concatenate([embed[...], jnp.zeros((4, embed.shape[1]), F32)], axis=0)


def left_side():
    return lax.axis_index("seq") * 2 < lax.axis_size("seq")


def local_rows(rows):
    edge = jnp.where(left_side(), rows[INNER : INNER + EDGE], rows[INNER + EDGE : INNER + 2 * EDGE])
    return jnp.concatenate([rows[:INNER], edge], axis=0)


def join_kernel(first, second, after, out):
    rows = first.shape[0]
    out[:rows, :] = first[...]
    out[rows:, :] = second[...]


def load_kernel(source, out, sems):
    fetch = Fetch(sems)
    fetch.start(source, out)
    fetch.wait(0)


def touch_kernel(value, after, out):
    out[...] = value[...]


def first_tables_kernel(
    embed_in, conv_in, mix_in, bias_in, out_in, after, table, local, mixed_table, conv, mix, bias, out_w, embed, sems,
):
    fetch = Fetch(sems)
    small = [fetch.start(embed_in, embed), fetch.start(bias_in, bias)]
    first = [fetch.start(conv_in.at[0, k], conv.at[0, k]) for k in range(3)]
    first += [fetch.start(mix_in.at[0], mix.at[0])]
    turn = fetch.start(out_in.at[0], out_w)
    second = [fetch.start(conv_in.at[1, k], conv.at[1, k]) for k in range(3)]
    second += [fetch.start(mix_in.at[1], mix.at[1])]
    hot = letter_hot()
    fetch.wait(*small)
    base = split(padded_base(embed))
    taps = []
    for k in range(4):
        fetch.wait(first[k])
        taps.append(dot3(base, split(conv[0, k] if k < 3 else mix[0])))
    taps = jnp.concatenate(taps, axis=0)
    mixed = dot2(hot, split(taps)) + bias[0:1, :]
    tanh_part, sig_part = gates(mixed)
    hidden = tanh_part * sig_part
    own = dot2(hot[:, 8:16], base)
    fetch.wait(turn)
    level = own + dot3(split(hidden), split(out_w[...]))
    table[...] = level
    local[...] = local_rows(level)
    mixed_table[...] = mixed
    fetch.wait(*second)


def second_tables_kernel(
    table, conv, mix, bias, out_in, cot_fwd_in, cot_rev_in, after, pre_high, pre_low, cot_high, cot_low, grad_hidden,
    out_w, cots, sems,
):
    length = cots.shape[1]
    fetch = Fetch(sems)
    fetch.start(out_in.at[1], out_w)
    fetch.start(cot_fwd_in, cots.at[0])
    fetch.start(cot_rev_in, cots.at[1])
    level = split(table[...])
    swap = permutation()
    partner = tuple(dot(swap, piece).astype(BF16) for piece in level)
    pre_high[TAPS:, :] = jnp.zeros((pre_high.shape[0] - TAPS, pre_high.shape[1]), BF16)
    pre_low[TAPS:, :] = jnp.zeros((pre_low.shape[0] - TAPS, pre_low.shape[1]), BF16)
    for k in range(3):
        value = dot3(level, split(conv[1, k]))
        if k == 1:
            value = value + dot3(partner, split(mix[1])) + bias[1:2, :]
        high, low = split(local_rows(value))
        pre_high[k * LOCAL : (k + 1) * LOCAL, :] = high
        pre_low[k * LOCAL : (k + 1) * LOCAL, :] = low
    fetch.wait(0)
    weight = split(out_w[...])
    for strand in range(2):
        rows = slice(strand * length, (strand + 1) * length)
        fetch.wait(1 + strand)
        cot = split(cots[strand])
        cot_high[rows, :] = cot[0]
        cot_low[rows, :] = cot[1]
        grad_hidden[rows, :] = dot3(cot, weight, 1, 1)


def windows(parts, count):
    length = parts[0].shape[1]
    place = lax.axis_index("seq")
    last = count - 1

    def block(at):
        total, begin = None, 0
        for part in parts:
            rows = lax.broadcasted_iota(jnp.int32, part.shape, 0) + begin
            piece = jnp.sum(jnp.where(rows == (place ^ at), part[...], 0), axis=0, keepdims=True)
            total = piece if total is None else total + piece
            begin += part.shape[0]
        return total

    def window(at):
        before = jnp.where(at == 0, -1, block(jnp.maximum(at - 1, 0))[:, length - HALO :])
        after = jnp.where(at == last, -1, block(jnp.minimum(at + 1, last))[:, :HALO])
        return [before, block(at), after]

    fwd = jnp.concatenate(window(place), axis=1)
    rev = jnp.concatenate(window(last - place), axis=1)
    rev = jnp.where(rev < 0, -1, 3 - rev)
    tiles = rev.shape[1] // 128
    blocks = [rev[:, i * 128 : (i + 1) * 128] for i in reversed(range(tiles))]
    blocks += [jnp.zeros((8 - tiles, 128), jnp.int32)]
    stacked = jnp.concatenate(blocks, axis=0).astype(F32).astype(BF16)
    rows = lax.broadcasted_iota(jnp.int32, (128, 128), 0)
    cols = lax.broadcasted_iota(jnp.int32, (128, 128), 1)
    flip = (rows + cols == 127).astype(F32).astype(BF16)
    turned = dot(stacked, flip).astype(jnp.int32)
    rev = jnp.concatenate([turned[i : i + 1, :] for i in range(tiles)], axis=1)
    return fwd, rev


def local_contexts(window, first, second, length):
    width = window.shape[1]
    base = jnp.broadcast_to(window, (8, width))
    l = pltpu.roll(base, first, 1)
    r = pltpu.roll(base, width - first, 1)
    index = jnp.where(l < 0, INNER + base * 4 + r, jnp.where(r < 0, INNER + l * 4 + base, l * 16 + base * 4 + r))
    index = jnp.where(base < 0, LOCAL, index)
    before = pltpu.roll(index, second, 1)
    after = pltpu.roll(index, width - second, 1)
    return [x[0:1, HALO : HALO + length] for x in (before, index, after)]


def hot_rows(index):
    rows = lax.broadcasted_iota(jnp.int32, (LOCAL, index.shape[1]), 0)
    return (rows == index).astype(F32).astype(BF16)


def deal(quarters, keep, send):
    bit = lax.axis_index("seq") & 1
    keep[...] = quarters[pl.ds(bit * 2, 2)]
    send[...] = quarters[pl.ds((1 - bit) * 2, 2)]


def main_kernel(count, dil, *refs):
    parts, refs = refs[: count.bit_length()], refs[count.bit_length() :]
    pre_high, pre_low, grad_hidden, keep, send, hidden_high, hidden_low, center, quarters = refs
    length = parts[0].shape[1]
    pre = (pre_high[...], pre_low[...])
    both = windows(parts, count)
    pad = jnp.zeros((pre_high.shape[0] - TAPS, length), BF16)
    total = None
    for strand in range(2):
        index = local_contexts(both[strand], dil[0], dil[1], length)
        hot = jnp.concatenate([hot_rows(x) for x in index] + [pad], axis=0)
        center[strand : strand + 1, :] = index[1]
        mixed = dot2(hot, pre, 0, 0)
        tanh_part, sig_part = gates(mixed)
        hidden = split(tanh_part * sig_part)
        rows = slice(strand * length, (strand + 1) * length)
        hidden_high[rows, :] = hidden[0]
        hidden_low[rows, :] = hidden[1]
        grads = split(jnp.concatenate(gate_grads(grad_hidden[rows, :], tanh_part, sig_part), axis=1))
        part = dot2(hot, grads)
        total = part if total is None else total + part
    for q in range(4):
        quarters[q] = total[:TAPS, q * 128 : (q + 1) * 128]
    deal(quarters, keep, send)


def halve_kernel(kept, received, keep, send):
    bit = (lax.axis_index("seq") >> 1) & 1
    send[...] = kept[1 - bit] + received[1 - bit]
    keep[...] = kept[bit] + received[bit]


def outputs_kernel(
    center, hidden_high, hidden_low, cot_high, cot_low, local, out_in, after, keep, send, out_fwd_out, out_rev_out,
    quarters, out_w, out_both, sems,
):
    length = center.shape[1]
    channels = out_w.shape[1]
    fetch = Fetch(sems)
    fetch.start(out_in.at[1], out_w)
    total_o = total_c = None
    hots = []
    for strand in range(2):
        rows = slice(strand * length, (strand + 1) * length)
        hidden = (hidden_high[rows, :], hidden_low[rows, :])
        cot = (cot_high[rows, :], cot_low[rows, :])
        hots.append(hot_rows(center[strand : strand + 1, :]))
        part_o = dot3(hidden, cot, 0, 0)
        part_c = dot2(hots[strand], cot)
        total_o = part_o if total_o is None else total_o + part_o
        total_c = part_c if total_c is None else total_c + part_c
    side = channels // 4
    for q in range(4):
        half = slice((q >> 1) * 128, (q >> 1) * 128 + 128)
        quarters[q, :side, :] = total_o[q * side : (q + 1) * side, :128]
        quarters[q, side : 2 * side, :] = total_o[q * side : (q + 1) * side, 128:]
        at = (q & 1) * INNER // 2
        quarters[q, 2 * side : 2 * side + INNER // 2, :] = total_c[at : at + INNER // 2, half]
        at = INNER + (q & 1) * EDGE // 2
        quarters[q, 2 * side + INNER // 2 :, :] = total_c[at : at + EDGE // 2, half]
    deal(quarters, keep, send)
    fetch.wait(0)
    weight = split(out_w[...])
    level = split(local[...])
    for strand, out in enumerate((out_fwd_out, out_rev_out)):
        rows = slice(strand * length, (strand + 1) * length)
        update = dot3((hidden_high[rows, :], hidden_low[rows, :]), weight)
        out_both[strand] = dot2(hots[strand], level, 0, 0) + update
        fetch.start(out_both.at[strand], out)
    fetch.wait(1, 2)


def prepare_kernel(
    conv, mix, out_w, table, after, first_high, first_low, second_high, second_low, turn_high, turn_low,
    level_high, level_low, partner_high, partner_low,
):
    level = split(table[...])
    swap = permutation()
    level_high[...], level_low[...] = level
    partner_high[...], partner_low[...] = tuple(dot(swap, piece).astype(BF16) for piece in level)
    for layer, high, low in ((1, second_high, second_low), (0, first_high, first_low)):
        for k in range(4):
            high[k], low[k] = split((conv[layer, k] if k < 3 else mix[layer]).T)
    turn_high[...], turn_low[...] = split(out_w[...].T)


def merge(mine, theirs, inner, edge):
    left = left_side()
    both = mine[inner, :] + theirs[inner, :]
    own, other = mine[edge, :], theirs[edge, :]
    return both, jnp.where(left, own, other), jnp.where(left, other, own)


def merge_taps_kernel(mine, theirs, after, after_too, out):
    for k in range(3):
        at = k * LOCAL
        pieces = merge(mine, theirs, slice(at, at + INNER), slice(at + INNER, at + LOCAL))
        at = k * CONTEXTS
        out[at : at + INNER, :], out[at + INNER : at + LOCAL, :], out[at + LOCAL : at + CONTEXTS, :] = pieces


def merge_rest_kernel(mine, theirs, out):
    rows = mine.shape[0]
    inner = rows - EDGE // 2
    pieces = merge(mine, theirs, slice(0, inner), slice(inner, rows))
    out[:inner, :], out[inner:rows, :], out[rows:, :] = pieces


def gather_quarters(pieces, quarters):
    place = lax.axis_index("seq")
    low, high = place & 1, (place >> 1) & 1
    for piece, x, y in zip(pieces, (0, 0, 1, 1), (0, 1, 0, 1)):
        quarters[(low ^ x) * 2 + (high ^ y)] = piece[...]


def last_layer_kernel(
    piece_00, piece_01, piece_10, piece_11, level_high, level_low, partner_high, partner_low, second_high, second_low,
    g_conv_out, g_mix_out, g_bias, partial,
    quarters, g_conv, g_mix, out_sems,
):
    store = Fetch(out_sems)
    gather_quarters((piece_00, piece_01, piece_10, piece_11), quarters)
    level = (level_high[...], level_low[...])
    partner = (partner_high[...], partner_low[...])
    grad_level = None
    for k in range(3):
        piece = jnp.concatenate([quarters[q, k * CONTEXTS : (k + 1) * CONTEXTS, :] for q in range(4)], axis=1)
        pair = split(piece)
        g_conv[k] = dot3(level, pair, 0, 0)
        store.start(g_conv.at[k], g_conv_out.at[1, k])
        part = dot3(pair, (second_high[k], second_low[k]))
        grad_level = part if grad_level is None else grad_level + part
        if k == 1:
            g_bias[...] = jnp.sum(piece, axis=0, keepdims=True)
            g_mix[...] = dot3(partner, pair, 0, 0)
            store.start(g_mix, g_mix_out.at[1])
            grad_level = grad_level + dot2(permutation(), split(dot3(pair, (second_high[3], second_low[3]))))
    partial[...] = grad_level
    store.wait(*range(len(store.copies)))


def first_layer_kernel(
    piece_00, piece_01, piece_10, piece_11, partial, mixed_table, bias_row, embed, first_high, first_low, turn_high, turn_low,
    g_conv_in, g_mix_in, g_conv_out, g_mix_out, g_embed_out, g_bias_out, g_out_out,
    quarters, g_conv, g_mix, g_embed, g_bias, g_out, out_sems,
):
    channels = embed.shape[1]
    store = Fetch(out_sems)
    gather_quarters((piece_00, piece_01, piece_10, piece_11), quarters)
    side = channels // 4
    half = INNER // 2
    inner, left, right = [], [], []
    for h in range(2):
        lanes = slice(h * 128, (h + 1) * 128)
        for q in range(4):
            g_out[1, q * side : (q + 1) * side, lanes] = quarters[q, h * side : (h + 1) * side, :]
        at = 2 * side
        low, high = quarters[2 * h], quarters[2 * h + 1]
        pick = lambda begin, rows: jnp.concatenate([low[begin : begin + rows], high[begin : begin + rows]], axis=0)
        inner.append(pick(at, half))
        left.append(pick(at + half, EDGE // 2))
        right.append(pick(at + half + EDGE // 2, EDGE // 2))
    store.start(g_out.at[1], g_out_out.at[1])
    rest = jnp.concatenate([jnp.concatenate(x, axis=1) for x in (inner, left, right)], axis=0)
    grad_level = split(partial[...] + rest)
    tanh_part, sig_part = gates(mixed_table[...])
    hidden = split(tanh_part * sig_part)
    grad_hidden = dot3(grad_level, (turn_high[...], turn_low[...]))
    grad_mixed = jnp.concatenate(gate_grads(grad_hidden, tanh_part, sig_part), axis=1)
    g_bias[0:1, :] = jnp.sum(grad_mixed, axis=0, keepdims=True)
    g_bias[1:2, :] = bias_row[...]
    store.start(g_bias, g_bias_out)
    hot = letter_hot()
    by_letter = dot2(hot, split(grad_mixed), 0, 0)
    base = split(padded_base(embed))
    stacked = jnp.concatenate([base[0].astype(F32), base[0].astype(F32), base[1].astype(F32)], axis=0).astype(BF16)
    pieces = []
    for k in range(4):
        piece = split(by_letter[k * 8 : (k + 1) * 8, :])
        pieces.append(piece)
        high, low = piece[0].astype(F32), piece[1].astype(F32)
        value = dot(stacked, jnp.concatenate([high, low, high], axis=0).astype(BF16), 0, 0)
        if k < 3:
            g_conv[k] = value
            store.start(g_conv.at[k], g_conv_out.at[0, k])
        else:
            g_mix[...] = value
            store.start(g_mix, g_mix_out.at[0])
    g_out[0] = dot3(hidden, grad_level, 0, 0)
    store.start(g_out.at[0], g_out_out.at[0])
    grad_base = dot2(hot[:, 8:16], grad_level, 0, 0)
    for k in range(4):
        grad_base = grad_base + dot3(pieces[k], (first_high[k], first_low[k]))
    g_embed[...] = grad_base[:4, :]
    store.start(g_embed, g_embed_out)
    store.wait(*range(len(store.copies)))


VMEM, SMEM, HBM = pltpu.VMEM, pltpu.SMEM, pltpu.HBM


def call(kernel, ins, outs, scratch=(), aliases=None):
    run = pl.pallas_call(
        kernel,
        out_shape=[space(shape, kind) for shape, kind, space in outs],
        in_specs=[pl.BlockSpec(memory_space=space) for space in ins],
        out_specs=[pl.BlockSpec(memory_space=space) for _, _, space in outs],
        scratch_shapes=list(scratch),
        input_output_aliases=aliases or {},
        compiler_params=pltpu.CompilerParams(vmem_limit_bytes=VMEM_LIMIT),
    )

    def placed(*args):
        return run(*[pltpu.with_memory_space_constraint(x, HBM) if space is HBM else x for x, space in zip(args, ins)])

    return placed


def swapped(value, mask):
    pairs = [(source, source ^ mask) for source in range(lax.axis_size("seq"))]
    return lax.ppermute(value, "seq", pairs)


def crossed(piece, count, rest):
    mask = 4
    while mask < count // 2:
        piece = piece + swapped(piece, mask)
        mask *= 2
    return rest(piece, swapped(piece, mask))


def on_device(
    tokens, dilations, embed, conv_weight, mix_weight, gate_bias, out_weight, cot_fwd, cot_rev
):
    channels = embed.shape[1]
    wide = 2 * channels
    length = tokens.shape[0]
    count = lax.axis_size("seq")
    sems = pltpu.SemaphoreType.DMA
    square = (channels, channels)

    def touched(value, after):
        return call(touch_kernel, [VMEM] * 2, [(value.shape, value.dtype, VMEM)])(value, after)[0]

    def joined(first, second, after):
        shape = (2 * first.shape[0], first.shape[1])
        return call(join_kernel, [VMEM] * 3, [(shape, first.dtype, VMEM)])(first, second, after)[0]

    known = tokens.reshape(1, length)
    own = call(load_kernel, [HBM], [(known.shape, known.dtype, VMEM)], [sems((1,))])(known)[0]
    parts = [own, swapped(known, 1)]
    known = joined(own, parts[-1], own)
    parts.append(swapped(known, 2))
    table, local, mixed_table, conv, mix, bias, turn = call(
        first_tables_kernel,
        [HBM] * 5 + [VMEM],
        [
            ((CONTEXTS, channels), F32, VMEM),
            ((LOCAL, channels), F32, VMEM),
            ((CONTEXTS, wide), F32, VMEM),
            (conv_weight.shape, F32, VMEM),
            (mix_weight.shape, F32, VMEM),
            (gate_bias.shape, F32, VMEM),
            (square, F32, VMEM),
        ],
        [VMEM(embed.shape, F32), sems((11,))],
    )(embed, conv_weight, mix_weight, gate_bias, out_weight, known)
    known = joined(known, parts[-1], table)
    parts.append(swapped(known, 4))
    deep = -(-TAPS // 128) * 128
    pre_high, pre_low, cot_high, cot_low, grad_hidden = call(
        second_tables_kernel,
        [VMEM] * 4 + [HBM] * 3 + [VMEM],
        [((deep, wide), BF16, VMEM)] * 2
        + [((2 * length, channels), BF16, VMEM)] * 2
        + [((2 * length, channels), F32, VMEM)],
        [VMEM(square, F32), VMEM((2, length, channels), F32), sems((3,))],
    )(table, conv, mix, bias, out_weight, cot_fwd, cot_rev, known)
    mask = 8
    while mask < count:
        known = joined(known, parts[-1], pre_low)
        parts.append(swapped(known, mask))
        mask *= 2

    keep_x, send_x, hidden_high, hidden_low, center = call(
        lambda *refs: main_kernel(count, *refs),
        [SMEM] + [VMEM] * (len(parts) + 3),
        [((2, TAPS, 128), F32, VMEM)] * 2
        + [((2 * length, channels), BF16, VMEM)] * 2
        + [((2, length), jnp.int32, VMEM)],
        [VMEM((4, TAPS, 128), F32)],
    )(dilations, *parts, pre_high, pre_low, grad_hidden)

    halve_x = call(halve_kernel, [VMEM] * 2, [((TAPS, 128), F32, VMEM)] * 2)
    keep_x, send_x = halve_x(keep_x, swapped(send_x, 1))

    rest_rows = channels // 2 + LOCAL // 2
    keep_y, send_y, out_fwd, out_rev = call(
        outputs_kernel,
        [VMEM] * 6 + [HBM, VMEM],
        [((2, rest_rows, 128), F32, VMEM)] * 2 + [((length, channels), F32, HBM)] * 2,
        [
            VMEM((4, rest_rows, 128), F32),
            VMEM(square, F32),
            VMEM((2, length, channels), F32),
            sems((3,)),
        ],
    )(center, hidden_high, hidden_low, cot_high, cot_low, local, out_weight, keep_x)
    halve_y = call(halve_kernel, [VMEM] * 2, [((rest_rows, 128), F32, VMEM)] * 2)
    keep_y, send_y = halve_y(keep_y, swapped(send_y, 1))

    first_high, first_low, second_high, second_low, turn_high, turn_low, *levels = call(
        prepare_kernel,
        [VMEM] * 5,
        [((4, wide, channels), BF16, VMEM)] * 4
        + [(square, BF16, VMEM)] * 2
        + [((CONTEXTS, channels), BF16, VMEM)] * 4,
    )(conv, mix, turn, table, keep_y)

    merge_x = call(merge_taps_kernel, [VMEM] * 4, [((3 * CONTEXTS, 128), F32, VMEM)])
    merge_y = call(merge_rest_kernel, [VMEM] * 2, [((rest_rows + EDGE // 2, 128), F32, VMEM)])
    sum_x = keep_x + swapped(send_x, 2)
    sum_y = keep_y + swapped(send_y, 2)
    piece_x = crossed(sum_x, count, lambda a, b: merge_x(a, b, turn_low, sum_y)[0])
    piece_y = crossed(sum_y, count, lambda a, b: merge_y(a, b)[0])
    piece_x01 = swapped(piece_x, 2)
    pieces_x = piece_x, piece_x01, swapped(piece_x, 1), swapped(piece_x01, 1)

    g_conv, g_mix, bias_row, partial = call(
        last_layer_kernel,
        [VMEM] * 10,
        [
            (conv_weight.shape, F32, HBM),
            (mix_weight.shape, F32, HBM),
            ((1, wide), F32, VMEM),
            ((CONTEXTS, channels), F32, VMEM),
        ],
        [
            VMEM((4, 3 * CONTEXTS, 128), F32),
            VMEM(conv_weight.shape[1:], F32),
            VMEM(mix_weight.shape[1:], F32),
            sems((4,)),
        ],
    )(*pieces_x, *levels, second_high, second_low)

    piece_y01 = touched(swapped(piece_y, 2), partial)
    pieces_y = piece_y, piece_y01, swapped(piece_y, 1), swapped(piece_y01, 1)
    g_conv, g_mix, g_embed, g_bias, g_out = call(
        first_layer_kernel,
        [VMEM] * 12 + [HBM] * 2,
        [
            (conv_weight.shape, F32, HBM),
            (mix_weight.shape, F32, HBM),
            (embed.shape, F32, HBM),
            (gate_bias.shape, F32, HBM),
            (out_weight.shape, F32, HBM),
        ],
        [
            VMEM((4, rest_rows + EDGE // 2, 128), F32),
            VMEM(conv_weight.shape[1:], F32),
            VMEM(mix_weight.shape[1:], F32),
            VMEM(embed.shape, F32),
            VMEM(gate_bias.shape, F32),
            VMEM(out_weight.shape, F32),
            sems((8,)),
        ],
        aliases={12: 0, 13: 1},
    )(*pieces_y, partial, mixed_table, bias_row, embed, first_high, first_low, turn_high, turn_low, g_conv, g_mix)
    return (out_fwd, out_rev, g_embed, g_conv, g_mix, g_bias, g_out)


def solution(mesh):
    in_specs = (
        P(("dp", "seq")),
        P(),
        P(),
        P(),
        P(),
        P(),
        P(),
        P(("dp", "seq"), None),
        P(("dp", "seq"), None),
    )
    out_specs = (
        P(("dp", "seq"), None),
        P(("dp", "seq"), None),
        P("dp", None),
        P("dp", None, None, None),
        P("dp", None, None),
        P("dp", None),
        P("dp", None, None),
    )
    return jax.shard_map(
        on_device, mesh=mesh, in_specs=in_specs, out_specs=out_specs, check_vma=False
    )
```

```python
import jax
import jax.numpy as jnp
from jax import lax
from jax.experimental import pallas as pl
from jax.experimental.pallas import tpu as pltpu
from jax.sharding import PartitionSpec as P

CONTEXTS = 96
INNER = 64
EDGE = 16
LOCAL = INNER + EDGE
TAPS = 3 * LOCAL
HALO = 128
F32 = jnp.float32
BF16 = jnp.bfloat16
VMEM_LIMIT = 40 * 1024 * 1024


def split(x):
    high = x.astype(BF16)
    return high, (x - high.astype(F32)).astype(BF16)


def dot(a, b, ca=1, cb=0):
    return lax.dot_general(a, b, (((ca,), (cb,)), ((), ())), preferred_element_type=F32)


def dot2(exact, pair, ca=1, cb=0):
    return dot(exact, pair[0], ca, cb) + dot(exact, pair[1], ca, cb)


def dot3(a, b, ca=1, cb=0):
    return dot(a[0], b[0], ca, cb) + (dot(a[0], b[1], ca, cb) + dot(a[1], b[0], ca, cb))


def letters(index):
    inner = index < 64
    left = (index >= 64) & (index < 80)
    low = index & 3
    mid = (index >> 2) & 3
    l = jnp.where(inner, (index >> 4) & 3, jnp.where(left, -1, mid))
    m = jnp.where(inner | left, mid, low)
    r = jnp.where(inner | left, low, -1)
    return l, m, r


def mirrored(index):
    low = 3 - (index & 3)
    mid = 3 - ((index >> 2) & 3)
    high = 3 - ((index >> 4) & 3)
    inner = low * 16 + mid * 4 + high
    left = 80 + low * 4 + mid
    right = 64 + low * 4 + mid
    return jnp.where(index < 64, inner, jnp.where(index < 80, left, right))


def permutation():
    rows = lax.broadcasted_iota(jnp.int32, (CONTEXTS, CONTEXTS), 0)
    cols = lax.broadcasted_iota(jnp.int32, (CONTEXTS, CONTEXTS), 1)
    return (mirrored(rows) == cols).astype(F32).astype(BF16)


def letter_hot():
    rows = lax.broadcasted_iota(jnp.int32, (CONTEXTS, 32), 0)
    cols = lax.broadcasted_iota(jnp.int32, (CONTEXTS, 32), 1)
    l, m, r = letters(rows)
    kind = cols >> 3
    value = jnp.where(kind == 0, l, jnp.where(kind == 1, m, jnp.where(kind == 2, r, 3 - m)))
    return (value == (cols & 7)).astype(F32).astype(BF16)


def gates(mixed):
    channels = mixed.shape[1] // 2
    tanh_part = jnp.tanh(mixed[:, :channels])
    sig_part = 0.5 + 0.5 * jnp.tanh(0.5 * mixed[:, channels:])
    return tanh_part, sig_part


def gate_grads(grad_hidden, tanh_part, sig_part):
    scaled = grad_hidden * sig_part
    return scaled * (1.0 - tanh_part * tanh_part), scaled * tanh_part * (1.0 - sig_part)


class Fetch:
    def __init__(self, sems):
        self.sems = sems
        self.copies = []

    def start(self, source, target):
        copy = pltpu.make_async_copy(source, target, self.sems.at[len(self.copies)])
        copy.start()
        self.copies.append(copy)
        return len(self.copies) - 1

    def wait(self, *which):
        for at in which:
            self.copies[at].wait()


def padded_base(embed):
    return jnp.concatenate([embed[...], jnp.zeros((4, embed.shape[1]), F32)], axis=0)


def left_side():
    return lax.axis_index("seq") * 2 < lax.axis_size("seq")


def local_rows(rows):
    edge = jnp.where(left_side(), rows[INNER : INNER + EDGE], rows[INNER + EDGE : INNER + 2 * EDGE])
    return jnp.concatenate([rows[:INNER], edge], axis=0)


def join_kernel(first, second, after, out):
    rows = first.shape[0]
    out[:rows, :] = first[...]
    out[rows:, :] = second[...]


def load_kernel(source, out, sems):
    fetch = Fetch(sems)
    fetch.start(source, out)
    fetch.wait(0)


def touch_kernel(value, after, out):
    out[...] = value[...]


def first_tables_kernel(
    embed_in, conv_in, mix_in, bias_in, out_in, after, table, local, mixed_table, conv, mix, bias, out_w, embed, sems,
):
    fetch = Fetch(sems)
    small = [fetch.start(embed_in, embed), fetch.start(bias_in, bias)]
    first = [fetch.start(conv_in.at[0, k], conv.at[0, k]) for k in range(3)]
    first += [fetch.start(mix_in.at[0], mix.at[0])]
    turn = fetch.start(out_in.at[0], out_w)
    second = [fetch.start(conv_in.at[1, k], conv.at[1, k]) for k in range(3)]
    second += [fetch.start(mix_in.at[1], mix.at[1])]
    hot = letter_hot()
    fetch.wait(*small)
    base = split(padded_base(embed))
    taps = []
    for k in range(4):
        fetch.wait(first[k])
        taps.append(dot3(base, split(conv[0, k] if k < 3 else mix[0])))
    taps = jnp.concatenate(taps, axis=0)
    mixed = dot2(hot, split(taps)) + bias[0:1, :]
    tanh_part, sig_part = gates(mixed)
    hidden = tanh_part * sig_part
    own = dot2(hot[:, 8:16], base)
    fetch.wait(turn)
    level = own + dot3(split(hidden), split(out_w[...]))
    table[...] = level
    local[...] = local_rows(level)
    mixed_table[...] = mixed
    fetch.wait(*second)


def second_tables_kernel(
    table, conv, mix, bias, out_in, cot_fwd_in, cot_rev_in, after, pre_high, pre_low, cot_high, cot_low, grad_hidden,
    out_w, cots, sems,
):
    length = cots.shape[1]
    fetch = Fetch(sems)
    fetch.start(out_in.at[1], out_w)
    fetch.start(cot_fwd_in, cots.at[0])
    fetch.start(cot_rev_in, cots.at[1])
    level = split(table[...])
    swap = permutation()
    partner = tuple(dot(swap, piece).astype(BF16) for piece in level)
    pre_high[TAPS:, :] = jnp.zeros((pre_high.shape[0] - TAPS, pre_high.shape[1]), BF16)
    pre_low[TAPS:, :] = jnp.zeros((pre_low.shape[0] - TAPS, pre_low.shape[1]), BF16)
    for k in range(3):
        value = dot3(level, split(conv[1, k]))
        if k == 1:
            value = value + dot3(partner, split(mix[1])) + bias[1:2, :]
        high, low = split(local_rows(value))
        pre_high[k * LOCAL : (k + 1) * LOCAL, :] = high
        pre_low[k * LOCAL : (k + 1) * LOCAL, :] = low
    fetch.wait(0)
    weight = split(out_w[...])
    for strand in range(2):
        rows = slice(strand * length, (strand + 1) * length)
        fetch.wait(1 + strand)
        cot = split(cots[strand])
        cot_high[rows, :] = cot[0]
        cot_low[rows, :] = cot[1]
        grad_hidden[rows, :] = dot3(cot, weight, 1, 1)


def windows(parts, count):
    length = parts[0].shape[1]
    place = lax.axis_index("seq")
    last = count - 1

    def block(at):
        total, begin = None, 0
        for part in parts:
            rows = lax.broadcasted_iota(jnp.int32, part.shape, 0) + begin
            piece = jnp.sum(jnp.where(rows == (place ^ at), part[...], 0), axis=0, keepdims=True)
            total = piece if total is None else total + piece
            begin += part.shape[0]
        return total

    def window(at):
        before = jnp.where(at == 0, -1, block(jnp.maximum(at - 1, 0))[:, length - HALO :])
        after = jnp.where(at == last, -1, block(jnp.minimum(at + 1, last))[:, :HALO])
        return [before, block(at), after]

    fwd = jnp.concatenate(window(place), axis=1)
    rev = jnp.concatenate(window(last - place), axis=1)
    rev = jnp.where(rev < 0, -1, 3 - rev)
    tiles = rev.shape[1] // 128
    blocks = [rev[:, i * 128 : (i + 1) * 128] for i in reversed(range(tiles))]
    blocks += [jnp.zeros((8 - tiles, 128), jnp.int32)]
    stacked = jnp.concatenate(blocks, axis=0).astype(F32).astype(BF16)
    rows = lax.broadcasted_iota(jnp.int32, (128, 128), 0)
    cols = lax.broadcasted_iota(jnp.int32, (128, 128), 1)
    flip = (rows + cols == 127).astype(F32).astype(BF16)
    turned = dot(stacked, flip).astype(jnp.int32)
    rev = jnp.concatenate([turned[i : i + 1, :] for i in range(tiles)], axis=1)
    return fwd, rev


def local_contexts(window, first, second, length):
    width = window.shape[1]
    base = jnp.broadcast_to(window, (8, width))
    l = pltpu.roll(base, first, 1)
    r = pltpu.roll(base, width - first, 1)
    index = jnp.where(l < 0, INNER + base * 4 + r, jnp.where(r < 0, INNER + l * 4 + base, l * 16 + base * 4 + r))
    index = jnp.where(base < 0, LOCAL, index)
    before = pltpu.roll(index, second, 1)
    after = pltpu.roll(index, width - second, 1)
    return [x[0:1, HALO : HALO + length] for x in (before, index, after)]


def hot_rows(index):
    rows = lax.broadcasted_iota(jnp.int32, (LOCAL, index.shape[1]), 0)
    return (rows == index).astype(F32).astype(BF16)


def deal(quarters, keep, send):
    bit = lax.axis_index("seq") & 1
    keep[...] = quarters[pl.ds(bit * 2, 2)]
    send[...] = quarters[pl.ds((1 - bit) * 2, 2)]


def main_kernel(count, dil, *refs):
    parts, refs = refs[: count.bit_length()], refs[count.bit_length() :]
    pre_high, pre_low, grad_hidden, keep, send, hidden_high, hidden_low, center, quarters = refs
    length = parts[0].shape[1]
    pre = (pre_high[...], pre_low[...])
    both = windows(parts, count)
    pad = jnp.zeros((pre_high.shape[0] - TAPS, length), BF16)
    total = None
    for strand in range(2):
        index = local_contexts(both[strand], dil[0], dil[1], length)
        hot = jnp.concatenate([hot_rows(x) for x in index] + [pad], axis=0)
        center[strand : strand + 1, :] = index[1]
        mixed = dot2(hot, pre, 0, 0)
        tanh_part, sig_part = gates(mixed)
        hidden = split(tanh_part * sig_part)
        rows = slice(strand * length, (strand + 1) * length)
        hidden_high[rows, :] = hidden[0]
        hidden_low[rows, :] = hidden[1]
        grads = split(jnp.concatenate(gate_grads(grad_hidden[rows, :], tanh_part, sig_part), axis=1))
        part = dot2(hot, grads)
        total = part if total is None else total + part
    for q in range(4):
        quarters[q] = total[:TAPS, q * 128 : (q + 1) * 128]
    deal(quarters, keep, send)


def halve_kernel(kept, received, keep, send):
    bit = (lax.axis_index("seq") >> 1) & 1
    send[...] = kept[1 - bit] + received[1 - bit]
    keep[...] = kept[bit] + received[bit]


def halve_after_kernel(kept, received, after, keep, send):
    halve_kernel(kept, received, keep, send)


def outputs_kernel(
    center, hidden_high, hidden_low, cot_high, cot_low, local, out_in, after, keep, send, out_fwd_out, out_rev_out,
    quarters, out_w, out_both, sems,
):
    length = center.shape[1]
    channels = out_w.shape[1]
    fetch = Fetch(sems)
    fetch.start(out_in.at[1], out_w)
    total_o = total_c = None
    hots = []
    for strand in range(2):
        rows = slice(strand * length, (strand + 1) * length)
        hidden = (hidden_high[rows, :], hidden_low[rows, :])
        cot = (cot_high[rows, :], cot_low[rows, :])
        hots.append(hot_rows(center[strand : strand + 1, :]))
        part_o = dot3(hidden, cot, 0, 0)
        part_c = dot2(hots[strand], cot)
        total_o = part_o if total_o is None else total_o + part_o
        total_c = part_c if total_c is None else total_c + part_c
    side = channels // 4
    for q in range(4):
        half = slice((q >> 1) * 128, (q >> 1) * 128 + 128)
        quarters[q, :side, :] = total_o[q * side : (q + 1) * side, :128]
        quarters[q, side : 2 * side, :] = total_o[q * side : (q + 1) * side, 128:]
        at = (q & 1) * INNER // 2
        quarters[q, 2 * side : 2 * side + INNER // 2, :] = total_c[at : at + INNER // 2, half]
        at = INNER + (q & 1) * EDGE // 2
        quarters[q, 2 * side + INNER // 2 :, :] = total_c[at : at + EDGE // 2, half]
    deal(quarters, keep, send)
    fetch.wait(0)
    weight = split(out_w[...])
    level = split(local[...])
    for strand, out in enumerate((out_fwd_out, out_rev_out)):
        rows = slice(strand * length, (strand + 1) * length)
        update = dot3((hidden_high[rows, :], hidden_low[rows, :]), weight)
        out_both[strand] = dot2(hots[strand], level, 0, 0) + update
        fetch.start(out_both.at[strand], out)
    fetch.wait(1, 2)


def prepare_kernel(
    conv, mix, out_w, table, after, first_high, first_low, second_high, second_low, turn_high, turn_low,
    level_high, level_low, partner_high, partner_low,
):
    level = split(table[...])
    swap = permutation()
    level_high[...], level_low[...] = level
    partner_high[...], partner_low[...] = tuple(dot(swap, piece).astype(BF16) for piece in level)
    for layer, high, low in ((1, second_high, second_low), (0, first_high, first_low)):
        for k in range(4):
            high[k], low[k] = split((conv[layer, k] if k < 3 else mix[layer]).T)
    turn_high[...], turn_low[...] = split(out_w[...].T)


def merge(mine, theirs, inner, edge):
    left = left_side()
    both = mine[inner, :] + theirs[inner, :]
    own, other = mine[edge, :], theirs[edge, :]
    return both, jnp.where(left, own, other), jnp.where(left, other, own)


def merge_taps_kernel(mine, theirs, after, out):
    for k in range(3):
        at = k * LOCAL
        pieces = merge(mine, theirs, slice(at, at + INNER), slice(at + INNER, at + LOCAL))
        at = k * CONTEXTS
        out[at : at + INNER, :], out[at + INNER : at + LOCAL, :], out[at + LOCAL : at + CONTEXTS, :] = pieces


def merge_rest_kernel(mine, theirs, out):
    rows = mine.shape[0]
    inner = rows - EDGE // 2
    pieces = merge(mine, theirs, slice(0, inner), slice(inner, rows))
    out[:inner, :], out[inner:rows, :], out[rows:, :] = pieces


def gather_quarters(pieces, quarters):
    place = lax.axis_index("seq")
    low, high = place & 1, (place >> 1) & 1
    for piece, x, y in zip(pieces, (0, 0, 1, 1), (0, 1, 0, 1)):
        quarters[(low ^ x) * 2 + (high ^ y)] = piece[...]


def last_layer_kernel(
    piece_00, piece_01, piece_10, piece_11, level_high, level_low, partner_high, partner_low, second_high, second_low,
    g_conv_out, g_mix_out, g_bias, partial,
    quarters, g_conv, g_mix, out_sems,
):
    store = Fetch(out_sems)
    gather_quarters((piece_00, piece_01, piece_10, piece_11), quarters)
    level = (level_high[...], level_low[...])
    partner = (partner_high[...], partner_low[...])
    grad_level = None
    for k in range(3):
        piece = jnp.concatenate([quarters[q, k * CONTEXTS : (k + 1) * CONTEXTS, :] for q in range(4)], axis=1)
        pair = split(piece)
        g_conv[k] = dot3(level, pair, 0, 0)
        store.start(g_conv.at[k], g_conv_out.at[1, k])
        part = dot3(pair, (second_high[k], second_low[k]))
        grad_level = part if grad_level is None else grad_level + part
        if k == 1:
            g_bias[...] = jnp.sum(piece, axis=0, keepdims=True)
            g_mix[...] = dot3(partner, pair, 0, 0)
            store.start(g_mix, g_mix_out.at[1])
            grad_level = grad_level + dot2(permutation(), split(dot3(pair, (second_high[3], second_low[3]))))
    partial[...] = grad_level
    store.wait(*range(len(store.copies)))


def first_layer_kernel(
    piece_00, piece_01, piece_10, piece_11, partial, mixed_table, bias_row, embed, first_high, first_low, turn_high, turn_low,
    g_conv_in, g_mix_in, g_conv_out, g_mix_out, g_embed_out, g_bias_out, g_out_out,
    quarters, g_conv, g_mix, g_embed, g_bias, g_out, out_sems,
):
    channels = embed.shape[1]
    store = Fetch(out_sems)
    gather_quarters((piece_00, piece_01, piece_10, piece_11), quarters)
    side = channels // 4
    half = INNER // 2
    inner, left, right = [], [], []
    for h in range(2):
        lanes = slice(h * 128, (h + 1) * 128)
        for q in range(4):
            g_out[1, q * side : (q + 1) * side, lanes] = quarters[q, h * side : (h + 1) * side, :]
        at = 2 * side
        low, high = quarters[2 * h], quarters[2 * h + 1]
        pick = lambda begin, rows: jnp.concatenate([low[begin : begin + rows], high[begin : begin + rows]], axis=0)
        inner.append(pick(at, half))
        left.append(pick(at + half, EDGE // 2))
        right.append(pick(at + half + EDGE // 2, EDGE // 2))
    store.start(g_out.at[1], g_out_out.at[1])
    rest = jnp.concatenate([jnp.concatenate(x, axis=1) for x in (inner, left, right)], axis=0)
    grad_level = split(partial[...] + rest)
    tanh_part, sig_part = gates(mixed_table[...])
    hidden = split(tanh_part * sig_part)
    grad_hidden = dot3(grad_level, (turn_high[...], turn_low[...]))
    grad_mixed = jnp.concatenate(gate_grads(grad_hidden, tanh_part, sig_part), axis=1)
    g_bias[0:1, :] = jnp.sum(grad_mixed, axis=0, keepdims=True)
    g_bias[1:2, :] = bias_row[...]
    store.start(g_bias, g_bias_out)
    hot = letter_hot()
    by_letter = dot2(hot, split(grad_mixed), 0, 0)
    base = split(padded_base(embed))
    stacked = jnp.concatenate([base[0].astype(F32), base[0].astype(F32), base[1].astype(F32)], axis=0).astype(BF16)
    pieces = []
    for k in range(4):
        piece = split(by_letter[k * 8 : (k + 1) * 8, :])
        pieces.append(piece)
        high, low = piece[0].astype(F32), piece[1].astype(F32)
        value = dot(stacked, jnp.concatenate([high, low, high], axis=0).astype(BF16), 0, 0)
        if k < 3:
            g_conv[k] = value
            store.start(g_conv.at[k], g_conv_out.at[0, k])
        else:
            g_mix[...] = value
            store.start(g_mix, g_mix_out.at[0])
    g_out[0] = dot3(hidden, grad_level, 0, 0)
    store.start(g_out.at[0], g_out_out.at[0])
    grad_base = dot2(hot[:, 8:16], grad_level, 0, 0)
    for k in range(4):
        grad_base = grad_base + dot3(pieces[k], (first_high[k], first_low[k]))
    g_embed[...] = grad_base[:4, :]
    store.start(g_embed, g_embed_out)
    store.wait(*range(len(store.copies)))


VMEM, SMEM, HBM = pltpu.VMEM, pltpu.SMEM, pltpu.HBM


def call(kernel, ins, outs, scratch=(), aliases=None, micros=0.001):
    run = pl.pallas_call(
        kernel,
        out_shape=[space(shape, kind) for shape, kind, space in outs],
        in_specs=[pl.BlockSpec(memory_space=space) for space in ins],
        out_specs=[pl.BlockSpec(memory_space=space) for _, _, space in outs],
        scratch_shapes=list(scratch),
        input_output_aliases=aliases or {},
        cost_estimate=pl.CostEstimate(flops=int(micros * 1.1e9), bytes_accessed=int(micros * 3e6), transcendentals=0),
        compiler_params=pltpu.CompilerParams(vmem_limit_bytes=VMEM_LIMIT),
    )

    def placed(*args):
        return run(*[pltpu.with_memory_space_constraint(x, HBM) if space is HBM else x for x, space in zip(args, ins)])

    return placed


def swapped(value, mask):
    pairs = [(source, source ^ mask) for source in range(lax.axis_size("seq"))]
    return lax.ppermute(value, "seq", pairs)


def crossed(piece, count, rest):
    mask = 4
    while mask < count // 2:
        piece = piece + swapped(piece, mask)
        mask *= 2
    return rest(piece, swapped(piece, mask))


def on_device(
    tokens, dilations, embed, conv_weight, mix_weight, gate_bias, out_weight, cot_fwd, cot_rev
):
    channels = embed.shape[1]
    wide = 2 * channels
    length = tokens.shape[0]
    count = lax.axis_size("seq")
    sems = pltpu.SemaphoreType.DMA
    square = (channels, channels)

    def touched(value, after):
        return call(touch_kernel, [VMEM] * 2, [(value.shape, value.dtype, VMEM)])(value, after)[0]

    def joined(first, second, after):
        shape = (2 * first.shape[0], first.shape[1])
        return call(join_kernel, [VMEM] * 3, [(shape, first.dtype, VMEM)])(first, second, after)[0]

    known = tokens.reshape(1, length)
    own = call(load_kernel, [HBM], [(known.shape, known.dtype, VMEM)], [sems((1,))], micros=0.7)(known)[0]
    parts = [own, swapped(known, 1)]
    known = joined(own, parts[-1], own)
    parts.append(swapped(known, 2))
    table, local, mixed_table, conv, mix, bias, turn = call(
        first_tables_kernel,
        [HBM] * 5 + [VMEM],
        [
            ((CONTEXTS, channels), F32, VMEM),
            ((LOCAL, channels), F32, VMEM),
            ((CONTEXTS, wide), F32, VMEM),
            (conv_weight.shape, F32, VMEM),
            (mix_weight.shape, F32, VMEM),
            (gate_bias.shape, F32, VMEM),
            (square, F32, VMEM),
        ],
        [VMEM(embed.shape, F32), sems((11,))],
        micros=2.6,
    )(embed, conv_weight, mix_weight, gate_bias, out_weight, known)
    known = joined(known, parts[-1], table)
    parts.append(swapped(known, 4))
    deep = -(-TAPS // 128) * 128
    pre_high, pre_low, cot_high, cot_low, grad_hidden = call(
        second_tables_kernel,
        [VMEM] * 4 + [HBM] * 3 + [VMEM],
        [((deep, wide), BF16, VMEM)] * 2
        + [((2 * length, channels), BF16, VMEM)] * 2
        + [((2 * length, channels), F32, VMEM)],
        [VMEM(square, F32), VMEM((2, length, channels), F32), sems((3,))],
        micros=2.8,
    )(table, conv, mix, bias, out_weight, cot_fwd, cot_rev, known)
    mask = 8
    while mask < count:
        known = joined(known, parts[-1], pre_low)
        parts.append(swapped(known, mask))
        mask *= 2

    keep_x, send_x, hidden_high, hidden_low, center = call(
        lambda *refs: main_kernel(count, *refs),
        [SMEM] + [VMEM] * (len(parts) + 3),
        [((2, TAPS, 128), F32, VMEM)] * 2
        + [((2 * length, channels), BF16, VMEM)] * 2
        + [((2, length), jnp.int32, VMEM)],
        [VMEM((4, TAPS, 128), F32)],
        micros=2.9,
    )(dilations, *parts, pre_high, pre_low, grad_hidden)

    halve_x = call(halve_kernel, [VMEM] * 2, [((TAPS, 128), F32, VMEM)] * 2)
    keep_x, send_x = halve_x(keep_x, swapped(send_x, 1))

    rest_rows = channels // 2 + LOCAL // 2
    keep_y, send_y, out_fwd, out_rev = call(
        outputs_kernel,
        [VMEM] * 6 + [HBM, VMEM],
        [((2, rest_rows, 128), F32, VMEM)] * 2 + [((length, channels), F32, HBM)] * 2,
        [
            VMEM((4, rest_rows, 128), F32),
            VMEM(square, F32),
            VMEM((2, length, channels), F32),
            sems((3,)),
        ],
        micros=3.7,
    )(center, hidden_high, hidden_low, cot_high, cot_low, local, out_weight, keep_x)
    first_high, first_low, second_high, second_low, turn_high, turn_low, *levels = call(
        prepare_kernel,
        [VMEM] * 5,
        [((4, wide, channels), BF16, VMEM)] * 4
        + [(square, BF16, VMEM)] * 2
        + [((CONTEXTS, channels), BF16, VMEM)] * 4,
        micros=1.3,
    )(conv, mix, turn, table, keep_y)

    halve_y = call(halve_after_kernel, [VMEM] * 3, [((rest_rows, 128), F32, VMEM)] * 2)
    keep_y, send_y = halve_y(keep_y, swapped(send_y, 1), turn_low)

    merge_x = call(merge_taps_kernel, [VMEM] * 3, [((3 * CONTEXTS, 128), F32, VMEM)])
    merge_y = call(merge_rest_kernel, [VMEM] * 2, [((rest_rows + EDGE // 2, 128), F32, VMEM)])
    sum_x = keep_x + swapped(send_x, 2)
    sum_y = keep_y + swapped(send_y, 2)
    piece_x = crossed(sum_x, count, lambda a, b: merge_x(a, b, sum_y)[0])
    piece_y = crossed(sum_y, count, lambda a, b: merge_y(a, b)[0])
    piece_x01 = swapped(piece_x, 2)
    pieces_x = piece_x, piece_x01, swapped(piece_x, 1), swapped(piece_x01, 1)

    g_conv, g_mix, bias_row, partial = call(
        last_layer_kernel,
        [VMEM] * 10,
        [
            (conv_weight.shape, F32, HBM),
            (mix_weight.shape, F32, HBM),
            ((1, wide), F32, VMEM),
            ((CONTEXTS, channels), F32, VMEM),
        ],
        [
            VMEM((4, 3 * CONTEXTS, 128), F32),
            VMEM(conv_weight.shape[1:], F32),
            VMEM(mix_weight.shape[1:], F32),
            sems((4,)),
        ],
        micros=0.05,
    )(*pieces_x, *levels, second_high, second_low)

    piece_y01 = touched(swapped(piece_y, 2), partial)
    pieces_y = piece_y, piece_y01, swapped(piece_y, 1), swapped(piece_y01, 1)
    g_conv, g_mix, g_embed, g_bias, g_out = call(
        first_layer_kernel,
        [VMEM] * 12 + [HBM] * 2,
        [
            (conv_weight.shape, F32, HBM),
            (mix_weight.shape, F32, HBM),
            (embed.shape, F32, HBM),
            (gate_bias.shape, F32, HBM),
            (out_weight.shape, F32, HBM),
        ],
        [
            VMEM((4, rest_rows + EDGE // 2, 128), F32),
            VMEM(conv_weight.shape[1:], F32),
            VMEM(mix_weight.shape[1:], F32),
            VMEM(embed.shape, F32),
            VMEM(gate_bias.shape, F32),
            VMEM(out_weight.shape, F32),
            sems((8,)),
        ],
        aliases={12: 0, 13: 1},
        micros=2.2,
    )(*pieces_y, partial, mixed_table, bias_row, embed, first_high, first_low, turn_high, turn_low, g_conv, g_mix)
    return (out_fwd, out_rev, g_embed, g_conv, g_mix, g_bias, g_out)


def solution(mesh):
    in_specs = (
        P(("dp", "seq")),
        P(),
        P(),
        P(),
        P(),
        P(),
        P(),
        P(("dp", "seq"), None),
        P(("dp", "seq"), None),
    )
    out_specs = (
        P(("dp", "seq"), None),
        P(("dp", "seq"), None),
        P("dp", None),
        P("dp", None, None, None),
        P("dp", None, None),
        P("dp", None),
        P("dp", None, None),
    )
    return jax.shard_map(
        on_device, mesh=mesh, in_specs=in_specs, out_specs=out_specs, check_vma=False
    )
```

```python
import jax
import jax.numpy as jnp
from jax import lax
from jax.experimental import pallas as pl
from jax.experimental.pallas import tpu as pltpu
from jax.sharding import PartitionSpec as P

CONTEXTS = 96
INNER = 64
EDGE = 16
LOCAL = INNER + EDGE
TAPS = 3 * LOCAL
HALO = 128
F32 = jnp.float32
BF16 = jnp.bfloat16
VMEM_LIMIT = 40 * 1024 * 1024


def split(x):
    high = x.astype(BF16)
    return high, (x - high.astype(F32)).astype(BF16)


def dot(a, b, ca=1, cb=0):
    return lax.dot_general(a, b, (((ca,), (cb,)), ((), ())), preferred_element_type=F32)


def dot2(exact, pair, ca=1, cb=0):
    return dot(exact, pair[0], ca, cb) + dot(exact, pair[1], ca, cb)


def dot3(a, b, ca=1, cb=0):
    return dot(a[0], b[0], ca, cb) + (dot(a[0], b[1], ca, cb) + dot(a[1], b[0], ca, cb))


def letters(index):
    inner = index < 64
    left = (index >= 64) & (index < 80)
    low = index & 3
    mid = (index >> 2) & 3
    l = jnp.where(inner, (index >> 4) & 3, jnp.where(left, -1, mid))
    m = jnp.where(inner | left, mid, low)
    r = jnp.where(inner | left, low, -1)
    return l, m, r


def mirrored(index):
    low = 3 - (index & 3)
    mid = 3 - ((index >> 2) & 3)
    high = 3 - ((index >> 4) & 3)
    inner = low * 16 + mid * 4 + high
    left = 80 + low * 4 + mid
    right = 64 + low * 4 + mid
    return jnp.where(index < 64, inner, jnp.where(index < 80, left, right))


def permutation():
    rows = lax.broadcasted_iota(jnp.int32, (CONTEXTS, CONTEXTS), 0)
    cols = lax.broadcasted_iota(jnp.int32, (CONTEXTS, CONTEXTS), 1)
    return (mirrored(rows) == cols).astype(F32).astype(BF16)


def letter_hot():
    rows = lax.broadcasted_iota(jnp.int32, (CONTEXTS, 32), 0)
    cols = lax.broadcasted_iota(jnp.int32, (CONTEXTS, 32), 1)
    l, m, r = letters(rows)
    kind = cols >> 3
    value = jnp.where(kind == 0, l, jnp.where(kind == 1, m, jnp.where(kind == 2, r, 3 - m)))
    return (value == (cols & 7)).astype(F32).astype(BF16)


def gates(mixed):
    channels = mixed.shape[1] // 2
    tanh_part = jnp.tanh(mixed[:, :channels])
    sig_part = 0.5 + 0.5 * jnp.tanh(0.5 * mixed[:, channels:])
    return tanh_part, sig_part


def gate_grads(grad_hidden, tanh_part, sig_part):
    scaled = grad_hidden * sig_part
    return scaled * (1.0 - tanh_part * tanh_part), scaled * tanh_part * (1.0 - sig_part)


class Fetch:
    def __init__(self, sems):
        self.sems = sems
        self.copies = []

    def start(self, source, target):
        copy = pltpu.make_async_copy(source, target, self.sems.at[len(self.copies)])
        copy.start()
        self.copies.append(copy)
        return len(self.copies) - 1

    def wait(self, *which):
        for at in which:
            self.copies[at].wait()


def padded_base(embed):
    return jnp.concatenate([embed[...], jnp.zeros((4, embed.shape[1]), F32)], axis=0)


def left_side():
    return lax.axis_index("seq") * 2 < lax.axis_size("seq")


def local_rows(rows):
    edge = jnp.where(left_side(), rows[INNER : INNER + EDGE], rows[INNER + EDGE : INNER + 2 * EDGE])
    return jnp.concatenate([rows[:INNER], edge], axis=0)


def join_kernel(first, second, after, out):
    rows = first.shape[0]
    out[:rows, :] = first[...]
    out[rows:, :] = second[...]


def load_kernel(source, out, sems):
    fetch = Fetch(sems)
    fetch.start(source, out)
    fetch.wait(0)


def touch_kernel(value, after, out):
    out[...] = value[...]


def first_tables_kernel(
    embed_in, conv_in, mix_in, bias_in, out_in, after, table, local, mixed_table, conv, mix, bias, out_w, embed, sems,
):
    fetch = Fetch(sems)
    small = [fetch.start(embed_in, embed), fetch.start(bias_in, bias)]
    first = [fetch.start(conv_in.at[0, k], conv.at[0, k]) for k in range(3)]
    first += [fetch.start(mix_in.at[0], mix.at[0])]
    turn = fetch.start(out_in.at[0], out_w)
    second = [fetch.start(conv_in.at[1, k], conv.at[1, k]) for k in range(3)]
    second += [fetch.start(mix_in.at[1], mix.at[1])]
    hot = letter_hot()
    fetch.wait(*small)
    base = split(padded_base(embed))
    taps = []
    for k in range(4):
        fetch.wait(first[k])
        taps.append(dot3(base, split(conv[0, k] if k < 3 else mix[0])))
    taps = jnp.concatenate(taps, axis=0)
    mixed = dot2(hot, split(taps)) + bias[0:1, :]
    tanh_part, sig_part = gates(mixed)
    hidden = tanh_part * sig_part
    own = dot2(hot[:, 8:16], base)
    fetch.wait(turn)
    level = own + dot3(split(hidden), split(out_w[...]))
    table[...] = level
    local[...] = local_rows(level)
    mixed_table[...] = mixed
    fetch.wait(*second)


def second_tables_kernel(
    table, conv, mix, bias, out_in, cot_fwd_in, cot_rev_in, after, pre_high, pre_low, cot_high, cot_low, grad_hidden,
    out_w, cots, sems,
):
    length = cots.shape[1]
    fetch = Fetch(sems)
    fetch.start(out_in.at[1], out_w)
    fetch.start(cot_fwd_in, cots.at[0])
    fetch.start(cot_rev_in, cots.at[1])
    level = split(table[...])
    swap = permutation()
    partner = tuple(dot(swap, piece).astype(BF16) for piece in level)
    pre_high[TAPS:, :] = jnp.zeros((pre_high.shape[0] - TAPS, pre_high.shape[1]), BF16)
    pre_low[TAPS:, :] = jnp.zeros((pre_low.shape[0] - TAPS, pre_low.shape[1]), BF16)
    for k in range(3):
        value = dot3(level, split(conv[1, k]))
        if k == 1:
            value = value + dot3(partner, split(mix[1])) + bias[1:2, :]
        high, low = split(local_rows(value))
        pre_high[k * LOCAL : (k + 1) * LOCAL, :] = high
        pre_low[k * LOCAL : (k + 1) * LOCAL, :] = low
    fetch.wait(0)
    weight = split(out_w[...])
    for strand in range(2):
        rows = slice(strand * length, (strand + 1) * length)
        fetch.wait(1 + strand)
        cot = split(cots[strand])
        cot_high[rows, :] = cot[0]
        cot_low[rows, :] = cot[1]
        grad_hidden[rows, :] = dot3(cot, weight, 1, 1)


def windows(parts, count):
    length = parts[0].shape[1]
    place = lax.axis_index("seq")
    last = count - 1

    def block(at):
        total, begin = None, 0
        for part in parts:
            rows = lax.broadcasted_iota(jnp.int32, part.shape, 0) + begin
            piece = jnp.sum(jnp.where(rows == (place ^ at), part[...], 0), axis=0, keepdims=True)
            total = piece if total is None else total + piece
            begin += part.shape[0]
        return total

    def window(at):
        before = jnp.where(at == 0, -1, block(jnp.maximum(at - 1, 0))[:, length - HALO :])
        after = jnp.where(at == last, -1, block(jnp.minimum(at + 1, last))[:, :HALO])
        return [before, block(at), after]

    fwd = jnp.concatenate(window(place), axis=1)
    rev = jnp.concatenate(window(last - place), axis=1)
    rev = jnp.where(rev < 0, -1, 3 - rev)
    tiles = rev.shape[1] // 128
    blocks = [rev[:, i * 128 : (i + 1) * 128] for i in reversed(range(tiles))]
    blocks += [jnp.zeros((8 - tiles, 128), jnp.int32)]
    stacked = jnp.concatenate(blocks, axis=0).astype(F32).astype(BF16)
    rows = lax.broadcasted_iota(jnp.int32, (128, 128), 0)
    cols = lax.broadcasted_iota(jnp.int32, (128, 128), 1)
    flip = (rows + cols == 127).astype(F32).astype(BF16)
    turned = dot(stacked, flip).astype(jnp.int32)
    rev = jnp.concatenate([turned[i : i + 1, :] for i in range(tiles)], axis=1)
    return fwd, rev


def local_contexts(window, first, second, length):
    width = window.shape[1]
    base = jnp.broadcast_to(window, (8, width))
    l = pltpu.roll(base, first, 1)
    r = pltpu.roll(base, width - first, 1)
    index = jnp.where(l < 0, INNER + base * 4 + r, jnp.where(r < 0, INNER + l * 4 + base, l * 16 + base * 4 + r))
    index = jnp.where(base < 0, LOCAL, index)
    before = pltpu.roll(index, second, 1)
    after = pltpu.roll(index, width - second, 1)
    return [x[0:1, HALO : HALO + length] for x in (before, index, after)]


def hot_rows(index):
    rows = lax.broadcasted_iota(jnp.int32, (LOCAL, index.shape[1]), 0)
    return (rows == index).astype(F32).astype(BF16)


def deal(quarters, keep, send):
    bit = lax.axis_index("seq") & 1
    keep[...] = quarters[pl.ds(bit * 2, 2)]
    send[...] = quarters[pl.ds((1 - bit) * 2, 2)]


def main_kernel(count, dil, *refs):
    parts, refs = refs[: count.bit_length()], refs[count.bit_length() :]
    pre_high, pre_low, grad_hidden, keep, send, hidden_high, hidden_low, center, quarters = refs
    length = parts[0].shape[1]
    pre = (pre_high[...], pre_low[...])
    both = windows(parts, count)
    pad = jnp.zeros((pre_high.shape[0] - TAPS, length), BF16)
    total = None
    for strand in range(2):
        index = local_contexts(both[strand], dil[0], dil[1], length)
        hot = jnp.concatenate([hot_rows(x) for x in index] + [pad], axis=0)
        center[strand : strand + 1, :] = index[1]
        mixed = dot2(hot, pre, 0, 0)
        tanh_part, sig_part = gates(mixed)
        hidden = split(tanh_part * sig_part)
        rows = slice(strand * length, (strand + 1) * length)
        hidden_high[rows, :] = hidden[0]
        hidden_low[rows, :] = hidden[1]
        grads = split(jnp.concatenate(gate_grads(grad_hidden[rows, :], tanh_part, sig_part), axis=1))
        part = dot2(hot, grads)
        total = part if total is None else total + part
    for q in range(4):
        quarters[q] = total[:TAPS, q * 128 : (q + 1) * 128]
    deal(quarters, keep, send)


def halve_kernel(kept, received, keep, send):
    bit = (lax.axis_index("seq") >> 1) & 1
    send[...] = kept[1 - bit] + received[1 - bit]
    keep[...] = kept[bit] + received[bit]


def add_after_kernel(kept, received, after, out):
    out[...] = kept[...] + received[...]


def halve_after_kernel(kept, received, after, keep, send):
    halve_kernel(kept, received, keep, send)


def center_hots(center):
    return [hot_rows(center[strand : strand + 1, :]) for strand in range(2)]


def rest_kernel(center, hidden_high, hidden_low, cot_high, cot_low, keep, send, quarters):
    length = center.shape[1]
    channels = cot_high.shape[1]
    total_o = total_c = None
    for strand, hot in enumerate(center_hots(center)):
        rows = slice(strand * length, (strand + 1) * length)
        hidden = (hidden_high[rows, :], hidden_low[rows, :])
        cot = (cot_high[rows, :], cot_low[rows, :])
        part_o = dot3(hidden, cot, 0, 0)
        part_c = dot2(hot, cot)
        total_o = part_o if total_o is None else total_o + part_o
        total_c = part_c if total_c is None else total_c + part_c
    side = channels // 4
    for q in range(4):
        half = slice((q >> 1) * 128, (q >> 1) * 128 + 128)
        quarters[q, :side, :] = total_o[q * side : (q + 1) * side, :128]
        quarters[q, side : 2 * side, :] = total_o[q * side : (q + 1) * side, 128:]
        at = (q & 1) * INNER // 2
        quarters[q, 2 * side : 2 * side + INNER // 2, :] = total_c[at : at + INNER // 2, half]
        at = INNER + (q & 1) * EDGE // 2
        quarters[q, 2 * side + INNER // 2 :, :] = total_c[at : at + EDGE // 2, half]
    deal(quarters, keep, send)


def outputs_kernel(
    center, hidden_high, hidden_low, local, out_in, after, out_fwd_out, out_rev_out, out_w, out_both, sems,
):
    length = center.shape[1]
    fetch = Fetch(sems)
    fetch.start(out_in.at[1], out_w)
    hots = center_hots(center)
    level = split(local[...])
    fetch.wait(0)
    weight = split(out_w[...])
    for strand, out in enumerate((out_fwd_out, out_rev_out)):
        rows = slice(strand * length, (strand + 1) * length)
        update = dot3((hidden_high[rows, :], hidden_low[rows, :]), weight)
        out_both[strand] = dot2(hots[strand], level, 0, 0) + update
        fetch.start(out_both.at[strand], out)
    fetch.wait(1, 2)


def prepare_kernel(
    conv, mix, out_w, table, after, first_high, first_low, second_high, second_low, turn_high, turn_low,
    level_high, level_low, partner_high, partner_low,
):
    level = split(table[...])
    swap = permutation()
    level_high[...], level_low[...] = level
    partner_high[...], partner_low[...] = tuple(dot(swap, piece).astype(BF16) for piece in level)
    for layer, high, low in ((1, second_high, second_low), (0, first_high, first_low)):
        for k in range(4):
            high[k], low[k] = split((conv[layer, k] if k < 3 else mix[layer]).T)
    turn_high[...], turn_low[...] = split(out_w[...].T)


def merge(mine, theirs, inner, edge):
    left = left_side()
    both = mine[inner, :] + theirs[inner, :]
    own, other = mine[edge, :], theirs[edge, :]
    return both, jnp.where(left, own, other), jnp.where(left, other, own)


def merge_taps_kernel(mine, theirs, after, after_too, out):
    for k in range(3):
        at = k * LOCAL
        pieces = merge(mine, theirs, slice(at, at + INNER), slice(at + INNER, at + LOCAL))
        at = k * CONTEXTS
        out[at : at + INNER, :], out[at + INNER : at + LOCAL, :], out[at + LOCAL : at + CONTEXTS, :] = pieces


def merge_rest_kernel(mine, theirs, out):
    rows = mine.shape[0]
    inner = rows - EDGE // 2
    pieces = merge(mine, theirs, slice(0, inner), slice(inner, rows))
    out[:inner, :], out[inner:rows, :], out[rows:, :] = pieces


def gather_quarters(pieces, quarters):
    place = lax.axis_index("seq")
    low, high = place & 1, (place >> 1) & 1
    for piece, x, y in zip(pieces, (0, 0, 1, 1), (0, 1, 0, 1)):
        quarters[(low ^ x) * 2 + (high ^ y)] = piece[...]


def last_layer_kernel(
    piece_00, piece_01, piece_10, piece_11, level_high, level_low, partner_high, partner_low, second_high, second_low,
    g_conv_out, g_mix_out, g_bias, partial,
    quarters, g_conv, g_mix, out_sems,
):
    store = Fetch(out_sems)
    gather_quarters((piece_00, piece_01, piece_10, piece_11), quarters)
    level = (level_high[...], level_low[...])
    partner = (partner_high[...], partner_low[...])
    grad_level = None
    for k in range(3):
        piece = jnp.concatenate([quarters[q, k * CONTEXTS : (k + 1) * CONTEXTS, :] for q in range(4)], axis=1)
        pair = split(piece)
        g_conv[k] = dot3(level, pair, 0, 0)
        store.start(g_conv.at[k], g_conv_out.at[1, k])
        part = dot3(pair, (second_high[k], second_low[k]))
        grad_level = part if grad_level is None else grad_level + part
        if k == 1:
            g_bias[...] = jnp.sum(piece, axis=0, keepdims=True)
            g_mix[...] = dot3(partner, pair, 0, 0)
            store.start(g_mix, g_mix_out.at[1])
            grad_level = grad_level + dot2(permutation(), split(dot3(pair, (second_high[3], second_low[3]))))
    partial[...] = grad_level
    store.wait(*range(len(store.copies)))


def first_layer_kernel(
    piece_00, piece_01, piece_10, piece_11, partial, mixed_table, bias_row, embed, first_high, first_low, turn_high, turn_low,
    g_conv_in, g_mix_in, g_conv_out, g_mix_out, g_embed_out, g_bias_out, g_out_out,
    quarters, g_conv, g_mix, g_embed, g_bias, g_out, out_sems,
):
    channels = embed.shape[1]
    store = Fetch(out_sems)
    gather_quarters((piece_00, piece_01, piece_10, piece_11), quarters)
    side = channels // 4
    half = INNER // 2
    inner, left, right = [], [], []
    for h in range(2):
        lanes = slice(h * 128, (h + 1) * 128)
        for q in range(4):
            g_out[1, q * side : (q + 1) * side, lanes] = quarters[q, h * side : (h + 1) * side, :]
        at = 2 * side
        low, high = quarters[2 * h], quarters[2 * h + 1]
        pick = lambda begin, rows: jnp.concatenate([low[begin : begin + rows], high[begin : begin + rows]], axis=0)
        inner.append(pick(at, half))
        left.append(pick(at + half, EDGE // 2))
        right.append(pick(at + half + EDGE // 2, EDGE // 2))
    store.start(g_out.at[1], g_out_out.at[1])
    rest = jnp.concatenate([jnp.concatenate(x, axis=1) for x in (inner, left, right)], axis=0)
    grad_level = split(partial[...] + rest)
    tanh_part, sig_part = gates(mixed_table[...])
    hidden = split(tanh_part * sig_part)
    grad_hidden = dot3(grad_level, (turn_high[...], turn_low[...]))
    grad_mixed = jnp.concatenate(gate_grads(grad_hidden, tanh_part, sig_part), axis=1)
    g_bias[0:1, :] = jnp.sum(grad_mixed, axis=0, keepdims=True)
    g_bias[1:2, :] = bias_row[...]
    store.start(g_bias, g_bias_out)
    hot = letter_hot()
    by_letter = dot2(hot, split(grad_mixed), 0, 0)
    base = split(padded_base(embed))
    stacked = jnp.concatenate([base[0].astype(F32), base[0].astype(F32), base[1].astype(F32)], axis=0).astype(BF16)
    pieces = []
    for k in range(4):
        piece = split(by_letter[k * 8 : (k + 1) * 8, :])
        pieces.append(piece)
        high, low = piece[0].astype(F32), piece[1].astype(F32)
        value = dot(stacked, jnp.concatenate([high, low, high], axis=0).astype(BF16), 0, 0)
        if k < 3:
            g_conv[k] = value
            store.start(g_conv.at[k], g_conv_out.at[0, k])
        else:
            g_mix[...] = value
            store.start(g_mix, g_mix_out.at[0])
    g_out[0] = dot3(hidden, grad_level, 0, 0)
    store.start(g_out.at[0], g_out_out.at[0])
    grad_base = dot2(hot[:, 8:16], grad_level, 0, 0)
    for k in range(4):
        grad_base = grad_base + dot3(pieces[k], (first_high[k], first_low[k]))
    g_embed[...] = grad_base[:4, :]
    store.start(g_embed, g_embed_out)
    store.wait(*range(len(store.copies)))


VMEM, SMEM, HBM = pltpu.VMEM, pltpu.SMEM, pltpu.HBM


def call(kernel, ins, outs, scratch=(), aliases=None, micros=0.001):
    run = pl.pallas_call(
        kernel,
        out_shape=[space(shape, kind) for shape, kind, space in outs],
        in_specs=[pl.BlockSpec(memory_space=space) for space in ins],
        out_specs=[pl.BlockSpec(memory_space=space) for _, _, space in outs],
        scratch_shapes=list(scratch),
        input_output_aliases=aliases or {},
        cost_estimate=pl.CostEstimate(flops=int(micros * 1.1e9), bytes_accessed=int(micros * 3e6), transcendentals=0),
        compiler_params=pltpu.CompilerParams(vmem_limit_bytes=VMEM_LIMIT),
    )

    def placed(*args):
        return run(*[pltpu.with_memory_space_constraint(x, HBM) if space is HBM else x for x, space in zip(args, ins)])

    return placed


def swapped(value, mask):
    pairs = [(source, source ^ mask) for source in range(lax.axis_size("seq"))]
    return lax.ppermute(value, "seq", pairs)


def crossed(piece, count, rest):
    mask = 4
    while mask < count // 2:
        piece = piece + swapped(piece, mask)
        mask *= 2
    return rest(piece, swapped(piece, mask))


def on_device(
    tokens, dilations, embed, conv_weight, mix_weight, gate_bias, out_weight, cot_fwd, cot_rev
):
    channels = embed.shape[1]
    wide = 2 * channels
    length = tokens.shape[0]
    count = lax.axis_size("seq")
    sems = pltpu.SemaphoreType.DMA
    square = (channels, channels)

    def touched(value, after):
        return call(touch_kernel, [VMEM] * 2, [(value.shape, value.dtype, VMEM)])(value, after)[0]

    def joined(first, second, after):
        shape = (2 * first.shape[0], first.shape[1])
        return call(join_kernel, [VMEM] * 3, [(shape, first.dtype, VMEM)])(first, second, after)[0]

    known = tokens.reshape(1, length)
    own = call(load_kernel, [HBM], [(known.shape, known.dtype, VMEM)], [sems((1,))], micros=0.7)(known)[0]
    parts = [own, swapped(known, 1)]
    known = joined(own, parts[-1], own)
    parts.append(swapped(known, 2))
    table, local, mixed_table, conv, mix, bias, turn = call(
        first_tables_kernel,
        [HBM] * 5 + [VMEM],
        [
            ((CONTEXTS, channels), F32, VMEM),
            ((LOCAL, channels), F32, VMEM),
            ((CONTEXTS, wide), F32, VMEM),
            (conv_weight.shape, F32, VMEM),
            (mix_weight.shape, F32, VMEM),
            (gate_bias.shape, F32, VMEM),
            (square, F32, VMEM),
        ],
        [VMEM(embed.shape, F32), sems((11,))],
        micros=2.6,
    )(embed, conv_weight, mix_weight, gate_bias, out_weight, known)
    known = joined(known, parts[-1], table)
    parts.append(swapped(known, 4))
    deep = -(-TAPS // 128) * 128
    pre_high, pre_low, cot_high, cot_low, grad_hidden = call(
        second_tables_kernel,
        [VMEM] * 4 + [HBM] * 3 + [VMEM],
        [((deep, wide), BF16, VMEM)] * 2
        + [((2 * length, channels), BF16, VMEM)] * 2
        + [((2 * length, channels), F32, VMEM)],
        [VMEM(square, F32), VMEM((2, length, channels), F32), sems((3,))],
        micros=2.8,
    )(table, conv, mix, bias, out_weight, cot_fwd, cot_rev, known)
    mask = 8
    while mask < count:
        known = joined(known, parts[-1], pre_low)
        parts.append(swapped(known, mask))
        mask *= 2

    keep_x, send_x, hidden_high, hidden_low, center = call(
        lambda *refs: main_kernel(count, *refs),
        [SMEM] + [VMEM] * (len(parts) + 3),
        [((2, TAPS, 128), F32, VMEM)] * 2
        + [((2 * length, channels), BF16, VMEM)] * 2
        + [((2, length), jnp.int32, VMEM)],
        [VMEM((4, TAPS, 128), F32)],
        micros=2.9,
    )(dilations, *parts, pre_high, pre_low, grad_hidden)

    halve_x = call(halve_kernel, [VMEM] * 2, [((TAPS, 128), F32, VMEM)] * 2)
    keep_x, send_x = halve_x(keep_x, swapped(send_x, 1))

    rest_rows = channels // 2 + LOCAL // 2
    keep_y, send_y = call(
        rest_kernel,
        [VMEM] * 5,
        [((2, rest_rows, 128), F32, VMEM)] * 2,
        [VMEM((4, rest_rows, 128), F32)],
        micros=1.6,
    )(center, hidden_high, hidden_low, cot_high, cot_low)
    out_fwd, out_rev = call(
        outputs_kernel,
        [VMEM] * 4 + [HBM, VMEM],
        [((length, channels), F32, HBM)] * 2,
        [VMEM(square, F32), VMEM((2, length, channels), F32), sems((3,))],
        micros=2.2,
    )(center, hidden_high, hidden_low, local, out_weight, keep_x)
    halve_y = call(halve_after_kernel, [VMEM] * 2 + [HBM], [((rest_rows, 128), F32, VMEM)] * 2)
    keep_y, send_y = halve_y(keep_y, swapped(send_y, 1), out_rev)

    first_high, first_low, second_high, second_low, turn_high, turn_low, *levels = call(
        prepare_kernel,
        [VMEM] * 5,
        [((4, wide, channels), BF16, VMEM)] * 4
        + [(square, BF16, VMEM)] * 2
        + [((CONTEXTS, channels), BF16, VMEM)] * 4,
        micros=1.3,
    )(conv, mix, turn, table, keep_y)

    merge_x = call(merge_taps_kernel, [VMEM] * 4, [((3 * CONTEXTS, 128), F32, VMEM)])
    merge_y = call(merge_rest_kernel, [VMEM] * 2, [((rest_rows + EDGE // 2, 128), F32, VMEM)], micros=2.0)
    sum_x = keep_x + swapped(send_x, 2)
    sum_y = call(add_after_kernel, [VMEM] * 3, [(keep_y.shape, F32, VMEM)])(keep_y, swapped(send_y, 2), sum_x)[0]
    piece_x = crossed(sum_x, count, lambda a, b: merge_x(a, b, sum_y, turn_low)[0])
    piece_y = crossed(sum_y, count, lambda a, b: merge_y(a, b)[0])
    piece_x01 = touched(swapped(piece_x, 2), piece_y)
    pieces_x = piece_x, piece_x01, swapped(piece_x, 1), swapped(piece_x01, 1)

    g_conv, g_mix, bias_row, partial = call(
        last_layer_kernel,
        [VMEM] * 10,
        [
            (conv_weight.shape, F32, HBM),
            (mix_weight.shape, F32, HBM),
            ((1, wide), F32, VMEM),
            ((CONTEXTS, channels), F32, VMEM),
        ],
        [
            VMEM((4, 3 * CONTEXTS, 128), F32),
            VMEM(conv_weight.shape[1:], F32),
            VMEM(mix_weight.shape[1:], F32),
            sems((4,)),
        ],
        micros=0.05,
    )(*pieces_x, *levels, second_high, second_low)

    piece_y01 = touched(swapped(piece_y, 2), partial)
    pieces_y = piece_y, piece_y01, swapped(piece_y, 1), swapped(piece_y01, 1)
    g_conv, g_mix, g_embed, g_bias, g_out = call(
        first_layer_kernel,
        [VMEM] * 12 + [HBM] * 2,
        [
            (conv_weight.shape, F32, HBM),
            (mix_weight.shape, F32, HBM),
            (embed.shape, F32, HBM),
            (gate_bias.shape, F32, HBM),
            (out_weight.shape, F32, HBM),
        ],
        [
            VMEM((4, rest_rows + EDGE // 2, 128), F32),
            VMEM(conv_weight.shape[1:], F32),
            VMEM(mix_weight.shape[1:], F32),
            VMEM(embed.shape, F32),
            VMEM(gate_bias.shape, F32),
            VMEM(out_weight.shape, F32),
            sems((8,)),
        ],
        aliases={12: 0, 13: 1},
        micros=2.2,
    )(*pieces_y, partial, mixed_table, bias_row, embed, first_high, first_low, turn_high, turn_low, g_conv, g_mix)
    return (out_fwd, out_rev, g_embed, g_conv, g_mix, g_bias, g_out)


def solution(mesh):
    in_specs = (
        P(("dp", "seq")),
        P(),
        P(),
        P(),
        P(),
        P(),
        P(),
        P(("dp", "seq"), None),
        P(("dp", "seq"), None),
    )
    out_specs = (
        P(("dp", "seq"), None),
        P(("dp", "seq"), None),
        P("dp", None),
        P("dp", None, None, None),
        P("dp", None, None),
        P("dp", None),
        P("dp", None, None),
    )
    return jax.shard_map(
        on_device, mesh=mesh, in_specs=in_specs, out_specs=out_specs, check_vma=False
    )
```

```python
import jax
import jax.numpy as jnp
from jax import lax
from jax.experimental import pallas as pl
from jax.experimental.pallas import tpu as pltpu
from jax.sharding import PartitionSpec as P

CONTEXTS = 96
INNER = 64
EDGE = 16
LOCAL = INNER + EDGE
TAPS = 3 * LOCAL
HALO = 128
F32 = jnp.float32
BF16 = jnp.bfloat16
VMEM_LIMIT = 40 * 1024 * 1024


def split(x):
    high = x.astype(BF16)
    return high, (x - high.astype(F32)).astype(BF16)


def dot(a, b, ca=1, cb=0):
    return lax.dot_general(a, b, (((ca,), (cb,)), ((), ())), preferred_element_type=F32)


def dot2(exact, pair, ca=1, cb=0):
    return dot(exact, pair[0], ca, cb) + dot(exact, pair[1], ca, cb)


def dot3(a, b, ca=1, cb=0):
    return dot(a[0], b[0], ca, cb) + (dot(a[0], b[1], ca, cb) + dot(a[1], b[0], ca, cb))


def letters(index):
    inner = index < 64
    left = (index >= 64) & (index < 80)
    low = index & 3
    mid = (index >> 2) & 3
    l = jnp.where(inner, (index >> 4) & 3, jnp.where(left, -1, mid))
    m = jnp.where(inner | left, mid, low)
    r = jnp.where(inner | left, low, -1)
    return l, m, r


def mirrored(index):
    low = 3 - (index & 3)
    mid = 3 - ((index >> 2) & 3)
    high = 3 - ((index >> 4) & 3)
    inner = low * 16 + mid * 4 + high
    left = 80 + low * 4 + mid
    right = 64 + low * 4 + mid
    return jnp.where(index < 64, inner, jnp.where(index < 80, left, right))


def permutation():
    rows = lax.broadcasted_iota(jnp.int32, (CONTEXTS, CONTEXTS), 0)
    cols = lax.broadcasted_iota(jnp.int32, (CONTEXTS, CONTEXTS), 1)
    return (mirrored(rows) == cols).astype(F32).astype(BF16)


def letter_hot():
    rows = lax.broadcasted_iota(jnp.int32, (CONTEXTS, 32), 0)
    cols = lax.broadcasted_iota(jnp.int32, (CONTEXTS, 32), 1)
    l, m, r = letters(rows)
    kind = cols >> 3
    value = jnp.where(kind == 0, l, jnp.where(kind == 1, m, jnp.where(kind == 2, r, 3 - m)))
    return (value == (cols & 7)).astype(F32).astype(BF16)


def gates(mixed):
    channels = mixed.shape[1] // 2
    tanh_part = jnp.tanh(mixed[:, :channels])
    sig_part = 0.5 + 0.5 * jnp.tanh(0.5 * mixed[:, channels:])
    return tanh_part, sig_part


def gate_grads(grad_hidden, tanh_part, sig_part):
    scaled = grad_hidden * sig_part
    return scaled * (1.0 - tanh_part * tanh_part), scaled * tanh_part * (1.0 - sig_part)


class Fetch:
    def __init__(self, sems):
        self.sems = sems
        self.copies = []

    def start(self, source, target):
        copy = pltpu.make_async_copy(source, target, self.sems.at[len(self.copies)])
        copy.start()
        self.copies.append(copy)
        return len(self.copies) - 1

    def wait(self, *which):
        for at in which:
            self.copies[at].wait()


def padded_base(embed):
    return jnp.concatenate([embed[...], jnp.zeros((4, embed.shape[1]), F32)], axis=0)


def left_side():
    return lax.axis_index("seq") * 2 < lax.axis_size("seq")


def local_rows(rows):
    edge = jnp.where(left_side(), rows[INNER : INNER + EDGE], rows[INNER + EDGE : INNER + 2 * EDGE])
    return jnp.concatenate([rows[:INNER], edge], axis=0)


def join_kernel(first, second, after, out):
    rows = first.shape[0]
    out[:rows, :] = first[...]
    out[rows:, :] = second[...]


def load_kernel(source, out, sems):
    fetch = Fetch(sems)
    fetch.start(source, out)
    fetch.wait(0)


def touch_kernel(value, after, out):
    out[...] = value[...]


def cut_kernel(value, after, first, second):
    half = first.shape[0]
    first[...] = value[:half, :]
    second[...] = value[half:, :]


def first_tables_kernel(
    embed_in, conv_in, mix_in, bias_in, out_in, after, table, local, mixed_table, conv, mix, bias, out_w, embed, sems,
):
    fetch = Fetch(sems)
    small = [fetch.start(embed_in, embed), fetch.start(bias_in, bias)]
    first = [fetch.start(conv_in.at[0, k], conv.at[k]) for k in range(3)]
    first += [fetch.start(mix_in.at[0], mix)]
    turn = fetch.start(out_in.at[0], out_w)
    hot = letter_hot()
    fetch.wait(*small)
    base = split(padded_base(embed))
    taps = []
    for k in range(4):
        fetch.wait(first[k])
        taps.append(dot3(base, split(conv[k] if k < 3 else mix[...])))
    taps = jnp.concatenate(taps, axis=0)
    mixed = dot2(hot, split(taps)) + bias[0:1, :]
    tanh_part, sig_part = gates(mixed)
    hidden = tanh_part * sig_part
    own = dot2(hot[:, 8:16], base)
    fetch.wait(turn)
    level = own + dot3(split(hidden), split(out_w[...]))
    table[...] = level
    local[...] = local_rows(level)
    mixed_table[...] = mixed


def second_tables_kernel(
    table, bias, conv_in, mix_in, out_in, cot_fwd_in, cot_rev_in, after, pre_high, pre_low, cot_high, cot_low, grad_hidden,
    conv, mix, out_w, cots, sems,
):
    length = cots.shape[1]
    fetch = Fetch(sems)
    fetch.start(out_in.at[1], out_w)
    fetch.start(cot_fwd_in, cots.at[0])
    second = [fetch.start(conv_in.at[1, k], conv.at[k]) for k in range(3)]
    second += [fetch.start(mix_in.at[1], mix)]
    last = fetch.start(cot_rev_in, cots.at[1])

    def cotangents(strand):
        rows = slice(strand * length, (strand + 1) * length)
        cot = split(cots[strand])
        cot_high[rows, :] = cot[0]
        cot_low[rows, :] = cot[1]
        grad_hidden[rows, :] = dot3(cot, weight, 1, 1)

    level = split(table[...])
    swap = permutation()
    partner = tuple(dot(swap, piece).astype(BF16) for piece in level)
    pre_high[TAPS:, :] = jnp.zeros((pre_high.shape[0] - TAPS, pre_high.shape[1]), BF16)
    pre_low[TAPS:, :] = jnp.zeros((pre_low.shape[0] - TAPS, pre_low.shape[1]), BF16)
    fetch.wait(0, 1)
    weight = split(out_w[...])
    cotangents(0)
    for k in (0, 2, 1):
        fetch.wait(second[k])
        value = dot3(level, split(conv[k]))
        if k == 1:
            fetch.wait(second[3])
            value = value + dot3(partner, split(mix[...])) + bias[1:2, :]
        high, low = split(local_rows(value))
        pre_high[k * LOCAL : (k + 1) * LOCAL, :] = high
        pre_low[k * LOCAL : (k + 1) * LOCAL, :] = low
    fetch.wait(last)
    cotangents(1)


def windows(parts, count):
    length = parts[0].shape[1]
    place = lax.axis_index("seq")
    last = count - 1

    def block(at):
        total, begin = None, 0
        for part in parts:
            rows = lax.broadcasted_iota(jnp.int32, part.shape, 0) + begin
            piece = jnp.sum(jnp.where(rows == (place ^ at), part[...], 0), axis=0, keepdims=True)
            total = piece if total is None else total + piece
            begin += part.shape[0]
        return total

    def window(at):
        before = jnp.where(at == 0, -1, block(jnp.maximum(at - 1, 0))[:, length - HALO :])
        after = jnp.where(at == last, -1, block(jnp.minimum(at + 1, last))[:, :HALO])
        return [before, block(at), after]

    fwd = jnp.concatenate(window(place), axis=1)
    rev = jnp.concatenate(window(last - place), axis=1)
    rev = jnp.where(rev < 0, -1, 3 - rev)
    tiles = rev.shape[1] // 128
    blocks = [rev[:, i * 128 : (i + 1) * 128] for i in reversed(range(tiles))]
    blocks += [jnp.zeros((8 - tiles, 128), jnp.int32)]
    stacked = jnp.concatenate(blocks, axis=0).astype(F32).astype(BF16)
    rows = lax.broadcasted_iota(jnp.int32, (128, 128), 0)
    cols = lax.broadcasted_iota(jnp.int32, (128, 128), 1)
    flip = (rows + cols == 127).astype(F32).astype(BF16)
    turned = dot(stacked, flip).astype(jnp.int32)
    rev = jnp.concatenate([turned[i : i + 1, :] for i in range(tiles)], axis=1)
    return fwd, rev


def local_contexts(window, first, second, length):
    width = window.shape[1]
    base = jnp.broadcast_to(window, (8, width))
    l = pltpu.roll(base, first, 1)
    r = pltpu.roll(base, width - first, 1)
    index = jnp.where(l < 0, INNER + base * 4 + r, jnp.where(r < 0, INNER + l * 4 + base, l * 16 + base * 4 + r))
    index = jnp.where(base < 0, LOCAL, index)
    before = pltpu.roll(index, second, 1)
    after = pltpu.roll(index, width - second, 1)
    return [x[0:1, HALO : HALO + length] for x in (before, index, after)]


def hot_rows(index):
    rows = lax.broadcasted_iota(jnp.int32, (LOCAL, index.shape[1]), 0)
    return (rows == index).astype(F32).astype(BF16)


def deal(quarters, keep, send):
    bit = lax.axis_index("seq") & 1
    keep[...] = quarters[pl.ds(bit * 2, 2)]
    send[...] = quarters[pl.ds((1 - bit) * 2, 2)]


def main_kernel(count, dil, *refs):
    parts, refs = refs[: count.bit_length()], refs[count.bit_length() :]
    pre_high, pre_low, grad_hidden, keep, send, hidden_high, hidden_low, center, quarters = refs
    length = parts[0].shape[1]
    pre = (pre_high[...], pre_low[...])
    both = windows(parts, count)
    pad = jnp.zeros((pre_high.shape[0] - TAPS, length), BF16)
    total = None
    for strand in range(2):
        index = local_contexts(both[strand], dil[0], dil[1], length)
        hot = jnp.concatenate([hot_rows(x) for x in index] + [pad], axis=0)
        center[strand : strand + 1, :] = index[1]
        mixed = dot2(hot, pre, 0, 0)
        tanh_part, sig_part = gates(mixed)
        hidden = split(tanh_part * sig_part)
        rows = slice(strand * length, (strand + 1) * length)
        hidden_high[rows, :] = hidden[0]
        hidden_low[rows, :] = hidden[1]
        grads = split(jnp.concatenate(gate_grads(grad_hidden[rows, :], tanh_part, sig_part), axis=1))
        part = dot2(hot, grads)
        total = part if total is None else total + part
    for q in range(4):
        quarters[q] = total[:TAPS, q * 128 : (q + 1) * 128]
    deal(quarters, keep, send)


def halve_kernel(kept, received, keep, send):
    bit = (lax.axis_index("seq") >> 1) & 1
    send[...] = kept[1 - bit] + received[1 - bit]
    keep[...] = kept[bit] + received[bit]


def add_after_kernel(kept, received, after, out):
    out[...] = kept[...] + received[...]


def halve_after_kernel(kept, received, after, keep, send):
    halve_kernel(kept, received, keep, send)


def center_hots(center):
    return [hot_rows(center[strand : strand + 1, :]) for strand in range(2)]


def rest_kernel(center, hidden_high, hidden_low, cot_high, cot_low, keep, send, quarters):
    length = center.shape[1]
    channels = cot_high.shape[1]
    total_o = total_c = None
    for strand, hot in enumerate(center_hots(center)):
        rows = slice(strand * length, (strand + 1) * length)
        hidden = (hidden_high[rows, :], hidden_low[rows, :])
        cot = (cot_high[rows, :], cot_low[rows, :])
        part_o = dot3(hidden, cot, 0, 0)
        part_c = dot2(hot, cot)
        total_o = part_o if total_o is None else total_o + part_o
        total_c = part_c if total_c is None else total_c + part_c
    side = channels // 4
    for q in range(4):
        half = slice((q >> 1) * 128, (q >> 1) * 128 + 128)
        quarters[q, :side, :] = total_o[q * side : (q + 1) * side, :128]
        quarters[q, side : 2 * side, :] = total_o[q * side : (q + 1) * side, 128:]
        at = (q & 1) * INNER // 2
        quarters[q, 2 * side : 2 * side + INNER // 2, :] = total_c[at : at + INNER // 2, half]
        at = INNER + (q & 1) * EDGE // 2
        quarters[q, 2 * side + INNER // 2 :, :] = total_c[at : at + EDGE // 2, half]
    deal(quarters, keep, send)


def outputs_kernel(
    center, hidden_high, hidden_low, local, out_in, after, out_fwd_out, out_rev_out, out_w, out_both, sems,
):
    length = center.shape[1]
    fetch = Fetch(sems)
    fetch.start(out_in.at[1], out_w)
    hots = center_hots(center)
    level = split(local[...])
    fetch.wait(0)
    weight = split(out_w[...])
    for strand, out in enumerate((out_fwd_out, out_rev_out)):
        rows = slice(strand * length, (strand + 1) * length)
        update = dot3((hidden_high[rows, :], hidden_low[rows, :]), weight)
        out_both[strand] = dot2(hots[strand], level, 0, 0) + update
        fetch.start(out_both.at[strand], out)
    fetch.wait(1, 2)


def prepare_kernel(
    first_conv, first_mix, second_conv, second_mix, out_w, table, after, first_high, first_low, second_high, second_low, turn_high, turn_low,
    level_high, level_low, partner_high, partner_low,
):
    level = split(table[...])
    swap = permutation()
    level_high[...], level_low[...] = level
    partner_high[...], partner_low[...] = tuple(dot(swap, piece).astype(BF16) for piece in level)
    for conv, mix, high, low in (
        (second_conv, second_mix, second_high, second_low),
        (first_conv, first_mix, first_high, first_low),
    ):
        for k in range(4):
            high[k], low[k] = split((conv[k] if k < 3 else mix[...]).T)
    turn_high[...], turn_low[...] = split(out_w[...].T)


def merge(mine, theirs, inner, edge):
    left = left_side()
    both = mine[inner, :] + theirs[inner, :]
    own, other = mine[edge, :], theirs[edge, :]
    return both, jnp.where(left, own, other), jnp.where(left, other, own)


def merge_taps_kernel(mine, theirs, after, after_too, out):
    for k in range(3):
        at = k * LOCAL
        pieces = merge(mine, theirs, slice(at, at + INNER), slice(at + INNER, at + LOCAL))
        at = k * CONTEXTS
        out[at : at + INNER, :], out[at + INNER : at + LOCAL, :], out[at + LOCAL : at + CONTEXTS, :] = pieces


def merge_rest_kernel(mine, theirs, out):
    rows = mine.shape[0]
    inner = rows - EDGE // 2
    pieces = merge(mine, theirs, slice(0, inner), slice(inner, rows))
    out[:inner, :], out[inner:rows, :], out[rows:, :] = pieces


def gather_quarters(pieces, quarters):
    place = lax.axis_index("seq")
    low, high = place & 1, (place >> 1) & 1
    for parts, x, y in zip(pieces, (0, 0, 1, 1), (0, 1, 0, 1)):
        begin = 0
        for part in parts:
            rows = part.shape[0]
            quarters[(low ^ x) * 2 + (high ^ y), begin : begin + rows, :] = part[...]
            begin += rows


def last_layer_kernel(
    piece_00, piece_01, piece_01_too, piece_10, piece_11, piece_11_too, level_high, level_low, partner_high, partner_low, second_high, second_low,
    g_conv_out, g_mix_out, g_bias, partial,
    quarters, g_conv, g_mix, out_sems,
):
    store = Fetch(out_sems)
    gather_quarters(((piece_00,), (piece_01, piece_01_too), (piece_10,), (piece_11, piece_11_too)), quarters)
    level = (level_high[...], level_low[...])
    partner = (partner_high[...], partner_low[...])
    grad_level = None
    for k in range(3):
        piece = jnp.concatenate([quarters[q, k * CONTEXTS : (k + 1) * CONTEXTS, :] for q in range(4)], axis=1)
        pair = split(piece)
        g_conv[k] = dot3(level, pair, 0, 0)
        store.start(g_conv.at[k], g_conv_out.at[1, k])
        part = dot3(pair, (second_high[k], second_low[k]))
        grad_level = part if grad_level is None else grad_level + part
        if k == 1:
            g_bias[...] = jnp.sum(piece, axis=0, keepdims=True)
            g_mix[...] = dot3(partner, pair, 0, 0)
            store.start(g_mix, g_mix_out.at[1])
            grad_level = grad_level + dot2(permutation(), split(dot3(pair, (second_high[3], second_low[3]))))
    partial[...] = grad_level
    store.wait(*range(len(store.copies)))


def first_layer_kernel(
    piece_00, piece_01, piece_10, piece_11, partial, mixed_table, bias_row, embed, first_high, first_low, turn_high, turn_low,
    g_conv_in, g_mix_in, g_conv_out, g_mix_out, g_embed_out, g_bias_out, g_out_out,
    quarters, g_conv, g_mix, g_embed, g_bias, g_out, out_sems,
):
    channels = embed.shape[1]
    store = Fetch(out_sems)
    gather_quarters([(piece,) for piece in (piece_00, piece_01, piece_10, piece_11)], quarters)
    side = channels // 4
    half = INNER // 2
    inner, left, right = [], [], []
    for h in range(2):
        lanes = slice(h * 128, (h + 1) * 128)
        for q in range(4):
            g_out[1, q * side : (q + 1) * side, lanes] = quarters[q, h * side : (h + 1) * side, :]
        at = 2 * side
        low, high = quarters[2 * h], quarters[2 * h + 1]
        pick = lambda begin, rows: jnp.concatenate([low[begin : begin + rows], high[begin : begin + rows]], axis=0)
        inner.append(pick(at, half))
        left.append(pick(at + half, EDGE // 2))
        right.append(pick(at + half + EDGE // 2, EDGE // 2))
    store.start(g_out.at[1], g_out_out.at[1])
    rest = jnp.concatenate([jnp.concatenate(x, axis=1) for x in (inner, left, right)], axis=0)
    grad_level = split(partial[...] + rest)
    tanh_part, sig_part = gates(mixed_table[...])
    hidden = split(tanh_part * sig_part)
    grad_hidden = dot3(grad_level, (turn_high[...], turn_low[...]))
    grad_mixed = jnp.concatenate(gate_grads(grad_hidden, tanh_part, sig_part), axis=1)
    g_bias[0:1, :] = jnp.sum(grad_mixed, axis=0, keepdims=True)
    g_bias[1:2, :] = bias_row[...]
    store.start(g_bias, g_bias_out)
    hot = letter_hot()
    by_letter = dot2(hot, split(grad_mixed), 0, 0)
    base = split(padded_base(embed))
    stacked = jnp.concatenate([base[0].astype(F32), base[0].astype(F32), base[1].astype(F32)], axis=0).astype(BF16)
    pieces = []
    for k in range(4):
        piece = split(by_letter[k * 8 : (k + 1) * 8, :])
        pieces.append(piece)
        high, low = piece[0].astype(F32), piece[1].astype(F32)
        value = dot(stacked, jnp.concatenate([high, low, high], axis=0).astype(BF16), 0, 0)
        if k < 3:
            g_conv[k] = value
            store.start(g_conv.at[k], g_conv_out.at[0, k])
        else:
            g_mix[...] = value
            store.start(g_mix, g_mix_out.at[0])
    g_out[0] = dot3(hidden, grad_level, 0, 0)
    store.start(g_out.at[0], g_out_out.at[0])
    grad_base = dot2(hot[:, 8:16], grad_level, 0, 0)
    for k in range(4):
        grad_base = grad_base + dot3(pieces[k], (first_high[k], first_low[k]))
    g_embed[...] = grad_base[:4, :]
    store.start(g_embed, g_embed_out)
    store.wait(*range(len(store.copies)))


VMEM, SMEM, HBM = pltpu.VMEM, pltpu.SMEM, pltpu.HBM


def call(kernel, ins, outs, scratch=(), aliases=None, micros=0.001):
    run = pl.pallas_call(
        kernel,
        out_shape=[space(shape, kind) for shape, kind, space in outs],
        in_specs=[pl.BlockSpec(memory_space=space) for space in ins],
        out_specs=[pl.BlockSpec(memory_space=space) for _, _, space in outs],
        scratch_shapes=list(scratch),
        input_output_aliases=aliases or {},
        cost_estimate=pl.CostEstimate(flops=int(micros * 1.1e9), bytes_accessed=int(micros * 3e6), transcendentals=0),
        compiler_params=pltpu.CompilerParams(vmem_limit_bytes=VMEM_LIMIT),
    )

    def placed(*args):
        return run(*[pltpu.with_memory_space_constraint(x, HBM) if space is HBM else x for x, space in zip(args, ins)])

    return placed


def swapped(value, mask):
    pairs = [(source, source ^ mask) for source in range(lax.axis_size("seq"))]
    return lax.ppermute(value, "seq", pairs)


def crossed(piece, count, rest):
    mask = 4
    while mask < count // 2:
        piece = piece + swapped(piece, mask)
        mask *= 2
    return rest(piece, swapped(piece, mask))


def on_device(
    tokens, dilations, embed, conv_weight, mix_weight, gate_bias, out_weight, cot_fwd, cot_rev
):
    channels = embed.shape[1]
    wide = 2 * channels
    length = tokens.shape[0]
    count = lax.axis_size("seq")
    sems = pltpu.SemaphoreType.DMA
    square = (channels, channels)

    def touched(value, after):
        return call(touch_kernel, [VMEM] * 2, [(value.shape, value.dtype, VMEM)])(value, after)[0]

    def joined(first, second, after):
        shape = (2 * first.shape[0], first.shape[1])
        return call(join_kernel, [VMEM] * 3, [(shape, first.dtype, VMEM)])(first, second, after)[0]

    known = tokens.reshape(1, length)
    own = call(load_kernel, [HBM], [(known.shape, known.dtype, VMEM)], [sems((1,))], micros=0.7)(known)[0]
    parts = [own, swapped(known, 1)]
    known = joined(own, parts[-1], own)
    parts.append(swapped(known, 2))
    layer_weights = [(conv_weight.shape[1:], F32, VMEM), (mix_weight.shape[1:], F32, VMEM)]
    table, local, mixed_table, first_conv, first_mix, bias, turn = call(
        first_tables_kernel,
        [HBM] * 5 + [VMEM],
        [
            ((CONTEXTS, channels), F32, VMEM),
            ((LOCAL, channels), F32, VMEM),
            ((CONTEXTS, wide), F32, VMEM),
            *layer_weights,
            (gate_bias.shape, F32, VMEM),
            (square, F32, VMEM),
        ],
        [VMEM(embed.shape, F32), sems((7,))],
        micros=2.6,
    )(embed, conv_weight, mix_weight, gate_bias, out_weight, known)
    known = joined(known, parts[-1], table)
    parts.append(swapped(known, 4))
    deep = -(-TAPS // 128) * 128
    pre_high, pre_low, cot_high, cot_low, grad_hidden, second_conv, second_mix = call(
        second_tables_kernel,
        [VMEM] * 2 + [HBM] * 5 + [VMEM],
        [((deep, wide), BF16, VMEM)] * 2
        + [((2 * length, channels), BF16, VMEM)] * 2
        + [((2 * length, channels), F32, VMEM)]
        + layer_weights,
        [VMEM(square, F32), VMEM((2, length, channels), F32), sems((7,))],
        micros=3.0,
    )(table, bias, conv_weight, mix_weight, out_weight, cot_fwd, cot_rev, known)
    mask = 8
    while mask < count:
        known = joined(known, parts[-1], pre_low)
        parts.append(swapped(known, mask))
        mask *= 2

    keep_x, send_x, hidden_high, hidden_low, center = call(
        lambda *refs: main_kernel(count, *refs),
        [SMEM] + [VMEM] * (len(parts) + 3),
        [((2, TAPS, 128), F32, VMEM)] * 2
        + [((2 * length, channels), BF16, VMEM)] * 2
        + [((2, length), jnp.int32, VMEM)],
        [VMEM((4, TAPS, 128), F32)],
        micros=2.9,
    )(dilations, *parts, pre_high, pre_low, grad_hidden)

    halve_x = call(halve_kernel, [VMEM] * 2, [((TAPS, 128), F32, VMEM)] * 2)
    keep_x, send_x = halve_x(keep_x, swapped(send_x, 1))

    rest_rows = channels // 2 + LOCAL // 2
    keep_y, send_y = call(
        rest_kernel,
        [VMEM] * 5,
        [((2, rest_rows, 128), F32, VMEM)] * 2,
        [VMEM((4, rest_rows, 128), F32)],
        micros=1.6,
    )(center, hidden_high, hidden_low, cot_high, cot_low)
    out_fwd, out_rev = call(
        outputs_kernel,
        [VMEM] * 4 + [HBM, VMEM],
        [((length, channels), F32, HBM)] * 2,
        [VMEM(square, F32), VMEM((2, length, channels), F32), sems((3,))],
        micros=2.2,
    )(center, hidden_high, hidden_low, local, out_weight, keep_x)
    halve_y = call(halve_after_kernel, [VMEM] * 2 + [HBM], [((rest_rows, 128), F32, VMEM)] * 2)
    keep_y, send_y = halve_y(keep_y, swapped(send_y, 1), out_rev)

    first_high, first_low, second_high, second_low, turn_high, turn_low, *levels = call(
        prepare_kernel,
        [VMEM] * 7,
        [((4, wide, channels), BF16, VMEM)] * 4
        + [(square, BF16, VMEM)] * 2
        + [((CONTEXTS, channels), BF16, VMEM)] * 4,
        micros=1.3,
    )(first_conv, first_mix, second_conv, second_mix, turn, table, keep_y)

    merge_x = call(merge_taps_kernel, [VMEM] * 4, [((3 * CONTEXTS, 128), F32, VMEM)])
    merge_y = call(merge_rest_kernel, [VMEM] * 2, [((rest_rows + EDGE // 2, 128), F32, VMEM)], micros=2.0)
    sum_x = keep_x + swapped(send_x, 2)
    sum_y = call(add_after_kernel, [VMEM] * 3, [(keep_y.shape, F32, VMEM)])(keep_y, swapped(send_y, 2), sum_x)[0]
    piece_x = crossed(sum_x, count, lambda a, b: merge_x(a, b, sum_y, turn_low)[0])
    piece_y = crossed(sum_y, count, lambda a, b: merge_y(a, b)[0])
    cut = call(cut_kernel, [VMEM] * 2, [((piece_x.shape[0] // 2, 128), F32, VMEM)] * 2)
    piece_x01 = cut(swapped(piece_x, 2), piece_y)
    pieces_x = piece_x, *piece_x01, swapped(piece_x, 1), *[swapped(x, 1) for x in piece_x01]

    g_conv, g_mix, bias_row, partial = call(
        last_layer_kernel,
        [VMEM] * 12,
        [
            (conv_weight.shape, F32, HBM),
            (mix_weight.shape, F32, HBM),
            ((1, wide), F32, VMEM),
            ((CONTEXTS, channels), F32, VMEM),
        ],
        [
            VMEM((4, 3 * CONTEXTS, 128), F32),
            VMEM(conv_weight.shape[1:], F32),
            VMEM(mix_weight.shape[1:], F32),
            sems((4,)),
        ],
        micros=0.05,
    )(*pieces_x, *levels, second_high, second_low)

    piece_y01 = touched(swapped(piece_y, 2), partial)
    pieces_y = piece_y, piece_y01, swapped(piece_y, 1), swapped(piece_y01, 1)
    g_conv, g_mix, g_embed, g_bias, g_out = call(
        first_layer_kernel,
        [VMEM] * 12 + [HBM] * 2,
        [
            (conv_weight.shape, F32, HBM),
            (mix_weight.shape, F32, HBM),
            (embed.shape, F32, HBM),
            (gate_bias.shape, F32, HBM),
            (out_weight.shape, F32, HBM),
        ],
        [
            VMEM((4, rest_rows + EDGE // 2, 128), F32),
            VMEM(conv_weight.shape[1:], F32),
            VMEM(mix_weight.shape[1:], F32),
            VMEM(embed.shape, F32),
            VMEM(gate_bias.shape, F32),
            VMEM(out_weight.shape, F32),
            sems((8,)),
        ],
        aliases={12: 0, 13: 1},
        micros=2.2,
    )(*pieces_y, partial, mixed_table, bias_row, embed, first_high, first_low, turn_high, turn_low, g_conv, g_mix)
    return (out_fwd, out_rev, g_embed, g_conv, g_mix, g_bias, g_out)


def solution(mesh):
    in_specs = (
        P(("dp", "seq")),
        P(),
        P(),
        P(),
        P(),
        P(),
        P(),
        P(("dp", "seq"), None),
        P(("dp", "seq"), None),
    )
    out_specs = (
        P(("dp", "seq"), None),
        P(("dp", "seq"), None),
        P("dp", None),
        P("dp", None, None, None),
        P("dp", None, None),
        P("dp", None),
        P("dp", None, None),
    )
    return jax.shard_map(
        on_device, mesh=mesh, in_specs=in_specs, out_specs=out_specs, check_vma=False
    )
```

```python
import jax
import jax.numpy as jnp
from jax import lax
from jax.experimental import pallas as pl
from jax.experimental.pallas import tpu as pltpu
from jax.sharding import PartitionSpec as P

CONTEXTS = 96
INNER = 64
EDGE = 16
LOCAL = INNER + EDGE
TAPS = 3 * LOCAL
HALO = 128
F32 = jnp.float32
BF16 = jnp.bfloat16
VMEM_LIMIT = 40 * 1024 * 1024


def split(x):
    high = x.astype(BF16)
    return high, (x - high.astype(F32)).astype(BF16)


def dot(a, b, ca=1, cb=0):
    return lax.dot_general(a, b, (((ca,), (cb,)), ((), ())), preferred_element_type=F32)


def dot2(exact, pair, ca=1, cb=0):
    return dot(exact, pair[0], ca, cb) + dot(exact, pair[1], ca, cb)


def dot3(a, b, ca=1, cb=0):
    return dot(a[0], b[0], ca, cb) + (dot(a[0], b[1], ca, cb) + dot(a[1], b[0], ca, cb))


def letters(index):
    inner = index < 64
    left = (index >= 64) & (index < 80)
    low = index & 3
    mid = (index >> 2) & 3
    l = jnp.where(inner, (index >> 4) & 3, jnp.where(left, -1, mid))
    m = jnp.where(inner | left, mid, low)
    r = jnp.where(inner | left, low, -1)
    return l, m, r


def mirrored(index):
    low = 3 - (index & 3)
    mid = 3 - ((index >> 2) & 3)
    high = 3 - ((index >> 4) & 3)
    inner = low * 16 + mid * 4 + high
    left = 80 + low * 4 + mid
    right = 64 + low * 4 + mid
    return jnp.where(index < 64, inner, jnp.where(index < 80, left, right))


def permutation():
    rows = lax.broadcasted_iota(jnp.int32, (CONTEXTS, CONTEXTS), 0)
    cols = lax.broadcasted_iota(jnp.int32, (CONTEXTS, CONTEXTS), 1)
    return (mirrored(rows) == cols).astype(F32).astype(BF16)


def letter_hot():
    rows = lax.broadcasted_iota(jnp.int32, (CONTEXTS, 32), 0)
    cols = lax.broadcasted_iota(jnp.int32, (CONTEXTS, 32), 1)
    l, m, r = letters(rows)
    kind = cols >> 3
    value = jnp.where(kind == 0, l, jnp.where(kind == 1, m, jnp.where(kind == 2, r, 3 - m)))
    return (value == (cols & 7)).astype(F32).astype(BF16)


def gates(mixed):
    channels = mixed.shape[1] // 2
    tanh_part = jnp.tanh(mixed[:, :channels])
    sig_part = 0.5 + 0.5 * jnp.tanh(0.5 * mixed[:, channels:])
    return tanh_part, sig_part


def gate_grads(grad_hidden, tanh_part, sig_part):
    scaled = grad_hidden * sig_part
    return scaled * (1.0 - tanh_part * tanh_part), scaled * tanh_part * (1.0 - sig_part)


class Fetch:
    def __init__(self, sems):
        self.sems = sems
        self.copies = []

    def start(self, source, target):
        copy = pltpu.make_async_copy(source, target, self.sems.at[len(self.copies)])
        copy.start()
        self.copies.append(copy)
        return len(self.copies) - 1

    def wait(self, *which):
        for at in which:
            self.copies[at].wait()


def padded_base(embed):
    return jnp.concatenate([embed[...], jnp.zeros((4, embed.shape[1]), F32)], axis=0)


def left_side():
    return lax.axis_index("seq") * 2 < lax.axis_size("seq")


def local_rows(rows):
    edge = jnp.where(left_side(), rows[INNER : INNER + EDGE], rows[INNER + EDGE : INNER + 2 * EDGE])
    return jnp.concatenate([rows[:INNER], edge], axis=0)


def join_kernel(first, second, after, out):
    rows = first.shape[0]
    out[:rows, :] = first[...]
    out[rows:, :] = second[...]


def load_kernel(source, out, sems):
    fetch = Fetch(sems)
    fetch.start(source, out)
    fetch.wait(0)


def touch_kernel(value, after, out):
    out[...] = value[...]


def cut_kernel(value, after, first, second):
    half = first.shape[0]
    first[...] = value[:half, :]
    second[...] = value[half:, :]


def first_tables_kernel(
    embed_in, conv_in, mix_in, bias_in, out_in, after, table, local, mixed_table, conv, mix, bias, out_w, embed, sems,
):
    fetch = Fetch(sems)
    small = [fetch.start(embed_in, embed), fetch.start(bias_in, bias)]
    first = [fetch.start(conv_in.at[0, k], conv.at[k]) for k in range(3)]
    first += [fetch.start(mix_in.at[0], mix)]
    turn = fetch.start(out_in.at[0], out_w)
    hot = letter_hot()
    fetch.wait(*small)
    base = split(padded_base(embed))
    taps = []
    for k in range(4):
        fetch.wait(first[k])
        taps.append(dot3(base, split(conv[k] if k < 3 else mix[...])))
    taps = jnp.concatenate(taps, axis=0)
    mixed = dot2(hot, split(taps)) + bias[0:1, :]
    tanh_part, sig_part = gates(mixed)
    hidden = tanh_part * sig_part
    own = dot2(hot[:, 8:16], base)
    fetch.wait(turn)
    level = own + dot3(split(hidden), split(out_w[...]))
    table[...] = level
    local[...] = local_rows(level)
    mixed_table[...] = mixed


def second_tables_kernel(
    table, bias, conv_in, mix_in, out_in, cot_fwd_in, cot_rev_in, after, pre_high, pre_low, cot_high, cot_low, grad_hidden,
    conv, mix, out_w, cots, sems,
):
    length = cots.shape[1]
    fetch = Fetch(sems)
    fetch.start(out_in.at[1], out_w)
    fetch.start(cot_fwd_in, cots.at[0])
    second = [fetch.start(conv_in.at[1, k], conv.at[k]) for k in range(3)]
    second += [fetch.start(mix_in.at[1], mix)]
    last = fetch.start(cot_rev_in, cots.at[1])

    def cotangents(strand):
        rows = slice(strand * length, (strand + 1) * length)
        cot = split(cots[strand])
        cot_high[rows, :] = cot[0]
        cot_low[rows, :] = cot[1]
        grad_hidden[rows, :] = dot3(cot, weight, 1, 1)

    level = split(table[...])
    swap = permutation()
    partner = tuple(dot(swap, piece).astype(BF16) for piece in level)
    pre_high[TAPS:, :] = jnp.zeros((pre_high.shape[0] - TAPS, pre_high.shape[1]), BF16)
    pre_low[TAPS:, :] = jnp.zeros((pre_low.shape[0] - TAPS, pre_low.shape[1]), BF16)
    fetch.wait(0, 1)
    weight = split(out_w[...])
    cotangents(0)
    for k in (0, 2, 1):
        fetch.wait(second[k])
        value = dot3(level, split(conv[k]))
        if k == 1:
            fetch.wait(second[3])
            value = value + dot3(partner, split(mix[...])) + bias[1:2, :]
        high, low = split(local_rows(value))
        pre_high[k * LOCAL : (k + 1) * LOCAL, :] = high
        pre_low[k * LOCAL : (k + 1) * LOCAL, :] = low
    fetch.wait(last)
    cotangents(1)


def windows(parts, count):
    length = parts[0].shape[1]
    place = lax.axis_index("seq")
    last = count - 1

    def block(at):
        total, begin = None, 0
        for part in parts:
            rows = lax.broadcasted_iota(jnp.int32, part.shape, 0) + begin
            piece = jnp.sum(jnp.where(rows == (place ^ at), part[...], 0), axis=0, keepdims=True)
            total = piece if total is None else total + piece
            begin += part.shape[0]
        return total

    def window(at):
        before = jnp.where(at == 0, -1, block(jnp.maximum(at - 1, 0))[:, length - HALO :])
        after = jnp.where(at == last, -1, block(jnp.minimum(at + 1, last))[:, :HALO])
        return [before, block(at), after]

    fwd = jnp.concatenate(window(place), axis=1)
    rev = jnp.concatenate(window(last - place), axis=1)
    rev = jnp.where(rev < 0, -1, 3 - rev)
    tiles = rev.shape[1] // 128
    blocks = [rev[:, i * 128 : (i + 1) * 128] for i in reversed(range(tiles))]
    blocks += [jnp.zeros((8 - tiles, 128), jnp.int32)]
    stacked = jnp.concatenate(blocks, axis=0).astype(F32).astype(BF16)
    rows = lax.broadcasted_iota(jnp.int32, (128, 128), 0)
    cols = lax.broadcasted_iota(jnp.int32, (128, 128), 1)
    flip = (rows + cols == 127).astype(F32).astype(BF16)
    turned = dot(stacked, flip).astype(jnp.int32)
    rev = jnp.concatenate([turned[i : i + 1, :] for i in range(tiles)], axis=1)
    return fwd, rev


def local_contexts(window, first, second, length):
    width = window.shape[1]
    base = jnp.broadcast_to(window, (8, width))
    l = pltpu.roll(base, first, 1)
    r = pltpu.roll(base, width - first, 1)
    index = jnp.where(l < 0, INNER + base * 4 + r, jnp.where(r < 0, INNER + l * 4 + base, l * 16 + base * 4 + r))
    index = jnp.where(base < 0, LOCAL, index)
    before = pltpu.roll(index, second, 1)
    after = pltpu.roll(index, width - second, 1)
    return [x[0:1, HALO : HALO + length] for x in (before, index, after)]


def hot_rows(index):
    rows = lax.broadcasted_iota(jnp.int32, (LOCAL, index.shape[1]), 0)
    return (rows == index).astype(F32).astype(BF16)


def deal(quarters, keep, send):
    bit = lax.axis_index("seq") & 1
    keep[...] = quarters[pl.ds(bit * 2, 2)]
    send[...] = quarters[pl.ds((1 - bit) * 2, 2)]


def main_kernel(count, dil, *refs):
    parts, refs = refs[: count.bit_length()], refs[count.bit_length() :]
    (pre_high, pre_low, grad_hidden, cot_high, cot_low, keep, send, hidden_high, hidden_low, center, quarters) = refs
    length = parts[0].shape[1]
    pre = (pre_high[...], pre_low[...])
    both = windows(parts, count)
    pad = jnp.zeros((pre_high.shape[0] - TAPS, length), BF16)
    total = total_c = None
    for strand in range(2):
        index = local_contexts(both[strand], dil[0], dil[1], length)
        hot = jnp.concatenate([hot_rows(x) for x in index] + [pad], axis=0)
        center[strand : strand + 1, :] = index[1]
        mixed = dot2(hot, pre, 0, 0)
        tanh_part, sig_part = gates(mixed)
        hidden = split(tanh_part * sig_part)
        rows = slice(strand * length, (strand + 1) * length)
        hidden_high[rows, :] = hidden[0]
        hidden_low[rows, :] = hidden[1]
        grads = split(jnp.concatenate(gate_grads(grad_hidden[rows, :], tanh_part, sig_part), axis=1))
        part = dot2(hot, grads)
        part_c = dot2(hot[LOCAL : 2 * LOCAL], (cot_high[rows, :], cot_low[rows, :]))
        total = part if total is None else total + part
        total_c = part_c if total_c is None else total_c + part_c
    for q in range(4):
        quarters[q, :TAPS, :] = total[:TAPS, q * 128 : (q + 1) * 128]
        lanes = slice((q >> 1) * 128, (q >> 1) * 128 + 128)
        for begin, count_c, at in ((0, INNER // 2, TAPS), (INNER, EDGE // 2, TAPS + INNER // 2)):
            begin += (q & 1) * count_c
            quarters[q, at : at + count_c, :] = total_c[begin : begin + count_c, lanes]
    deal(quarters, keep, send)


def halve_kernel(kept, received, keep, send):
    bit = (lax.axis_index("seq") >> 1) & 1
    send[...] = kept[1 - bit] + received[1 - bit]
    keep[...] = kept[bit] + received[bit]


def add_after_kernel(kept, received, after, out):
    out[...] = kept[...] + received[...]


def halve_after_kernel(kept, received, after, keep, send):
    halve_kernel(kept, received, keep, send)


def center_hots(center):
    return [hot_rows(center[strand : strand + 1, :]) for strand in range(2)]


def turn_kernel(hidden_high, hidden_low, cot_high, cot_low, keep, send, quarters):
    hidden = (hidden_high[...], hidden_low[...])
    total = dot3(hidden, (cot_high[...], cot_low[...]), 0, 0)
    side = total.shape[0] // 4
    for q in range(4):
        quarters[q, :side, :] = total[q * side : (q + 1) * side, :128]
        quarters[q, side:, :] = total[q * side : (q + 1) * side, 128:]
    deal(quarters, keep, send)


def outputs_kernel(
    center, hidden_high, hidden_low, local, out_in, after, out_fwd_out, out_rev_out, out_w, out_both, sems,
):
    length = center.shape[1]
    fetch = Fetch(sems)
    fetch.start(out_in.at[1], out_w)
    hots = center_hots(center)
    level = split(local[...])
    fetch.wait(0)
    weight = split(out_w[...])
    for strand, out in enumerate((out_fwd_out, out_rev_out)):
        rows = slice(strand * length, (strand + 1) * length)
        update = dot3((hidden_high[rows, :], hidden_low[rows, :]), weight)
        out_both[strand] = dot2(hots[strand], level, 0, 0) + update
        fetch.start(out_both.at[strand], out)
    fetch.wait(1, 2)


def prepare_kernel(
    first_conv, first_mix, second_conv, second_mix, out_w, table, after, first_high, first_low, second_high, second_low, turn_high, turn_low,
    level_high, level_low, partner_high, partner_low,
):
    level = split(table[...])
    swap = permutation()
    level_high[...], level_low[...] = level
    partner_high[...], partner_low[...] = tuple(dot(swap, piece).astype(BF16) for piece in level)
    for conv, mix, high, low in (
        (second_conv, second_mix, second_high, second_low),
        (first_conv, first_mix, first_high, first_low),
    ):
        for k in range(4):
            high[k], low[k] = split((conv[k] if k < 3 else mix[...]).T)
    turn_high[...], turn_low[...] = split(out_w[...].T)


def merge(mine, theirs, inner, edge):
    left = left_side()
    both = mine[inner, :] + theirs[inner, :]
    own, other = mine[edge, :], theirs[edge, :]
    return both, jnp.where(left, own, other), jnp.where(left, other, own)


def merge_taps_kernel(mine, theirs, after, out):
    for at, to, inner, edge in [(k * LOCAL, k * CONTEXTS, INNER, EDGE) for k in range(3)] + [
        (TAPS, 3 * CONTEXTS, INNER // 2, EDGE // 2)
    ]:
        pieces = merge(mine, theirs, slice(at, at + inner), slice(at + inner, at + inner + edge))
        out[to : to + inner, :] = pieces[0]
        out[to + inner : to + inner + edge, :] = pieces[1]
        out[to + inner + edge : to + inner + 2 * edge, :] = pieces[2]


def gather_quarters(pieces, quarters):
    place = lax.axis_index("seq")
    low, high = place & 1, (place >> 1) & 1
    for parts, x, y in zip(pieces, (0, 0, 1, 1), (0, 1, 0, 1)):
        begin = 0
        for part in parts:
            rows = part.shape[0]
            quarters[(low ^ x) * 2 + (high ^ y), begin : begin + rows, :] = part[...]
            begin += rows


def last_layer_kernel(
    piece_00, piece_01, piece_01_too, piece_10, piece_11, piece_11_too, level_high, level_low, partner_high, partner_low, second_high, second_low,
    g_conv_out, g_mix_out, g_bias, partial,
    quarters, g_conv, g_mix, out_sems,
):
    store = Fetch(out_sems)
    gather_quarters(((piece_00,), (piece_01, piece_01_too), (piece_10,), (piece_11, piece_11_too)), quarters)
    level = (level_high[...], level_low[...])
    partner = (partner_high[...], partner_low[...])
    grad_level = []
    for begin, rows in ((0, INNER // 2), (INNER // 2, EDGE // 2), (INNER // 2 + EDGE // 2, EDGE // 2)):
        begin += 3 * CONTEXTS
        sides = [[quarters[2 * h + i, begin : begin + rows, :] for i in range(2)] for h in range(2)]
        grad_level.append(jnp.concatenate([jnp.concatenate(x, axis=0) for x in sides], axis=1))
    grad_level = jnp.concatenate(grad_level, axis=0)
    for k in range(3):
        piece = jnp.concatenate([quarters[q, k * CONTEXTS : (k + 1) * CONTEXTS, :] for q in range(4)], axis=1)
        pair = split(piece)
        g_conv[k] = dot3(level, pair, 0, 0)
        store.start(g_conv.at[k], g_conv_out.at[1, k])
        grad_level = grad_level + dot3(pair, (second_high[k], second_low[k]))
        if k == 1:
            g_bias[...] = jnp.sum(piece, axis=0, keepdims=True)
            g_mix[...] = dot3(partner, pair, 0, 0)
            store.start(g_mix, g_mix_out.at[1])
            grad_level = grad_level + dot2(permutation(), split(dot3(pair, (second_high[3], second_low[3]))))
    partial[...] = grad_level
    store.wait(*range(len(store.copies)))


def first_layer_kernel(
    partial, mixed_table, bias_row, embed, first_high, first_low, turn_high, turn_low,
    g_conv_in, g_mix_in, g_conv_out, g_mix_out, g_embed_out, g_bias_out, g_out_out,
    g_conv, g_mix, g_embed, g_bias, g_out, out_sems,
):
    store = Fetch(out_sems)
    grad_level = split(partial[...])
    tanh_part, sig_part = gates(mixed_table[...])
    hidden = split(tanh_part * sig_part)
    grad_hidden = dot3(grad_level, (turn_high[...], turn_low[...]))
    grad_mixed = jnp.concatenate(gate_grads(grad_hidden, tanh_part, sig_part), axis=1)
    g_bias[0:1, :] = jnp.sum(grad_mixed, axis=0, keepdims=True)
    g_bias[1:2, :] = bias_row[...]
    store.start(g_bias, g_bias_out)
    hot = letter_hot()
    by_letter = dot2(hot, split(grad_mixed), 0, 0)
    base = split(padded_base(embed))
    stacked = jnp.concatenate([base[0].astype(F32), base[0].astype(F32), base[1].astype(F32)], axis=0).astype(BF16)
    pieces = []
    for k in range(4):
        piece = split(by_letter[k * 8 : (k + 1) * 8, :])
        pieces.append(piece)
        high, low = piece[0].astype(F32), piece[1].astype(F32)
        value = dot(stacked, jnp.concatenate([high, low, high], axis=0).astype(BF16), 0, 0)
        if k < 3:
            g_conv[k] = value
            store.start(g_conv.at[k], g_conv_out.at[0, k])
        else:
            g_mix[...] = value
            store.start(g_mix, g_mix_out.at[0])
    g_out[...] = dot3(hidden, grad_level, 0, 0)
    store.start(g_out, g_out_out.at[0])
    grad_base = dot2(hot[:, 8:16], grad_level, 0, 0)
    for k in range(4):
        grad_base = grad_base + dot3(pieces[k], (first_high[k], first_low[k]))
    g_embed[...] = grad_base[:4, :]
    store.start(g_embed, g_embed_out)
    store.wait(*range(len(store.copies)))


def store_kernel(piece_00, piece_01, piece_10, piece_11, g_out_in, g_out_out, quarters, g_out, out_sems):
    store = Fetch(out_sems)
    gather_quarters([(piece,) for piece in (piece_00, piece_01, piece_10, piece_11)], quarters)
    side = quarters.shape[1] // 2
    for q in range(4):
        for h in range(2):
            g_out[q * side : (q + 1) * side, h * 128 : (h + 1) * 128] = quarters[q, h * side : (h + 1) * side, :]
    store.start(g_out, g_out_out.at[1])
    store.wait(0)


VMEM, SMEM, HBM = pltpu.VMEM, pltpu.SMEM, pltpu.HBM


def call(kernel, ins, outs, scratch=(), aliases=None, micros=0.001):
    run = pl.pallas_call(
        kernel,
        out_shape=[space(shape, kind) for shape, kind, space in outs],
        in_specs=[pl.BlockSpec(memory_space=space) for space in ins],
        out_specs=[pl.BlockSpec(memory_space=space) for _, _, space in outs],
        scratch_shapes=list(scratch),
        input_output_aliases=aliases or {},
        cost_estimate=pl.CostEstimate(flops=int(micros * 1.1e9), bytes_accessed=int(micros * 3e6), transcendentals=0),
        compiler_params=pltpu.CompilerParams(vmem_limit_bytes=VMEM_LIMIT),
    )

    def placed(*args):
        return run(*[pltpu.with_memory_space_constraint(x, HBM) if space is HBM else x for x, space in zip(args, ins)])

    return placed


def swapped(value, mask):
    pairs = [(source, source ^ mask) for source in range(lax.axis_size("seq"))]
    return lax.ppermute(value, "seq", pairs)


def crossed(piece, count, rest):
    mask = 4
    while mask < count // 2:
        piece = piece + swapped(piece, mask)
        mask *= 2
    return rest(piece, swapped(piece, mask))


def on_device(
    tokens, dilations, embed, conv_weight, mix_weight, gate_bias, out_weight, cot_fwd, cot_rev
):
    channels = embed.shape[1]
    wide = 2 * channels
    length = tokens.shape[0]
    count = lax.axis_size("seq")
    sems = pltpu.SemaphoreType.DMA
    square = (channels, channels)

    def touched(value, after):
        return call(touch_kernel, [VMEM] * 2, [(value.shape, value.dtype, VMEM)])(value, after)[0]

    def joined(first, second, after):
        shape = (2 * first.shape[0], first.shape[1])
        return call(join_kernel, [VMEM] * 3, [(shape, first.dtype, VMEM)])(first, second, after)[0]

    known = tokens.reshape(1, length)
    own = call(load_kernel, [HBM], [(known.shape, known.dtype, VMEM)], [sems((1,))], micros=0.7)(known)[0]
    parts = [own, swapped(known, 1)]
    known = joined(own, parts[-1], own)
    parts.append(swapped(known, 2))
    layer_weights = [(conv_weight.shape[1:], F32, VMEM), (mix_weight.shape[1:], F32, VMEM)]
    table, local, mixed_table, first_conv, first_mix, bias, turn = call(
        first_tables_kernel,
        [HBM] * 5 + [VMEM],
        [
            ((CONTEXTS, channels), F32, VMEM),
            ((LOCAL, channels), F32, VMEM),
            ((CONTEXTS, wide), F32, VMEM),
            *layer_weights,
            (gate_bias.shape, F32, VMEM),
            (square, F32, VMEM),
        ],
        [VMEM(embed.shape, F32), sems((7,))],
        micros=2.6,
    )(embed, conv_weight, mix_weight, gate_bias, out_weight, known)
    known = joined(known, parts[-1], table)
    parts.append(swapped(known, 4))
    deep = -(-TAPS // 128) * 128
    pre_high, pre_low, cot_high, cot_low, grad_hidden, second_conv, second_mix = call(
        second_tables_kernel,
        [VMEM] * 2 + [HBM] * 5 + [VMEM],
        [((deep, wide), BF16, VMEM)] * 2
        + [((2 * length, channels), BF16, VMEM)] * 2
        + [((2 * length, channels), F32, VMEM)]
        + layer_weights,
        [VMEM(square, F32), VMEM((2, length, channels), F32), sems((7,))],
        micros=3.0,
    )(table, bias, conv_weight, mix_weight, out_weight, cot_fwd, cot_rev, known)
    mask = 8
    while mask < count:
        known = joined(known, parts[-1], pre_low)
        parts.append(swapped(known, mask))
        mask *= 2

    sum_rows = TAPS + LOCAL // 2
    keep_x, send_x, hidden_high, hidden_low, center = call(
        lambda *refs: main_kernel(count, *refs),
        [SMEM] + [VMEM] * (len(parts) + 5),
        [((2, sum_rows, 128), F32, VMEM)] * 2
        + [((2 * length, channels), BF16, VMEM)] * 2
        + [((2, length), jnp.int32, VMEM)],
        [VMEM((4, sum_rows, 128), F32)],
        micros=2.9,
    )(dilations, *parts, pre_high, pre_low, grad_hidden, cot_high, cot_low)

    halve_x = call(halve_kernel, [VMEM] * 2, [((sum_rows, 128), F32, VMEM)] * 2)
    keep_x, send_x = halve_x(keep_x, swapped(send_x, 1))

    turn_rows = channels // 2
    keep_y, send_y = call(
        turn_kernel,
        [VMEM] * 4,
        [((2, turn_rows, 128), F32, VMEM)] * 2,
        [VMEM((4, turn_rows, 128), F32)],
        micros=0.8,
    )(hidden_high, hidden_low, cot_high, cot_low)
    halve_y = call(halve_after_kernel, [VMEM] * 3, [((turn_rows, 128), F32, VMEM)] * 2)
    keep_y, send_y = halve_y(keep_y, swapped(send_y, 1), keep_x)

    add_x = call(add_after_kernel, [VMEM] * 3, [((sum_rows, 128), F32, VMEM)])
    add_y = call(add_after_kernel, [VMEM] * 3, [((turn_rows, 128), F32, VMEM)])
    sum_x = add_x(keep_x, swapped(send_x, 2), keep_y)[0]
    out_fwd, out_rev = call(
        outputs_kernel,
        [VMEM] * 4 + [HBM, VMEM],
        [((length, channels), F32, HBM)] * 2,
        [VMEM(square, F32), VMEM((2, length, channels), F32), sems((3,))],
        micros=2.7,
    )(center, hidden_high, hidden_low, local, out_weight, sum_x)

    first_high, first_low, second_high, second_low, turn_high, turn_low, *levels = call(
        prepare_kernel,
        [VMEM] * 6 + [HBM],
        [((4, wide, channels), BF16, VMEM)] * 4
        + [(square, BF16, VMEM)] * 2
        + [((CONTEXTS, channels), BF16, VMEM)] * 4,
        micros=1.3,
    )(first_conv, first_mix, second_conv, second_mix, turn, table, out_rev)

    merged_rows = 3 * CONTEXTS + CONTEXTS // 2
    merge_x = call(merge_taps_kernel, [VMEM] * 3, [((merged_rows, 128), F32, VMEM)])
    sum_y = add_y(keep_y, swapped(send_y, 2), turn_low)[0]
    piece_x = crossed(sum_x, count, lambda a, b: merge_x(a, b, sum_y)[0])
    cross_y = call(add_after_kernel, [VMEM] * 3, [((turn_rows, 128), F32, VMEM)], micros=2.0)
    piece_y = crossed(sum_y, count, lambda a, b: cross_y(a, b, piece_x)[0])
    cut = call(cut_kernel, [VMEM] * 2, [((merged_rows // 2, 128), F32, VMEM)] * 2)
    piece_x01 = cut(swapped(piece_x, 2), piece_y)
    pieces_x = piece_x, *piece_x01, swapped(piece_x, 1), *[swapped(x, 1) for x in piece_x01]

    g_conv, g_mix, bias_row, partial = call(
        last_layer_kernel,
        [VMEM] * 12,
        [
            (conv_weight.shape, F32, HBM),
            (mix_weight.shape, F32, HBM),
            ((1, wide), F32, VMEM),
            ((CONTEXTS, channels), F32, VMEM),
        ],
        [
            VMEM((4, merged_rows, 128), F32),
            VMEM(conv_weight.shape[1:], F32),
            VMEM(mix_weight.shape[1:], F32),
            sems((4,)),
        ],
        micros=0.05,
    )(*pieces_x, *levels, second_high, second_low)

    piece_y01 = touched(swapped(piece_y, 2), partial)
    pieces_y = piece_y, piece_y01, swapped(piece_y, 1), swapped(piece_y01, 1)
    g_conv, g_mix, g_embed, g_bias, g_out = call(
        first_layer_kernel,
        [VMEM] * 8 + [HBM] * 2,
        [
            (conv_weight.shape, F32, HBM),
            (mix_weight.shape, F32, HBM),
            (embed.shape, F32, HBM),
            (gate_bias.shape, F32, HBM),
            (out_weight.shape, F32, HBM),
        ],
        [
            VMEM(conv_weight.shape[1:], F32),
            VMEM(mix_weight.shape[1:], F32),
            VMEM(embed.shape, F32),
            VMEM(gate_bias.shape, F32),
            VMEM(square, F32),
            sems((7,)),
        ],
        aliases={8: 0, 9: 1},
        micros=2.2,
    )(partial, mixed_table, bias_row, embed, first_high, first_low, turn_high, turn_low, g_conv, g_mix)
    g_out = call(
        store_kernel,
        [VMEM] * 4 + [HBM],
        [(out_weight.shape, F32, HBM)],
        [VMEM((4, turn_rows, 128), F32), VMEM(square, F32), sems((1,))],
        aliases={4: 0},
    )(*pieces_y, g_out)[0]
    return (out_fwd, out_rev, g_embed, g_conv, g_mix, g_bias, g_out)


def solution(mesh):
    in_specs = (
        P(("dp", "seq")),
        P(),
        P(),
        P(),
        P(),
        P(),
        P(),
        P(("dp", "seq"), None),
        P(("dp", "seq"), None),
    )
    out_specs = (
        P(("dp", "seq"), None),
        P(("dp", "seq"), None),
        P("dp", None),
        P("dp", None, None, None),
        P("dp", None, None),
        P("dp", None),
        P("dp", None, None),
    )
    return jax.shard_map(
        on_device, mesh=mesh, in_specs=in_specs, out_specs=out_specs, check_vma=False
    )
```

```python
import jax
import jax.numpy as jnp
from jax import lax
from jax.experimental import pallas as pl
from jax.experimental.pallas import tpu as pltpu
from jax.sharding import PartitionSpec as P

CONTEXTS = 96
INNER = 64
EDGE = 16
LOCAL = INNER + EDGE
TAPS = 3 * LOCAL
HALO = 128
F32 = jnp.float32
BF16 = jnp.bfloat16
VMEM_LIMIT = 40 * 1024 * 1024


def split(x):
    high = x.astype(BF16)
    return high, (x - high.astype(F32)).astype(BF16)


def dot(a, b, ca=1, cb=0):
    return lax.dot_general(a, b, (((ca,), (cb,)), ((), ())), preferred_element_type=F32)


def dot2(exact, pair, ca=1, cb=0):
    return dot(exact, pair[0], ca, cb) + dot(exact, pair[1], ca, cb)


def dot3(a, b, ca=1, cb=0):
    return dot(a[0], b[0], ca, cb) + (dot(a[0], b[1], ca, cb) + dot(a[1], b[0], ca, cb))


def letters(index):
    inner = index < 64
    left = (index >= 64) & (index < 80)
    low = index & 3
    mid = (index >> 2) & 3
    l = jnp.where(inner, (index >> 4) & 3, jnp.where(left, -1, mid))
    m = jnp.where(inner | left, mid, low)
    r = jnp.where(inner | left, low, -1)
    return l, m, r


def mirrored(index):
    low = 3 - (index & 3)
    mid = 3 - ((index >> 2) & 3)
    high = 3 - ((index >> 4) & 3)
    inner = low * 16 + mid * 4 + high
    left = 80 + low * 4 + mid
    right = 64 + low * 4 + mid
    return jnp.where(index < 64, inner, jnp.where(index < 80, left, right))


def permutation():
    rows = lax.broadcasted_iota(jnp.int32, (CONTEXTS, CONTEXTS), 0)
    cols = lax.broadcasted_iota(jnp.int32, (CONTEXTS, CONTEXTS), 1)
    return (mirrored(rows) == cols).astype(F32).astype(BF16)


def letter_hot():
    rows = lax.broadcasted_iota(jnp.int32, (CONTEXTS, 32), 0)
    cols = lax.broadcasted_iota(jnp.int32, (CONTEXTS, 32), 1)
    l, m, r = letters(rows)
    kind = cols >> 3
    value = jnp.where(kind == 0, l, jnp.where(kind == 1, m, jnp.where(kind == 2, r, 3 - m)))
    return (value == (cols & 7)).astype(F32).astype(BF16)


def gates(mixed):
    channels = mixed.shape[1] // 2
    tanh_part = jnp.tanh(mixed[:, :channels])
    sig_part = 0.5 + 0.5 * jnp.tanh(0.5 * mixed[:, channels:])
    return tanh_part, sig_part


def gate_grads(grad_hidden, tanh_part, sig_part):
    scaled = grad_hidden * sig_part
    return scaled * (1.0 - tanh_part * tanh_part), scaled * tanh_part * (1.0 - sig_part)


class Fetch:
    def __init__(self, sems):
        self.sems = sems
        self.copies = []

    def start(self, source, target):
        copy = pltpu.make_async_copy(source, target, self.sems.at[len(self.copies)])
        copy.start()
        self.copies.append(copy)
        return len(self.copies) - 1

    def wait(self, *which):
        for at in which:
            self.copies[at].wait()


def padded_base(embed):
    return jnp.concatenate([embed[...], jnp.zeros((4, embed.shape[1]), F32)], axis=0)


def left_side():
    return lax.axis_index("seq") * 2 < lax.axis_size("seq")


def local_rows(rows):
    edge = jnp.where(left_side(), rows[INNER : INNER + EDGE], rows[INNER + EDGE : INNER + 2 * EDGE])
    return jnp.concatenate([rows[:INNER], edge], axis=0)


def join_kernel(first, second, after, out):
    rows = first.shape[0]
    out[:rows, :] = first[...]
    out[rows:, :] = second[...]


def load_kernel(source, out, sems):
    fetch = Fetch(sems)
    fetch.start(source, out)
    fetch.wait(0)


def touch_kernel(value, after, *outs):
    begin = 0
    for out in outs:
        out[...] = value[begin : begin + out.shape[0], :]
        begin += out.shape[0]


def first_tables_kernel(
    embed_in, conv_in, mix_in, bias_in, out_in, after, table, local, mixed_table, conv, mix, bias, out_w, embed, sems,
):
    fetch = Fetch(sems)
    small = [fetch.start(embed_in, embed), fetch.start(bias_in, bias)]
    first = [fetch.start(conv_in.at[0, k], conv.at[k]) for k in range(3)]
    first += [fetch.start(mix_in.at[0], mix)]
    turn = fetch.start(out_in.at[0], out_w)
    hot = letter_hot()
    fetch.wait(*small)
    base = split(padded_base(embed))
    taps = []
    for k in range(4):
        fetch.wait(first[k])
        taps.append(dot3(base, split(conv[k] if k < 3 else mix[...])))
    taps = jnp.concatenate(taps, axis=0)
    mixed = dot2(hot, split(taps)) + bias[0:1, :]
    tanh_part, sig_part = gates(mixed)
    hidden = tanh_part * sig_part
    own = dot2(hot[:, 8:16], base)
    fetch.wait(turn)
    level = own + dot3(split(hidden), split(out_w[...]))
    table[...] = level
    local[...] = local_rows(level)
    mixed_table[...] = mixed


def second_tables_kernel(
    table, bias, conv_in, mix_in, out_in, cot_fwd_in, cot_rev_in, after, pre_high, pre_low, cot_high, cot_low, grad_hidden,
    conv, mix, out_w, cots, sems,
):
    length = cots.shape[1]
    fetch = Fetch(sems)
    fetch.start(out_in.at[1], out_w)
    fetch.start(cot_fwd_in, cots.at[0])
    second = [fetch.start(conv_in.at[1, k], conv.at[k]) for k in range(3)]
    second += [fetch.start(mix_in.at[1], mix)]
    last = fetch.start(cot_rev_in, cots.at[1])

    def cotangents(strand):
        rows = slice(strand * length, (strand + 1) * length)
        cot = split(cots[strand])
        cot_high[rows, :] = cot[0]
        cot_low[rows, :] = cot[1]
        grad_hidden[rows, :] = dot3(cot, weight, 1, 1)

    level = split(table[...])
    swap = permutation()
    partner = tuple(dot(swap, piece).astype(BF16) for piece in level)
    pre_high[TAPS:, :] = jnp.zeros((pre_high.shape[0] - TAPS, pre_high.shape[1]), BF16)
    pre_low[TAPS:, :] = jnp.zeros((pre_low.shape[0] - TAPS, pre_low.shape[1]), BF16)
    fetch.wait(0, 1)
    weight = split(out_w[...])
    cotangents(0)
    for k in (0, 2, 1):
        fetch.wait(second[k])
        value = dot3(level, split(conv[k]))
        if k == 1:
            fetch.wait(second[3])
            value = value + dot3(partner, split(mix[...])) + bias[1:2, :]
        high, low = split(local_rows(value))
        pre_high[k * LOCAL : (k + 1) * LOCAL, :] = high
        pre_low[k * LOCAL : (k + 1) * LOCAL, :] = low
    fetch.wait(last)
    cotangents(1)


def windows(parts, count):
    length = parts[0].shape[1]
    place = lax.axis_index("seq")
    last = count - 1

    def block(at):
        total, begin = None, 0
        for part in parts:
            rows = lax.broadcasted_iota(jnp.int32, part.shape, 0) + begin
            piece = jnp.sum(jnp.where(rows == (place ^ at), part[...], 0), axis=0, keepdims=True)
            total = piece if total is None else total + piece
            begin += part.shape[0]
        return total

    def window(at):
        before = jnp.where(at == 0, -1, block(jnp.maximum(at - 1, 0))[:, length - HALO :])
        after = jnp.where(at == last, -1, block(jnp.minimum(at + 1, last))[:, :HALO])
        return [before, block(at), after]

    fwd = jnp.concatenate(window(place), axis=1)
    rev = jnp.concatenate(window(last - place), axis=1)
    rev = jnp.where(rev < 0, -1, 3 - rev)
    tiles = rev.shape[1] // 128
    blocks = [rev[:, i * 128 : (i + 1) * 128] for i in reversed(range(tiles))]
    blocks += [jnp.zeros((8 - tiles, 128), jnp.int32)]
    stacked = jnp.concatenate(blocks, axis=0).astype(F32).astype(BF16)
    rows = lax.broadcasted_iota(jnp.int32, (128, 128), 0)
    cols = lax.broadcasted_iota(jnp.int32, (128, 128), 1)
    flip = (rows + cols == 127).astype(F32).astype(BF16)
    turned = dot(stacked, flip).astype(jnp.int32)
    rev = jnp.concatenate([turned[i : i + 1, :] for i in range(tiles)], axis=1)
    return fwd, rev


def local_contexts(window, first, second, length):
    width = window.shape[1]
    base = jnp.broadcast_to(window, (8, width))
    l = pltpu.roll(base, first, 1)
    r = pltpu.roll(base, width - first, 1)
    index = jnp.where(l < 0, INNER + base * 4 + r, jnp.where(r < 0, INNER + l * 4 + base, l * 16 + base * 4 + r))
    index = jnp.where(base < 0, LOCAL, index)
    before = pltpu.roll(index, second, 1)
    after = pltpu.roll(index, width - second, 1)
    return [x[0:1, HALO : HALO + length] for x in (before, index, after)]


def hot_rows(index):
    rows = lax.broadcasted_iota(jnp.int32, (LOCAL, index.shape[1]), 0)
    return (rows == index).astype(F32).astype(BF16)


def deal(quarters, keep, send):
    bit = lax.axis_index("seq") & 1
    keep[...] = quarters[pl.ds(bit * 2, 2)]
    send[...] = quarters[pl.ds((1 - bit) * 2, 2)]


def main_kernel(count, dil, *refs):
    parts, refs = refs[: count.bit_length()], refs[count.bit_length() :]
    (pre_high, pre_low, grad_hidden, cot_high, cot_low, keep, send, hidden_high, hidden_low, center, quarters) = refs
    length = parts[0].shape[1]
    pre = (pre_high[...], pre_low[...])
    both = windows(parts, count)
    pad = jnp.zeros((pre_high.shape[0] - TAPS, length), BF16)
    total = total_c = None
    for strand in range(2):
        index = local_contexts(both[strand], dil[0], dil[1], length)
        hot = jnp.concatenate([hot_rows(x) for x in index] + [pad], axis=0)
        center[strand : strand + 1, :] = index[1]
        mixed = dot2(hot, pre, 0, 0)
        tanh_part, sig_part = gates(mixed)
        hidden = split(tanh_part * sig_part)
        rows = slice(strand * length, (strand + 1) * length)
        hidden_high[rows, :] = hidden[0]
        hidden_low[rows, :] = hidden[1]
        grads = split(jnp.concatenate(gate_grads(grad_hidden[rows, :], tanh_part, sig_part), axis=1))
        part = dot2(hot, grads)
        part_c = dot2(hot[LOCAL : 2 * LOCAL], (cot_high[rows, :], cot_low[rows, :]))
        total = part if total is None else total + part
        total_c = part_c if total_c is None else total_c + part_c
    for q in range(4):
        for at, k in enumerate((0, 2, 1)):
            piece = total[k * LOCAL : (k + 1) * LOCAL, q * 128 : (q + 1) * 128]
            quarters[q, at * LOCAL : (at + 1) * LOCAL, :] = piece
        lanes = slice((q >> 1) * 128, (q >> 1) * 128 + 128)
        for begin, count_c, at in ((0, INNER // 2, TAPS), (INNER, EDGE // 2, TAPS + INNER // 2)):
            begin += (q & 1) * count_c
            quarters[q, at : at + count_c, :] = total_c[begin : begin + count_c, lanes]
    deal(quarters, keep, send)


def halve_kernel(kept, received, keep, send):
    bit = (lax.axis_index("seq") >> 1) & 1
    send[...] = kept[1 - bit] + received[1 - bit]
    keep[...] = kept[bit] + received[bit]


def halve_taps_kernel(kept, received, keep_a, send_a, keep_b, send_b):
    bit = (lax.axis_index("seq") >> 1) & 1
    rows = keep_a.shape[0]
    for at, (first, second) in ((bit, (keep_a, keep_b)), (1 - bit, (send_a, send_b))):
        first[...] = kept[at, :rows, :] + received[at, :rows, :]
        second[...] = kept[at, rows:, :] + received[at, rows:, :]


def add_after_kernel(kept, received, after, out):
    out[...] = kept[...] + received[...]


def halve_after_kernel(kept, received, after, keep, send):
    halve_kernel(kept, received, keep, send)


def turn_kernel(hidden_high, hidden_low, cot_high, cot_low, after, keep, send, quarters):
    hidden = (hidden_high[...], hidden_low[...])
    total = dot3(hidden, (cot_high[...], cot_low[...]), 0, 0)
    side = total.shape[0] // 4
    for q in range(4):
        quarters[q, :side, :] = total[q * side : (q + 1) * side, :128]
        quarters[q, side:, :] = total[q * side : (q + 1) * side, 128:]
    deal(quarters, keep, send)


def output_kernel(strand, center, hidden_high, hidden_low, local, out_in, after, out, out_w, value, sems):
    length = center.shape[1]
    fetch = Fetch(sems)
    fetch.start(out_in.at[1], out_w)
    hot = hot_rows(center[strand : strand + 1, :])
    rows = slice(strand * length, (strand + 1) * length)
    own = dot2(hot, split(local[...]), 0, 0)
    fetch.wait(0)
    value[...] = own + dot3((hidden_high[rows, :], hidden_low[rows, :]), split(out_w[...]))
    fetch.start(value, out)
    fetch.wait(1)


def prepare_kernel(
    first_conv, first_mix, second_conv, second_mix, out_w, table, after, first_high, first_low, second_high, second_low, turn_high, turn_low,
    level_high, level_low, partner_high, partner_low,
):
    level = split(table[...])
    swap = permutation()
    level_high[...], level_low[...] = level
    partner_high[...], partner_low[...] = tuple(dot(swap, piece).astype(BF16) for piece in level)
    for conv, mix, high, low in (
        (second_conv, second_mix, second_high, second_low),
        (first_conv, first_mix, first_high, first_low),
    ):
        for k in range(4):
            high[k], low[k] = split((conv[k] if k < 3 else mix[...]).T)
    turn_high[...], turn_low[...] = split(out_w[...].T)


def merge(mine, theirs, inner, edge):
    left = left_side()
    both = mine[inner, :] + theirs[inner, :]
    own, other = mine[edge, :], theirs[edge, :]
    return both, jnp.where(left, own, other), jnp.where(left, other, own)


def merge_blocks(mine, theirs, out, sizes):
    at = to = 0
    for inner, edge in sizes:
        pieces = merge(mine, theirs, slice(at, at + inner), slice(at + inner, at + inner + edge))
        out[to : to + inner, :] = pieces[0]
        out[to + inner : to + inner + edge, :] = pieces[1]
        out[to + inner + edge : to + inner + 2 * edge, :] = pieces[2]
        at, to = at + inner + edge, to + inner + 2 * edge


def merge_sides_kernel(mine, theirs, after, out):
    merge_blocks(mine, theirs, out, [(INNER, EDGE)] * 2)


def merge_middle_kernel(mine, theirs, after, out):
    merge_blocks(mine, theirs, out, [(INNER, EDGE), (INNER // 2, EDGE // 2)])


def gather_quarters(pieces, quarters):
    place = lax.axis_index("seq")
    low, high = place & 1, (place >> 1) & 1
    for parts, x, y in zip(pieces, (0, 0, 1, 1), (0, 1, 0, 1)):
        begin = 0
        for part in parts:
            rows = part.shape[0]
            quarters[(low ^ x) * 2 + (high ^ y), begin : begin + rows, :] = part[...]
            begin += rows


def tap_of(quarters, at):
    return jnp.concatenate([quarters[q, at : at + CONTEXTS, :] for q in range(4)], axis=1)


def sides_kernel(
    piece_00, piece_01, piece_01_too, piece_10, piece_11, piece_11_too, level_high, level_low, second_high, second_low, after,
    g_conv_out, partial, quarters, g_conv, out_sems,
):
    store = Fetch(out_sems)
    gather_quarters(((piece_00,), (piece_01, piece_01_too), (piece_10,), (piece_11, piece_11_too)), quarters)
    level = (level_high[...], level_low[...])
    grad_level = None
    for at, k in enumerate((0, 2)):
        pair = split(tap_of(quarters, at * CONTEXTS))
        g_conv[at] = dot3(level, pair, 0, 0)
        store.start(g_conv.at[at], g_conv_out.at[1, k])
        part = dot3(pair, (second_high[k], second_low[k]))
        grad_level = part if grad_level is None else grad_level + part
    partial[...] = grad_level
    store.wait(0, 1)


def middle_kernel(
    piece_00, piece_01, piece_10, piece_11, level_high, level_low, partner_high, partner_low, second_high, second_low,
    partial, g_conv_in, g_conv_out, g_mix_out, g_bias, total, quarters, g_conv, g_mix, out_sems,
):
    store = Fetch(out_sems)
    gather_quarters([(piece,) for piece in (piece_00, piece_01, piece_10, piece_11)], quarters)
    level = (level_high[...], level_low[...])
    partner = (partner_high[...], partner_low[...])
    grad_level = []
    for begin, rows in ((0, INNER // 2), (INNER // 2, EDGE // 2), (INNER // 2 + EDGE // 2, EDGE // 2)):
        begin += CONTEXTS
        halves = [[quarters[2 * h + i, begin : begin + rows, :] for i in range(2)] for h in range(2)]
        grad_level.append(jnp.concatenate([jnp.concatenate(x, axis=0) for x in halves], axis=1))
    piece = tap_of(quarters, 0)
    pair = split(piece)
    grad_level = jnp.concatenate(grad_level, axis=0) + partial[...] + dot3(pair, (second_high[1], second_low[1]))
    total[...] = grad_level + dot2(permutation(), split(dot3(pair, (second_high[3], second_low[3]))))
    g_conv[...] = dot3(level, pair, 0, 0)
    store.start(g_conv, g_conv_out.at[1, 1])
    g_mix[...] = dot3(partner, pair, 0, 0)
    store.start(g_mix, g_mix_out.at[1])
    g_bias[...] = jnp.sum(piece, axis=0, keepdims=True)
    store.wait(0, 1)


def first_layer_kernel(
    partial, mixed_table, bias_row, embed, first_high, first_low, turn_high, turn_low,
    g_conv_in, g_mix_in, g_conv_out, g_mix_out, g_embed_out, g_bias_out, g_out_out,
    g_conv, g_mix, g_embed, g_bias, g_out, out_sems,
):
    store = Fetch(out_sems)
    grad_level = split(partial[...])
    tanh_part, sig_part = gates(mixed_table[...])
    hidden = split(tanh_part * sig_part)
    grad_hidden = dot3(grad_level, (turn_high[...], turn_low[...]))
    grad_mixed = jnp.concatenate(gate_grads(grad_hidden, tanh_part, sig_part), axis=1)
    g_bias[0:1, :] = jnp.sum(grad_mixed, axis=0, keepdims=True)
    g_bias[1:2, :] = bias_row[...]
    store.start(g_bias, g_bias_out)
    hot = letter_hot()
    by_letter = dot2(hot, split(grad_mixed), 0, 0)
    base = split(padded_base(embed))
    stacked = jnp.concatenate([base[0].astype(F32), base[0].astype(F32), base[1].astype(F32)], axis=0).astype(BF16)
    pieces = []
    for k in range(4):
        piece = split(by_letter[k * 8 : (k + 1) * 8, :])
        pieces.append(piece)
        high, low = piece[0].astype(F32), piece[1].astype(F32)
        value = dot(stacked, jnp.concatenate([high, low, high], axis=0).astype(BF16), 0, 0)
        if k < 3:
            g_conv[k] = value
            store.start(g_conv.at[k], g_conv_out.at[0, k])
        else:
            g_mix[...] = value
            store.start(g_mix, g_mix_out.at[0])
    g_out[...] = dot3(hidden, grad_level, 0, 0)
    store.start(g_out, g_out_out.at[0])
    grad_base = dot2(hot[:, 8:16], grad_level, 0, 0)
    for k in range(4):
        grad_base = grad_base + dot3(pieces[k], (first_high[k], first_low[k]))
    g_embed[...] = grad_base[:4, :]
    store.start(g_embed, g_embed_out)
    store.wait(*range(len(store.copies)))


def store_kernel(piece_00, piece_01, piece_10, piece_11, g_out_in, g_out_out, quarters, g_out, out_sems):
    store = Fetch(out_sems)
    gather_quarters([(piece,) for piece in (piece_00, piece_01, piece_10, piece_11)], quarters)
    side = quarters.shape[1] // 2
    for q in range(4):
        for h in range(2):
            g_out[q * side : (q + 1) * side, h * 128 : (h + 1) * 128] = quarters[q, h * side : (h + 1) * side, :]
    store.start(g_out, g_out_out.at[1])
    store.wait(0)


VMEM, SMEM, HBM = pltpu.VMEM, pltpu.SMEM, pltpu.HBM


def call(kernel, ins, outs, scratch=(), aliases=None, micros=0.001):
    run = pl.pallas_call(
        kernel,
        out_shape=[space(shape, kind) for shape, kind, space in outs],
        in_specs=[pl.BlockSpec(memory_space=space) for space in ins],
        out_specs=[pl.BlockSpec(memory_space=space) for _, _, space in outs],
        scratch_shapes=list(scratch),
        input_output_aliases=aliases or {},
        cost_estimate=pl.CostEstimate(flops=int(micros * 1.1e9), bytes_accessed=int(micros * 3e6), transcendentals=0),
        compiler_params=pltpu.CompilerParams(vmem_limit_bytes=VMEM_LIMIT),
    )

    def placed(*args):
        return run(*[pltpu.with_memory_space_constraint(x, HBM) if space is HBM else x for x, space in zip(args, ins)])

    return placed


def swapped(value, mask):
    pairs = [(source, source ^ mask) for source in range(lax.axis_size("seq"))]
    return lax.ppermute(value, "seq", pairs)


def crossed(piece, count, rest):
    mask = 4
    while mask < count // 2:
        piece = piece + swapped(piece, mask)
        mask *= 2
    return rest(piece, swapped(piece, mask))


def on_device(
    tokens, dilations, embed, conv_weight, mix_weight, gate_bias, out_weight, cot_fwd, cot_rev
):
    channels = embed.shape[1]
    wide = 2 * channels
    length = tokens.shape[0]
    count = lax.axis_size("seq")
    sems = pltpu.SemaphoreType.DMA
    square = (channels, channels)

    def touched(value, after, space=VMEM, cuts=1):
        shape = (value.shape[0] // cuts, value.shape[1])
        return call(touch_kernel, [VMEM, space], [(shape, value.dtype, VMEM)] * cuts)(value, after)

    def joined(first, second, after):
        shape = (2 * first.shape[0], first.shape[1])
        return call(join_kernel, [VMEM] * 3, [(shape, first.dtype, VMEM)])(first, second, after)[0]

    known = tokens.reshape(1, length)
    own = call(load_kernel, [HBM], [(known.shape, known.dtype, VMEM)], [sems((1,))], micros=0.7)(known)[0]
    parts = [own, swapped(known, 1)]
    known = joined(own, parts[-1], own)
    parts.append(swapped(known, 2))
    layer_weights = [(conv_weight.shape[1:], F32, VMEM), (mix_weight.shape[1:], F32, VMEM)]
    table, local, mixed_table, first_conv, first_mix, bias, turn = call(
        first_tables_kernel,
        [HBM] * 5 + [VMEM],
        [
            ((CONTEXTS, channels), F32, VMEM),
            ((LOCAL, channels), F32, VMEM),
            ((CONTEXTS, wide), F32, VMEM),
            *layer_weights,
            (gate_bias.shape, F32, VMEM),
            (square, F32, VMEM),
        ],
        [VMEM(embed.shape, F32), sems((7,))],
        micros=2.6,
    )(embed, conv_weight, mix_weight, gate_bias, out_weight, known)
    known = joined(known, parts[-1], table)
    parts.append(swapped(known, 4))
    deep = -(-TAPS // 128) * 128
    pre_high, pre_low, cot_high, cot_low, grad_hidden, second_conv, second_mix = call(
        second_tables_kernel,
        [VMEM] * 2 + [HBM] * 5 + [VMEM],
        [((deep, wide), BF16, VMEM)] * 2
        + [((2 * length, channels), BF16, VMEM)] * 2
        + [((2 * length, channels), F32, VMEM)]
        + layer_weights,
        [VMEM(square, F32), VMEM((2, length, channels), F32), sems((7,))],
        micros=3.0,
    )(table, bias, conv_weight, mix_weight, out_weight, cot_fwd, cot_rev, known)
    mask = 8
    while mask < count:
        known = joined(known, parts[-1], pre_low)
        parts.append(swapped(known, mask))
        mask *= 2

    sum_rows = TAPS + LOCAL // 2
    keep_x, send_x, hidden_high, hidden_low, center = call(
        lambda *refs: main_kernel(count, *refs),
        [SMEM] + [VMEM] * (len(parts) + 5),
        [((2, sum_rows, 128), F32, VMEM)] * 2
        + [((2 * length, channels), BF16, VMEM)] * 2
        + [((2, length), jnp.int32, VMEM)],
        [VMEM((4, sum_rows, 128), F32)],
        micros=2.9,
    )(dilations, *parts, pre_high, pre_low, grad_hidden, cot_high, cot_low)

    rows_a, rows_b, rows_y = 2 * LOCAL, LOCAL + LOCAL // 2, channels // 2
    keep_a, send_a, keep_b, send_b = call(
        halve_taps_kernel, [VMEM] * 2, [((rows, 128), F32, VMEM) for rows in (rows_a, rows_a, rows_b, rows_b)]
    )(keep_x, swapped(send_x, 1))

    keep_y, send_y = call(
        turn_kernel,
        [VMEM] * 5,
        [((2, rows_y, 128), F32, VMEM)] * 2,
        [VMEM((4, rows_y, 128), F32)],
        micros=0.8,
    )(hidden_high, hidden_low, cot_high, cot_low, keep_a)

    def output(strand, after):
        return call(
            lambda *refs: output_kernel(strand, *refs),
            [VMEM] * 4 + [HBM, VMEM],
            [((length, channels), F32, HBM)],
            [VMEM(square, F32), VMEM((length, channels), F32), sems((2,))],
            micros=1.5,
        )(center, hidden_high, hidden_low, local, out_weight, after)[0]

    def added(kept, received, after, space=VMEM, micros=0.001):
        return call(add_after_kernel, [VMEM] * 2 + [space], [(kept.shape, F32, VMEM)], micros=micros)(
            kept, received, after
        )[0]

    out_fwd = output(0, keep_y)
    sum_a = added(keep_a, swapped(send_a, 2), out_fwd, HBM)
    sum_b = added(keep_b, swapped(send_b, 2), sum_a)
    halve_y = call(halve_after_kernel, [VMEM] * 3, [((rows_y, 128), F32, VMEM)] * 2)
    keep_y, send_y = halve_y(keep_y, swapped(send_y, 1), sum_a)

    first_high, first_low, second_high, second_low, turn_high, turn_low, *levels = call(
        prepare_kernel,
        [VMEM] * 7,
        [((4, wide, channels), BF16, VMEM)] * 4
        + [(square, BF16, VMEM)] * 2
        + [((CONTEXTS, channels), BF16, VMEM)] * 4,
        micros=1.3,
    )(first_conv, first_mix, second_conv, second_mix, turn, table, sum_b)

    merged_a, merged_b = 2 * CONTEXTS, CONTEXTS + CONTEXTS // 2
    merge_a = call(merge_sides_kernel, [VMEM] * 3, [((merged_a, 128), F32, VMEM)])
    merge_b = call(merge_middle_kernel, [VMEM] * 3, [((merged_b, 128), F32, VMEM)])
    piece_a = crossed(sum_a, count, lambda x, y: merge_a(x, y, turn_low)[0])
    sum_y = added(keep_y, swapped(send_y, 2), piece_a)
    piece_b = crossed(sum_b, count, lambda x, y: merge_b(x, y, sum_y)[0])
    out_rev = output(1, piece_b)

    def spread(piece, after, space=VMEM, cuts=1):
        other = touched(swapped(piece, 2), after, space, cuts)
        return piece, *other, swapped(piece, 1), *[swapped(x, 1) for x in other]

    g_conv, partial = call(
        sides_kernel,
        [VMEM] * 10 + [HBM],
        [(conv_weight.shape, F32, HBM), ((CONTEXTS, channels), F32, VMEM)],
        [
            VMEM((4, merged_a, 128), F32),
            VMEM((2, channels, wide), F32),
            sems((2,)),
        ],
        micros=0.05,
    )(*spread(piece_a, out_rev, HBM, 2), *levels[:2], second_high, second_low, out_rev)

    piece_y = crossed(sum_y, count, lambda x, y: added(x, y, partial, micros=0.001))
    g_conv, g_mix, bias_row, total = call(
        middle_kernel,
        [VMEM] * 11 + [HBM],
        [
            (conv_weight.shape, F32, HBM),
            (mix_weight.shape, F32, HBM),
            ((1, wide), F32, VMEM),
            ((CONTEXTS, channels), F32, VMEM),
        ],
        [
            VMEM((4, merged_b, 128), F32),
            VMEM((channels, wide), F32),
            VMEM((channels, wide), F32),
            sems((2,)),
        ],
        aliases={11: 0},
        micros=1.3,
    )(*spread(piece_b, piece_y), *levels, second_high, second_low, partial, g_conv)

    pieces_y = spread(piece_y, total)
    g_conv, g_mix, g_embed, g_bias, g_out = call(
        first_layer_kernel,
        [VMEM] * 8 + [HBM] * 2,
        [
            (conv_weight.shape, F32, HBM),
            (mix_weight.shape, F32, HBM),
            (embed.shape, F32, HBM),
            (gate_bias.shape, F32, HBM),
            (out_weight.shape, F32, HBM),
        ],
        [
            VMEM(conv_weight.shape[1:], F32),
            VMEM(mix_weight.shape[1:], F32),
            VMEM(embed.shape, F32),
            VMEM(gate_bias.shape, F32),
            VMEM(square, F32),
            sems((7,)),
        ],
        aliases={8: 0, 9: 1},
        micros=2.2,
    )(total, mixed_table, bias_row, embed, first_high, first_low, turn_high, turn_low, g_conv, g_mix)
    g_out = call(
        store_kernel,
        [VMEM] * 4 + [HBM],
        [(out_weight.shape, F32, HBM)],
        [VMEM((4, rows_y, 128), F32), VMEM(square, F32), sems((1,))],
        aliases={4: 0},
    )(*pieces_y, g_out)[0]
    return (out_fwd, out_rev, g_embed, g_conv, g_mix, g_bias, g_out)


def solution(mesh):
    in_specs = (
        P(("dp", "seq")),
        P(),
        P(),
        P(),
        P(),
        P(),
        P(),
        P(("dp", "seq"), None),
        P(("dp", "seq"), None),
    )
    out_specs = (
        P(("dp", "seq"), None),
        P(("dp", "seq"), None),
        P("dp", None),
        P("dp", None, None, None),
        P("dp", None, None),
        P("dp", None),
        P("dp", None, None),
    )
    return jax.shard_map(
        on_device, mesh=mesh, in_specs=in_specs, out_specs=out_specs, check_vma=False
    )
```

```python
import jax
import jax.numpy as jnp
from jax import lax
from jax.experimental import pallas as pl
from jax.experimental.pallas import tpu as pltpu
from jax.sharding import PartitionSpec as P

CONTEXTS = 96
INNER = 64
EDGE = 16
LOCAL = INNER + EDGE
TAPS = 3 * LOCAL
HALO = 128
F32 = jnp.float32
BF16 = jnp.bfloat16
VMEM_LIMIT = 40 * 1024 * 1024


def split(x):
    high = x.astype(BF16)
    return high, (x - high.astype(F32)).astype(BF16)


def dot(a, b, ca=1, cb=0):
    return lax.dot_general(a, b, (((ca,), (cb,)), ((), ())), preferred_element_type=F32)


def dot2(exact, pair, ca=1, cb=0):
    return dot(exact, pair[0], ca, cb) + dot(exact, pair[1], ca, cb)


def dot3(a, b, ca=1, cb=0):
    return dot(a[0], b[0], ca, cb) + (dot(a[0], b[1], ca, cb) + dot(a[1], b[0], ca, cb))


def letters(index):
    inner = index < 64
    left = (index >= 64) & (index < 80)
    low = index & 3
    mid = (index >> 2) & 3
    l = jnp.where(inner, (index >> 4) & 3, jnp.where(left, -1, mid))
    m = jnp.where(inner | left, mid, low)
    r = jnp.where(inner | left, low, -1)
    return l, m, r


def mirrored(index):
    low = 3 - (index & 3)
    mid = 3 - ((index >> 2) & 3)
    high = 3 - ((index >> 4) & 3)
    inner = low * 16 + mid * 4 + high
    left = 80 + low * 4 + mid
    right = 64 + low * 4 + mid
    return jnp.where(index < 64, inner, jnp.where(index < 80, left, right))


def permutation():
    rows = lax.broadcasted_iota(jnp.int32, (CONTEXTS, CONTEXTS), 0)
    cols = lax.broadcasted_iota(jnp.int32, (CONTEXTS, CONTEXTS), 1)
    return (mirrored(rows) == cols).astype(F32).astype(BF16)


def letter_hot():
    rows = lax.broadcasted_iota(jnp.int32, (CONTEXTS, 32), 0)
    cols = lax.broadcasted_iota(jnp.int32, (CONTEXTS, 32), 1)
    l, m, r = letters(rows)
    kind = cols >> 3
    value = jnp.where(kind == 0, l, jnp.where(kind == 1, m, jnp.where(kind == 2, r, 3 - m)))
    return (value == (cols & 7)).astype(F32).astype(BF16)


def gates(mixed):
    channels = mixed.shape[1] // 2
    tanh_part = jnp.tanh(mixed[:, :channels])
    sig_part = 0.5 + 0.5 * jnp.tanh(0.5 * mixed[:, channels:])
    return tanh_part, sig_part


def gate_grads(grad_hidden, tanh_part, sig_part):
    scaled = grad_hidden * sig_part
    return scaled * (1.0 - tanh_part * tanh_part), scaled * tanh_part * (1.0 - sig_part)


class Fetch:
    def __init__(self, sems):
        self.sems = sems
        self.copies = []

    def start(self, source, target):
        copy = pltpu.make_async_copy(source, target, self.sems.at[len(self.copies)])
        copy.start()
        self.copies.append(copy)
        return len(self.copies) - 1

    def wait(self, *which):
        for at in which:
            self.copies[at].wait()


def padded_base(embed):
    return jnp.concatenate([embed[...], jnp.zeros((4, embed.shape[1]), F32)], axis=0)


def left_side():
    return lax.axis_index("seq") * 2 < lax.axis_size("seq")


def local_rows(rows):
    edge = jnp.where(left_side(), rows[INNER : INNER + EDGE], rows[INNER + EDGE : INNER + 2 * EDGE])
    return jnp.concatenate([rows[:INNER], edge], axis=0)


def join_kernel(first, second, after, out):
    rows = first.shape[0]
    out[:rows, :] = first[...]
    out[rows:, :] = second[...]


def load_kernel(source, out, sems):
    fetch = Fetch(sems)
    fetch.start(source, out)
    fetch.wait(0)


def touch_kernel(value, after, *outs):
    begin = 0
    for out in outs:
        out[...] = value[begin : begin + out.shape[0], :]
        begin += out.shape[0]


def first_tables_kernel(
    embed_in, conv_in, mix_in, bias_in, out_in, after, table, local, mixed_table, conv, mix, bias, out_w, embed, sems,
):
    fetch = Fetch(sems)
    small = [fetch.start(embed_in, embed), fetch.start(bias_in, bias)]
    first = [fetch.start(conv_in.at[0, k], conv.at[k]) for k in range(3)]
    first += [fetch.start(mix_in.at[0], mix)]
    turn = fetch.start(out_in.at[0], out_w)
    hot = letter_hot()
    fetch.wait(*small)
    base = split(padded_base(embed))
    taps = []
    for k in range(4):
        fetch.wait(first[k])
        taps.append(dot3(base, split(conv[k] if k < 3 else mix[...])))
    taps = jnp.concatenate(taps, axis=0)
    mixed = dot2(hot, split(taps)) + bias[0:1, :]
    tanh_part, sig_part = gates(mixed)
    hidden = tanh_part * sig_part
    own = dot2(hot[:, 8:16], base)
    fetch.wait(turn)
    level = own + dot3(split(hidden), split(out_w[...]))
    table[...] = level
    local[...] = local_rows(level)
    mixed_table[...] = mixed


def second_tables_kernel(
    table, bias, conv_in, mix_in, out_in, cot_fwd_in, cot_rev_in, after, pre_high, pre_low, cot_high, cot_low, grad_hidden,
    conv, mix, last_high, last_low, out_w, cots, sems,
):
    length = cots.shape[1]
    fetch = Fetch(sems)
    fetch.start(out_in.at[1], out_w)
    fetch.start(cot_fwd_in, cots.at[0])
    second = [fetch.start(conv_in.at[1, k], conv.at[k]) for k in range(3)]
    second += [fetch.start(mix_in.at[1], mix)]
    last = fetch.start(cot_rev_in, cots.at[1])

    def cotangents(strand):
        rows = slice(strand * length, (strand + 1) * length)
        cot = split(cots[strand])
        cot_high[rows, :] = cot[0]
        cot_low[rows, :] = cot[1]
        grad_hidden[rows, :] = dot3(cot, weight, 1, 1)

    level = split(table[...])
    swap = permutation()
    partner = tuple(dot(swap, piece).astype(BF16) for piece in level)
    pre_high[TAPS:, :] = jnp.zeros((pre_high.shape[0] - TAPS, pre_high.shape[1]), BF16)
    pre_low[TAPS:, :] = jnp.zeros((pre_low.shape[0] - TAPS, pre_low.shape[1]), BF16)
    fetch.wait(0, 1)
    weight = split(out_w[...])
    last_high[...], last_low[...] = weight
    cotangents(0)
    for k in (0, 2, 1):
        fetch.wait(second[k])
        value = dot3(level, split(conv[k]))
        if k == 1:
            fetch.wait(second[3])
            value = value + dot3(partner, split(mix[...])) + bias[1:2, :]
        high, low = split(local_rows(value))
        pre_high[k * LOCAL : (k + 1) * LOCAL, :] = high
        pre_low[k * LOCAL : (k + 1) * LOCAL, :] = low
    fetch.wait(last)
    cotangents(1)


def windows(parts, count):
    length = parts[0].shape[1]
    place = lax.axis_index("seq")
    last = count - 1

    def block(at):
        total, begin = None, 0
        for part in parts:
            rows = lax.broadcasted_iota(jnp.int32, part.shape, 0) + begin
            piece = jnp.sum(jnp.where(rows == (place ^ at), part[...], 0), axis=0, keepdims=True)
            total = piece if total is None else total + piece
            begin += part.shape[0]
        return total

    def window(at):
        before = jnp.where(at == 0, -1, block(jnp.maximum(at - 1, 0))[:, length - HALO :])
        after = jnp.where(at == last, -1, block(jnp.minimum(at + 1, last))[:, :HALO])
        return [before, block(at), after]

    fwd = jnp.concatenate(window(place), axis=1)
    rev = jnp.concatenate(window(last - place), axis=1)
    rev = jnp.where(rev < 0, -1, 3 - rev)
    tiles = rev.shape[1] // 128
    blocks = [rev[:, i * 128 : (i + 1) * 128] for i in reversed(range(tiles))]
    blocks += [jnp.zeros((8 - tiles, 128), jnp.int32)]
    stacked = jnp.concatenate(blocks, axis=0).astype(F32).astype(BF16)
    rows = lax.broadcasted_iota(jnp.int32, (128, 128), 0)
    cols = lax.broadcasted_iota(jnp.int32, (128, 128), 1)
    flip = (rows + cols == 127).astype(F32).astype(BF16)
    turned = dot(stacked, flip).astype(jnp.int32)
    rev = jnp.concatenate([turned[i : i + 1, :] for i in range(tiles)], axis=1)
    return fwd, rev


def local_contexts(window, first, second, length):
    width = window.shape[1]
    base = jnp.broadcast_to(window, (8, width))
    l = pltpu.roll(base, first, 1)
    r = pltpu.roll(base, width - first, 1)
    index = jnp.where(l < 0, INNER + base * 4 + r, jnp.where(r < 0, INNER + l * 4 + base, l * 16 + base * 4 + r))
    index = jnp.where(base < 0, LOCAL, index)
    before = pltpu.roll(index, second, 1)
    after = pltpu.roll(index, width - second, 1)
    return [x[0:1, HALO : HALO + length] for x in (before, index, after)]


def hot_rows(index):
    rows = lax.broadcasted_iota(jnp.int32, (LOCAL, index.shape[1]), 0)
    return (rows == index).astype(F32).astype(BF16)


def deal(quarters, keep, send):
    bit = lax.axis_index("seq") & 1
    keep[...] = quarters[pl.ds(bit * 2, 2)]
    send[...] = quarters[pl.ds((1 - bit) * 2, 2)]


def forward_kernel(count, dil, *refs):
    parts, refs = refs[: count.bit_length()], refs[count.bit_length() :]
    (pre_high, pre_low, cot_high, cot_low, keep, send, hidden_high, hidden_low, hots, slopes, quarters) = refs
    length = parts[0].shape[1]
    channels = cot_high.shape[1]
    pre = (pre_high[...], pre_low[...])
    both = windows(parts, count)
    pad = jnp.zeros((pre_high.shape[0] - TAPS, length), BF16)
    total_o = total_c = None
    for strand in range(2):
        index = local_contexts(both[strand], dil[0], dil[1], length)
        hot = jnp.concatenate([hot_rows(x) for x in index] + [pad], axis=0)
        hots[strand] = hot
        mixed = dot2(hot, pre, 0, 0)
        tanh_part, sig_part = gates(mixed)
        product = tanh_part * sig_part
        hidden = split(product)
        rows = slice(strand * length, (strand + 1) * length)
        hidden_high[rows, :] = hidden[0]
        hidden_low[rows, :] = hidden[1]
        slopes[rows, :channels] = sig_part - product * tanh_part
        slopes[rows, channels:] = product - product * sig_part
        cot = (cot_high[rows, :], cot_low[rows, :])
        part_o = dot3(hidden, cot, 0, 0)
        part_c = dot2(hot[LOCAL : 2 * LOCAL], cot)
        total_o = part_o if total_o is None else total_o + part_o
        total_c = part_c if total_c is None else total_c + part_c
    side = channels // 4
    for q in range(4):
        lanes = slice((q >> 1) * 128, (q >> 1) * 128 + 128)
        quarters[q, :side, :] = total_o[q * side : (q + 1) * side, :128]
        quarters[q, side : 2 * side, :] = total_o[q * side : (q + 1) * side, 128:]
        for begin, rows, at in ((0, INNER // 2, 2 * side), (INNER, EDGE // 2, 2 * side + INNER // 2)):
            begin += (q & 1) * rows
            quarters[q, at : at + rows, :] = total_c[begin : begin + rows, lanes]
    deal(quarters, keep, send)


def taps_kernel(hots, slopes, grad_hidden, keep, send, quarters):
    length = hots.shape[2]
    total = None
    for strand in range(2):
        rows = slice(strand * length, (strand + 1) * length)
        grad = grad_hidden[rows, :]
        part = dot2(hots[strand], split(slopes[rows, :] * jnp.concatenate([grad, grad], axis=1)))
        total = part if total is None else total + part
    for q in range(4):
        quarters[q] = total[:TAPS, q * 128 : (q + 1) * 128]
    deal(quarters, keep, send)


def halve_kernel(kept, received, keep, send):
    bit = (lax.axis_index("seq") >> 1) & 1
    send[...] = kept[1 - bit] + received[1 - bit]
    keep[...] = kept[bit] + received[bit]


def add_after_kernel(kept, received, after, out):
    out[...] = kept[...] + received[...]


def halve_after_kernel(kept, received, after, keep, send):
    halve_kernel(kept, received, keep, send)


def outputs_kernel(hots, hidden_high, hidden_low, local, last_high, last_low, after, out_fwd, out_rev, values, sems):
    length = hots.shape[2]
    fetch = Fetch(sems)
    weight = (last_high[...], last_low[...])
    level = split(local[...])
    for strand, out in enumerate((out_fwd, out_rev)):
        rows = slice(strand * length, (strand + 1) * length)
        own = dot2(hots[strand, LOCAL : 2 * LOCAL, :], level, 0, 0)
        values[strand] = own + dot3((hidden_high[rows, :], hidden_low[rows, :]), weight)
        fetch.start(values.at[strand], out)
    fetch.wait(0, 1)


def prepare_kernel(
    first_conv, first_mix, second_conv, second_mix, out_w, table, after, first_high, first_low, second_high, second_low, turn_high, turn_low,
    level_high, level_low, partner_high, partner_low,
):
    level = split(table[...])
    swap = permutation()
    level_high[...], level_low[...] = level
    partner_high[...], partner_low[...] = tuple(dot(swap, piece).astype(BF16) for piece in level)
    for conv, mix, high, low in (
        (second_conv, second_mix, second_high, second_low),
        (first_conv, first_mix, first_high, first_low),
    ):
        for k in range(4):
            high[k], low[k] = split((conv[k] if k < 3 else mix[...]).T)
    turn_high[...], turn_low[...] = split(out_w[...].T)


def merge(mine, theirs, inner, edge):
    left = left_side()
    both = mine[inner, :] + theirs[inner, :]
    own, other = mine[edge, :], theirs[edge, :]
    return both, jnp.where(left, own, other), jnp.where(left, other, own)


def merge_blocks(mine, theirs, out, sizes):
    at = to = 0
    for inner, edge in sizes:
        pieces = merge(mine, theirs, slice(at, at + inner), slice(at + inner, at + inner + edge))
        out[to : to + inner, :] = pieces[0]
        out[to + inner : to + inner + edge, :] = pieces[1]
        out[to + inner + edge : to + inner + 2 * edge, :] = pieces[2]
        at, to = at + inner + edge, to + inner + 2 * edge


def merge_taps_kernel(mine, theirs, after, out):
    merge_blocks(mine, theirs, out, [(INNER, EDGE)] * 3)


def merge_rest_kernel(mine, theirs, after, out):
    merge_blocks(mine, theirs, out, [(mine.shape[0] - EDGE // 2, EDGE // 2)])


def gather_quarters(pieces, quarters):
    place = lax.axis_index("seq")
    low, high = place & 1, (place >> 1) & 1
    for parts, x, y in zip(pieces, (0, 0, 1, 1), (0, 1, 0, 1)):
        begin = 0
        for part in parts:
            rows = part.shape[0]
            quarters[(low ^ x) * 2 + (high ^ y), begin : begin + rows, :] = part[...]
            begin += rows


def columns_kernel(
    other, own_piece, core_piece, level_high, level_low, partner_high, partner_low, second_high, second_low, *refs
):
    if other:
        partial, g_conv_in, g_mix_in, *refs = refs
    g_conv_out, g_mix_out, bias, total, pair_at, g_conv, g_mix, out_sems = refs
    place = lax.axis_index("seq")
    low, high = place & 1, (place >> 1) & 1
    high = 1 - high if other else high
    pair_at[low] = own_piece[...]
    pair_at[1 - low] = core_piece[...]
    store = Fetch(out_sems)
    first = pl.multiple_of(high * 128, 128)
    blocks = [pl.ds(first, 128), pl.ds(pl.multiple_of(first + 256, 128), 128)]
    level = (level_high[...], level_low[...])
    partner = (partner_high[...], partner_low[...])

    def weight(k):
        return [jnp.concatenate([ref[k, block, :] for block in blocks], axis=0) for ref in (second_high, second_low)]

    def stored(value, source, target):
        source[...] = value
        for at, block in enumerate(blocks):
            store.start(source.at[:, pl.ds(at * 128, 128)], target.at[:, block])

    grad_level = partial[...] if other else None
    for k in range(3):
        rows = slice(k * CONTEXTS, (k + 1) * CONTEXTS)
        piece = jnp.concatenate([pair_at[0, rows, :], pair_at[1, rows, :]], axis=1)
        pair = split(piece)
        part = dot3(pair, weight(k))
        grad_level = part if grad_level is None else grad_level + part
        stored(dot3(level, pair, 0, 0), g_conv.at[k], g_conv_out.at[1, k])
        if k == 1:
            grad_level = grad_level + dot2(permutation(), split(dot3(pair, weight(3))))
            stored(dot3(partner, pair, 0, 0), g_mix, g_mix_out.at[1])
            bias[...] = jnp.sum(piece, axis=0, keepdims=True)
    total[...] = grad_level
    store.wait(*range(len(store.copies)))


def first_layer_kernel(
    piece_00, piece_01, piece_10, piece_11, partial, mixed_table, bias_own, bias_other, embed,
    first_high, first_low, turn_high, turn_low,
    g_conv_in, g_mix_in, g_conv_out, g_mix_out, g_embed_out, g_bias_out, g_out_out,
    quarters, bias_rows, g_conv, g_mix, g_embed, g_bias, g_out, out_sems,
):
    channels = embed.shape[1]
    store = Fetch(out_sems)
    gather_quarters([(piece,) for piece in (piece_00, piece_01, piece_10, piece_11)], quarters)
    side = channels // 4
    rest = []
    for begin, rows in ((0, INNER // 2), (INNER // 2, EDGE // 2), (INNER // 2 + EDGE // 2, EDGE // 2)):
        begin += 2 * side
        halves = [[quarters[2 * h + i, begin : begin + rows, :] for i in range(2)] for h in range(2)]
        rest.append(jnp.concatenate([jnp.concatenate(x, axis=0) for x in halves], axis=1))
    grad_level = split(partial[...] + jnp.concatenate(rest, axis=0))
    high = (lax.axis_index("seq") >> 1) & 1
    for bias, at in ((bias_own, high), (bias_other, 1 - high)):
        bias_rows[at] = bias[:, :128]
        bias_rows[2 + at] = bias[:, 128:]
    bias_row = jnp.concatenate([bias_rows[q] for q in range(4)], axis=1)
    tanh_part, sig_part = gates(mixed_table[...])
    hidden = split(tanh_part * sig_part)
    grad_hidden = dot3(grad_level, (turn_high[...], turn_low[...]))
    grad_mixed = jnp.concatenate(gate_grads(grad_hidden, tanh_part, sig_part), axis=1)
    g_bias[0:1, :] = jnp.sum(grad_mixed, axis=0, keepdims=True)
    g_bias[1:2, :] = bias_row
    store.start(g_bias, g_bias_out)
    hot = letter_hot()
    by_letter = dot2(hot, split(grad_mixed), 0, 0)
    base = split(padded_base(embed))
    stacked = jnp.concatenate([base[0].astype(F32), base[0].astype(F32), base[1].astype(F32)], axis=0).astype(BF16)
    pieces = []
    for k in range(4):
        piece = split(by_letter[k * 8 : (k + 1) * 8, :])
        pieces.append(piece)
        high, low = piece[0].astype(F32), piece[1].astype(F32)
        value = dot(stacked, jnp.concatenate([high, low, high], axis=0).astype(BF16), 0, 0)
        if k < 3:
            g_conv[k] = value
            store.start(g_conv.at[k], g_conv_out.at[0, k])
        else:
            g_mix[...] = value
            store.start(g_mix, g_mix_out.at[0])
    g_out[0] = dot3(hidden, grad_level, 0, 0)
    for q in range(4):
        for h in range(2):
            g_out[1, q * side : (q + 1) * side, h * 128 : (h + 1) * 128] = quarters[q, h * side : (h + 1) * side, :]
    store.start(g_out, g_out_out)
    grad_base = dot2(hot[:, 8:16], grad_level, 0, 0)
    for k in range(4):
        grad_base = grad_base + dot3(pieces[k], (first_high[k], first_low[k]))
    g_embed[...] = grad_base[:4, :]
    store.start(g_embed, g_embed_out)
    store.wait(*range(len(store.copies)))


VMEM, SMEM, HBM = pltpu.VMEM, pltpu.SMEM, pltpu.HBM


def call(kernel, ins, outs, scratch=(), aliases=None, micros=0.001):
    run = pl.pallas_call(
        kernel,
        out_shape=[space(shape, kind) for shape, kind, space in outs],
        in_specs=[pl.BlockSpec(memory_space=space) for space in ins],
        out_specs=[pl.BlockSpec(memory_space=space) for _, _, space in outs],
        scratch_shapes=list(scratch),
        input_output_aliases=aliases or {},
        cost_estimate=pl.CostEstimate(flops=int(micros * 1.1e9), bytes_accessed=int(micros * 3e6), transcendentals=0),
        compiler_params=pltpu.CompilerParams(vmem_limit_bytes=VMEM_LIMIT),
    )

    def placed(*args):
        return run(*[pltpu.with_memory_space_constraint(x, HBM) if space is HBM else x for x, space in zip(args, ins)])

    return placed


def swapped(value, mask):
    pairs = [(source, source ^ mask) for source in range(lax.axis_size("seq"))]
    return lax.ppermute(value, "seq", pairs)


def crossed(piece, count, rest):
    mask = 4
    while mask < count // 2:
        piece = piece + swapped(piece, mask)
        mask *= 2
    return rest(piece, swapped(piece, mask))


def on_device(
    tokens, dilations, embed, conv_weight, mix_weight, gate_bias, out_weight, cot_fwd, cot_rev
):
    channels = embed.shape[1]
    wide = 2 * channels
    length = tokens.shape[0]
    count = lax.axis_size("seq")
    sems = pltpu.SemaphoreType.DMA
    square = (channels, channels)

    def joined(first, second, after):
        shape = (2 * first.shape[0], first.shape[1])
        return call(join_kernel, [VMEM] * 3, [(shape, first.dtype, VMEM)])(first, second, after)[0]

    known = tokens.reshape(1, length)
    own = call(load_kernel, [HBM], [(known.shape, known.dtype, VMEM)], [sems((1,))], micros=0.7)(known)[0]
    parts = [own, swapped(known, 1)]
    known = joined(own, parts[-1], own)
    parts.append(swapped(known, 2))
    layer_weights = [(conv_weight.shape[1:], F32, VMEM), (mix_weight.shape[1:], F32, VMEM)]
    table, local, mixed_table, first_conv, first_mix, bias, turn = call(
        first_tables_kernel,
        [HBM] * 5 + [VMEM],
        [
            ((CONTEXTS, channels), F32, VMEM),
            ((LOCAL, channels), F32, VMEM),
            ((CONTEXTS, wide), F32, VMEM),
            *layer_weights,
            (gate_bias.shape, F32, VMEM),
            (square, F32, VMEM),
        ],
        [VMEM(embed.shape, F32), sems((7,))],
        micros=2.6,
    )(embed, conv_weight, mix_weight, gate_bias, out_weight, known)
    known = joined(known, parts[-1], table)
    parts.append(swapped(known, 4))
    deep = -(-TAPS // 128) * 128
    pre_high, pre_low, cot_high, cot_low, grad_hidden, second_conv, second_mix, last_high, last_low = call(
        second_tables_kernel,
        [VMEM] * 2 + [HBM] * 5 + [VMEM],
        [((deep, wide), BF16, VMEM)] * 2
        + [((2 * length, channels), BF16, VMEM)] * 2
        + [((2 * length, channels), F32, VMEM)]
        + layer_weights
        + [(square, BF16, VMEM)] * 2,
        [VMEM(square, F32), VMEM((2, length, channels), F32), sems((7,))],
        micros=3.0,
    )(table, bias, conv_weight, mix_weight, out_weight, cot_fwd, cot_rev, known)
    mask = 8
    while mask < count:
        known = joined(known, parts[-1], pre_low)
        parts.append(swapped(known, mask))
        mask *= 2

    rows_x, rows_y = TAPS, channels // 2 + LOCAL // 2
    keep_y, send_y, hidden_high, hidden_low, hots, slopes = call(
        lambda *refs: forward_kernel(count, *refs),
        [SMEM] + [VMEM] * (len(parts) + 4),
        [((2, rows_y, 128), F32, VMEM)] * 2
        + [((2 * length, channels), BF16, VMEM)] * 2
        + [((2, deep, length), BF16, VMEM), ((2 * length, wide), F32, VMEM)],
        [VMEM((4, rows_y, 128), F32)],
        micros=2.0,
    )(dilations, *parts, pre_high, pre_low, cot_high, cot_low)
    keep_x, send_x = call(
        taps_kernel,
        [VMEM] * 3,
        [((2, rows_x, 128), F32, VMEM)] * 2,
        [VMEM((4, rows_x, 128), F32)],
        micros=1.5,
    )(hots, slopes, grad_hidden)

    def halved(keep, received, after):
        outs = [(keep.shape[1:], F32, VMEM)] * 2
        return call(halve_after_kernel, [VMEM] * 3, outs)(keep, received, after)

    def added(kept, received, after, space=VMEM):
        return call(add_after_kernel, [VMEM] * 2 + [space], [(kept.shape, F32, VMEM)])(kept, received, after)[0]

    def touched(value, after, cuts=1):
        shape = (value.shape[0] // cuts, value.shape[1])
        return call(touch_kernel, [VMEM] * 2, [(shape, value.dtype, VMEM)] * cuts)(value, after)

    keep_y, send_y = halved(keep_y, swapped(send_y, 1), keep_x)
    keep_x, send_x = halved(keep_x, swapped(send_x, 1), keep_y)
    sum_y = added(keep_y, swapped(send_y, 2), keep_x)
    out_fwd, out_rev = call(
        outputs_kernel,
        [VMEM] * 7,
        [((length, channels), F32, HBM)] * 2,
        [VMEM((2, length, channels), F32), sems((2,))],
        micros=2.0,
    )(hots, hidden_high, hidden_low, local, last_high, last_low, sum_y)
    sum_x = added(keep_x, swapped(send_x, 2), out_rev, HBM)
    first_high, first_low, second_high, second_low, turn_high, turn_low, *levels = call(
        prepare_kernel,
        [VMEM] * 7,
        [((4, wide, channels), BF16, VMEM)] * 4
        + [(square, BF16, VMEM)] * 2
        + [((CONTEXTS, channels), BF16, VMEM)] * 4,
        micros=1.3,
    )(first_conv, first_mix, second_conv, second_mix, turn, table, sum_x)

    def merged(kernel, rows, mine, theirs, after):
        return call(kernel, [VMEM] * 3, [((rows, 128), F32, VMEM)])(mine, theirs, after)[0]

    merged_x, merged_y = 3 * CONTEXTS, rows_y + EDGE // 2
    piece_y = crossed(sum_y, count, lambda x, y: merged(merge_rest_kernel, merged_y, x, y, turn_low))
    other_y = swapped(piece_y, 2)
    piece_x = crossed(sum_x, count, lambda x, y: merged(merge_taps_kernel, merged_x, x, y, other_y))
    core_y, far_y = swapped(piece_y, 1), swapped(other_y, 1)
    core_x = swapped(piece_x, 1)

    def columns(other, pieces, *before):
        return call(
            lambda *refs: columns_kernel(other, *refs),
            [VMEM] * 8 + ([VMEM] + [HBM] * 2 if other else []),
            [
                (conv_weight.shape, F32, HBM),
                (mix_weight.shape, F32, HBM),
                ((1, channels), F32, VMEM),
                ((CONTEXTS, channels), F32, VMEM),
            ],
            [
                VMEM((2, merged_x, 128), F32),
                VMEM((3, channels, channels), F32),
                VMEM((channels, channels), F32),
                sems((8,)),
            ],
            aliases={9: 0, 10: 1} if other else None,
            micros=1.3,
        )(*pieces, *levels, second_high, second_low, *before)

    g_conv, g_mix, bias_own, partial = columns(False, (piece_x, core_x))
    other_x = touched(swapped(piece_x, 2), partial)[0]
    g_conv, g_mix, bias_other, partial = columns(True, (other_x, swapped(other_x, 1)), partial, g_conv, g_mix)
    g_conv, g_mix, g_embed, g_bias, g_out = call(
        first_layer_kernel,
        [VMEM] * 13 + [HBM] * 2,
        [
            (conv_weight.shape, F32, HBM),
            (mix_weight.shape, F32, HBM),
            (embed.shape, F32, HBM),
            (gate_bias.shape, F32, HBM),
            (out_weight.shape, F32, HBM),
        ],
        [
            VMEM((4, merged_y, 128), F32),
            VMEM((4, 1, 128), F32),
            VMEM(conv_weight.shape[1:], F32),
            VMEM(mix_weight.shape[1:], F32),
            VMEM(embed.shape, F32),
            VMEM(gate_bias.shape, F32),
            VMEM(out_weight.shape, F32),
            sems((7,)),
        ],
        aliases={13: 0, 14: 1},
        micros=2.2,
    )(
        piece_y, other_y, core_y, far_y, partial, mixed_table, bias_own, bias_other, embed,
        first_high, first_low, turn_high, turn_low, g_conv, g_mix,
    )
    return (out_fwd, out_rev, g_embed, g_conv, g_mix, g_bias, g_out)


def solution(mesh):
    in_specs = (
        P(("dp", "seq")),
        P(),
        P(),
        P(),
        P(),
        P(),
        P(),
        P(("dp", "seq"), None),
        P(("dp", "seq"), None),
    )
    out_specs = (
        P(("dp", "seq"), None),
        P(("dp", "seq"), None),
        P("dp", None),
        P("dp", None, None, None),
        P("dp", None, None),
        P("dp", None),
        P("dp", None, None),
    )
    return jax.shard_map(
        on_device, mesh=mesh, in_specs=in_specs, out_specs=out_specs, check_vma=False
    )
```

```python
import jax
import jax.numpy as jnp
from jax import lax
from jax.experimental import pallas as pl
from jax.experimental.pallas import tpu as pltpu
from jax.sharding import PartitionSpec as P

CONTEXTS = 96
INNER = 64
EDGE = 16
LOCAL = INNER + EDGE
TAPS = 3 * LOCAL
HALO = 128
F32 = jnp.float32
BF16 = jnp.bfloat16
VMEM_LIMIT = 40 * 1024 * 1024


def split(x):
    high = x.astype(BF16)
    return high, (x - high.astype(F32)).astype(BF16)


def dot(a, b, ca=1, cb=0):
    return lax.dot_general(a, b, (((ca,), (cb,)), ((), ())), preferred_element_type=F32)


def dot2(exact, pair, ca=1, cb=0):
    return dot(exact, pair[0], ca, cb) + dot(exact, pair[1], ca, cb)


def dot3(a, b, ca=1, cb=0):
    return dot(a[0], b[0], ca, cb) + (dot(a[0], b[1], ca, cb) + dot(a[1], b[0], ca, cb))


def letters(index):
    inner = index < 64
    left = (index >= 64) & (index < 80)
    low = index & 3
    mid = (index >> 2) & 3
    l = jnp.where(inner, (index >> 4) & 3, jnp.where(left, -1, mid))
    m = jnp.where(inner | left, mid, low)
    r = jnp.where(inner | left, low, -1)
    return l, m, r


def mirrored(index):
    low = 3 - (index & 3)
    mid = 3 - ((index >> 2) & 3)
    high = 3 - ((index >> 4) & 3)
    inner = low * 16 + mid * 4 + high
    left = 80 + low * 4 + mid
    right = 64 + low * 4 + mid
    return jnp.where(index < 64, inner, jnp.where(index < 80, left, right))


def permutation():
    rows = lax.broadcasted_iota(jnp.int32, (CONTEXTS, CONTEXTS), 0)
    cols = lax.broadcasted_iota(jnp.int32, (CONTEXTS, CONTEXTS), 1)
    return (mirrored(rows) == cols).astype(F32).astype(BF16)


def letter_hot():
    rows = lax.broadcasted_iota(jnp.int32, (CONTEXTS, 32), 0)
    cols = lax.broadcasted_iota(jnp.int32, (CONTEXTS, 32), 1)
    l, m, r = letters(rows)
    kind = cols >> 3
    value = jnp.where(kind == 0, l, jnp.where(kind == 1, m, jnp.where(kind == 2, r, 3 - m)))
    return (value == (cols & 7)).astype(F32).astype(BF16)


def gates(mixed):
    channels = mixed.shape[1] // 2
    tanh_part = jnp.tanh(mixed[:, :channels])
    sig_part = 0.5 + 0.5 * jnp.tanh(0.5 * mixed[:, channels:])
    return tanh_part, sig_part


def gate_grads(grad_hidden, tanh_part, sig_part):
    scaled = grad_hidden * sig_part
    return scaled * (1.0 - tanh_part * tanh_part), scaled * tanh_part * (1.0 - sig_part)


class Fetch:
    def __init__(self, sems):
        self.sems = sems
        self.copies = []

    def start(self, source, target):
        copy = pltpu.make_async_copy(source, target, self.sems.at[len(self.copies)])
        copy.start()
        self.copies.append(copy)
        return len(self.copies) - 1

    def wait(self, *which):
        for at in which:
            self.copies[at].wait()


def padded_base(embed):
    return jnp.concatenate([embed[...], jnp.zeros((4, embed.shape[1]), F32)], axis=0)


def left_side():
    return lax.axis_index("seq") * 2 < lax.axis_size("seq")


def local_rows(rows):
    edge = jnp.where(left_side(), rows[INNER : INNER + EDGE], rows[INNER + EDGE : INNER + 2 * EDGE])
    return jnp.concatenate([rows[:INNER], edge], axis=0)


def join_four_kernel(first, second, third, fourth, after, out):
    for at, part in enumerate((first, second, third, fourth)):
        out[at : at + 1, :] = part[...]


def load_kernel(source, out, sems):
    fetch = Fetch(sems)
    fetch.start(source, out)
    fetch.wait(0)


def touch_kernel(value, after, *outs):
    begin = 0
    for out in outs:
        out[...] = value[begin : begin + out.shape[0], :]
        begin += out.shape[0]


def first_tables_kernel(
    embed_in, conv_in, mix_in, bias_in, out_in, after, table, local, mixed_table, conv, mix, bias, out_w, embed, sems,
):
    fetch = Fetch(sems)
    small = [fetch.start(embed_in, embed), fetch.start(bias_in, bias)]
    first = [fetch.start(conv_in.at[0, k], conv.at[k]) for k in range(3)]
    first += [fetch.start(mix_in.at[0], mix)]
    turn = fetch.start(out_in.at[0], out_w)
    hot = letter_hot()
    fetch.wait(*small)
    base = split(padded_base(embed))
    taps = []
    for k in range(4):
        fetch.wait(first[k])
        taps.append(dot3(base, split(conv[k] if k < 3 else mix[...])))
    taps = jnp.concatenate(taps, axis=0)
    mixed = dot2(hot, split(taps)) + bias[0:1, :]
    tanh_part, sig_part = gates(mixed)
    hidden = tanh_part * sig_part
    own = dot2(hot[:, 8:16], base)
    fetch.wait(turn)
    level = own + dot3(split(hidden), split(out_w[...]))
    table[...] = level
    local[...] = local_rows(level)
    mixed_table[...] = mixed


def second_tables_kernel(
    table, bias, conv_in, mix_in, out_in, cot_fwd_in, cot_rev_in, after, pre_high, pre_low, cot_high, cot_low, grad_hidden,
    conv, mix, last_high, last_low, out_w, cots, sems,
):
    length = cots.shape[1]
    fetch = Fetch(sems)
    fetch.start(out_in.at[1], out_w)
    fetch.start(cot_fwd_in, cots.at[0])
    second = [fetch.start(conv_in.at[1, k], conv.at[k]) for k in range(3)]
    second += [fetch.start(mix_in.at[1], mix)]
    last = fetch.start(cot_rev_in, cots.at[1])

    def cotangents(strand):
        rows = slice(strand * length, (strand + 1) * length)
        cot = split(cots[strand])
        cot_high[rows, :] = cot[0]
        cot_low[rows, :] = cot[1]
        grad_hidden[rows, :] = dot3(cot, weight, 1, 1)

    level = split(table[...])
    swap = permutation()
    partner = tuple(dot(swap, piece).astype(BF16) for piece in level)
    pre_high[TAPS:, :] = jnp.zeros((pre_high.shape[0] - TAPS, pre_high.shape[1]), BF16)
    pre_low[TAPS:, :] = jnp.zeros((pre_low.shape[0] - TAPS, pre_low.shape[1]), BF16)
    fetch.wait(0, 1)
    weight = split(out_w[...])
    last_high[...], last_low[...] = weight
    cotangents(0)
    for k in (0, 2, 1):
        fetch.wait(second[k])
        value = dot3(level, split(conv[k]))
        if k == 1:
            fetch.wait(second[3])
            value = value + dot3(partner, split(mix[...])) + bias[1:2, :]
        high, low = split(local_rows(value))
        pre_high[k * LOCAL : (k + 1) * LOCAL, :] = high
        pre_low[k * LOCAL : (k + 1) * LOCAL, :] = low
    fetch.wait(last)
    cotangents(1)


def windows(parts, count):
    length = parts[0].shape[1]
    place = lax.axis_index("seq")
    last = count - 1

    def block(at):
        total, begin = None, 0
        for part in parts:
            rows = lax.broadcasted_iota(jnp.int32, part.shape, 0) + begin
            piece = jnp.sum(jnp.where(rows == (place ^ at), part[...], 0), axis=0, keepdims=True)
            total = piece if total is None else total + piece
            begin += part.shape[0]
        return total

    def window(at):
        before = jnp.where(at == 0, -1, block(jnp.maximum(at - 1, 0))[:, length - HALO :])
        after = jnp.where(at == last, -1, block(jnp.minimum(at + 1, last))[:, :HALO])
        return [before, block(at), after]

    fwd = jnp.concatenate(window(place), axis=1)
    rev = jnp.concatenate(window(last - place), axis=1)
    rev = jnp.where(rev < 0, -1, 3 - rev)
    tiles = rev.shape[1] // 128
    blocks = [rev[:, i * 128 : (i + 1) * 128] for i in reversed(range(tiles))]
    blocks += [jnp.zeros((8 - tiles, 128), jnp.int32)]
    stacked = jnp.concatenate(blocks, axis=0).astype(F32).astype(BF16)
    rows = lax.broadcasted_iota(jnp.int32, (128, 128), 0)
    cols = lax.broadcasted_iota(jnp.int32, (128, 128), 1)
    flip = (rows + cols == 127).astype(F32).astype(BF16)
    turned = dot(stacked, flip).astype(jnp.int32)
    rev = jnp.concatenate([turned[i : i + 1, :] for i in range(tiles)], axis=1)
    return fwd, rev


def local_contexts(window, first, second, length):
    width = window.shape[1]
    base = jnp.broadcast_to(window, (8, width))
    l = pltpu.roll(base, first, 1)
    r = pltpu.roll(base, width - first, 1)
    index = jnp.where(l < 0, INNER + base * 4 + r, jnp.where(r < 0, INNER + l * 4 + base, l * 16 + base * 4 + r))
    index = jnp.where(base < 0, LOCAL, index)
    before = pltpu.roll(index, second, 1)
    after = pltpu.roll(index, width - second, 1)
    return [x[0:1, HALO : HALO + length] for x in (before, index, after)]


def hot_rows(index):
    rows = lax.broadcasted_iota(jnp.int32, (LOCAL, index.shape[1]), 0)
    return (rows == index).astype(F32).astype(BF16)


def deal(quarters, keep, send):
    bit = lax.axis_index("seq") & 1
    keep[...] = quarters[pl.ds(bit * 2, 2)]
    send[...] = quarters[pl.ds((1 - bit) * 2, 2)]


def forward_kernel(count, dil, *refs):
    steps = count.bit_length() - 2
    parts, refs = refs[:steps], refs[steps:]
    (pre_high, pre_low, cot_high, cot_low, keep, send, hidden_high, hidden_low, hots, slopes, quarters) = refs
    length = parts[0].shape[1]
    channels = cot_high.shape[1]
    pre = (pre_high[...], pre_low[...])
    both = windows(parts, count)
    pad = jnp.zeros((pre_high.shape[0] - TAPS, length), BF16)
    total_o = total_c = None
    for strand in range(2):
        index = local_contexts(both[strand], dil[0], dil[1], length)
        hot = jnp.concatenate([hot_rows(x) for x in index] + [pad], axis=0)
        hots[strand] = hot
        mixed = dot2(hot, pre, 0, 0)
        tanh_part, sig_part = gates(mixed)
        product = tanh_part * sig_part
        hidden = split(product)
        rows = slice(strand * length, (strand + 1) * length)
        hidden_high[rows, :] = hidden[0]
        hidden_low[rows, :] = hidden[1]
        slopes[rows, :channels] = sig_part - product * tanh_part
        slopes[rows, channels:] = product - product * sig_part
        cot = (cot_high[rows, :], cot_low[rows, :])
        part_o = dot3(hidden, cot, 0, 0)
        part_c = dot2(hot[LOCAL : 2 * LOCAL], cot)
        total_o = part_o if total_o is None else total_o + part_o
        total_c = part_c if total_c is None else total_c + part_c
    side = channels // 4
    for q in range(4):
        lanes = slice((q >> 1) * 128, (q >> 1) * 128 + 128)
        quarters[q, :side, :] = total_o[q * side : (q + 1) * side, :128]
        quarters[q, side : 2 * side, :] = total_o[q * side : (q + 1) * side, 128:]
        for begin, rows, at in ((0, INNER // 2, 2 * side), (INNER, EDGE // 2, 2 * side + INNER // 2)):
            begin += (q & 1) * rows
            quarters[q, at : at + rows, :] = total_c[begin : begin + rows, lanes]
    deal(quarters, keep, send)


def taps_kernel(hots, slopes, grad_hidden, keep, send, quarters):
    length = hots.shape[2]
    total = None
    for strand in range(2):
        rows = slice(strand * length, (strand + 1) * length)
        grad = grad_hidden[rows, :]
        part = dot2(hots[strand], split(slopes[rows, :] * jnp.concatenate([grad, grad], axis=1)))
        total = part if total is None else total + part
    for q in range(4):
        quarters[q] = total[:TAPS, q * 128 : (q + 1) * 128]
    deal(quarters, keep, send)


def halve_kernel(kept, received, keep, send):
    bit = (lax.axis_index("seq") >> 1) & 1
    send[...] = kept[1 - bit] + received[1 - bit]
    keep[...] = kept[bit] + received[bit]


def add_after_kernel(kept, received, after, out):
    out[...] = kept[...] + received[...]


def halve_after_kernel(kept, received, after, keep, send):
    halve_kernel(kept, received, keep, send)


def outputs_kernel(hots, hidden_high, hidden_low, local, last_high, last_low, after, out_fwd, out_rev, values, sems):
    length = hots.shape[2]
    fetch = Fetch(sems)
    weight = (last_high[...], last_low[...])
    level = split(local[...])
    for strand, out in enumerate((out_fwd, out_rev)):
        rows = slice(strand * length, (strand + 1) * length)
        own = dot2(hots[strand, LOCAL : 2 * LOCAL, :], level, 0, 0)
        values[strand] = own + dot3((hidden_high[rows, :], hidden_low[rows, :]), weight)
        fetch.start(values.at[strand], out)
    fetch.wait(0, 1)


def prepare_kernel(
    first_conv, first_mix, second_conv, second_mix, out_w, table, after, first_high, first_low, second_high, second_low, turn_high, turn_low,
    level_high, level_low, partner_high, partner_low,
):
    level = split(table[...])
    swap = permutation()
    level_high[...], level_low[...] = level
    partner_high[...], partner_low[...] = tuple(dot(swap, piece).astype(BF16) for piece in level)
    for conv, mix, high, low in (
        (second_conv, second_mix, second_high, second_low),
        (first_conv, first_mix, first_high, first_low),
    ):
        for k in range(4):
            high[k], low[k] = split((conv[k] if k < 3 else mix[...]).T)
    turn_high[...], turn_low[...] = split(out_w[...].T)


def merge(mine, theirs, inner, edge):
    left = left_side()
    both = mine[inner, :] + theirs[inner, :]
    own, other = mine[edge, :], theirs[edge, :]
    return both, jnp.where(left, own, other), jnp.where(left, other, own)


def merge_blocks(mine, theirs, out, sizes):
    at = to = 0
    for inner, edge in sizes:
        pieces = merge(mine, theirs, slice(at, at + inner), slice(at + inner, at + inner + edge))
        out[to : to + inner, :] = pieces[0]
        out[to + inner : to + inner + edge, :] = pieces[1]
        out[to + inner + edge : to + inner + 2 * edge, :] = pieces[2]
        at, to = at + inner + edge, to + inner + 2 * edge


def merge_taps_kernel(mine, theirs, after, out):
    merge_blocks(mine, theirs, out, [(INNER, EDGE)] * 3)


def merge_rest_kernel(mine, theirs, after, out):
    merge_blocks(mine, theirs, out, [(mine.shape[0] - EDGE // 2, EDGE // 2)])


def gather_quarters(pieces, quarters):
    place = lax.axis_index("seq")
    low, high = place & 1, (place >> 1) & 1
    for parts, x, y in zip(pieces, (0, 0, 1, 1), (0, 1, 0, 1)):
        begin = 0
        for part in parts:
            rows = part.shape[0]
            quarters[(low ^ x) * 2 + (high ^ y), begin : begin + rows, :] = part[...]
            begin += rows


def columns_kernel(other, *refs):
    parts = 2 if other else 1
    own_parts, core_parts, refs = refs[:parts], refs[parts : 2 * parts], refs[2 * parts :]
    level_high, level_low, partner_high, partner_low, second_high, second_low, *refs = refs
    if other:
        partial, g_conv_in, g_mix_in, *refs = refs
    g_conv_out, g_mix_out, bias, total, pair_at, g_conv, g_mix, out_sems = refs
    place = lax.axis_index("seq")
    low, high = place & 1, (place >> 1) & 1
    high = 1 - high if other else high
    rows = own_parts[0].shape[0]
    for at, (own_part, core_part) in enumerate(zip(own_parts, core_parts)):
        pair_at[low, at * rows : (at + 1) * rows, :] = own_part[...]
        pair_at[1 - low, at * rows : (at + 1) * rows, :] = core_part[...]
    store = Fetch(out_sems)
    first = pl.multiple_of(high * 128, 128)
    blocks = [pl.ds(first, 128), pl.ds(pl.multiple_of(first + 256, 128), 128)]
    level = (level_high[...], level_low[...])
    partner = (partner_high[...], partner_low[...])

    def weight(k):
        return [jnp.concatenate([ref[k, block, :] for block in blocks], axis=0) for ref in (second_high, second_low)]

    def stored(value, source, target):
        source[...] = value
        for at, block in enumerate(blocks):
            store.start(source.at[:, pl.ds(at * 128, 128)], target.at[:, block])

    pairs = []
    for k in (1, 0, 2):
        rows = slice(k * CONTEXTS, (k + 1) * CONTEXTS)
        piece = jnp.concatenate([pair_at[0, rows, :], pair_at[1, rows, :]], axis=1)
        pair = split(piece)
        pairs.append((k, pair))
        stored(dot3(level, pair, 0, 0), g_conv.at[k], g_conv_out.at[1, k])
        if k == 1:
            stored(dot3(partner, pair, 0, 0), g_mix, g_mix_out.at[1])
            bias[...] = jnp.sum(piece, axis=0, keepdims=True)
    grad_level = dot2(permutation(), split(dot3(pairs[0][1], weight(3))))
    for k, pair in pairs:
        grad_level = grad_level + dot3(pair, weight(k))
    if other:
        grad_level = grad_level + partial[...]
    total[...] = grad_level
    store.wait(*range(len(store.copies)))


def first_layer_kernel(
    piece_00, piece_01, piece_10, piece_11, partial, mixed_table, bias_own, bias_other, embed,
    first_high, first_low, turn_high, turn_low,
    g_conv_in, g_mix_in, g_conv_out, g_mix_out, g_embed_out, g_bias_out, g_out_out,
    quarters, bias_rows, g_conv, g_mix, g_embed, g_bias, g_out, out_sems,
):
    channels = embed.shape[1]
    store = Fetch(out_sems)
    gather_quarters([(piece,) for piece in (piece_00, piece_01, piece_10, piece_11)], quarters)
    side = channels // 4
    rest = []
    for begin, rows in ((0, INNER // 2), (INNER // 2, EDGE // 2), (INNER // 2 + EDGE // 2, EDGE // 2)):
        begin += 2 * side
        halves = [[quarters[2 * h + i, begin : begin + rows, :] for i in range(2)] for h in range(2)]
        rest.append(jnp.concatenate([jnp.concatenate(x, axis=0) for x in halves], axis=1))
    grad_level = split(partial[...] + jnp.concatenate(rest, axis=0))
    high = (lax.axis_index("seq") >> 1) & 1
    for bias, at in ((bias_own, high), (bias_other, 1 - high)):
        bias_rows[at] = bias[:, :128]
        bias_rows[2 + at] = bias[:, 128:]
    bias_row = jnp.concatenate([bias_rows[q] for q in range(4)], axis=1)
    tanh_part, sig_part = gates(mixed_table[...])
    hidden = split(tanh_part * sig_part)
    grad_hidden = dot3(grad_level, (turn_high[...], turn_low[...]))
    grad_mixed = jnp.concatenate(gate_grads(grad_hidden, tanh_part, sig_part), axis=1)
    g_bias[0:1, :] = jnp.sum(grad_mixed, axis=0, keepdims=True)
    g_bias[1:2, :] = bias_row
    store.start(g_bias, g_bias_out)
    hot = letter_hot()
    by_letter = dot2(hot, split(grad_mixed), 0, 0)
    base = split(padded_base(embed))
    stacked = jnp.concatenate([base[0].astype(F32), base[0].astype(F32), base[1].astype(F32)], axis=0).astype(BF16)
    pieces = []
    for k in range(4):
        piece = split(by_letter[k * 8 : (k + 1) * 8, :])
        pieces.append(piece)
        high, low = piece[0].astype(F32), piece[1].astype(F32)
        value = dot(stacked, jnp.concatenate([high, low, high], axis=0).astype(BF16), 0, 0)
        if k < 3:
            g_conv[k] = value
            store.start(g_conv.at[k], g_conv_out.at[0, k])
        else:
            g_mix[...] = value
            store.start(g_mix, g_mix_out.at[0])
    g_out[0] = dot3(hidden, grad_level, 0, 0)
    for q in range(4):
        for h in range(2):
            g_out[1, q * side : (q + 1) * side, h * 128 : (h + 1) * 128] = quarters[q, h * side : (h + 1) * side, :]
    store.start(g_out, g_out_out)
    grad_base = dot2(hot[:, 8:16], grad_level, 0, 0)
    for k in range(4):
        grad_base = grad_base + dot3(pieces[k], (first_high[k], first_low[k]))
    g_embed[...] = grad_base[:4, :]
    store.start(g_embed, g_embed_out)
    store.wait(*range(len(store.copies)))


VMEM, SMEM, HBM = pltpu.VMEM, pltpu.SMEM, pltpu.HBM


def call(kernel, ins, outs, scratch=(), aliases=None, micros=0.001):
    run = pl.pallas_call(
        kernel,
        out_shape=[space(shape, kind) for shape, kind, space in outs],
        in_specs=[pl.BlockSpec(memory_space=space) for space in ins],
        out_specs=[pl.BlockSpec(memory_space=space) for _, _, space in outs],
        scratch_shapes=list(scratch),
        input_output_aliases=aliases or {},
        cost_estimate=pl.CostEstimate(flops=int(micros * 1.1e9), bytes_accessed=int(micros * 3e6), transcendentals=0),
        compiler_params=pltpu.CompilerParams(vmem_limit_bytes=VMEM_LIMIT),
    )

    def placed(*args):
        return run(*[pltpu.with_memory_space_constraint(x, HBM) if space is HBM else x for x, space in zip(args, ins)])

    return placed


def swapped(value, mask):
    pairs = [(source, source ^ mask) for source in range(lax.axis_size("seq"))]
    return lax.ppermute(value, "seq", pairs)


def crossed(piece, count, rest):
    mask = 4
    while mask < count // 2:
        piece = piece + swapped(piece, mask)
        mask *= 2
    return rest(piece, swapped(piece, mask))


def on_device(
    tokens, dilations, embed, conv_weight, mix_weight, gate_bias, out_weight, cot_fwd, cot_rev
):
    channels = embed.shape[1]
    wide = 2 * channels
    length = tokens.shape[0]
    count = lax.axis_size("seq")
    sems = pltpu.SemaphoreType.DMA
    square = (channels, channels)

    row = tokens.reshape(1, length)
    own = call(load_kernel, [HBM], [(row.shape, row.dtype, VMEM)], [sems((1,))], micros=0.7)(row)[0]
    near = [swapped(row, mask) for mask in (1, 2, 3)]
    layer_weights = [(conv_weight.shape[1:], F32, VMEM), (mix_weight.shape[1:], F32, VMEM)]
    table, local, mixed_table, first_conv, first_mix, bias, turn = call(
        first_tables_kernel,
        [HBM] * 5 + [VMEM],
        [
            ((CONTEXTS, channels), F32, VMEM),
            ((LOCAL, channels), F32, VMEM),
            ((CONTEXTS, wide), F32, VMEM),
            *layer_weights,
            (gate_bias.shape, F32, VMEM),
            (square, F32, VMEM),
        ],
        [VMEM(embed.shape, F32), sems((7,))],
        micros=2.6,
    )(embed, conv_weight, mix_weight, gate_bias, out_weight, own)
    known = call(join_four_kernel, [VMEM] * 5, [((4, length), row.dtype, VMEM)])(own, *near, table)[0]
    parts = [known, swapped(known, 4)]
    deep = -(-TAPS // 128) * 128
    pre_high, pre_low, cot_high, cot_low, grad_hidden, second_conv, second_mix, last_high, last_low = call(
        second_tables_kernel,
        [VMEM] * 2 + [HBM] * 5 + [VMEM],
        [((deep, wide), BF16, VMEM)] * 2
        + [((2 * length, channels), BF16, VMEM)] * 2
        + [((2 * length, channels), F32, VMEM)]
        + layer_weights
        + [(square, BF16, VMEM)] * 2,
        [VMEM(square, F32), VMEM((2, length, channels), F32), sems((7,))],
        micros=3.0,
    )(table, bias, conv_weight, mix_weight, out_weight, cot_fwd, cot_rev, known)
    mask = 8
    while mask < count:
        known = jnp.concatenate([known, parts[-1]], axis=0)
        parts.append(swapped(known, mask))
        mask *= 2

    rows_x, rows_y = TAPS, channels // 2 + LOCAL // 2
    keep_y, send_y, hidden_high, hidden_low, hots, slopes = call(
        lambda *refs: forward_kernel(count, *refs),
        [SMEM] + [VMEM] * (len(parts) + 4),
        [((2, rows_y, 128), F32, VMEM)] * 2
        + [((2 * length, channels), BF16, VMEM)] * 2
        + [((2, deep, length), BF16, VMEM), ((2 * length, wide), F32, VMEM)],
        [VMEM((4, rows_y, 128), F32)],
        micros=2.0,
    )(dilations, *parts, pre_high, pre_low, cot_high, cot_low)
    keep_x, send_x = call(
        taps_kernel,
        [VMEM] * 3,
        [((2, rows_x, 128), F32, VMEM)] * 2,
        [VMEM((4, rows_x, 128), F32)],
        micros=1.5,
    )(hots, slopes, grad_hidden)

    def halved(keep, received, after):
        outs = [(keep.shape[1:], F32, VMEM)] * 2
        return call(halve_after_kernel, [VMEM] * 3, outs)(keep, received, after)

    def added(kept, received, after, space=VMEM):
        return call(add_after_kernel, [VMEM] * 2 + [space], [(kept.shape, F32, VMEM)])(kept, received, after)[0]

    def touched(value, after, cuts=1):
        shape = (value.shape[0] // cuts, value.shape[1])
        return call(touch_kernel, [VMEM] * 2, [(shape, value.dtype, VMEM)] * cuts)(value, after)

    keep_y, send_y = halved(keep_y, swapped(send_y, 1), keep_x)
    keep_x, send_x = halved(keep_x, swapped(send_x, 1), keep_y)
    sum_y = added(keep_y, swapped(send_y, 2), keep_x)
    out_fwd, out_rev = call(
        outputs_kernel,
        [VMEM] * 7,
        [((length, channels), F32, HBM)] * 2,
        [VMEM((2, length, channels), F32), sems((2,))],
        micros=2.0,
    )(hots, hidden_high, hidden_low, local, last_high, last_low, sum_y)
    sum_x = added(keep_x, swapped(send_x, 2), out_rev, HBM)
    first_high, first_low, second_high, second_low, turn_high, turn_low, *levels = call(
        prepare_kernel,
        [VMEM] * 7,
        [((4, wide, channels), BF16, VMEM)] * 4
        + [(square, BF16, VMEM)] * 2
        + [((CONTEXTS, channels), BF16, VMEM)] * 4,
        micros=1.3,
    )(first_conv, first_mix, second_conv, second_mix, turn, table, sum_x)

    def merged(kernel, rows, mine, theirs, after):
        return call(kernel, [VMEM] * 3, [((rows, 128), F32, VMEM)])(mine, theirs, after)[0]

    merged_x, merged_y = 3 * CONTEXTS, rows_y + EDGE // 2
    piece_y = crossed(sum_y, count, lambda x, y: merged(merge_rest_kernel, merged_y, x, y, turn_low))
    piece_x = crossed(sum_x, count, lambda x, y: merged(merge_taps_kernel, merged_x, x, y, piece_y))
    core_x = swapped(piece_x, 1)

    def columns(other, pieces, *before):
        return call(
            lambda *refs: columns_kernel(other, *refs),
            [VMEM] * 11 + [HBM] * 2 if other else [VMEM] * 8,
            [
                (conv_weight.shape, F32, HBM),
                (mix_weight.shape, F32, HBM),
                ((1, channels), F32, VMEM),
                ((CONTEXTS, channels), F32, VMEM),
            ],
            [
                VMEM((2, merged_x, 128), F32),
                VMEM((3, channels, channels), F32),
                VMEM((channels, channels), F32),
                sems((8,)),
            ],
            aliases={11: 0, 12: 1} if other else None,
            micros=0.05 if other else 1.3,
        )(*pieces, *levels, second_high, second_low, *before)

    g_conv, g_mix, bias_own, partial = columns(False, (piece_x, core_x))
    later_y = touched(piece_y, partial)[0]
    core_y, other_y, far_y = swapped(piece_y, 1), swapped(later_y, 2), swapped(later_y, 3)
    other_x = touched(swapped(piece_x, 2), later_y, 2)
    far_x = [swapped(x, 1) for x in other_x]
    g_conv, g_mix, bias_other, partial = columns(True, (*other_x, *far_x), partial, g_conv, g_mix)
    g_conv, g_mix, g_embed, g_bias, g_out = call(
        first_layer_kernel,
        [VMEM] * 13 + [HBM] * 2,
        [
            (conv_weight.shape, F32, HBM),
            (mix_weight.shape, F32, HBM),
            (embed.shape, F32, HBM),
            (gate_bias.shape, F32, HBM),
            (out_weight.shape, F32, HBM),
        ],
        [
            VMEM((4, merged_y, 128), F32),
            VMEM((4, 1, 128), F32),
            VMEM(conv_weight.shape[1:], F32),
            VMEM(mix_weight.shape[1:], F32),
            VMEM(embed.shape, F32),
            VMEM(gate_bias.shape, F32),
            VMEM(out_weight.shape, F32),
            sems((7,)),
        ],
        aliases={13: 0, 14: 1},
        micros=2.2,
    )(
        piece_y, other_y, core_y, far_y, partial, mixed_table, bias_own, bias_other, embed,
        first_high, first_low, turn_high, turn_low, g_conv, g_mix,
    )
    return (out_fwd, out_rev, g_embed, g_conv, g_mix, g_bias, g_out)


def solution(mesh):
    in_specs = (
        P(("dp", "seq")),
        P(),
        P(),
        P(),
        P(),
        P(),
        P(),
        P(("dp", "seq"), None),
        P(("dp", "seq"), None),
    )
    out_specs = (
        P(("dp", "seq"), None),
        P(("dp", "seq"), None),
        P("dp", None),
        P("dp", None, None, None),
        P("dp", None, None),
        P("dp", None),
        P("dp", None, None),
    )
    return jax.shard_map(
        on_device, mesh=mesh, in_specs=in_specs, out_specs=out_specs, check_vma=False
    )
```

```python
import jax
import jax.numpy as jnp
from jax import lax
from jax.experimental import pallas as pl
from jax.experimental.pallas import tpu as pltpu
from jax.sharding import PartitionSpec as P

CONTEXTS = 96
INNER = 64
EDGE = 16
LOCAL = INNER + EDGE
TAPS = 3 * LOCAL
HALO = 128
F32 = jnp.float32
BF16 = jnp.bfloat16
VMEM_LIMIT = 40 * 1024 * 1024


def split(x):
    high = x.astype(BF16)
    return high, (x - high.astype(F32)).astype(BF16)


def dot(a, b, ca=1, cb=0):
    return lax.dot_general(a, b, (((ca,), (cb,)), ((), ())), preferred_element_type=F32)


def dot2(exact, pair, ca=1, cb=0):
    return dot(exact, pair[0], ca, cb) + dot(exact, pair[1], ca, cb)


def dot3(a, b, ca=1, cb=0):
    return dot(a[0], b[0], ca, cb) + (dot(a[0], b[1], ca, cb) + dot(a[1], b[0], ca, cb))


def letters(index):
    inner = index < 64
    left = (index >= 64) & (index < 80)
    low = index & 3
    mid = (index >> 2) & 3
    l = jnp.where(inner, (index >> 4) & 3, jnp.where(left, -1, mid))
    m = jnp.where(inner | left, mid, low)
    r = jnp.where(inner | left, low, -1)
    return l, m, r


def mirrored(index):
    low = 3 - (index & 3)
    mid = 3 - ((index >> 2) & 3)
    high = 3 - ((index >> 4) & 3)
    inner = low * 16 + mid * 4 + high
    left = 80 + low * 4 + mid
    right = 64 + low * 4 + mid
    return jnp.where(index < 64, inner, jnp.where(index < 80, left, right))


def permutation():
    rows = lax.broadcasted_iota(jnp.int32, (CONTEXTS, CONTEXTS), 0)
    cols = lax.broadcasted_iota(jnp.int32, (CONTEXTS, CONTEXTS), 1)
    return (mirrored(rows) == cols).astype(F32).astype(BF16)


def letter_hot():
    rows = lax.broadcasted_iota(jnp.int32, (CONTEXTS, 32), 0)
    cols = lax.broadcasted_iota(jnp.int32, (CONTEXTS, 32), 1)
    l, m, r = letters(rows)
    kind = cols >> 3
    value = jnp.where(kind == 0, l, jnp.where(kind == 1, m, jnp.where(kind == 2, r, 3 - m)))
    return (value == (cols & 7)).astype(F32).astype(BF16)


def gates(mixed):
    channels = mixed.shape[1] // 2
    tanh_part = jnp.tanh(mixed[:, :channels])
    sig_part = 0.5 + 0.5 * jnp.tanh(0.5 * mixed[:, channels:])
    return tanh_part, sig_part


def gate_grads(grad_hidden, tanh_part, sig_part):
    scaled = grad_hidden * sig_part
    return scaled * (1.0 - tanh_part * tanh_part), scaled * tanh_part * (1.0 - sig_part)


class Fetch:
    def __init__(self, sems):
        self.sems = sems
        self.copies = []

    def start(self, source, target):
        copy = pltpu.make_async_copy(source, target, self.sems.at[len(self.copies)])
        copy.start()
        self.copies.append(copy)
        return len(self.copies) - 1

    def wait(self, *which):
        for at in which:
            self.copies[at].wait()


def padded_base(embed):
    return jnp.concatenate([embed[...], jnp.zeros((4, embed.shape[1]), F32)], axis=0)


def left_side():
    return lax.axis_index("seq") * 2 < lax.axis_size("seq")


def local_rows(rows):
    edge = jnp.where(left_side(), rows[INNER : INNER + EDGE], rows[INNER + EDGE : INNER + 2 * EDGE])
    return jnp.concatenate([rows[:INNER], edge], axis=0)


def join_four_kernel(first, second, third, fourth, after, out):
    for at, part in enumerate((first, second, third, fourth)):
        out[at : at + 1, :] = part[...]


def touch_kernel(value, after, *outs):
    begin = 0
    for out in outs:
        out[...] = value[begin : begin + out.shape[0], :]
        begin += out.shape[0]


def first_tables_kernel(
    tokens_in, embed_in, conv_in, mix_in, out_in, own, taps, conv, mix, out_w, embed, sems,
):
    fetch = Fetch(sems)
    fetch.start(embed_in, embed)
    first = [fetch.start(conv_in.at[0, k], conv.at[k]) for k in range(3)]
    first += [fetch.start(mix_in.at[0], mix)]
    rest = [fetch.start(tokens_in, own), fetch.start(out_in.at[0], out_w)]
    fetch.wait(0)
    base = split(padded_base(embed))
    for k in range(4):
        fetch.wait(first[k])
        taps[k * 8 : (k + 1) * 8, :] = dot3(base, split(conv[k] if k < 3 else mix[...]))
    fetch.wait(*rest)


def second_tables_kernel(
    taps, embed, bias, turn, conv_in, mix_in, out_in, cot_fwd_in, cot_rev_in, after,
    table, local, mixed_table, pre_high, pre_low, cot_high, cot_low, grad_hidden, conv, mix, last_high, last_low,
    out_w, cots, sems,
):
    length = cots.shape[1]
    fetch = Fetch(sems)
    second = [fetch.start(conv_in.at[1, k], conv.at[k]) for k in range(3)]
    second += [fetch.start(mix_in.at[1], mix)]
    last = [fetch.start(out_in.at[1], out_w)]
    last += [fetch.start(cot_in, cots.at[strand]) for strand, cot_in in enumerate((cot_fwd_in, cot_rev_in))]
    hot = letter_hot()
    mixed = dot2(hot, split(taps[...])) + bias[0:1, :]
    tanh_part, sig_part = gates(mixed)
    own = dot2(hot[:, 8:16], split(padded_base(embed)))
    level = own + dot3(split(tanh_part * sig_part), split(turn[...]))
    table[...] = level
    local[...] = local_rows(level)
    mixed_table[...] = mixed
    level = split(level)
    swap = permutation()
    partner = tuple(dot(swap, piece).astype(BF16) for piece in level)
    pre_high[TAPS:, :] = jnp.zeros((pre_high.shape[0] - TAPS, pre_high.shape[1]), BF16)
    pre_low[TAPS:, :] = jnp.zeros((pre_low.shape[0] - TAPS, pre_low.shape[1]), BF16)
    for k in (0, 2, 1):
        fetch.wait(second[k])
        value = dot3(level, split(conv[k]))
        if k == 1:
            fetch.wait(second[3])
            value = value + dot3(partner, split(mix[...])) + bias[1:2, :]
        high, low = split(local_rows(value))
        pre_high[k * LOCAL : (k + 1) * LOCAL, :] = high
        pre_low[k * LOCAL : (k + 1) * LOCAL, :] = low
    fetch.wait(last[0])
    weight = split(out_w[...])
    last_high[...], last_low[...] = weight
    for strand in range(2):
        rows = slice(strand * length, (strand + 1) * length)
        fetch.wait(last[1 + strand])
        cot = split(cots[strand])
        cot_high[rows, :] = cot[0]
        cot_low[rows, :] = cot[1]
        grad_hidden[rows, :] = dot3(cot, weight, 1, 1)


def windows(parts, count):
    length = parts[0].shape[1]
    place = lax.axis_index("seq")
    last = count - 1

    def block(at):
        total, begin = None, 0
        for part in parts:
            rows = lax.broadcasted_iota(jnp.int32, part.shape, 0) + begin
            piece = jnp.sum(jnp.where(rows == (place ^ at), part[...], 0), axis=0, keepdims=True)
            total = piece if total is None else total + piece
            begin += part.shape[0]
        return total

    def window(at):
        before = jnp.where(at == 0, -1, block(jnp.maximum(at - 1, 0))[:, length - HALO :])
        after = jnp.where(at == last, -1, block(jnp.minimum(at + 1, last))[:, :HALO])
        return [before, block(at), after]

    fwd = jnp.concatenate(window(place), axis=1)
    rev = jnp.concatenate(window(last - place), axis=1)
    rev = jnp.where(rev < 0, -1, 3 - rev)
    tiles = rev.shape[1] // 128
    blocks = [rev[:, i * 128 : (i + 1) * 128] for i in reversed(range(tiles))]
    blocks += [jnp.zeros((8 - tiles, 128), jnp.int32)]
    stacked = jnp.concatenate(blocks, axis=0).astype(F32).astype(BF16)
    rows = lax.broadcasted_iota(jnp.int32, (128, 128), 0)
    cols = lax.broadcasted_iota(jnp.int32, (128, 128), 1)
    flip = (rows + cols == 127).astype(F32).astype(BF16)
    turned = dot(stacked, flip).astype(jnp.int32)
    rev = jnp.concatenate([turned[i : i + 1, :] for i in range(tiles)], axis=1)
    return fwd, rev


def local_contexts(window, first, second, length):
    width = window.shape[1]
    base = jnp.broadcast_to(window, (8, width))
    l = pltpu.roll(base, first, 1)
    r = pltpu.roll(base, width - first, 1)
    index = jnp.where(l < 0, INNER + base * 4 + r, jnp.where(r < 0, INNER + l * 4 + base, l * 16 + base * 4 + r))
    index = jnp.where(base < 0, LOCAL, index)
    before = pltpu.roll(index, second, 1)
    after = pltpu.roll(index, width - second, 1)
    return [x[0:1, HALO : HALO + length] for x in (before, index, after)]


def hot_rows(index):
    rows = lax.broadcasted_iota(jnp.int32, (LOCAL, index.shape[1]), 0)
    return (rows == index).astype(F32).astype(BF16)


def deal(quarters, keep, send):
    bit = lax.axis_index("seq") & 1
    keep[...] = quarters[pl.ds(bit * 2, 2)]
    send[...] = quarters[pl.ds((1 - bit) * 2, 2)]


def forward_kernel(count, dil, *refs):
    steps = count.bit_length() - 2
    parts, refs = refs[:steps], refs[steps:]
    (pre_high, pre_low, cot_high, cot_low, keep, send, hidden_high, hidden_low, hots, slopes, quarters) = refs
    length = parts[0].shape[1]
    channels = cot_high.shape[1]
    pre = (pre_high[...], pre_low[...])
    both = windows(parts, count)
    pad = jnp.zeros((pre_high.shape[0] - TAPS, length), BF16)
    total_o = total_c = None
    for strand in range(2):
        index = local_contexts(both[strand], dil[0], dil[1], length)
        hot = jnp.concatenate([hot_rows(x) for x in index] + [pad], axis=0)
        hots[strand] = hot
        mixed = dot2(hot, pre, 0, 0)
        tanh_part, sig_part = gates(mixed)
        product = tanh_part * sig_part
        hidden = split(product)
        rows = slice(strand * length, (strand + 1) * length)
        hidden_high[rows, :] = hidden[0]
        hidden_low[rows, :] = hidden[1]
        slopes[rows, :channels] = sig_part - product * tanh_part
        slopes[rows, channels:] = product - product * sig_part
        cot = (cot_high[rows, :], cot_low[rows, :])
        part_o = dot3(hidden, cot, 0, 0)
        part_c = dot2(hot[LOCAL : 2 * LOCAL], cot)
        total_o = part_o if total_o is None else total_o + part_o
        total_c = part_c if total_c is None else total_c + part_c
    side = channels // 4
    for q in range(4):
        lanes = slice((q >> 1) * 128, (q >> 1) * 128 + 128)
        quarters[q, :side, :] = total_o[q * side : (q + 1) * side, :128]
        quarters[q, side : 2 * side, :] = total_o[q * side : (q + 1) * side, 128:]
        for begin, rows, at in ((0, INNER // 2, 2 * side), (INNER, EDGE // 2, 2 * side + INNER // 2)):
            begin += (q & 1) * rows
            quarters[q, at : at + rows, :] = total_c[begin : begin + rows, lanes]
    deal(quarters, keep, send)


def taps_kernel(hots, slopes, grad_hidden, keep, send, quarters):
    length = hots.shape[2]
    total = None
    for strand in range(2):
        rows = slice(strand * length, (strand + 1) * length)
        grad = grad_hidden[rows, :]
        part = dot2(hots[strand], split(slopes[rows, :] * jnp.concatenate([grad, grad], axis=1)))
        total = part if total is None else total + part
    for q in range(4):
        quarters[q] = total[:TAPS, q * 128 : (q + 1) * 128]
    deal(quarters, keep, send)


def halve_kernel(kept, received, keep, send):
    bit = (lax.axis_index("seq") >> 1) & 1
    send[...] = kept[1 - bit] + received[1 - bit]
    keep[...] = kept[bit] + received[bit]


def add_after_kernel(kept, received, after, out):
    out[...] = kept[...] + received[...]


def halve_after_kernel(kept, received, after, keep, send):
    halve_kernel(kept, received, keep, send)


def outputs_kernel(hots, hidden_high, hidden_low, local, last_high, last_low, after, out_fwd, out_rev, values, sems):
    length = hots.shape[2]
    fetch = Fetch(sems)
    weight = (last_high[...], last_low[...])
    level = split(local[...])
    for strand, out in enumerate((out_fwd, out_rev)):
        rows = slice(strand * length, (strand + 1) * length)
        own = dot2(hots[strand, LOCAL : 2 * LOCAL, :], level, 0, 0)
        values[strand] = own + dot3((hidden_high[rows, :], hidden_low[rows, :]), weight)
        fetch.start(values.at[strand], out)
    fetch.wait(0, 1)


def prepare_kernel(
    first_conv, first_mix, second_conv, second_mix, out_w, table, mixed_table, after,
    first_high, first_low, second_high, second_low, turn_high, turn_low,
    level_high, level_low, partner_high, partner_low, hidden_high, hidden_low, slopes, hot,
):
    level = split(table[...])
    swap = permutation()
    level_high[...], level_low[...] = level
    partner_high[...], partner_low[...] = tuple(dot(swap, piece).astype(BF16) for piece in level)
    for conv, mix, high, low in (
        (second_conv, second_mix, second_high, second_low),
        (first_conv, first_mix, first_high, first_low),
    ):
        for k in range(4):
            high[k], low[k] = split((conv[k] if k < 3 else mix[...]).T)
    turn_high[...], turn_low[...] = split(out_w[...].T)
    tanh_part, sig_part = gates(mixed_table[...])
    product = tanh_part * sig_part
    hidden_high[...], hidden_low[...] = split(product)
    channels = product.shape[1]
    slopes[:, :channels] = sig_part - product * tanh_part
    slopes[:, channels:] = product - product * sig_part
    hot[...] = letter_hot()


def merge(mine, theirs, inner, edge):
    left = left_side()
    both = mine[inner, :] + theirs[inner, :]
    own, other = mine[edge, :], theirs[edge, :]
    return both, jnp.where(left, own, other), jnp.where(left, other, own)


def merge_blocks(mine, theirs, out, sizes):
    at = to = 0
    for inner, edge in sizes:
        pieces = merge(mine, theirs, slice(at, at + inner), slice(at + inner, at + inner + edge))
        out[to : to + inner, :] = pieces[0]
        out[to + inner : to + inner + edge, :] = pieces[1]
        out[to + inner + edge : to + inner + 2 * edge, :] = pieces[2]
        at, to = at + inner + edge, to + inner + 2 * edge


def merge_taps_kernel(mine, theirs, after, out):
    merge_blocks(mine, theirs, out, [(INNER, EDGE)] * 3)


def merge_rest_kernel(mine, theirs, after, out):
    merge_blocks(mine, theirs, out, [(mine.shape[0] - EDGE // 2, EDGE // 2)])


def gather_quarters(pieces, quarters):
    place = lax.axis_index("seq")
    low, high = place & 1, (place >> 1) & 1
    for parts, x, y in zip(pieces, (0, 0, 1, 1), (0, 1, 0, 1)):
        begin = 0
        for part in parts:
            rows = part.shape[0]
            quarters[(low ^ x) * 2 + (high ^ y), begin : begin + rows, :] = part[...]
            begin += rows


def columns_kernel(own, cores, *refs):
    count = len(cores)
    parts = 1 if own else 2
    pieces, refs = refs[: parts * count], refs[parts * count :]
    level_high, level_low, partner_high, partner_low, second_high, second_low, *refs = refs
    if not own:
        partial, g_conv_in, g_mix_in, *refs = refs
    g_conv_out, g_mix_out, bias, total, taps, g_conv, g_mix, out_sems = refs
    place = lax.axis_index("seq")
    low, high = place & 1, (place >> 1) & 1
    high = high if own else 1 - high
    store = Fetch(out_sems)
    level = (level_high[...], level_low[...])
    partner = (partner_high[...], partner_low[...])
    grad_level = None if own else partial[...]
    for at, core in enumerate(cores):
        rows = pieces[at * parts].shape[0]
        for part in range(parts):
            taps[part * rows : (part + 1) * rows, :] = pieces[at * parts + part][...]
        column = pl.multiple_of(((low ^ core) * 2 + high) * 128, 128)
        block = pl.ds(column, 128)

        def weight(k):
            return second_high[k, block, :], second_low[k, block, :]

        pairs = [split(taps[k * CONTEXTS : (k + 1) * CONTEXTS, :]) for k in range(3)]
        for k, pair in enumerate(pairs):
            g_conv[at, k] = dot3(level, pair, 0, 0)
            store.start(g_conv.at[at, k], g_conv_out.at[1, k, :, block])
        g_mix[at] = dot3(partner, pairs[1], 0, 0)
        store.start(g_mix.at[at], g_mix_out.at[1, :, block])
        bias[at : at + 1, :] = jnp.sum(taps[CONTEXTS : 2 * CONTEXTS, :], axis=0, keepdims=True)
        part = dot2(permutation(), split(dot3(pairs[1], weight(3))))
        for k, pair in enumerate(pairs):
            part = part + dot3(pair, weight(k))
        grad_level = part if grad_level is None else grad_level + part
    total[...] = grad_level
    store.wait(*range(len(store.copies)))


def first_layer_kernel(
    piece_00, piece_01, piece_10, piece_11, partial, bias_own, bias_other, bias_far, embed,
    first_high, first_low, turn_high, turn_low, hidden_high, hidden_low, slopes, hot_in,
    g_conv_in, g_mix_in, g_conv_out, g_mix_out, g_embed_out, g_bias_out, g_out_out,
    quarters, bias_rows, g_conv, g_mix, g_embed, g_bias, g_out, out_sems,
):
    channels = embed.shape[1]
    store = Fetch(out_sems)
    gather_quarters([(piece,) for piece in (piece_00, piece_01, piece_10, piece_11)], quarters)
    side = channels // 4
    rest = []
    for begin, rows in ((0, INNER // 2), (INNER // 2, EDGE // 2), (INNER // 2 + EDGE // 2, EDGE // 2)):
        begin += 2 * side
        halves = [[quarters[2 * h + i, begin : begin + rows, :] for i in range(2)] for h in range(2)]
        rest.append(jnp.concatenate([jnp.concatenate(x, axis=0) for x in halves], axis=1))
    grad_level = split(partial[...] + jnp.concatenate(rest, axis=0))
    grad_hidden = dot3(grad_level, (turn_high[...], turn_low[...]))
    grad_mixed = slopes[...] * jnp.concatenate([grad_hidden, grad_hidden], axis=1)
    hot = hot_in[...]
    by_letter = dot2(hot, split(grad_mixed), 0, 0)
    base = split(padded_base(embed))
    stacked = jnp.concatenate([base[0].astype(F32), base[0].astype(F32), base[1].astype(F32)], axis=0).astype(BF16)
    pieces = []
    for k in range(4):
        piece = split(by_letter[k * 8 : (k + 1) * 8, :])
        pieces.append(piece)
        high, low = piece[0].astype(F32), piece[1].astype(F32)
        value = dot(stacked, jnp.concatenate([high, low, high], axis=0).astype(BF16), 0, 0)
        if k < 3:
            g_conv[k] = value
            store.start(g_conv.at[k], g_conv_out.at[0, k])
        else:
            g_mix[...] = value
            store.start(g_mix, g_mix_out.at[0])
    g_out[0] = dot3((hidden_high[...], hidden_low[...]), grad_level, 0, 0)
    for q in range(4):
        for h in range(2):
            g_out[1, q * side : (q + 1) * side, h * 128 : (h + 1) * 128] = quarters[q, h * side : (h + 1) * side, :]
    store.start(g_out, g_out_out)
    place = lax.axis_index("seq")
    low, high = place & 1, (place >> 1) & 1
    for row, x, y in (
        (bias_own[0:1, :], 0, 0), (bias_own[1:2, :], 1, 0), (bias_other[...], 0, 1), (bias_far[...], 1, 1)
    ):
        bias_rows[(low ^ x) * 2 + (high ^ y)] = row
    g_bias[0:1, :] = jnp.sum(grad_mixed, axis=0, keepdims=True)
    g_bias[1:2, :] = jnp.concatenate([bias_rows[q] for q in range(4)], axis=1)
    store.start(g_bias, g_bias_out)
    grad_base = dot2(hot[:, 8:16], grad_level, 0, 0)
    for k in range(4):
        grad_base = grad_base + dot3(pieces[k], (first_high[k], first_low[k]))
    g_embed[...] = grad_base[:4, :]
    store.start(g_embed, g_embed_out)
    store.wait(*range(len(store.copies)))


VMEM, SMEM, HBM = pltpu.VMEM, pltpu.SMEM, pltpu.HBM


def call(kernel, ins, outs, scratch=(), aliases=None, micros=0.001):
    run = pl.pallas_call(
        kernel,
        out_shape=[space(shape, kind) for shape, kind, space in outs],
        in_specs=[pl.BlockSpec(memory_space=space) for space in ins],
        out_specs=[pl.BlockSpec(memory_space=space) for _, _, space in outs],
        scratch_shapes=list(scratch),
        input_output_aliases=aliases or {},
        cost_estimate=pl.CostEstimate(flops=int(micros * 1.1e9), bytes_accessed=int(micros * 3e6), transcendentals=0),
        compiler_params=pltpu.CompilerParams(vmem_limit_bytes=VMEM_LIMIT),
    )

    def placed(*args):
        return run(*[pltpu.with_memory_space_constraint(x, HBM) if space is HBM else x for x, space in zip(args, ins)])

    return placed


def swapped(value, mask):
    pairs = [(source, source ^ mask) for source in range(lax.axis_size("seq"))]
    return lax.ppermute(value, "seq", pairs)


def crossed(piece, count, rest):
    mask = 4
    while mask < count // 2:
        piece = piece + swapped(piece, mask)
        mask *= 2
    return rest(piece, swapped(piece, mask))


def on_device(
    tokens, dilations, embed, conv_weight, mix_weight, gate_bias, out_weight, cot_fwd, cot_rev
):
    channels = embed.shape[1]
    wide = 2 * channels
    length = tokens.shape[0]
    count = lax.axis_size("seq")
    sems = pltpu.SemaphoreType.DMA
    square = (channels, channels)

    row = tokens.reshape(1, length)
    near = [swapped(row, mask) for mask in (1, 2, 3)]
    layer_weights = [(conv_weight.shape[1:], F32, VMEM), (mix_weight.shape[1:], F32, VMEM)]
    own, taps, first_conv, first_mix, turn = call(
        first_tables_kernel,
        [HBM] * 5,
        [(row.shape, row.dtype, VMEM), ((32, wide), F32, VMEM), *layer_weights, (square, F32, VMEM)],
        [VMEM(embed.shape, F32), sems((7,))],
        micros=1.7,
    )(row, embed, conv_weight, mix_weight, out_weight)
    known = call(join_four_kernel, [VMEM] * 5, [((4, length), row.dtype, VMEM)])(own, *near, taps)[0]
    parts = [known, swapped(known, 4)]
    deep = -(-TAPS // 128) * 128
    (table, local, mixed_table, pre_high, pre_low, cot_high, cot_low, grad_hidden,
     second_conv, second_mix, last_high, last_low) = call(
        second_tables_kernel,
        [VMEM] * 4 + [HBM] * 5 + [VMEM],
        [((CONTEXTS, channels), F32, VMEM), ((LOCAL, channels), F32, VMEM), ((CONTEXTS, wide), F32, VMEM)]
        + [((deep, wide), BF16, VMEM)] * 2
        + [((2 * length, channels), BF16, VMEM)] * 2
        + [((2 * length, channels), F32, VMEM)]
        + layer_weights
        + [(square, BF16, VMEM)] * 2,
        [VMEM(square, F32), VMEM((2, length, channels), F32), sems((7,))],
        micros=4.0,
    )(taps, embed, gate_bias, turn, conv_weight, mix_weight, out_weight, cot_fwd, cot_rev, known)
    mask = 8
    while mask < count:
        known = jnp.concatenate([known, parts[-1]], axis=0)
        parts.append(swapped(known, mask))
        mask *= 2

    rows_x, rows_y = TAPS, channels // 2 + LOCAL // 2
    keep_y, send_y, hidden_high, hidden_low, hots, slopes = call(
        lambda *refs: forward_kernel(count, *refs),
        [SMEM] + [VMEM] * (len(parts) + 4),
        [((2, rows_y, 128), F32, VMEM)] * 2
        + [((2 * length, channels), BF16, VMEM)] * 2
        + [((2, deep, length), BF16, VMEM), ((2 * length, wide), F32, VMEM)],
        [VMEM((4, rows_y, 128), F32)],
        micros=2.0,
    )(dilations, *parts, pre_high, pre_low, cot_high, cot_low)
    keep_x, send_x = call(
        taps_kernel,
        [VMEM] * 3,
        [((2, rows_x, 128), F32, VMEM)] * 2,
        [VMEM((4, rows_x, 128), F32)],
        micros=1.5,
    )(hots, slopes, grad_hidden)

    def halved(keep, received, after):
        outs = [(keep.shape[1:], F32, VMEM)] * 2
        return call(halve_after_kernel, [VMEM] * 3, outs)(keep, received, after)

    def added(kept, received, after, space=VMEM):
        return call(add_after_kernel, [VMEM] * 2 + [space], [(kept.shape, F32, VMEM)])(kept, received, after)[0]

    def touched(value, after, cuts=1):
        shape = (value.shape[0] // cuts, value.shape[1])
        return call(touch_kernel, [VMEM] * 2, [(shape, value.dtype, VMEM)] * cuts)(value, after)

    keep_y, send_y = halved(keep_y, swapped(send_y, 1), keep_x)
    keep_x, send_x = halved(keep_x, swapped(send_x, 1), keep_y)
    sum_y = added(keep_y, swapped(send_y, 2), keep_x)
    out_fwd, out_rev = call(
        outputs_kernel,
        [VMEM] * 7,
        [((length, channels), F32, HBM)] * 2,
        [VMEM((2, length, channels), F32), sems((2,))],
        micros=2.0,
    )(hots, hidden_high, hidden_low, local, last_high, last_low, sum_y)
    sum_x = added(keep_x, swapped(send_x, 2), out_rev, HBM)
    first_high, first_low, second_high, second_low, turn_high, turn_low, *tables = call(
        prepare_kernel,
        [VMEM] * 8,
        [((4, wide, channels), BF16, VMEM)] * 4
        + [(square, BF16, VMEM)] * 2
        + [((CONTEXTS, channels), BF16, VMEM)] * 6
        + [((CONTEXTS, wide), F32, VMEM), ((CONTEXTS, 32), BF16, VMEM)],
        micros=1.4,
    )(first_conv, first_mix, second_conv, second_mix, turn, table, mixed_table, sum_x)
    levels, tables = tables[:4], tables[4:]

    def merged(kernel, rows, mine, theirs, after):
        return call(kernel, [VMEM] * 3, [((rows, 128), F32, VMEM)])(mine, theirs, after)[0]

    merged_x, merged_y = 3 * CONTEXTS, rows_y + EDGE // 2
    piece_y = crossed(sum_y, count, lambda x, y: merged(merge_rest_kernel, merged_y, x, y, turn_low))
    piece_x = crossed(sum_x, count, lambda x, y: merged(merge_taps_kernel, merged_x, x, y, piece_y))
    core_x = swapped(piece_x, 1)

    def columns(own, cores, pieces, before=(), micros=0.05):
        inner = len(pieces) + 6
        return call(
            lambda *refs: columns_kernel(own, cores, *refs),
            [VMEM] * inner + ([VMEM] + [HBM] * 2 if before else []),
            [
                (conv_weight.shape, F32, HBM),
                (mix_weight.shape, F32, HBM),
                ((len(cores), 128), F32, VMEM),
                ((CONTEXTS, channels), F32, VMEM),
            ],
            [
                VMEM((merged_x, 128), F32),
                VMEM((len(cores), 3, channels, 128), F32),
                VMEM((len(cores), channels, 128), F32),
                sems((4 * len(cores),)),
            ],
            aliases={inner + 1: 0, inner + 2: 1} if before else None,
            micros=micros,
        )(*pieces, *levels, second_high, second_low, *before)

    g_conv, g_mix, bias_own, partial = columns(True, (0, 1), (piece_x, core_x), micros=1.3)
    later_y = touched(piece_y, partial)[0]
    other_x = touched(swapped(piece_x, 2), later_y, 2)
    far_x = [swapped(x, 1) for x in other_x]
    g_conv, g_mix, bias_other, partial = columns(False, (0,), other_x, (partial, g_conv, g_mix))
    other_y = touched(swapped(later_y, 2), partial)[0]
    core_y, far_y = swapped(piece_y, 1), swapped(other_y, 1)
    g_conv, g_mix, bias_far, partial = columns(False, (1,), far_x, (partial, g_conv, g_mix), micros=1.2)
    g_conv, g_mix, g_embed, g_bias, g_out = call(
        first_layer_kernel,
        [VMEM] * 17 + [HBM] * 2,
        [
            (conv_weight.shape, F32, HBM),
            (mix_weight.shape, F32, HBM),
            (embed.shape, F32, HBM),
            (gate_bias.shape, F32, HBM),
            (out_weight.shape, F32, HBM),
        ],
        [
            VMEM((4, merged_y, 128), F32),
            VMEM((4, 1, 128), F32),
            VMEM(conv_weight.shape[1:], F32),
            VMEM(mix_weight.shape[1:], F32),
            VMEM(embed.shape, F32),
            VMEM(gate_bias.shape, F32),
            VMEM(out_weight.shape, F32),
            sems((7,)),
        ],
        aliases={17: 0, 18: 1},
        micros=2.2,
    )(
        piece_y, other_y, core_y, far_y, partial, bias_own, bias_other, bias_far, embed,
        first_high, first_low, turn_high, turn_low, *tables, g_conv, g_mix,
    )
    return (out_fwd, out_rev, g_embed, g_conv, g_mix, g_bias, g_out)


def solution(mesh):
    in_specs = (
        P(("dp", "seq")),
        P(),
        P(),
        P(),
        P(),
        P(),
        P(),
        P(("dp", "seq"), None),
        P(("dp", "seq"), None),
    )
    out_specs = (
        P(("dp", "seq"), None),
        P(("dp", "seq"), None),
        P("dp", None),
        P("dp", None, None, None),
        P("dp", None, None),
        P("dp", None),
        P("dp", None, None),
    )
    return jax.shard_map(
        on_device, mesh=mesh, in_specs=in_specs, out_specs=out_specs, check_vma=False
    )
```

```python
import jax
import jax.numpy as jnp
from jax import lax
from jax.experimental import pallas as pl
from jax.experimental.pallas import tpu as pltpu
from jax.sharding import PartitionSpec as P

CONTEXTS = 96
INNER = 64
EDGE = 16
LOCAL = INNER + EDGE
TAPS = 3 * LOCAL
HALO = 128
F32 = jnp.float32
BF16 = jnp.bfloat16
VMEM_LIMIT = 40 * 1024 * 1024


def split(x):
    high = x.astype(BF16)
    return high, (x - high.astype(F32)).astype(BF16)


def dot(a, b, ca=1, cb=0):
    return lax.dot_general(a, b, (((ca,), (cb,)), ((), ())), preferred_element_type=F32)


def dot2(exact, pair, ca=1, cb=0):
    return dot(exact, pair[0], ca, cb) + dot(exact, pair[1], ca, cb)


def dot3(a, b, ca=1, cb=0):
    return dot(a[0], b[0], ca, cb) + (dot(a[0], b[1], ca, cb) + dot(a[1], b[0], ca, cb))


def letters(index):
    inner = index < 64
    left = (index >= 64) & (index < 80)
    low = index & 3
    mid = (index >> 2) & 3
    l = jnp.where(inner, (index >> 4) & 3, jnp.where(left, -1, mid))
    m = jnp.where(inner | left, mid, low)
    r = jnp.where(inner | left, low, -1)
    return l, m, r


def mirrored(index):
    low = 3 - (index & 3)
    mid = 3 - ((index >> 2) & 3)
    high = 3 - ((index >> 4) & 3)
    inner = low * 16 + mid * 4 + high
    left = 80 + low * 4 + mid
    right = 64 + low * 4 + mid
    return jnp.where(index < 64, inner, jnp.where(index < 80, left, right))


def permutation():
    rows = lax.broadcasted_iota(jnp.int32, (CONTEXTS, CONTEXTS), 0)
    cols = lax.broadcasted_iota(jnp.int32, (CONTEXTS, CONTEXTS), 1)
    return (mirrored(rows) == cols).astype(F32).astype(BF16)


def letter_hot():
    rows = lax.broadcasted_iota(jnp.int32, (CONTEXTS, 32), 0)
    cols = lax.broadcasted_iota(jnp.int32, (CONTEXTS, 32), 1)
    l, m, r = letters(rows)
    kind = cols >> 3
    value = jnp.where(kind == 0, l, jnp.where(kind == 1, m, jnp.where(kind == 2, r, 3 - m)))
    return (value == (cols & 7)).astype(F32).astype(BF16)


def gates(mixed):
    channels = mixed.shape[1] // 2
    tanh_part = jnp.tanh(mixed[:, :channels])
    sig_part = 0.5 + 0.5 * jnp.tanh(0.5 * mixed[:, channels:])
    return tanh_part, sig_part


def gate_grads(grad_hidden, tanh_part, sig_part):
    scaled = grad_hidden * sig_part
    return scaled * (1.0 - tanh_part * tanh_part), scaled * tanh_part * (1.0 - sig_part)


class Fetch:
    def __init__(self, sems):
        self.sems = sems
        self.copies = []

    def start(self, source, target):
        copy = pltpu.make_async_copy(source, target, self.sems.at[len(self.copies)])
        copy.start()
        self.copies.append(copy)
        return len(self.copies) - 1

    def wait(self, *which):
        for at in which:
            self.copies[at].wait()


def padded_base(embed):
    return jnp.concatenate([embed[...], jnp.zeros((4, embed.shape[1]), F32)], axis=0)


def left_side():
    return lax.axis_index("seq") * 2 < lax.axis_size("seq")


def local_rows(rows):
    edge = jnp.where(left_side(), rows[INNER : INNER + EDGE], rows[INNER + EDGE : INNER + 2 * EDGE])
    return jnp.concatenate([rows[:INNER], edge], axis=0)


def join_four_kernel(first, second, third, fourth, after, out):
    for at, part in enumerate((first, second, third, fourth)):
        out[at : at + 1, :] = part[...]


def touch_kernel(value, after, *outs):
    begin = 0
    for out in outs:
        out[...] = value[begin : begin + out.shape[0], :]
        begin += out.shape[0]


def first_tables_kernel(
    tokens_in, embed_in, conv_in, mix_in, out_in, own, taps, conv, mix, out_w, embed, sems,
):
    fetch = Fetch(sems)
    fetch.start(embed_in, embed)
    first = [fetch.start(conv_in.at[0, k], conv.at[k]) for k in range(3)]
    first += [fetch.start(mix_in.at[0], mix)]
    rest = [fetch.start(tokens_in, own), fetch.start(out_in.at[0], out_w)]
    fetch.wait(0)
    base = split(padded_base(embed))
    for k in range(4):
        fetch.wait(first[k])
        taps[k * 8 : (k + 1) * 8, :] = dot3(base, split(conv[k] if k < 3 else mix[...]))
    fetch.wait(*rest)


def second_tables_kernel(
    taps, embed, bias, turn, conv_in, mix_in, out_in, cot_fwd_in, cot_rev_in, after,
    table, local, mixed_table, pre_high, pre_low, cot_high, cot_low, grad_hidden, conv, mix, last_high, last_low,
    out_w, cots, sems,
):
    length = cots.shape[1]
    fetch = Fetch(sems)
    second = [fetch.start(conv_in.at[1, k], conv.at[k]) for k in range(3)]
    second += [fetch.start(mix_in.at[1], mix)]
    last = [fetch.start(out_in.at[1], out_w)]
    last += [fetch.start(cot_in, cots.at[strand]) for strand, cot_in in enumerate((cot_fwd_in, cot_rev_in))]
    hot = letter_hot()
    mixed = dot2(hot, split(taps[...])) + bias[0:1, :]
    tanh_part, sig_part = gates(mixed)
    own = dot2(hot[:, 8:16], split(padded_base(embed)))
    level = own + dot3(split(tanh_part * sig_part), split(turn[...]))
    table[...] = level
    local[...] = local_rows(level)
    mixed_table[...] = mixed
    level = split(level)
    swap = permutation()
    partner = tuple(dot(swap, piece).astype(BF16) for piece in level)
    pre_high[TAPS:, :] = jnp.zeros((pre_high.shape[0] - TAPS, pre_high.shape[1]), BF16)
    pre_low[TAPS:, :] = jnp.zeros((pre_low.shape[0] - TAPS, pre_low.shape[1]), BF16)
    for k in (0, 2, 1):
        fetch.wait(second[k])
        value = dot3(level, split(conv[k]))
        if k == 1:
            fetch.wait(second[3])
            value = value + dot3(partner, split(mix[...])) + bias[1:2, :]
        high, low = split(local_rows(value))
        pre_high[k * LOCAL : (k + 1) * LOCAL, :] = high
        pre_low[k * LOCAL : (k + 1) * LOCAL, :] = low
    fetch.wait(last[0])
    last_high[...], last_low[...] = split(out_w[...])
    weight = split(out_w[...].T)
    for strand in range(2):
        rows = slice(strand * length, (strand + 1) * length)
        fetch.wait(last[1 + strand])
        cot = split(cots[strand])
        cot_high[rows, :] = cot[0]
        cot_low[rows, :] = cot[1]
        grad_hidden[rows, :] = dot3(cot, weight)


def windows(parts, count):
    length = parts[0].shape[1]
    place = lax.axis_index("seq")
    last = count - 1

    def block(at):
        total, begin = None, 0
        for part in parts:
            rows = lax.broadcasted_iota(jnp.int32, part.shape, 0) + begin
            piece = jnp.sum(jnp.where(rows == (place ^ at), part[...], 0), axis=0, keepdims=True)
            total = piece if total is None else total + piece
            begin += part.shape[0]
        return total

    def window(at):
        before = jnp.where(at == 0, -1, block(jnp.maximum(at - 1, 0))[:, length - HALO :])
        after = jnp.where(at == last, -1, block(jnp.minimum(at + 1, last))[:, :HALO])
        return [before, block(at), after]

    fwd = jnp.concatenate(window(place), axis=1)
    rev = jnp.concatenate(window(last - place), axis=1)
    rev = jnp.where(rev < 0, -1, 3 - rev)
    tiles = rev.shape[1] // 128
    blocks = [rev[:, i * 128 : (i + 1) * 128] for i in reversed(range(tiles))]
    blocks += [jnp.zeros((8 - tiles, 128), jnp.int32)]
    stacked = jnp.concatenate(blocks, axis=0).astype(F32).astype(BF16)
    rows = lax.broadcasted_iota(jnp.int32, (128, 128), 0)
    cols = lax.broadcasted_iota(jnp.int32, (128, 128), 1)
    flip = (rows + cols == 127).astype(F32).astype(BF16)
    turned = dot(stacked, flip).astype(jnp.int32)
    rev = jnp.concatenate([turned[i : i + 1, :] for i in range(tiles)], axis=1)
    return fwd, rev


def local_contexts(window, first, second, length):
    width = window.shape[1]
    base = jnp.broadcast_to(window, (8, width))
    l = pltpu.roll(base, first, 1)
    r = pltpu.roll(base, width - first, 1)
    index = jnp.where(l < 0, INNER + base * 4 + r, jnp.where(r < 0, INNER + l * 4 + base, l * 16 + base * 4 + r))
    index = jnp.where(base < 0, LOCAL, index)
    before = pltpu.roll(index, second, 1)
    after = pltpu.roll(index, width - second, 1)
    return [x[0:1, HALO : HALO + length] for x in (before, index, after)]


def hot_rows(index):
    rows = lax.broadcasted_iota(jnp.int32, (LOCAL, index.shape[1]), 0)
    return (rows == index).astype(F32).astype(BF16)


def hot_columns(index, width):
    length = index[0].shape[1]
    shifted = [jnp.where(x < LOCAL, x + k * LOCAL, -1) for k, x in enumerate(index)]
    rows = jnp.concatenate(shifted + [jnp.zeros((5, length), jnp.int32)], axis=0)
    places = rows.astype(F32).T
    columns = lax.broadcasted_iota(jnp.int32, (length, width), 1).astype(F32)
    hit = (columns == places[:, 0:1]) | (columns == places[:, 1:2]) | (columns == places[:, 2:3])
    return hit.astype(F32).astype(BF16)


def deal(quarters, keep, send):
    bit = lax.axis_index("seq") & 1
    keep[...] = quarters[pl.ds(bit * 2, 2)]
    send[...] = quarters[pl.ds((1 - bit) * 2, 2)]


def forward_kernel(count, dil, *refs):
    steps = count.bit_length() - 2
    parts, refs = refs[:steps], refs[steps:]
    (pre_high, pre_low, cot_high, cot_low, keep, send, hidden_high, hidden_low, hots, slopes, quarters) = refs
    length = parts[0].shape[1]
    channels = cot_high.shape[1]
    pre = (pre_high[...], pre_low[...])
    both = windows(parts, count)
    pad = jnp.zeros((pre_high.shape[0] - TAPS, length), BF16)
    total_o = total_c = None
    for strand in range(2):
        index = local_contexts(both[strand], dil[0], dil[1], length)
        hot = jnp.concatenate([hot_rows(x) for x in index] + [pad], axis=0)
        hots[strand] = hot
        mixed = dot2(hot_columns(index, pre_high.shape[0]), pre)
        tanh_part, sig_part = gates(mixed)
        product = tanh_part * sig_part
        hidden = split(product)
        rows = slice(strand * length, (strand + 1) * length)
        hidden_high[rows, :] = hidden[0]
        hidden_low[rows, :] = hidden[1]
        slopes[rows, :channels] = sig_part - product * tanh_part
        slopes[rows, channels:] = product - product * sig_part
        cot = (cot_high[rows, :], cot_low[rows, :])
        part_o = dot3(split(product.T), cot)
        part_c = dot2(hot[LOCAL : 2 * LOCAL], cot)
        total_o = part_o if total_o is None else total_o + part_o
        total_c = part_c if total_c is None else total_c + part_c
    side = channels // 4
    for q in range(4):
        lanes = slice((q >> 1) * 128, (q >> 1) * 128 + 128)
        quarters[q, :side, :] = total_o[q * side : (q + 1) * side, :128]
        quarters[q, side : 2 * side, :] = total_o[q * side : (q + 1) * side, 128:]
        for begin, rows, at in ((0, INNER // 2, 2 * side), (INNER, EDGE // 2, 2 * side + INNER // 2)):
            begin += (q & 1) * rows
            quarters[q, at : at + rows, :] = total_c[begin : begin + rows, lanes]
    deal(quarters, keep, send)


def taps_kernel(hots, slopes, grad_hidden, keep, send, quarters):
    length = hots.shape[2]
    total = None
    for strand in range(2):
        rows = slice(strand * length, (strand + 1) * length)
        grad = grad_hidden[rows, :]
        part = dot2(hots[strand], split(slopes[rows, :] * jnp.concatenate([grad, grad], axis=1)))
        total = part if total is None else total + part
    for q in range(4):
        quarters[q] = total[:TAPS, q * 128 : (q + 1) * 128]
    deal(quarters, keep, send)


def halve_kernel(kept, received, keep, send):
    bit = (lax.axis_index("seq") >> 1) & 1
    send[...] = kept[1 - bit] + received[1 - bit]
    keep[...] = kept[bit] + received[bit]


def add_after_kernel(kept, received, after, out):
    out[...] = kept[...] + received[...]


def halve_after_kernel(kept, received, after, keep, send):
    halve_kernel(kept, received, keep, send)


def outputs_kernel(hots, hidden_high, hidden_low, local, last_high, last_low, after, out_fwd, out_rev, values, sems):
    length = hots.shape[2]
    fetch = Fetch(sems)
    weight = (last_high[...], last_low[...])
    level = split(local[...])
    for strand, out in enumerate((out_fwd, out_rev)):
        rows = slice(strand * length, (strand + 1) * length)
        own = dot2(hots[strand, LOCAL : 2 * LOCAL, :], level, 0, 0)
        values[strand] = own + dot3((hidden_high[rows, :], hidden_low[rows, :]), weight)
        fetch.start(values.at[strand], out)
    fetch.wait(0, 1)


def prepare_kernel(
    first_conv, first_mix, second_conv, second_mix, out_w, table, mixed_table, after,
    first_high, first_low, second_high, second_low, turn_high, turn_low,
    level_high, level_low, partner_high, partner_low, hidden_high, hidden_low, slopes, hot,
):
    level_high[...], level_low[...] = split(table[...].T)
    swap = permutation()
    partner = [dot(swap, piece) for piece in split(table[...])]
    partner_high[...], partner_low[...] = [piece.T.astype(BF16) for piece in partner]
    for conv, mix, high, low in (
        (second_conv, second_mix, second_high, second_low),
        (first_conv, first_mix, first_high, first_low),
    ):
        for k in range(4):
            high[k], low[k] = split((conv[k] if k < 3 else mix[...]).T)
    turn_high[...], turn_low[...] = split(out_w[...].T)
    tanh_part, sig_part = gates(mixed_table[...])
    product = tanh_part * sig_part
    hidden_high[...], hidden_low[...] = split(product.T)
    channels = product.shape[1]
    slopes[:, :channels] = sig_part - product * tanh_part
    slopes[:, channels:] = product - product * sig_part
    hot[...] = letter_hot().astype(F32).T.astype(BF16)


def merge(mine, theirs, inner, edge):
    left = left_side()
    both = mine[inner, :] + theirs[inner, :]
    own, other = mine[edge, :], theirs[edge, :]
    return both, jnp.where(left, own, other), jnp.where(left, other, own)


def merge_blocks(mine, theirs, out, sizes):
    at = to = 0
    for inner, edge in sizes:
        pieces = merge(mine, theirs, slice(at, at + inner), slice(at + inner, at + inner + edge))
        out[to : to + inner, :] = pieces[0]
        out[to + inner : to + inner + edge, :] = pieces[1]
        out[to + inner + edge : to + inner + 2 * edge, :] = pieces[2]
        at, to = at + inner + edge, to + inner + 2 * edge


def merge_taps_kernel(mine, theirs, after, out):
    merge_blocks(mine, theirs, out, [(INNER, EDGE)] * 3)


def merge_rest_kernel(mine, theirs, after, out):
    merge_blocks(mine, theirs, out, [(mine.shape[0] - EDGE // 2, EDGE // 2)])


def gather_quarters(pieces, quarters):
    place = lax.axis_index("seq")
    low, high = place & 1, (place >> 1) & 1
    for parts, x, y in zip(pieces, (0, 0, 1, 1), (0, 1, 0, 1)):
        begin = 0
        for part in parts:
            rows = part.shape[0]
            quarters[(low ^ x) * 2 + (high ^ y), begin : begin + rows, :] = part[...]
            begin += rows


def columns_kernel(own, cores, *refs):
    count = len(cores)
    parts = 2 if count == 1 else 3
    pieces, refs = refs[:parts], refs[parts:]
    pieces = [pieces] if count == 1 else [pieces[:1], pieces[1:]]
    level_high, level_low, partner_high, partner_low, second_high, second_low, *refs = refs
    if not own:
        partial, g_conv_in, g_mix_in, *refs = refs
    g_conv_out, g_mix_out, bias, total, taps, g_conv, g_mix, out_sems = refs
    place = lax.axis_index("seq")
    low, high = place & 1, (place >> 1) & 1
    high = high if own else 1 - high
    store = Fetch(out_sems)
    level = (level_high[...], level_low[...])
    partner = (partner_high[...], partner_low[...])
    grad_level = None if own else partial[...]
    for at, core in enumerate(cores):
        begin = 0
        for piece in pieces[at]:
            rows = piece.shape[0]
            taps[begin : begin + rows, :] = piece[...]
            begin += rows
        column = pl.multiple_of(((low ^ core) * 2 + high) * 128, 128)
        block = pl.ds(column, 128)

        def weight(k):
            return second_high[k, block, :], second_low[k, block, :]

        pairs = [split(taps[k * CONTEXTS : (k + 1) * CONTEXTS, :]) for k in range(3)]
        for k, pair in enumerate(pairs):
            g_conv[at, k] = dot3(level, pair)
            store.start(g_conv.at[at, k], g_conv_out.at[1, k, :, block])
        g_mix[at] = dot3(partner, pairs[1])
        store.start(g_mix.at[at], g_mix_out.at[1, :, block])
        bias[at : at + 1, :] = jnp.sum(taps[CONTEXTS : 2 * CONTEXTS, :], axis=0, keepdims=True)
        part = dot2(permutation(), split(dot3(pairs[1], weight(3))))
        for k, pair in enumerate(pairs):
            part = part + dot3(pair, weight(k))
        grad_level = part if grad_level is None else grad_level + part
    total[...] = grad_level
    store.wait(*range(len(store.copies)))


def first_layer_kernel(
    piece_00, piece_01, piece_10, piece_11, partial, bias_own, bias_other, bias_far, embed,
    first_high, first_low, turn_high, turn_low, hidden_high, hidden_low, slopes, hot_in,
    g_conv_in, g_mix_in, g_conv_out, g_mix_out, g_embed_out, g_bias_out, g_out_out,
    quarters, bias_rows, g_conv, g_mix, g_embed, g_bias, g_out, out_sems,
):
    channels = embed.shape[1]
    store = Fetch(out_sems)
    gather_quarters([(piece,) for piece in (piece_00, piece_01, piece_10, piece_11)], quarters)
    side = channels // 4
    rest = []
    for begin, rows in ((0, INNER // 2), (INNER // 2, EDGE // 2), (INNER // 2 + EDGE // 2, EDGE // 2)):
        begin += 2 * side
        halves = [[quarters[2 * h + i, begin : begin + rows, :] for i in range(2)] for h in range(2)]
        rest.append(jnp.concatenate([jnp.concatenate(x, axis=0) for x in halves], axis=1))
    grad_level = split(partial[...] + jnp.concatenate(rest, axis=0))
    grad_hidden = dot3(grad_level, (turn_high[...], turn_low[...]))
    grad_mixed = slopes[...] * jnp.concatenate([grad_hidden, grad_hidden], axis=1)
    hot = hot_in[...]
    by_letter = dot2(hot, split(grad_mixed))
    base = split(padded_base(embed))
    stacked = jnp.concatenate([base[i].astype(F32) for i in (0, 0, 1)], axis=0).T.astype(BF16)
    pieces = []
    for k in range(4):
        piece = split(by_letter[k * 8 : (k + 1) * 8, :])
        pieces.append(piece)
        high, low = piece[0].astype(F32), piece[1].astype(F32)
        value = dot(stacked, jnp.concatenate([high, low, high], axis=0).astype(BF16))
        if k < 3:
            g_conv[k] = value
            store.start(g_conv.at[k], g_conv_out.at[0, k])
        else:
            g_mix[...] = value
            store.start(g_mix, g_mix_out.at[0])
    g_out[0] = dot3((hidden_high[...], hidden_low[...]), grad_level)
    for q in range(4):
        for h in range(2):
            g_out[1, q * side : (q + 1) * side, h * 128 : (h + 1) * 128] = quarters[q, h * side : (h + 1) * side, :]
    store.start(g_out, g_out_out)
    place = lax.axis_index("seq")
    low, high = place & 1, (place >> 1) & 1
    for row, x, y in (
        (bias_own[0:1, :], 0, 0), (bias_own[1:2, :], 1, 0), (bias_other[...], 0, 1), (bias_far[...], 1, 1)
    ):
        bias_rows[(low ^ x) * 2 + (high ^ y)] = row
    g_bias[0:1, :] = jnp.sum(grad_mixed, axis=0, keepdims=True)
    g_bias[1:2, :] = jnp.concatenate([bias_rows[q] for q in range(4)], axis=1)
    store.start(g_bias, g_bias_out)
    grad_base = dot2(hot, grad_level)[8:16]
    for k in range(4):
        grad_base = grad_base + dot3(pieces[k], (first_high[k], first_low[k]))
    g_embed[...] = grad_base[:4, :]
    store.start(g_embed, g_embed_out)
    store.wait(*range(len(store.copies)))


VMEM, SMEM, HBM = pltpu.VMEM, pltpu.SMEM, pltpu.HBM


def call(kernel, ins, outs, scratch=(), aliases=None, micros=0.001):
    run = pl.pallas_call(
        kernel,
        out_shape=[space(shape, kind) for shape, kind, space in outs],
        in_specs=[pl.BlockSpec(memory_space=space) for space in ins],
        out_specs=[pl.BlockSpec(memory_space=space) for _, _, space in outs],
        scratch_shapes=list(scratch),
        input_output_aliases=aliases or {},
        cost_estimate=pl.CostEstimate(flops=int(micros * 1.1e9), bytes_accessed=int(micros * 3e6), transcendentals=0),
        compiler_params=pltpu.CompilerParams(vmem_limit_bytes=VMEM_LIMIT),
    )

    def placed(*args):
        return run(*[pltpu.with_memory_space_constraint(x, HBM) if space is HBM else x for x, space in zip(args, ins)])

    return placed


def swapped(value, mask):
    pairs = [(source, source ^ mask) for source in range(lax.axis_size("seq"))]
    return lax.ppermute(value, "seq", pairs)


def crossed(piece, count, rest):
    mask = 4
    while mask < count // 2:
        piece = piece + swapped(piece, mask)
        mask *= 2
    return rest(piece, swapped(piece, mask))


def on_device(
    tokens, dilations, embed, conv_weight, mix_weight, gate_bias, out_weight, cot_fwd, cot_rev
):
    channels = embed.shape[1]
    wide = 2 * channels
    length = tokens.shape[0]
    count = lax.axis_size("seq")
    sems = pltpu.SemaphoreType.DMA
    square = (channels, channels)

    row = tokens.reshape(1, length)
    near = [swapped(row, mask) for mask in (1, 2, 3)]
    layer_weights = [(conv_weight.shape[1:], F32, VMEM), (mix_weight.shape[1:], F32, VMEM)]
    own, taps, first_conv, first_mix, turn = call(
        first_tables_kernel,
        [HBM] * 5,
        [(row.shape, row.dtype, VMEM), ((32, wide), F32, VMEM), *layer_weights, (square, F32, VMEM)],
        [VMEM(embed.shape, F32), sems((7,))],
        micros=1.7,
    )(row, embed, conv_weight, mix_weight, out_weight)
    known = call(join_four_kernel, [VMEM] * 5, [((4, length), row.dtype, VMEM)])(own, *near, taps)[0]
    parts = [known, swapped(known, 4)]
    deep = -(-TAPS // 128) * 128
    (table, local, mixed_table, pre_high, pre_low, cot_high, cot_low, grad_hidden,
     second_conv, second_mix, last_high, last_low) = call(
        second_tables_kernel,
        [VMEM] * 4 + [HBM] * 5 + [VMEM],
        [((CONTEXTS, channels), F32, VMEM), ((LOCAL, channels), F32, VMEM), ((CONTEXTS, wide), F32, VMEM)]
        + [((deep, wide), BF16, VMEM)] * 2
        + [((2 * length, channels), BF16, VMEM)] * 2
        + [((2 * length, channels), F32, VMEM)]
        + layer_weights
        + [(square, BF16, VMEM)] * 2,
        [VMEM(square, F32), VMEM((2, length, channels), F32), sems((7,))],
        micros=4.0,
    )(taps, embed, gate_bias, turn, conv_weight, mix_weight, out_weight, cot_fwd, cot_rev, known)
    mask = 8
    while mask < count:
        known = jnp.concatenate([known, parts[-1]], axis=0)
        parts.append(swapped(known, mask))
        mask *= 2

    rows_x, rows_y = TAPS, channels // 2 + LOCAL // 2
    keep_y, send_y, hidden_high, hidden_low, hots, slopes = call(
        lambda *refs: forward_kernel(count, *refs),
        [SMEM] + [VMEM] * (len(parts) + 4),
        [((2, rows_y, 128), F32, VMEM)] * 2
        + [((2 * length, channels), BF16, VMEM)] * 2
        + [((2, deep, length), BF16, VMEM), ((2 * length, wide), F32, VMEM)],
        [VMEM((4, rows_y, 128), F32)],
        micros=2.0,
    )(dilations, *parts, pre_high, pre_low, cot_high, cot_low)
    keep_x, send_x = call(
        taps_kernel,
        [VMEM] * 3,
        [((2, rows_x, 128), F32, VMEM)] * 2,
        [VMEM((4, rows_x, 128), F32)],
        micros=1.5,
    )(hots, slopes, grad_hidden)

    def halved(keep, received, after):
        outs = [(keep.shape[1:], F32, VMEM)] * 2
        return call(halve_after_kernel, [VMEM] * 3, outs)(keep, received, after)

    def added(kept, received, after, space=VMEM):
        return call(add_after_kernel, [VMEM] * 2 + [space], [(kept.shape, F32, VMEM)])(kept, received, after)[0]

    def touched(value, after, cuts=1):
        shape = (value.shape[0] // cuts, value.shape[1])
        return call(touch_kernel, [VMEM] * 2, [(shape, value.dtype, VMEM)] * cuts)(value, after)

    keep_y, send_y = halved(keep_y, swapped(send_y, 1), keep_x)
    keep_x, send_x = halved(keep_x, swapped(send_x, 1), keep_y)
    sum_y = added(keep_y, swapped(send_y, 2), keep_x)
    out_fwd, out_rev = call(
        outputs_kernel,
        [VMEM] * 7,
        [((length, channels), F32, HBM)] * 2,
        [VMEM((2, length, channels), F32), sems((2,))],
        micros=2.0,
    )(hots, hidden_high, hidden_low, local, last_high, last_low, sum_y)
    sum_x = added(keep_x, swapped(send_x, 2), out_rev, HBM)
    first_high, first_low, second_high, second_low, turn_high, turn_low, *tables = call(
        prepare_kernel,
        [VMEM] * 8,
        [((4, wide, channels), BF16, VMEM)] * 4
        + [(square, BF16, VMEM)] * 2
        + [((channels, CONTEXTS), BF16, VMEM)] * 6
        + [((CONTEXTS, wide), F32, VMEM), ((32, CONTEXTS), BF16, VMEM)],
        micros=1.4,
    )(first_conv, first_mix, second_conv, second_mix, turn, table, mixed_table, sum_x)
    levels, tables = tables[:4], tables[4:]

    def merged(kernel, rows, mine, theirs, after):
        return call(kernel, [VMEM] * 3, [((rows, 128), F32, VMEM)])(mine, theirs, after)[0]

    merged_x, merged_y = 3 * CONTEXTS, rows_y + EDGE // 2
    piece_y = crossed(sum_y, count, lambda x, y: merged(merge_rest_kernel, merged_y, x, y, turn_low))
    piece_x = crossed(sum_x, count, lambda x, y: merged(merge_taps_kernel, merged_x, x, y, piece_y))
    core_x = [swapped(x, 1) for x in touched(piece_x, sum_x, 2)]

    def columns(own, cores, pieces, before=(), micros=0.05):
        inner = len(pieces) + 6
        return call(
            lambda *refs: columns_kernel(own, cores, *refs),
            [VMEM] * inner + ([VMEM] + [HBM] * 2 if before else []),
            [
                (conv_weight.shape, F32, HBM),
                (mix_weight.shape, F32, HBM),
                ((len(cores), 128), F32, VMEM),
                ((CONTEXTS, channels), F32, VMEM),
            ],
            [
                VMEM((merged_x, 128), F32),
                VMEM((len(cores), 3, channels, 128), F32),
                VMEM((len(cores), channels, 128), F32),
                sems((4 * len(cores),)),
            ],
            aliases={inner + 1: 0, inner + 2: 1} if before else None,
            micros=micros,
        )(*pieces, *levels, second_high, second_low, *before)

    g_conv, g_mix, bias_own, partial = columns(True, (0, 1), (piece_x, *core_x))
    later_y = touched(piece_y, partial)[0]
    other_x = touched(swapped(piece_x, 2), later_y, 2)
    far_x = [swapped(x, 1) for x in other_x]
    g_conv, g_mix, bias_other, partial = columns(False, (0,), other_x, (partial, g_conv, g_mix))
    other_y = touched(swapped(later_y, 2), partial)[0]
    core_y, far_y = swapped(piece_y, 1), swapped(other_y, 1)
    g_conv, g_mix, bias_far, partial = columns(False, (1,), far_x, (partial, g_conv, g_mix), micros=1.2)
    g_conv, g_mix, g_embed, g_bias, g_out = call(
        first_layer_kernel,
        [VMEM] * 17 + [HBM] * 2,
        [
            (conv_weight.shape, F32, HBM),
            (mix_weight.shape, F32, HBM),
            (embed.shape, F32, HBM),
            (gate_bias.shape, F32, HBM),
            (out_weight.shape, F32, HBM),
        ],
        [
            VMEM((4, merged_y, 128), F32),
            VMEM((4, 1, 128), F32),
            VMEM(conv_weight.shape[1:], F32),
            VMEM(mix_weight.shape[1:], F32),
            VMEM(embed.shape, F32),
            VMEM(gate_bias.shape, F32),
            VMEM(out_weight.shape, F32),
            sems((7,)),
        ],
        aliases={17: 0, 18: 1},
        micros=2.2,
    )(
        piece_y, other_y, core_y, far_y, partial, bias_own, bias_other, bias_far, embed,
        first_high, first_low, turn_high, turn_low, *tables, g_conv, g_mix,
    )
    return (out_fwd, out_rev, g_embed, g_conv, g_mix, g_bias, g_out)


def solution(mesh):
    in_specs = (
        P(("dp", "seq")),
        P(),
        P(),
        P(),
        P(),
        P(),
        P(),
        P(("dp", "seq"), None),
        P(("dp", "seq"), None),
    )
    out_specs = (
        P(("dp", "seq"), None),
        P(("dp", "seq"), None),
        P("dp", None),
        P("dp", None, None, None),
        P("dp", None, None),
        P("dp", None),
        P("dp", None, None),
    )
    return jax.shard_map(
        on_device, mesh=mesh, in_specs=in_specs, out_specs=out_specs, check_vma=False
    )
```

```python
import jax
import jax.numpy as jnp
from jax import lax
from jax.experimental import pallas as pl
from jax.experimental.pallas import tpu as pltpu
from jax.sharding import PartitionSpec as P

CONTEXTS = 96
INNER = 64
EDGE = 16
LOCAL = INNER + EDGE
TAPS = 3 * LOCAL
HALO = 128
F32 = jnp.float32
BF16 = jnp.bfloat16
VMEM_LIMIT = 40 * 1024 * 1024


def split(x):
    high = x.astype(BF16)
    return high, (x - high.astype(F32)).astype(BF16)


def dot(a, b, ca=1, cb=0):
    return lax.dot_general(a, b, (((ca,), (cb,)), ((), ())), preferred_element_type=F32)


def dot2(exact, pair, ca=1, cb=0):
    return dot(exact, pair[0], ca, cb) + dot(exact, pair[1], ca, cb)


def dot3(a, b, ca=1, cb=0):
    return dot(a[0], b[0], ca, cb) + (dot(a[0], b[1], ca, cb) + dot(a[1], b[0], ca, cb))


def dot3_few(a, b):
    rows = a[0].shape[0]
    both = dot(jnp.concatenate([a[0].astype(F32), a[1].astype(F32)], axis=0).astype(BF16), b[0])
    return both[:rows] + (both[rows:] + dot(a[0], b[1]))


def letters(index):
    inner = index < 64
    left = (index >= 64) & (index < 80)
    low = index & 3
    mid = (index >> 2) & 3
    l = jnp.where(inner, (index >> 4) & 3, jnp.where(left, -1, mid))
    m = jnp.where(inner | left, mid, low)
    r = jnp.where(inner | left, low, -1)
    return l, m, r


def mirrored(index):
    low = 3 - (index & 3)
    mid = 3 - ((index >> 2) & 3)
    high = 3 - ((index >> 4) & 3)
    inner = low * 16 + mid * 4 + high
    left = 80 + low * 4 + mid
    right = 64 + low * 4 + mid
    return jnp.where(index < 64, inner, jnp.where(index < 80, left, right))


def permutation():
    rows = lax.broadcasted_iota(jnp.int32, (CONTEXTS, CONTEXTS), 0)
    cols = lax.broadcasted_iota(jnp.int32, (CONTEXTS, CONTEXTS), 1)
    return (mirrored(rows) == cols).astype(F32).astype(BF16)


def letter_hot():
    rows = lax.broadcasted_iota(jnp.int32, (CONTEXTS, 32), 0)
    cols = lax.broadcasted_iota(jnp.int32, (CONTEXTS, 32), 1)
    l, m, r = letters(rows)
    kind = cols >> 3
    value = jnp.where(kind == 0, l, jnp.where(kind == 1, m, jnp.where(kind == 2, r, 3 - m)))
    return (value == (cols & 7)).astype(F32).astype(BF16)


def gates(mixed):
    channels = mixed.shape[1] // 2
    tanh_part = jnp.tanh(mixed[:, :channels])
    sig_part = 0.5 + 0.5 * jnp.tanh(0.5 * mixed[:, channels:])
    return tanh_part, sig_part


def gate_grads(grad_hidden, tanh_part, sig_part):
    scaled = grad_hidden * sig_part
    return scaled * (1.0 - tanh_part * tanh_part), scaled * tanh_part * (1.0 - sig_part)


class Fetch:
    def __init__(self, sems):
        self.sems = sems
        self.copies = []

    def start(self, source, target):
        copy = pltpu.make_async_copy(source, target, self.sems.at[len(self.copies)])
        copy.start()
        self.copies.append(copy)
        return len(self.copies) - 1

    def wait(self, *which):
        for at in which:
            self.copies[at].wait()


def padded_base(embed):
    return jnp.concatenate([embed[...], jnp.zeros((4, embed.shape[1]), F32)], axis=0)


def left_side():
    return lax.axis_index("seq") * 2 < lax.axis_size("seq")


def local_rows(rows):
    edge = jnp.where(left_side(), rows[INNER : INNER + EDGE], rows[INNER + EDGE : INNER + 2 * EDGE])
    return jnp.concatenate([rows[:INNER], edge], axis=0)


def join_four_kernel(first, second, third, fourth, after, out):
    for at, part in enumerate((first, second, third, fourth)):
        out[at : at + 1, :] = part[...]


def touch_kernel(value, after, *outs):
    begin = 0
    for out in outs:
        out[...] = value[begin : begin + out.shape[0], :]
        begin += out.shape[0]


def first_tables_kernel(
    tokens_in, embed_in, conv_in, mix_in, out_in, own, taps, conv, mix, out_w, embed, sems,
):
    fetch = Fetch(sems)
    fetch.start(embed_in, embed)
    first = [fetch.start(conv_in.at[0, k], conv.at[k]) for k in range(3)]
    first += [fetch.start(mix_in.at[0], mix)]
    rest = [fetch.start(tokens_in, own), fetch.start(out_in.at[0], out_w)]
    fetch.wait(0)
    base = split(padded_base(embed))
    for k in range(4):
        fetch.wait(first[k])
        taps[k * 8 : (k + 1) * 8, :] = dot3_few(base, split(conv[k] if k < 3 else mix[...]))
    fetch.wait(*rest)


def second_tables_kernel(
    taps, embed, bias, turn, conv_in, mix_in, out_in, cot_fwd_in, cot_rev_in, after,
    table, local, mixed_table, pre_high, pre_low, cot_high, cot_low, conv, mix, out_w,
    cots, sems,
):
    length = cots.shape[1]
    fetch = Fetch(sems)
    second = [fetch.start(conv_in.at[1, k], conv.at[k]) for k in range(3)]
    second += [fetch.start(mix_in.at[1], mix)]
    last = [fetch.start(out_in.at[1], out_w)]
    last += [fetch.start(cot_in, cots.at[strand]) for strand, cot_in in enumerate((cot_fwd_in, cot_rev_in))]
    hot = letter_hot()
    mixed = dot2(hot, split(taps[...])) + bias[0:1, :]
    tanh_part, sig_part = gates(mixed)
    own = dot2(hot[:, 8:16], split(padded_base(embed)))
    level = own + dot3_few(split(tanh_part * sig_part), split(turn[...]))
    table[...] = level
    local[...] = local_rows(level)
    mixed_table[...] = mixed
    level = split(level)
    swap = permutation()
    partner = tuple(dot(swap, piece).astype(BF16) for piece in level)
    pre_high[TAPS:, :] = jnp.zeros((pre_high.shape[0] - TAPS, pre_high.shape[1]), BF16)
    pre_low[TAPS:, :] = jnp.zeros((pre_low.shape[0] - TAPS, pre_low.shape[1]), BF16)
    for k in (0, 2, 1):
        fetch.wait(second[k])
        value = dot3_few(level, split(conv[k]))
        if k == 1:
            fetch.wait(second[3])
            value = value + dot3_few(partner, split(mix[...])) + bias[1:2, :]
        high, low = split(local_rows(value))
        pre_high[k * LOCAL : (k + 1) * LOCAL, :] = high
        pre_low[k * LOCAL : (k + 1) * LOCAL, :] = low
    for strand in range(2):
        rows = slice(strand * length, (strand + 1) * length)
        fetch.wait(last[1 + strand])
        cot_high[rows, :], cot_low[rows, :] = split(cots[strand])
    fetch.wait(last[0])


def windows(parts, count):
    length = parts[0].shape[1]
    place = lax.axis_index("seq")
    last = count - 1

    def block(at):
        total, begin = None, 0
        for part in parts:
            rows = lax.broadcasted_iota(jnp.int32, part.shape, 0) + begin
            piece = jnp.sum(jnp.where(rows == (place ^ at), part[...], 0), axis=0, keepdims=True)
            total = piece if total is None else total + piece
            begin += part.shape[0]
        return total

    def window(at):
        before = jnp.where(at == 0, -1, block(jnp.maximum(at - 1, 0))[:, length - HALO :])
        after = jnp.where(at == last, -1, block(jnp.minimum(at + 1, last))[:, :HALO])
        return [before, block(at), after]

    fwd = jnp.concatenate(window(place), axis=1)
    rev = jnp.concatenate(window(last - place), axis=1)
    rev = jnp.where(rev < 0, -1, 3 - rev)
    tiles = rev.shape[1] // 128
    blocks = [rev[:, i * 128 : (i + 1) * 128] for i in reversed(range(tiles))]
    blocks += [jnp.zeros((8 - tiles, 128), jnp.int32)]
    stacked = jnp.concatenate(blocks, axis=0).astype(F32).astype(BF16)
    rows = lax.broadcasted_iota(jnp.int32, (128, 128), 0)
    cols = lax.broadcasted_iota(jnp.int32, (128, 128), 1)
    flip = (rows + cols == 127).astype(F32).astype(BF16)
    turned = dot(stacked, flip).astype(jnp.int32)
    rev = jnp.concatenate([turned[i : i + 1, :] for i in range(tiles)], axis=1)
    return fwd, rev


def local_contexts(window, first, second, length):
    width = window.shape[1]
    base = jnp.broadcast_to(window, (8, width))
    l = pltpu.roll(base, first, 1)
    r = pltpu.roll(base, width - first, 1)
    index = jnp.where(l < 0, INNER + base * 4 + r, jnp.where(r < 0, INNER + l * 4 + base, l * 16 + base * 4 + r))
    index = jnp.where(base < 0, LOCAL, index)
    before = pltpu.roll(index, second, 1)
    after = pltpu.roll(index, width - second, 1)
    return [x[0:1, HALO : HALO + length] for x in (before, index, after)]


def hot_rows(index):
    rows = lax.broadcasted_iota(jnp.int32, (LOCAL, index.shape[1]), 0)
    return (rows == index).astype(F32).astype(BF16)


def deal(quarters, keep, send):
    bit = lax.axis_index("seq") & 1
    keep[...] = quarters[pl.ds(bit * 2, 2)]
    send[...] = quarters[pl.ds((1 - bit) * 2, 2)]


def forward_kernel(count, dil, *refs):
    steps = count.bit_length() - 2
    parts, refs = refs[:steps], refs[steps:]
    (pre_high, pre_low, cot_high, cot_low, keep, send, hidden_high, hidden_low, hots, slopes, quarters) = refs
    length = parts[0].shape[1]
    channels = cot_high.shape[1]
    pre = (pre_high[...], pre_low[...])
    both = windows(parts, count)
    pad = jnp.zeros((pre_high.shape[0] - TAPS, length), BF16)
    total_o = total_c = None
    for strand in range(2):
        index = local_contexts(both[strand], dil[0], dil[1], length)
        hot = jnp.concatenate([hot_rows(x) for x in index] + [pad], axis=0)
        hots[strand] = hot
        mixed = dot2(hot, pre, 0, 0)
        tanh_part, sig_part = gates(mixed)
        product = tanh_part * sig_part
        hidden = split(product)
        rows = slice(strand * length, (strand + 1) * length)
        hidden_high[rows, :] = hidden[0]
        hidden_low[rows, :] = hidden[1]
        slopes[rows, :channels] = sig_part - product * tanh_part
        slopes[rows, channels:] = product - product * sig_part
        cot = (cot_high[rows, :], cot_low[rows, :])
        part_o = dot3(hidden, cot, 0, 0)
        part_c = dot2(hot[LOCAL : 2 * LOCAL], cot)
        total_o = part_o if total_o is None else total_o + part_o
        total_c = part_c if total_c is None else total_c + part_c
    side = channels // 4
    for q in range(4):
        lanes = slice((q >> 1) * 128, (q >> 1) * 128 + 128)
        quarters[q, :side, :] = total_o[q * side : (q + 1) * side, :128]
        quarters[q, side : 2 * side, :] = total_o[q * side : (q + 1) * side, 128:]
        for begin, rows, at in ((0, INNER // 2, 2 * side), (INNER, EDGE // 2, 2 * side + INNER // 2)):
            begin += (q & 1) * rows
            quarters[q, at : at + rows, :] = total_c[begin : begin + rows, lanes]
    deal(quarters, keep, send)


def taps_kernel(hots, slopes, cot_high, cot_low, out_w, keep, send, quarters):
    length = hots.shape[2]
    weight = split(out_w[...])
    total = None
    for strand in range(2):
        rows = slice(strand * length, (strand + 1) * length)
        grad = dot3((cot_high[rows, :], cot_low[rows, :]), weight, 1, 1)
        part = dot2(hots[strand], split(slopes[rows, :] * jnp.concatenate([grad, grad], axis=1)))
        total = part if total is None else total + part
    for q in range(4):
        quarters[q] = total[:TAPS, q * 128 : (q + 1) * 128]
    deal(quarters, keep, send)


def halve_kernel(kept, received, keep, send):
    bit = (lax.axis_index("seq") >> 1) & 1
    send[...] = kept[1 - bit] + received[1 - bit]
    keep[...] = kept[bit] + received[bit]


def add_after_kernel(kept, received, after, out):
    out[...] = kept[...] + received[...]


def halve_after_kernel(kept, received, after, keep, send):
    halve_kernel(kept, received, keep, send)


def outputs_kernel(hots, hidden_high, hidden_low, local, out_w, after, out_fwd, out_rev, values, sems):
    length = hots.shape[2]
    fetch = Fetch(sems)
    weight = split(out_w[...])
    level = split(local[...])
    for strand, out in enumerate((out_fwd, out_rev)):
        rows = slice(strand * length, (strand + 1) * length)
        own = dot2(hots[strand, LOCAL : 2 * LOCAL, :], level, 0, 0)
        values[strand] = own + dot3((hidden_high[rows, :], hidden_low[rows, :]), weight)
        fetch.start(values.at[strand], out)
    fetch.wait(0, 1)


def prepare_kernel(
    first_conv, first_mix, second_conv, second_mix, out_w, table, mixed_table, after,
    first_high, first_low, second_high, second_low, turn_high, turn_low,
    level_high, level_low, partner_high, partner_low, hidden_high, hidden_low, slopes, hot,
):
    level = split(table[...])
    swap = permutation()
    level_high[...], level_low[...] = level
    partner_high[...], partner_low[...] = tuple(dot(swap, piece).astype(BF16) for piece in level)
    for conv, mix, high, low in (
        (second_conv, second_mix, second_high, second_low),
        (first_conv, first_mix, first_high, first_low),
    ):
        for k in range(4):
            high[k], low[k] = split((conv[k] if k < 3 else mix[...]).T)
    turn_high[...], turn_low[...] = split(out_w[...].T)
    tanh_part, sig_part = gates(mixed_table[...])
    product = tanh_part * sig_part
    hidden_high[...], hidden_low[...] = split(product)
    channels = product.shape[1]
    slopes[:, :channels] = sig_part - product * tanh_part
    slopes[:, channels:] = product - product * sig_part
    hot[...] = letter_hot()


def merge(mine, theirs, inner, edge):
    left = left_side()
    both = mine[inner, :] + theirs[inner, :]
    own, other = mine[edge, :], theirs[edge, :]
    return both, jnp.where(left, own, other), jnp.where(left, other, own)


def merge_blocks(mine, theirs, out, sizes):
    at = to = 0
    for inner, edge in sizes:
        pieces = merge(mine, theirs, slice(at, at + inner), slice(at + inner, at + inner + edge))
        out[to : to + inner, :] = pieces[0]
        out[to + inner : to + inner + edge, :] = pieces[1]
        out[to + inner + edge : to + inner + 2 * edge, :] = pieces[2]
        at, to = at + inner + edge, to + inner + 2 * edge


def merge_taps_kernel(mine, theirs, after, out):
    merge_blocks(mine, theirs, out, [(INNER, EDGE)] * 3)


def merge_rest_kernel(mine, theirs, after, out):
    merge_blocks(mine, theirs, out, [(mine.shape[0] - EDGE // 2, EDGE // 2)])


def gather_quarters(pieces, quarters):
    place = lax.axis_index("seq")
    low, high = place & 1, (place >> 1) & 1
    for parts, x, y in zip(pieces, (0, 0, 1, 1), (0, 1, 0, 1)):
        begin = 0
        for part in parts:
            rows = part.shape[0]
            quarters[(low ^ x) * 2 + (high ^ y), begin : begin + rows, :] = part[...]
            begin += rows


def columns_kernel(own, cores, *refs):
    pieces = [refs[:1], refs[1:3]] if own else [refs[:1]]
    refs = refs[sum(len(piece) for piece in pieces) :]
    level_high, level_low, partner_high, partner_low, second_high, second_low, *refs = refs
    if not own:
        partial, g_conv_in, g_mix_in, *refs = refs
    g_conv_out, g_mix_out, bias, total, taps, g_conv, g_mix, out_sems = refs
    place = lax.axis_index("seq")
    low, high = place & 1, (place >> 1) & 1
    high = high if own else 1 - high
    store = Fetch(out_sems)
    level = (level_high[...], level_low[...])
    partner = (partner_high[...], partner_low[...])
    grad_level = None if own else partial[...]
    for at, core in enumerate(cores):
        begin = 0
        for piece in pieces[at]:
            rows = piece.shape[0]
            taps[begin : begin + rows, :] = piece[...]
            begin += rows
        column = pl.multiple_of(((low ^ core) * 2 + high) * 128, 128)
        block = pl.ds(column, 128)

        def weight(k):
            return second_high[k, block, :], second_low[k, block, :]

        pairs = [split(taps[k * CONTEXTS : (k + 1) * CONTEXTS, :]) for k in range(3)]
        for k, pair in enumerate(pairs):
            g_conv[at, k] = dot3(level, pair, 0, 0)
            store.start(g_conv.at[at, k], g_conv_out.at[1, k, :, block])
        g_mix[at] = dot3(partner, pairs[1], 0, 0)
        store.start(g_mix.at[at], g_mix_out.at[1, :, block])
        bias[at : at + 1, :] = jnp.sum(taps[CONTEXTS : 2 * CONTEXTS, :], axis=0, keepdims=True)
        part = dot2(permutation(), split(dot3_few(pairs[1], weight(3))))
        for k, pair in enumerate(pairs):
            part = part + dot3_few(pair, weight(k))
        grad_level = part if grad_level is None else grad_level + part
    total[...] = grad_level
    store.wait(*range(len(store.copies)))


def first_layer_kernel(
    piece_00, piece_01, piece_10, piece_11, partial, bias_own, bias_other, bias_far, embed,
    first_high, first_low, turn_high, turn_low, hidden_high, hidden_low, slopes, hot_in,
    g_conv_in, g_mix_in, g_conv_out, g_mix_out, g_embed_out, g_bias_out, g_out_out,
    quarters, bias_rows, g_conv, g_mix, g_embed, g_bias, g_out, out_sems,
):
    channels = embed.shape[1]
    store = Fetch(out_sems)
    gather_quarters([(piece,) for piece in (piece_00, piece_01, piece_10, piece_11)], quarters)
    side = channels // 4
    rest = []
    for begin, rows in ((0, INNER // 2), (INNER // 2, EDGE // 2), (INNER // 2 + EDGE // 2, EDGE // 2)):
        begin += 2 * side
        halves = [[quarters[2 * h + i, begin : begin + rows, :] for i in range(2)] for h in range(2)]
        rest.append(jnp.concatenate([jnp.concatenate(x, axis=0) for x in halves], axis=1))
    grad_level = split(partial[...] + jnp.concatenate(rest, axis=0))
    grad_hidden = dot3_few(grad_level, (turn_high[...], turn_low[...]))
    grad_mixed = slopes[...] * jnp.concatenate([grad_hidden, grad_hidden], axis=1)
    hot = hot_in[...]
    by_letter = dot2(hot, split(grad_mixed), 0, 0)
    base = split(padded_base(embed))
    stacked = jnp.concatenate([base[0].astype(F32), base[0].astype(F32), base[1].astype(F32)], axis=0).astype(BF16)
    pieces = []
    for k in range(4):
        piece = split(by_letter[k * 8 : (k + 1) * 8, :])
        pieces.append(piece)
        high, low = piece[0].astype(F32), piece[1].astype(F32)
        value = dot(stacked, jnp.concatenate([high, low, high], axis=0).astype(BF16), 0, 0)
        if k < 3:
            g_conv[k] = value
            store.start(g_conv.at[k], g_conv_out.at[0, k])
        else:
            g_mix[...] = value
            store.start(g_mix, g_mix_out.at[0])
    g_out[0] = dot3((hidden_high[...], hidden_low[...]), grad_level, 0, 0)
    for q in range(4):
        for h in range(2):
            g_out[1, q * side : (q + 1) * side, h * 128 : (h + 1) * 128] = quarters[q, h * side : (h + 1) * side, :]
    store.start(g_out, g_out_out)
    place = lax.axis_index("seq")
    low, high = place & 1, (place >> 1) & 1
    for row, x, y in (
        (bias_own[0:1, :], 0, 0), (bias_own[1:2, :], 1, 0), (bias_other[...], 0, 1), (bias_far[...], 1, 1)
    ):
        bias_rows[(low ^ x) * 2 + (high ^ y)] = row
    g_bias[0:1, :] = jnp.sum(grad_mixed, axis=0, keepdims=True)
    g_bias[1:2, :] = jnp.concatenate([bias_rows[q] for q in range(4)], axis=1)
    store.start(g_bias, g_bias_out)
    grad_base = dot2(hot[:, 8:16], grad_level, 0, 0)
    for k in range(4):
        grad_base = grad_base + dot3_few(pieces[k], (first_high[k], first_low[k]))
    g_embed[...] = grad_base[:4, :]
    store.start(g_embed, g_embed_out)
    store.wait(*range(len(store.copies)))


VMEM, SMEM, HBM = pltpu.VMEM, pltpu.SMEM, pltpu.HBM


def call(kernel, ins, outs, scratch=(), aliases=None, micros=0.001):
    run = pl.pallas_call(
        kernel,
        out_shape=[space(shape, kind) for shape, kind, space in outs],
        in_specs=[pl.BlockSpec(memory_space=space) for space in ins],
        out_specs=[pl.BlockSpec(memory_space=space) for _, _, space in outs],
        scratch_shapes=list(scratch),
        input_output_aliases=aliases or {},
        cost_estimate=pl.CostEstimate(flops=int(micros * 1.1e9), bytes_accessed=int(micros * 3e6), transcendentals=0),
        compiler_params=pltpu.CompilerParams(vmem_limit_bytes=VMEM_LIMIT),
    )

    def placed(*args):
        return run(*[pltpu.with_memory_space_constraint(x, HBM) if space is HBM else x for x, space in zip(args, ins)])

    return placed


def swapped(value, mask):
    pairs = [(source, source ^ mask) for source in range(lax.axis_size("seq"))]
    return lax.ppermute(value, "seq", pairs)


def crossed(piece, count, rest):
    mask = 4
    while mask < count // 2:
        piece = piece + swapped(piece, mask)
        mask *= 2
    return rest(piece, swapped(piece, mask))


def on_device(
    tokens, dilations, embed, conv_weight, mix_weight, gate_bias, out_weight, cot_fwd, cot_rev
):
    channels = embed.shape[1]
    wide = 2 * channels
    length = tokens.shape[0]
    count = lax.axis_size("seq")
    sems = pltpu.SemaphoreType.DMA
    square = (channels, channels)

    row = tokens.reshape(1, length)
    near = [swapped(row, mask) for mask in (1, 2, 3)]
    layer_weights = [(conv_weight.shape[1:], F32, VMEM), (mix_weight.shape[1:], F32, VMEM)]
    own, taps, first_conv, first_mix, turn = call(
        first_tables_kernel,
        [HBM] * 5,
        [(row.shape, row.dtype, VMEM), ((32, wide), F32, VMEM), *layer_weights, (square, F32, VMEM)],
        [VMEM(embed.shape, F32), sems((7,))],
        micros=1.7,
    )(row, embed, conv_weight, mix_weight, out_weight)
    known = call(join_four_kernel, [VMEM] * 5, [((4, length), row.dtype, VMEM)])(own, *near, taps)[0]
    parts = [known, swapped(known, 4)]
    deep = -(-TAPS // 128) * 128
    (table, local, mixed_table, pre_high, pre_low, cot_high, cot_low,
     second_conv, second_mix, last_weight) = call(
        second_tables_kernel,
        [VMEM] * 4 + [HBM] * 5 + [VMEM],
        [((CONTEXTS, channels), F32, VMEM), ((LOCAL, channels), F32, VMEM), ((CONTEXTS, wide), F32, VMEM)]
        + [((deep, wide), BF16, VMEM)] * 2
        + [((2 * length, channels), BF16, VMEM)] * 2
        + layer_weights
        + [(square, F32, VMEM)],
        [VMEM((2, length, channels), F32), sems((7,))],
        micros=3.0,
    )(taps, embed, gate_bias, turn, conv_weight, mix_weight, out_weight, cot_fwd, cot_rev, known)
    mask = 8
    while mask < count:
        known = jnp.concatenate([known, parts[-1]], axis=0)
        parts.append(swapped(known, mask))
        mask *= 2

    rows_x, rows_y = TAPS, channels // 2 + LOCAL // 2
    keep_y, send_y, hidden_high, hidden_low, hots, slopes = call(
        lambda *refs: forward_kernel(count, *refs),
        [SMEM] + [VMEM] * (len(parts) + 4),
        [((2, rows_y, 128), F32, VMEM)] * 2
        + [((2 * length, channels), BF16, VMEM)] * 2
        + [((2, deep, length), BF16, VMEM), ((2 * length, wide), F32, VMEM)],
        [VMEM((4, rows_y, 128), F32)],
        micros=2.0,
    )(dilations, *parts, pre_high, pre_low, cot_high, cot_low)
    keep_x, send_x = call(
        taps_kernel,
        [VMEM] * 5,
        [((2, rows_x, 128), F32, VMEM)] * 2,
        [VMEM((4, rows_x, 128), F32)],
        micros=1.5,
    )(hots, slopes, cot_high, cot_low, last_weight)

    def halved(keep, received, after):
        outs = [(keep.shape[1:], F32, VMEM)] * 2
        return call(halve_after_kernel, [VMEM] * 3, outs)(keep, received, after)

    def added(kept, received, after, space=VMEM):
        return call(add_after_kernel, [VMEM] * 2 + [space], [(kept.shape, F32, VMEM)])(kept, received, after)[0]

    def touched(value, after, cuts=1):
        shape = (value.shape[0] // cuts, value.shape[1])
        return call(touch_kernel, [VMEM] * 2, [(shape, value.dtype, VMEM)] * cuts)(value, after)

    keep_y, send_y = halved(keep_y, swapped(send_y, 1), keep_x)
    keep_x, send_x = halved(keep_x, swapped(send_x, 1), keep_y)
    sum_y = added(keep_y, swapped(send_y, 2), keep_x)
    out_fwd, out_rev = call(
        outputs_kernel,
        [VMEM] * 6,
        [((length, channels), F32, HBM)] * 2,
        [VMEM((2, length, channels), F32), sems((2,))],
        micros=2.0,
    )(hots, hidden_high, hidden_low, local, last_weight, sum_y)
    sum_x = added(keep_x, swapped(send_x, 2), out_rev, HBM)
    first_high, first_low, second_high, second_low, turn_high, turn_low, *tables = call(
        prepare_kernel,
        [VMEM] * 8,
        [((4, wide, channels), BF16, VMEM)] * 4
        + [(square, BF16, VMEM)] * 2
        + [((CONTEXTS, channels), BF16, VMEM)] * 6
        + [((CONTEXTS, wide), F32, VMEM), ((CONTEXTS, 32), BF16, VMEM)],
        micros=1.4,
    )(first_conv, first_mix, second_conv, second_mix, turn, table, mixed_table, sum_x)
    levels, tables = tables[:4], tables[4:]

    def merged(kernel, rows, mine, theirs, after):
        return call(kernel, [VMEM] * 3, [((rows, 128), F32, VMEM)])(mine, theirs, after)[0]

    merged_x, merged_y = 3 * CONTEXTS, rows_y + EDGE // 2
    piece_y = crossed(sum_y, count, lambda x, y: merged(merge_rest_kernel, merged_y, x, y, turn_low))
    piece_x = crossed(sum_x, count, lambda x, y: merged(merge_taps_kernel, merged_x, x, y, piece_y))
    other_y = swapped(piece_y, 2)
    core_x = [swapped(x, 1) for x in touched(piece_x, other_y, 2)]

    def columns(own, cores, pieces, before=(), micros=0.05):
        inner = len(pieces) + 6
        return call(
            lambda *refs: columns_kernel(own, cores, *refs),
            [VMEM] * inner + ([VMEM] + [HBM] * 2 if before else []),
            [
                (conv_weight.shape, F32, HBM),
                (mix_weight.shape, F32, HBM),
                ((len(cores), 128), F32, VMEM),
                ((CONTEXTS, channels), F32, VMEM),
            ],
            [
                VMEM((merged_x, 128), F32),
                VMEM((len(cores), 3, channels, 128), F32),
                VMEM((len(cores), channels, 128), F32),
                sems((4 * len(cores),)),
            ],
            aliases={inner + 1: 0, inner + 2: 1} if before else None,
            micros=micros,
        )(*pieces, *levels, second_high, second_low, *before)

    core_y, far_y = swapped(piece_y, 1), swapped(other_y, 1)
    g_conv, g_mix, bias_own, partial = columns(True, (0, 1), (piece_x, *core_x))
    other_x = swapped(piece_x, 2)
    rest_y = touched(far_y, partial)[0]
    far_x = [swapped(x, 1) for x in touched(other_x, rest_y)]
    g_conv, g_mix, bias_other, partial = columns(False, (0,), (other_x,), (partial, g_conv, g_mix))
    g_conv, g_mix, bias_far, partial = columns(False, (1,), far_x, (partial, g_conv, g_mix), micros=1.2)
    g_conv, g_mix, g_embed, g_bias, g_out = call(
        first_layer_kernel,
        [VMEM] * 17 + [HBM] * 2,
        [
            (conv_weight.shape, F32, HBM),
            (mix_weight.shape, F32, HBM),
            (embed.shape, F32, HBM),
            (gate_bias.shape, F32, HBM),
            (out_weight.shape, F32, HBM),
        ],
        [
            VMEM((4, merged_y, 128), F32),
            VMEM((4, 1, 128), F32),
            VMEM(conv_weight.shape[1:], F32),
            VMEM(mix_weight.shape[1:], F32),
            VMEM(embed.shape, F32),
            VMEM(gate_bias.shape, F32),
            VMEM(out_weight.shape, F32),
            sems((7,)),
        ],
        aliases={17: 0, 18: 1},
        micros=2.2,
    )(
        piece_y, other_y, core_y, rest_y, partial, bias_own, bias_other, bias_far, embed,
        first_high, first_low, turn_high, turn_low, *tables, g_conv, g_mix,
    )
    return (out_fwd, out_rev, g_embed, g_conv, g_mix, g_bias, g_out)


def solution(mesh):
    in_specs = (
        P(("dp", "seq")),
        P(),
        P(),
        P(),
        P(),
        P(),
        P(),
        P(("dp", "seq"), None),
        P(("dp", "seq"), None),
    )
    out_specs = (
        P(("dp", "seq"), None),
        P(("dp", "seq"), None),
        P("dp", None),
        P("dp", None, None, None),
        P("dp", None, None),
        P("dp", None),
        P("dp", None, None),
    )
    return jax.shard_map(
        on_device, mesh=mesh, in_specs=in_specs, out_specs=out_specs, check_vma=False
    )
```

```python
import jax
import jax.numpy as jnp
from jax import lax
from jax.experimental import pallas as pl
from jax.experimental.pallas import tpu as pltpu
from jax.sharding import PartitionSpec as P

CONTEXTS = 96
INNER = 64
EDGE = 16
LOCAL = INNER + EDGE
TAPS = 3 * LOCAL
HALO = 128
F32 = jnp.float32
BF16 = jnp.bfloat16
VMEM_LIMIT = 40 * 1024 * 1024


def split(x):
    high = x.astype(BF16)
    return high, (x - high.astype(F32)).astype(BF16)


def dot(a, b, ca=1, cb=0):
    return lax.dot_general(a, b, (((ca,), (cb,)), ((), ())), preferred_element_type=F32)


def dot2(exact, pair, ca=1, cb=0):
    return dot(exact, pair[0], ca, cb) + dot(exact, pair[1], ca, cb)


def dot3(a, b, ca=1, cb=0):
    return dot(a[0], b[0], ca, cb) + (dot(a[0], b[1], ca, cb) + dot(a[1], b[0], ca, cb))


def dot3_few(a, b):
    rows = a[0].shape[0]
    both = dot(jnp.concatenate([a[0].astype(F32), a[1].astype(F32)], axis=0).astype(BF16), b[0])
    return both[:rows] + (both[rows:] + dot(a[0], b[1]))


def letters(index):
    inner = index < 64
    left = (index >= 64) & (index < 80)
    low = index & 3
    mid = (index >> 2) & 3
    l = jnp.where(inner, (index >> 4) & 3, jnp.where(left, -1, mid))
    m = jnp.where(inner | left, mid, low)
    r = jnp.where(inner | left, low, -1)
    return l, m, r


def mirrored(index):
    low = 3 - (index & 3)
    mid = 3 - ((index >> 2) & 3)
    high = 3 - ((index >> 4) & 3)
    inner = low * 16 + mid * 4 + high
    left = 80 + low * 4 + mid
    right = 64 + low * 4 + mid
    return jnp.where(index < 64, inner, jnp.where(index < 80, left, right))


def permutation():
    rows = lax.broadcasted_iota(jnp.int32, (CONTEXTS, CONTEXTS), 0)
    cols = lax.broadcasted_iota(jnp.int32, (CONTEXTS, CONTEXTS), 1)
    return (mirrored(rows) == cols).astype(F32).astype(BF16)


def letter_hot():
    rows = lax.broadcasted_iota(jnp.int32, (CONTEXTS, 32), 0)
    cols = lax.broadcasted_iota(jnp.int32, (CONTEXTS, 32), 1)
    l, m, r = letters(rows)
    kind = cols >> 3
    value = jnp.where(kind == 0, l, jnp.where(kind == 1, m, jnp.where(kind == 2, r, 3 - m)))
    return (value == (cols & 7)).astype(F32).astype(BF16)


def gates(mixed):
    channels = mixed.shape[1] // 2
    tanh_part = jnp.tanh(mixed[:, :channels])
    sig_part = 0.5 + 0.5 * jnp.tanh(0.5 * mixed[:, channels:])
    return tanh_part, sig_part


def gate_grads(grad_hidden, tanh_part, sig_part):
    scaled = grad_hidden * sig_part
    return scaled * (1.0 - tanh_part * tanh_part), scaled * tanh_part * (1.0 - sig_part)


class Fetch:
    def __init__(self, sems):
        self.sems = sems
        self.copies = []

    def start(self, source, target):
        copy = pltpu.make_async_copy(source, target, self.sems.at[len(self.copies)])
        copy.start()
        self.copies.append(copy)
        return len(self.copies) - 1

    def wait(self, *which):
        for at in which:
            self.copies[at].wait()


def padded_base(embed):
    return jnp.concatenate([embed[...], jnp.zeros((4, embed.shape[1]), F32)], axis=0)


def left_side():
    return lax.axis_index("seq") * 2 < lax.axis_size("seq")


def local_rows(rows):
    edge = jnp.where(left_side(), rows[INNER : INNER + EDGE], rows[INNER + EDGE : INNER + 2 * EDGE])
    return jnp.concatenate([rows[:INNER], edge], axis=0)


def join_four_kernel(first, second, third, fourth, after, out):
    for at, part in enumerate((first, second, third, fourth)):
        out[at : at + 1, :] = part[...]


def touch_kernel(value, after, *outs):
    begin = 0
    for out in outs:
        out[...] = value[begin : begin + out.shape[0], :]
        begin += out.shape[0]


def first_tables_kernel(
    tokens_in, embed_in, conv_in, mix_in, out_in, cot_fwd_in, cot_rev_in,
    own, taps, conv, mix, turn, last_weight, cot_high, cot_low, grad_hidden, embed, cots, sems,
):
    length = cots.shape[1]
    fetch = Fetch(sems)
    fetch.start(embed_in, embed)
    first = [fetch.start(conv_in.at[0, k], conv.at[k]) for k in range(3)]
    first += [fetch.start(mix_in.at[0], mix)]
    last = [fetch.start(out_in.at[1], last_weight)]
    last += [fetch.start(cot_in, cots.at[strand]) for strand, cot_in in enumerate((cot_fwd_in, cot_rev_in))]
    rest = [fetch.start(tokens_in, own), fetch.start(out_in.at[0], turn)]
    fetch.wait(0)
    base = split(padded_base(embed))
    for k in range(4):
        fetch.wait(first[k])
        taps[k * 8 : (k + 1) * 8, :] = dot3_few(base, split(conv[k] if k < 3 else mix[...]))
    fetch.wait(last[0])
    weight = split(last_weight[...])
    for strand in range(2):
        rows = slice(strand * length, (strand + 1) * length)
        fetch.wait(last[1 + strand])
        cot = split(cots[strand])
        cot_high[rows, :], cot_low[rows, :] = cot
        grad_hidden[rows, :] = dot3(cot, weight, 1, 1)
    fetch.wait(*rest)


def second_tables_kernel(
    taps, embed, bias, turn, conv_in, mix_in, after, table, local, mixed_table, pre_high, pre_low, conv, mix, sems,
):
    fetch = Fetch(sems)
    second = [fetch.start(conv_in.at[1, k], conv.at[k]) for k in range(3)]
    second += [fetch.start(mix_in.at[1], mix)]
    hot = letter_hot()
    mixed = dot2(hot, split(taps[...])) + bias[0:1, :]
    tanh_part, sig_part = gates(mixed)
    own = dot2(hot[:, 8:16], split(padded_base(embed)))
    level = own + dot3_few(split(tanh_part * sig_part), split(turn[...]))
    table[...] = level
    local[...] = local_rows(level)
    mixed_table[...] = mixed
    level = split(level)
    swap = permutation()
    partner = tuple(dot(swap, piece).astype(BF16) for piece in level)
    pre_high[TAPS:, :] = jnp.zeros((pre_high.shape[0] - TAPS, pre_high.shape[1]), BF16)
    pre_low[TAPS:, :] = jnp.zeros((pre_low.shape[0] - TAPS, pre_low.shape[1]), BF16)
    for k in (0, 2, 1):
        fetch.wait(second[k])
        value = dot3_few(level, split(conv[k]))
        if k == 1:
            fetch.wait(second[3])
            value = value + dot3_few(partner, split(mix[...])) + bias[1:2, :]
        high, low = split(local_rows(value))
        pre_high[k * LOCAL : (k + 1) * LOCAL, :] = high
        pre_low[k * LOCAL : (k + 1) * LOCAL, :] = low


def windows(parts, count):
    length = parts[0].shape[1]
    place = lax.axis_index("seq")
    last = count - 1

    def block(at):
        total, begin = None, 0
        for part in parts:
            rows = lax.broadcasted_iota(jnp.int32, part.shape, 0) + begin
            piece = jnp.sum(jnp.where(rows == (place ^ at), part[...], 0), axis=0, keepdims=True)
            total = piece if total is None else total + piece
            begin += part.shape[0]
        return total

    def window(at):
        before = jnp.where(at == 0, -1, block(jnp.maximum(at - 1, 0))[:, length - HALO :])
        after = jnp.where(at == last, -1, block(jnp.minimum(at + 1, last))[:, :HALO])
        return [before, block(at), after]

    fwd = jnp.concatenate(window(place), axis=1)
    rev = jnp.concatenate(window(last - place), axis=1)
    rev = jnp.where(rev < 0, -1, 3 - rev)
    tiles = rev.shape[1] // 128
    blocks = [rev[:, i * 128 : (i + 1) * 128] for i in reversed(range(tiles))]
    blocks += [jnp.zeros((8 - tiles, 128), jnp.int32)]
    stacked = jnp.concatenate(blocks, axis=0).astype(F32).astype(BF16)
    rows = lax.broadcasted_iota(jnp.int32, (128, 128), 0)
    cols = lax.broadcasted_iota(jnp.int32, (128, 128), 1)
    flip = (rows + cols == 127).astype(F32).astype(BF16)
    turned = dot(stacked, flip).astype(jnp.int32)
    rev = jnp.concatenate([turned[i : i + 1, :] for i in range(tiles)], axis=1)
    return fwd, rev


def local_contexts(window, first, second, length):
    width = window.shape[1]
    base = jnp.broadcast_to(window, (8, width))
    l = pltpu.roll(base, first, 1)
    r = pltpu.roll(base, width - first, 1)
    index = jnp.where(l < 0, INNER + base * 4 + r, jnp.where(r < 0, INNER + l * 4 + base, l * 16 + base * 4 + r))
    index = jnp.where(base < 0, LOCAL, index)
    before = pltpu.roll(index, second, 1)
    after = pltpu.roll(index, width - second, 1)
    return [x[0:1, HALO : HALO + length] for x in (before, index, after)]


def hot_rows(index):
    rows = lax.broadcasted_iota(jnp.int32, (LOCAL, index.shape[1]), 0)
    return (rows == index).astype(F32).astype(BF16)


def deal(quarters, keep, send):
    bit = lax.axis_index("seq") & 1
    keep[...] = quarters[pl.ds(bit * 2, 2)]
    send[...] = quarters[pl.ds((1 - bit) * 2, 2)]


def forward_kernel(count, dil, *refs):
    steps = count.bit_length() - 2
    parts, refs = refs[:steps], refs[steps:]
    (pre_high, pre_low, cot_high, cot_low, keep, send, hidden_high, hidden_low, hots, slopes, quarters) = refs
    length = parts[0].shape[1]
    channels = cot_high.shape[1]
    pre = (pre_high[...], pre_low[...])
    both = windows(parts, count)
    pad = jnp.zeros((pre_high.shape[0] - TAPS, length), BF16)
    total_o = total_c = None
    for strand in range(2):
        index = local_contexts(both[strand], dil[0], dil[1], length)
        hot = jnp.concatenate([hot_rows(x) for x in index] + [pad], axis=0)
        hots[strand] = hot
        mixed = dot2(hot, pre, 0, 0)
        tanh_part, sig_part = gates(mixed)
        product = tanh_part * sig_part
        hidden = split(product)
        rows = slice(strand * length, (strand + 1) * length)
        hidden_high[rows, :] = hidden[0]
        hidden_low[rows, :] = hidden[1]
        slopes[rows, :channels] = sig_part - product * tanh_part
        slopes[rows, channels:] = product - product * sig_part
        cot = (cot_high[rows, :], cot_low[rows, :])
        part_o = dot3(hidden, cot, 0, 0)
        part_c = dot2(hot[LOCAL : 2 * LOCAL], cot)
        total_o = part_o if total_o is None else total_o + part_o
        total_c = part_c if total_c is None else total_c + part_c
    side = channels // 4
    for q in range(4):
        lanes = slice((q >> 1) * 128, (q >> 1) * 128 + 128)
        quarters[q, :side, :] = total_o[q * side : (q + 1) * side, :128]
        quarters[q, side : 2 * side, :] = total_o[q * side : (q + 1) * side, 128:]
        for begin, rows, at in ((0, INNER // 2, 2 * side), (INNER, EDGE // 2, 2 * side + INNER // 2)):
            begin += (q & 1) * rows
            quarters[q, at : at + rows, :] = total_c[begin : begin + rows, lanes]
    deal(quarters, keep, send)


def taps_kernel(hots, slopes, grad_hidden, keep, send, quarters):
    length = hots.shape[2]
    total = None
    for strand in range(2):
        rows = slice(strand * length, (strand + 1) * length)
        grad = grad_hidden[rows, :]
        part = dot2(hots[strand], split(slopes[rows, :] * jnp.concatenate([grad, grad], axis=1)))
        total = part if total is None else total + part
    for q in range(4):
        quarters[q] = total[:TAPS, q * 128 : (q + 1) * 128]
    deal(quarters, keep, send)


def halve_kernel(kept, received, keep, send):
    bit = (lax.axis_index("seq") >> 1) & 1
    send[...] = kept[1 - bit] + received[1 - bit]
    keep[...] = kept[bit] + received[bit]


def add_after_kernel(kept, received, after, out):
    out[...] = kept[...] + received[...]


def halve_after_kernel(kept, received, after, keep, send):
    halve_kernel(kept, received, keep, send)


def outputs_kernel(hots, hidden_high, hidden_low, local, out_w, after, out_fwd, out_rev, values, sems):
    length = hots.shape[2]
    fetch = Fetch(sems)
    weight = split(out_w[...])
    level = split(local[...])
    for strand, out in enumerate((out_fwd, out_rev)):
        rows = slice(strand * length, (strand + 1) * length)
        own = dot2(hots[strand, LOCAL : 2 * LOCAL, :], level, 0, 0)
        values[strand] = own + dot3((hidden_high[rows, :], hidden_low[rows, :]), weight)
        fetch.start(values.at[strand], out)
    fetch.wait(0, 1)


def prepare_kernel(
    first_conv, first_mix, second_conv, second_mix, out_w, table, mixed_table, after,
    first_high, first_low, second_high, second_low, turn_high, turn_low,
    level_high, level_low, partner_high, partner_low, hidden_high, hidden_low, slopes, hot,
):
    level = split(table[...])
    swap = permutation()
    level_high[...], level_low[...] = level
    partner_high[...], partner_low[...] = tuple(dot(swap, piece).astype(BF16) for piece in level)
    for conv, mix, high, low in (
        (second_conv, second_mix, second_high, second_low),
        (first_conv, first_mix, first_high, first_low),
    ):
        for k in range(4):
            high[k], low[k] = split((conv[k] if k < 3 else mix[...]).T)
    turn_high[...], turn_low[...] = split(out_w[...].T)
    tanh_part, sig_part = gates(mixed_table[...])
    product = tanh_part * sig_part
    hidden_high[...], hidden_low[...] = split(product)
    channels = product.shape[1]
    slopes[:, :channels] = sig_part - product * tanh_part
    slopes[:, channels:] = product - product * sig_part
    hot[...] = letter_hot()


def merge(mine, theirs, inner, edge):
    left = left_side()
    both = mine[inner, :] + theirs[inner, :]
    own, other = mine[edge, :], theirs[edge, :]
    return both, jnp.where(left, own, other), jnp.where(left, other, own)


def merge_blocks(mine, theirs, out, sizes):
    at = to = 0
    for inner, edge in sizes:
        pieces = merge(mine, theirs, slice(at, at + inner), slice(at + inner, at + inner + edge))
        out[to : to + inner, :] = pieces[0]
        out[to + inner : to + inner + edge, :] = pieces[1]
        out[to + inner + edge : to + inner + 2 * edge, :] = pieces[2]
        at, to = at + inner + edge, to + inner + 2 * edge


def merge_taps_kernel(mine, theirs, after, out):
    merge_blocks(mine, theirs, out, [(INNER, EDGE)] * 3)


def merge_rest_kernel(mine, theirs, after, out):
    merge_blocks(mine, theirs, out, [(mine.shape[0] - EDGE // 2, EDGE // 2)])


def gather_quarters(pieces, quarters):
    place = lax.axis_index("seq")
    low, high = place & 1, (place >> 1) & 1
    for parts, x, y in zip(pieces, (0, 0, 1, 1), (0, 1, 0, 1)):
        begin = 0
        for part in parts:
            rows = part.shape[0]
            quarters[(low ^ x) * 2 + (high ^ y), begin : begin + rows, :] = part[...]
            begin += rows


def quarter_columns(taps, column, levels, seconds, g_conv, g_mix, bias):
    level_high, level_low, partner_high, partner_low = levels
    level = (level_high[...], level_low[...])
    partner = (partner_high[...], partner_low[...])
    weights = [tuple(ref[k, pl.ds(column, 128), :] for ref in seconds) for k in range(4)]
    pairs = [split(taps[k * CONTEXTS : (k + 1) * CONTEXTS, :]) for k in range(3)]
    for k, pair in enumerate(pairs):
        g_conv[k] = dot3(level, pair, 0, 0)
    g_mix[...] = dot3(partner, pairs[1], 0, 0)
    bias[...] = jnp.sum(taps[CONTEXTS : 2 * CONTEXTS, :], axis=0, keepdims=True)
    part = dot2(permutation(), split(dot3_few(pairs[1], weights[3])))
    for k, pair in enumerate(pairs):
        part = part + dot3_few(pair, weights[k])
    return part


def column_of(core, chip):
    place = lax.axis_index("seq")
    low, high = place & 1, (place >> 1) & 1
    return pl.multiple_of(((low ^ core) * 2 + (high ^ chip)) * 128, 128)


def store_columns(store, column, g_conv, g_mix, g_conv_out, g_mix_out):
    block = pl.ds(column, 128)
    for k in range(3):
        store.start(g_conv.at[k], g_conv_out.at[1, k, :, block])
    store.start(g_mix, g_mix_out.at[1, :, block])


def own_columns_kernel(own_piece, core_first, core_second, *refs):
    levels, seconds, refs = refs[:4], refs[4:6], refs[6:]
    g_conv_out, g_mix_out, bias, total, taps, g_conv, g_mix, out_sems = refs
    store = Fetch(out_sems)
    half = core_first.shape[0]
    taps[0] = own_piece[...]
    taps[1, :half, :] = core_first[...]
    taps[1, half:, :] = core_second[...]
    grad_level = None
    for core in range(2):
        column = column_of(core, 0)
        part = quarter_columns(
            taps.at[core], column, levels, seconds, g_conv.at[core], g_mix.at[core], bias.at[core : core + 1]
        )
        store_columns(store, column, g_conv.at[core], g_mix.at[core], g_conv_out, g_mix_out)
        grad_level = part if grad_level is None else grad_level + part
    total[...] = grad_level
    store.wait(*range(len(store.copies)))


def other_columns_kernel(piece, *refs):
    levels, seconds, refs = refs[:4], refs[4:6], refs[6:]
    partial, g_conv_in, g_mix_in, g_conv_out, g_mix_out, bias, total, g_conv, g_mix, out_sems = refs
    store = Fetch(out_sems)
    column = column_of(0, 1)
    total[...] = partial[...] + quarter_columns(piece, column, levels, seconds, g_conv, g_mix, bias)
    store_columns(store, column, g_conv, g_mix, g_conv_out, g_mix_out)
    store.wait(*range(len(store.copies)))


def first_layer_kernel(
    far_piece, level_high, level_low, partner_high, partner_low, second_high, second_low,
    piece_00, piece_01, piece_10, piece_11, partial, bias_own, bias_other, embed,
    first_high, first_low, turn_high, turn_low, hidden_high, hidden_low, slopes, hot_in,
    g_conv_in, g_mix_in, g_conv_out, g_mix_out, g_embed_out, g_bias_out, g_out_out,
    quarters, bias_rows, bias_far, far_conv, far_mix, g_conv, g_mix, g_embed, g_bias, g_out, out_sems,
):
    channels = embed.shape[1]
    store = Fetch(out_sems)
    column = column_of(1, 1)
    levels = (level_high, level_low, partner_high, partner_low)
    far_part = quarter_columns(far_piece, column, levels, (second_high, second_low), far_conv, far_mix, bias_far)
    gather_quarters([(piece,) for piece in (piece_00, piece_01, piece_10, piece_11)], quarters)
    side = channels // 4
    rest = []
    for begin, rows in ((0, INNER // 2), (INNER // 2, EDGE // 2), (INNER // 2 + EDGE // 2, EDGE // 2)):
        begin += 2 * side
        halves = [[quarters[2 * h + i, begin : begin + rows, :] for i in range(2)] for h in range(2)]
        rest.append(jnp.concatenate([jnp.concatenate(x, axis=0) for x in halves], axis=1))
    grad_level = split(partial[...] + far_part + jnp.concatenate(rest, axis=0))
    grad_hidden = dot3_few(grad_level, (turn_high[...], turn_low[...]))
    grad_mixed = slopes[...] * jnp.concatenate([grad_hidden, grad_hidden], axis=1)
    store_columns(store, column, far_conv, far_mix, g_conv_out, g_mix_out)
    hot = hot_in[...]
    by_letter = dot2(hot, split(grad_mixed), 0, 0)
    base = split(padded_base(embed))
    stacked = jnp.concatenate([base[0].astype(F32), base[0].astype(F32), base[1].astype(F32)], axis=0).astype(BF16)
    pieces = []
    for k in range(4):
        piece = split(by_letter[k * 8 : (k + 1) * 8, :])
        pieces.append(piece)
        high, low = piece[0].astype(F32), piece[1].astype(F32)
        value = dot(stacked, jnp.concatenate([high, low, high], axis=0).astype(BF16), 0, 0)
        if k < 3:
            g_conv[k] = value
            store.start(g_conv.at[k], g_conv_out.at[0, k])
        else:
            g_mix[...] = value
            store.start(g_mix, g_mix_out.at[0])
    g_out[0] = dot3((hidden_high[...], hidden_low[...]), grad_level, 0, 0)
    for q in range(4):
        for h in range(2):
            g_out[1, q * side : (q + 1) * side, h * 128 : (h + 1) * 128] = quarters[q, h * side : (h + 1) * side, :]
    store.start(g_out, g_out_out)
    place = lax.axis_index("seq")
    low, high = place & 1, (place >> 1) & 1
    for row, x, y in (
        (bias_own[0:1, :], 0, 0), (bias_own[1:2, :], 1, 0), (bias_other[...], 0, 1), (bias_far[...], 1, 1)
    ):
        bias_rows[(low ^ x) * 2 + (high ^ y)] = row
    g_bias[0:1, :] = jnp.sum(grad_mixed, axis=0, keepdims=True)
    g_bias[1:2, :] = jnp.concatenate([bias_rows[q] for q in range(4)], axis=1)
    store.start(g_bias, g_bias_out)
    grad_base = dot2(hot[:, 8:16], grad_level, 0, 0)
    for k in range(4):
        grad_base = grad_base + dot3_few(pieces[k], (first_high[k], first_low[k]))
    g_embed[...] = grad_base[:4, :]
    store.start(g_embed, g_embed_out)
    store.wait(*range(len(store.copies)))


VMEM, SMEM, HBM = pltpu.VMEM, pltpu.SMEM, pltpu.HBM


def call(kernel, ins, outs, scratch=(), aliases=None, micros=0.001):
    run = pl.pallas_call(
        kernel,
        out_shape=[space(shape, kind) for shape, kind, space in outs],
        in_specs=[pl.BlockSpec(memory_space=space) for space in ins],
        out_specs=[pl.BlockSpec(memory_space=space) for _, _, space in outs],
        scratch_shapes=list(scratch),
        input_output_aliases=aliases or {},
        cost_estimate=pl.CostEstimate(flops=int(micros * 1.1e9), bytes_accessed=int(micros * 3e6), transcendentals=0),
        compiler_params=pltpu.CompilerParams(vmem_limit_bytes=VMEM_LIMIT),
    )

    def placed(*args):
        return run(*[pltpu.with_memory_space_constraint(x, HBM) if space is HBM else x for x, space in zip(args, ins)])

    return placed


def swapped(value, mask):
    pairs = [(source, source ^ mask) for source in range(lax.axis_size("seq"))]
    return lax.ppermute(value, "seq", pairs)


def crossed(piece, count, rest):
    mask = 4
    while mask < count // 2:
        piece = piece + swapped(piece, mask)
        mask *= 2
    return rest(piece, swapped(piece, mask))


def on_device(
    tokens, dilations, embed, conv_weight, mix_weight, gate_bias, out_weight, cot_fwd, cot_rev
):
    channels = embed.shape[1]
    wide = 2 * channels
    length = tokens.shape[0]
    count = lax.axis_size("seq")
    sems = pltpu.SemaphoreType.DMA
    square = (channels, channels)

    row = tokens.reshape(1, length)
    near = [swapped(row, mask) for mask in (1, 2, 3)]
    layer_weights = [(conv_weight.shape[1:], F32, VMEM), (mix_weight.shape[1:], F32, VMEM)]
    own, taps, first_conv, first_mix, turn, last_weight, cot_high, cot_low, grad_hidden = call(
        first_tables_kernel,
        [HBM] * 7,
        [(row.shape, row.dtype, VMEM), ((32, wide), F32, VMEM), *layer_weights]
        + [(square, F32, VMEM)] * 2
        + [((2 * length, channels), BF16, VMEM)] * 2
        + [((2 * length, channels), F32, VMEM)],
        [VMEM(embed.shape, F32), VMEM((2, length, channels), F32), sems((10,))],
        micros=2.7,
    )(row, embed, conv_weight, mix_weight, out_weight, cot_fwd, cot_rev)
    known = call(join_four_kernel, [VMEM] * 5, [((4, length), row.dtype, VMEM)])(own, *near, taps)[0]
    parts = [known, swapped(known, 4)]
    deep = -(-TAPS // 128) * 128
    table, local, mixed_table, pre_high, pre_low, second_conv, second_mix = call(
        second_tables_kernel,
        [VMEM] * 4 + [HBM] * 2 + [VMEM],
        [((CONTEXTS, channels), F32, VMEM), ((LOCAL, channels), F32, VMEM), ((CONTEXTS, wide), F32, VMEM)]
        + [((deep, wide), BF16, VMEM)] * 2
        + layer_weights,
        [sems((4,))],
        micros=2.5,
    )(taps, embed, gate_bias, turn, conv_weight, mix_weight, known)
    mask = 8
    while mask < count:
        known = jnp.concatenate([known, parts[-1]], axis=0)
        parts.append(swapped(known, mask))
        mask *= 2

    rows_x, rows_y = TAPS, channels // 2 + LOCAL // 2
    keep_y, send_y, hidden_high, hidden_low, hots, slopes = call(
        lambda *refs: forward_kernel(count, *refs),
        [SMEM] + [VMEM] * (len(parts) + 4),
        [((2, rows_y, 128), F32, VMEM)] * 2
        + [((2 * length, channels), BF16, VMEM)] * 2
        + [((2, deep, length), BF16, VMEM), ((2 * length, wide), F32, VMEM)],
        [VMEM((4, rows_y, 128), F32)],
        micros=2.0,
    )(dilations, *parts, pre_high, pre_low, cot_high, cot_low)
    keep_x, send_x = call(
        taps_kernel,
        [VMEM] * 3,
        [((2, rows_x, 128), F32, VMEM)] * 2,
        [VMEM((4, rows_x, 128), F32)],
        micros=1.5,
    )(hots, slopes, grad_hidden)

    def halved(keep, received, after):
        outs = [(keep.shape[1:], F32, VMEM)] * 2
        return call(halve_after_kernel, [VMEM] * 3, outs)(keep, received, after)

    def added(kept, received, after, space=VMEM):
        return call(add_after_kernel, [VMEM] * 2 + [space], [(kept.shape, F32, VMEM)])(kept, received, after)[0]

    def touched(value, after, cuts=1):
        shape = (value.shape[0] // cuts, value.shape[1])
        return call(touch_kernel, [VMEM] * 2, [(shape, value.dtype, VMEM)] * cuts)(value, after)

    keep_y, send_y = halved(keep_y, swapped(send_y, 1), keep_x)
    keep_x, send_x = halved(keep_x, swapped(send_x, 1), keep_y)
    sum_y = added(keep_y, swapped(send_y, 2), keep_x)
    out_fwd, out_rev = call(
        outputs_kernel,
        [VMEM] * 6,
        [((length, channels), F32, HBM)] * 2,
        [VMEM((2, length, channels), F32), sems((2,))],
        micros=2.0,
    )(hots, hidden_high, hidden_low, local, last_weight, sum_y)
    sum_x = added(keep_x, swapped(send_x, 2), out_rev, HBM)
    first_high, first_low, second_high, second_low, turn_high, turn_low, *tables = call(
        prepare_kernel,
        [VMEM] * 8,
        [((4, wide, channels), BF16, VMEM)] * 4
        + [(square, BF16, VMEM)] * 2
        + [((CONTEXTS, channels), BF16, VMEM)] * 6
        + [((CONTEXTS, wide), F32, VMEM), ((CONTEXTS, 32), BF16, VMEM)],
        micros=1.4,
    )(first_conv, first_mix, second_conv, second_mix, turn, table, mixed_table, sum_x)
    levels, tables = tables[:4], tables[4:]

    def merged(kernel, rows, mine, theirs, after):
        return call(kernel, [VMEM] * 3, [((rows, 128), F32, VMEM)])(mine, theirs, after)[0]

    merged_x, merged_y = 3 * CONTEXTS, rows_y + EDGE // 2
    piece_y = crossed(sum_y, count, lambda x, y: merged(merge_rest_kernel, merged_y, x, y, turn_low))
    piece_x = crossed(sum_x, count, lambda x, y: merged(merge_taps_kernel, merged_x, x, y, piece_y))
    other_y = swapped(piece_y, 2)
    core_x = [swapped(x, 1) for x in touched(piece_x, other_y, 2)]

    core_y, far_y = swapped(piece_y, 1), swapped(other_y, 1)
    shared = (*levels, second_high, second_low)
    large = [(conv_weight.shape, F32, HBM), (mix_weight.shape, F32, HBM)]
    level_out = ((CONTEXTS, channels), F32, VMEM)
    quarter_conv, quarter_mix = (3, channels, 128), (channels, 128)
    g_conv, g_mix, bias_own, partial = call(
        own_columns_kernel,
        [VMEM] * 9,
        [*large, ((2, 128), F32, VMEM), level_out],
        [
            VMEM((2, merged_x, 128), F32),
            VMEM((2, *quarter_conv), F32),
            VMEM((2, *quarter_mix), F32),
            sems((8,)),
        ],
        micros=0.05,
    )(piece_x, *core_x, *shared)
    other_x = swapped(piece_x, 2)
    rest_y = touched(far_y, partial)[0]
    core_y = touched(core_y, rest_y)[0]
    far_x = swapped(touched(other_x, core_y)[0], 1)
    g_conv, g_mix, bias_other, partial = call(
        other_columns_kernel,
        [VMEM] * 8 + [HBM] * 2,
        [*large, ((1, 128), F32, VMEM), level_out],
        [VMEM(quarter_conv, F32), VMEM(quarter_mix, F32), sems((4,))],
        aliases={8: 0, 9: 1},
        micros=0.05,
    )(other_x, *shared, partial, g_conv, g_mix)
    g_conv, g_mix, g_embed, g_bias, g_out = call(
        first_layer_kernel,
        [VMEM] * 23 + [HBM] * 2,
        [*large] + [(shape, F32, HBM) for shape in (embed.shape, gate_bias.shape, out_weight.shape)],
        [
            VMEM((4, merged_y, 128), F32),
            VMEM((4, 1, 128), F32),
            VMEM((1, 128), F32),
            VMEM(quarter_conv, F32),
            VMEM(quarter_mix, F32),
            VMEM(conv_weight.shape[1:], F32),
            VMEM(mix_weight.shape[1:], F32),
            VMEM(embed.shape, F32),
            VMEM(gate_bias.shape, F32),
            VMEM(out_weight.shape, F32),
            sems((11,)),
        ],
        aliases={23: 0, 24: 1},
        micros=2.7,
    )(
        far_x, *shared, piece_y, other_y, core_y, rest_y, partial, bias_own, bias_other, embed,
        first_high, first_low, turn_high, turn_low, *tables, g_conv, g_mix,
    )
    return (out_fwd, out_rev, g_embed, g_conv, g_mix, g_bias, g_out)


def solution(mesh):
    in_specs = (
        P(("dp", "seq")),
        P(),
        P(),
        P(),
        P(),
        P(),
        P(),
        P(("dp", "seq"), None),
        P(("dp", "seq"), None),
    )
    out_specs = (
        P(("dp", "seq"), None),
        P(("dp", "seq"), None),
        P("dp", None),
        P("dp", None, None, None),
        P("dp", None, None),
        P("dp", None),
        P("dp", None, None),
    )
    return jax.shard_map(
        on_device, mesh=mesh, in_specs=in_specs, out_specs=out_specs, check_vma=False
    )
```

```python
import jax
import jax.numpy as jnp
from jax import lax
from jax.experimental import pallas as pl
from jax.experimental.pallas import tpu as pltpu
from jax.sharding import PartitionSpec as P

CONTEXTS = 96
INNER = 64
EDGE = 16
LOCAL = INNER + EDGE
TAPS = 3 * LOCAL
HALO = 128
F32 = jnp.float32
BF16 = jnp.bfloat16
VMEM_LIMIT = 40 * 1024 * 1024


def split(x):
    high = x.astype(BF16)
    return high, (x - high.astype(F32)).astype(BF16)


def dot(a, b, ca=1, cb=0):
    return lax.dot_general(a, b, (((ca,), (cb,)), ((), ())), preferred_element_type=F32)


def dot2(exact, pair, ca=1, cb=0):
    return dot(exact, pair[0], ca, cb) + dot(exact, pair[1], ca, cb)


def dot3(a, b, ca=1, cb=0):
    return dot(a[0], b[0], ca, cb) + (dot(a[0], b[1], ca, cb) + dot(a[1], b[0], ca, cb))


def dot3_few(a, b):
    rows = a[0].shape[0]
    both = dot(jnp.concatenate([a[0].astype(F32), a[1].astype(F32)], axis=0).astype(BF16), b[0])
    return both[:rows] + (both[rows:] + dot(a[0], b[1]))


def letters(index):
    inner = index < 64
    left = (index >= 64) & (index < 80)
    low = index & 3
    mid = (index >> 2) & 3
    l = jnp.where(inner, (index >> 4) & 3, jnp.where(left, -1, mid))
    m = jnp.where(inner | left, mid, low)
    r = jnp.where(inner | left, low, -1)
    return l, m, r


def mirrored(index):
    low = 3 - (index & 3)
    mid = 3 - ((index >> 2) & 3)
    high = 3 - ((index >> 4) & 3)
    inner = low * 16 + mid * 4 + high
    left = 80 + low * 4 + mid
    right = 64 + low * 4 + mid
    return jnp.where(index < 64, inner, jnp.where(index < 80, left, right))


def permutation():
    rows = lax.broadcasted_iota(jnp.int32, (CONTEXTS, CONTEXTS), 0)
    cols = lax.broadcasted_iota(jnp.int32, (CONTEXTS, CONTEXTS), 1)
    return (mirrored(rows) == cols).astype(F32).astype(BF16)


def letter_hot():
    rows = lax.broadcasted_iota(jnp.int32, (CONTEXTS, 32), 0)
    cols = lax.broadcasted_iota(jnp.int32, (CONTEXTS, 32), 1)
    l, m, r = letters(rows)
    kind = cols >> 3
    value = jnp.where(kind == 0, l, jnp.where(kind == 1, m, jnp.where(kind == 2, r, 3 - m)))
    return (value == (cols & 7)).astype(F32).astype(BF16)


def gates(mixed):
    channels = mixed.shape[1] // 2
    tanh_part = jnp.tanh(mixed[:, :channels])
    sig_part = 0.5 + 0.5 * jnp.tanh(0.5 * mixed[:, channels:])
    return tanh_part, sig_part


def gate_grads(grad_hidden, tanh_part, sig_part):
    scaled = grad_hidden * sig_part
    return scaled * (1.0 - tanh_part * tanh_part), scaled * tanh_part * (1.0 - sig_part)


class Fetch:
    def __init__(self, sems):
        self.sems = sems
        self.copies = []

    def start(self, source, target):
        copy = pltpu.make_async_copy(source, target, self.sems.at[len(self.copies)])
        copy.start()
        self.copies.append(copy)
        return len(self.copies) - 1

    def wait(self, *which):
        for at in which:
            self.copies[at].wait()


def padded_base(embed):
    return jnp.concatenate([embed[...], jnp.zeros((4, embed.shape[1]), F32)], axis=0)


def left_side():
    return lax.axis_index("seq") * 2 < lax.axis_size("seq")


def local_rows(rows):
    edge = jnp.where(left_side(), rows[INNER : INNER + EDGE], rows[INNER + EDGE : INNER + 2 * EDGE])
    return jnp.concatenate([rows[:INNER], edge], axis=0)


def join_four_kernel(first, second, third, fourth, after, out):
    for at, part in enumerate((first, second, third, fourth)):
        out[at : at + 1, :] = part[...]


def touch_kernel(value, after, *outs):
    begin = 0
    for out in outs:
        out[...] = value[begin : begin + out.shape[0], :]
        begin += out.shape[0]


def first_tables_kernel(
    tokens_in, embed_in, conv_in, mix_in, out_in, own, taps, conv, mix, turn, embed, sems,
):
    fetch = Fetch(sems)
    fetch.start(embed_in, embed)
    first = [fetch.start(conv_in.at[0, k], conv.at[k]) for k in range(3)]
    first += [fetch.start(mix_in.at[0], mix)]
    rest = [fetch.start(tokens_in, own), fetch.start(out_in.at[0], turn)]
    fetch.wait(0)
    base = split(padded_base(embed))
    for k in range(4):
        fetch.wait(first[k])
        taps[k * 8 : (k + 1) * 8, :] = dot3_few(base, split(conv[k] if k < 3 else mix[...]))
    fetch.wait(*rest)


def second_tables_kernel(
    taps, embed, bias, turn, conv_in, mix_in, out_in, cot_fwd_in, cot_rev_in, after,
    table, local, mixed_table, pre_high, pre_low, conv, mix, last_weight, cot_high, cot_low, grad_hidden, cots, sems,
):
    length = cots.shape[1]
    fetch = Fetch(sems)
    second = [fetch.start(conv_in.at[1, k], conv.at[k]) for k in range(3)]
    second += [fetch.start(mix_in.at[1], mix)]
    last = [fetch.start(out_in.at[1], last_weight)]
    last += [fetch.start(cot_in, cots.at[strand]) for strand, cot_in in enumerate((cot_fwd_in, cot_rev_in))]
    hot = letter_hot()
    mixed = dot2(hot, split(taps[...])) + bias[0:1, :]
    tanh_part, sig_part = gates(mixed)
    own = dot2(hot[:, 8:16], split(padded_base(embed)))
    level = own + dot3_few(split(tanh_part * sig_part), split(turn[...]))
    table[...] = level
    local[...] = local_rows(level)
    mixed_table[...] = mixed
    level = split(level)
    swap = permutation()
    partner = tuple(dot(swap, piece).astype(BF16) for piece in level)
    pre_high[TAPS:, :] = jnp.zeros((pre_high.shape[0] - TAPS, pre_high.shape[1]), BF16)
    pre_low[TAPS:, :] = jnp.zeros((pre_low.shape[0] - TAPS, pre_low.shape[1]), BF16)
    for k in (0, 2, 1):
        fetch.wait(second[k])
        value = dot3_few(level, split(conv[k]))
        if k == 1:
            fetch.wait(second[3])
            value = value + dot3_few(partner, split(mix[...])) + bias[1:2, :]
        high, low = split(local_rows(value))
        pre_high[k * LOCAL : (k + 1) * LOCAL, :] = high
        pre_low[k * LOCAL : (k + 1) * LOCAL, :] = low
    fetch.wait(last[0])
    weight = split(last_weight[...])
    for strand in range(2):
        rows = slice(strand * length, (strand + 1) * length)
        fetch.wait(last[1 + strand])
        cot = split(cots[strand])
        cot_high[rows, :], cot_low[rows, :] = cot
        grad_hidden[rows, :] = dot3(cot, weight, 1, 1)


def windows(parts, count):
    length = parts[0].shape[1]
    place = lax.axis_index("seq")
    last = count - 1

    def block(at):
        total, begin = None, 0
        for part in parts:
            rows = lax.broadcasted_iota(jnp.int32, part.shape, 0) + begin
            piece = jnp.sum(jnp.where(rows == (place ^ at), part[...], 0), axis=0, keepdims=True)
            total = piece if total is None else total + piece
            begin += part.shape[0]
        return total

    def window(at):
        before = jnp.where(at == 0, -1, block(jnp.maximum(at - 1, 0))[:, length - HALO :])
        after = jnp.where(at == last, -1, block(jnp.minimum(at + 1, last))[:, :HALO])
        return [before, block(at), after]

    fwd = jnp.concatenate(window(place), axis=1)
    rev = jnp.concatenate(window(last - place), axis=1)
    rev = jnp.where(rev < 0, -1, 3 - rev)
    tiles = rev.shape[1] // 128
    blocks = [rev[:, i * 128 : (i + 1) * 128] for i in reversed(range(tiles))]
    blocks += [jnp.zeros((8 - tiles, 128), jnp.int32)]
    stacked = jnp.concatenate(blocks, axis=0).astype(F32).astype(BF16)
    rows = lax.broadcasted_iota(jnp.int32, (128, 128), 0)
    cols = lax.broadcasted_iota(jnp.int32, (128, 128), 1)
    flip = (rows + cols == 127).astype(F32).astype(BF16)
    turned = dot(stacked, flip).astype(jnp.int32)
    rev = jnp.concatenate([turned[i : i + 1, :] for i in range(tiles)], axis=1)
    return fwd, rev


def local_contexts(window, first, second, length):
    width = window.shape[1]
    base = jnp.broadcast_to(window, (8, width))
    l = pltpu.roll(base, first, 1)
    r = pltpu.roll(base, width - first, 1)
    index = jnp.where(l < 0, INNER + base * 4 + r, jnp.where(r < 0, INNER + l * 4 + base, l * 16 + base * 4 + r))
    index = jnp.where(base < 0, LOCAL, index)
    before = pltpu.roll(index, second, 1)
    after = pltpu.roll(index, width - second, 1)
    return [x[0:1, HALO : HALO + length] for x in (before, index, after)]


def hot_rows(index):
    rows = lax.broadcasted_iota(jnp.int32, (LOCAL, index.shape[1]), 0)
    return (rows == index).astype(F32).astype(BF16)


def deal(quarters, keep, send):
    bit = lax.axis_index("seq") & 1
    keep[...] = quarters[pl.ds(bit * 2, 2)]
    send[...] = quarters[pl.ds((1 - bit) * 2, 2)]


def forward_kernel(count, dil, *refs):
    steps = count.bit_length() - 2
    parts, refs = refs[:steps], refs[steps:]
    (pre_high, pre_low, cot_high, cot_low, keep, send, hidden_high, hidden_low, hots, slopes, quarters) = refs
    length = parts[0].shape[1]
    channels = cot_high.shape[1]
    pre = (pre_high[...], pre_low[...])
    both = windows(parts, count)
    pad = jnp.zeros((pre_high.shape[0] - TAPS, length), BF16)
    total_o = total_c = None
    for strand in range(2):
        index = local_contexts(both[strand], dil[0], dil[1], length)
        hot = jnp.concatenate([hot_rows(x) for x in index] + [pad], axis=0)
        hots[strand] = hot
        mixed = dot2(hot, pre, 0, 0)
        tanh_part, sig_part = gates(mixed)
        product = tanh_part * sig_part
        hidden = split(product)
        rows = slice(strand * length, (strand + 1) * length)
        hidden_high[rows, :] = hidden[0]
        hidden_low[rows, :] = hidden[1]
        slopes[rows, :channels] = sig_part - product * tanh_part
        slopes[rows, channels:] = product - product * sig_part
        cot = (cot_high[rows, :], cot_low[rows, :])
        part_o = dot3(hidden, cot, 0, 0)
        part_c = dot2(hot[LOCAL : 2 * LOCAL], cot)
        total_o = part_o if total_o is None else total_o + part_o
        total_c = part_c if total_c is None else total_c + part_c
    side = channels // 4
    for q in range(4):
        lanes = slice((q >> 1) * 128, (q >> 1) * 128 + 128)
        quarters[q, :side, :] = total_o[q * side : (q + 1) * side, :128]
        quarters[q, side : 2 * side, :] = total_o[q * side : (q + 1) * side, 128:]
        for begin, rows, at in ((0, INNER // 2, 2 * side), (INNER, EDGE // 2, 2 * side + INNER // 2)):
            begin += (q & 1) * rows
            quarters[q, at : at + rows, :] = total_c[begin : begin + rows, lanes]
    deal(quarters, keep, send)


def taps_kernel(hots, slopes, grad_hidden, keep, send, quarters):
    length = hots.shape[2]
    total = None
    for strand in range(2):
        rows = slice(strand * length, (strand + 1) * length)
        grad = grad_hidden[rows, :]
        part = dot2(hots[strand], split(slopes[rows, :] * jnp.concatenate([grad, grad], axis=1)))
        total = part if total is None else total + part
    for q in range(4):
        quarters[q] = total[:TAPS, q * 128 : (q + 1) * 128]
    deal(quarters, keep, send)


def halve_kernel(kept, received, keep, send):
    bit = (lax.axis_index("seq") >> 1) & 1
    send[...] = kept[1 - bit] + received[1 - bit]
    keep[...] = kept[bit] + received[bit]


def add_after_kernel(kept, received, after, out):
    out[...] = kept[...] + received[...]


def halve_after_kernel(kept, received, after, keep, send):
    halve_kernel(kept, received, keep, send)


def outputs_kernel(hots, hidden_high, hidden_low, local, out_w, after, out_fwd, out_rev, values, sems):
    length = hots.shape[2]
    fetch = Fetch(sems)
    weight = split(out_w[...])
    level = split(local[...])
    for strand, out in enumerate((out_fwd, out_rev)):
        rows = slice(strand * length, (strand + 1) * length)
        own = dot2(hots[strand, LOCAL : 2 * LOCAL, :], level, 0, 0)
        values[strand] = own + dot3((hidden_high[rows, :], hidden_low[rows, :]), weight)
        fetch.start(values.at[strand], out)
    fetch.wait(0, 1)


def prepare_kernel(
    first_conv, first_mix, second_conv, second_mix, out_w, table, mixed_table, after,
    first_high, first_low, second_high, second_low, turn_high, turn_low,
    level_high, level_low, partner_high, partner_low, hidden_high, hidden_low, slopes, hot,
):
    level = split(table[...])
    swap = permutation()
    level_high[...], level_low[...] = level
    partner_high[...], partner_low[...] = tuple(dot(swap, piece).astype(BF16) for piece in level)
    for conv, mix, high, low in (
        (second_conv, second_mix, second_high, second_low),
        (first_conv, first_mix, first_high, first_low),
    ):
        for k in range(4):
            high[k], low[k] = split((conv[k] if k < 3 else mix[...]).T)
    turn_high[...], turn_low[...] = split(out_w[...].T)
    tanh_part, sig_part = gates(mixed_table[...])
    product = tanh_part * sig_part
    hidden_high[...], hidden_low[...] = split(product)
    channels = product.shape[1]
    slopes[:, :channels] = sig_part - product * tanh_part
    slopes[:, channels:] = product - product * sig_part
    hot[...] = letter_hot()


def merge(mine, theirs, inner, edge):
    left = left_side()
    both = mine[inner, :] + theirs[inner, :]
    own, other = mine[edge, :], theirs[edge, :]
    return both, jnp.where(left, own, other), jnp.where(left, other, own)


def merge_blocks(mine, theirs, out, sizes):
    at = to = 0
    for inner, edge in sizes:
        pieces = merge(mine, theirs, slice(at, at + inner), slice(at + inner, at + inner + edge))
        out[to : to + inner, :] = pieces[0]
        out[to + inner : to + inner + edge, :] = pieces[1]
        out[to + inner + edge : to + inner + 2 * edge, :] = pieces[2]
        at, to = at + inner + edge, to + inner + 2 * edge


def merge_taps_kernel(mine, theirs, after, out):
    merge_blocks(mine, theirs, out, [(INNER, EDGE)] * 3)


def merge_rest_kernel(mine, theirs, after, out):
    merge_blocks(mine, theirs, out, [(mine.shape[0] - EDGE // 2, EDGE // 2)])


def gather_quarters(pieces, quarters):
    place = lax.axis_index("seq")
    low, high = place & 1, (place >> 1) & 1
    for parts, x, y in zip(pieces, (0, 0, 1, 1), (0, 1, 0, 1)):
        begin = 0
        for part in parts:
            rows = part.shape[0]
            quarters[(low ^ x) * 2 + (high ^ y), begin : begin + rows, :] = part[...]
            begin += rows


def tap_pairs(taps):
    return [split(taps[k * CONTEXTS : (k + 1) * CONTEXTS, :]) for k in range(3)]


def quarter_weights(pairs, taps, levels, g_conv, g_mix, bias):
    level_high, level_low, partner_high, partner_low = levels
    level = (level_high[...], level_low[...])
    partner = (partner_high[...], partner_low[...])
    for k, pair in enumerate(pairs):
        g_conv[k] = dot3(level, pair, 0, 0)
    g_mix[...] = dot3(partner, pairs[1], 0, 0)
    bias[...] = jnp.sum(taps[CONTEXTS : 2 * CONTEXTS, :], axis=0, keepdims=True)


def quarter_part(pairs, column, seconds):
    weights = [tuple(ref[k, pl.ds(column, 128), :] for ref in seconds) for k in range(4)]
    part = dot2(permutation(), split(dot3_few(pairs[1], weights[3])))
    for k, pair in enumerate(pairs):
        part = part + dot3_few(pair, weights[k])
    return part


def column_of(core, chip):
    place = lax.axis_index("seq")
    low, high = place & 1, (place >> 1) & 1
    return pl.multiple_of(((low ^ core) * 2 + (high ^ chip)) * 128, 128)


def store_columns(store, column, g_conv, g_mix, g_conv_out, g_mix_out):
    block = pl.ds(column, 128)
    for k in range(3):
        store.start(g_conv.at[k], g_conv_out.at[1, k, :, block])
    store.start(g_mix, g_mix_out.at[1, :, block])


def own_columns_kernel(own_piece, core_first, core_second, *refs):
    levels, seconds, refs = refs[:4], refs[4:6], refs[6:]
    g_conv_out, g_mix_out, bias, total, taps, g_conv, g_mix, out_sems = refs
    store = Fetch(out_sems)
    half = core_first.shape[0]
    taps[0] = own_piece[...]
    taps[1, :half, :] = core_first[...]
    taps[1, half:, :] = core_second[...]
    grad_level = None
    for core in range(2):
        column = column_of(core, 0)
        pairs = tap_pairs(taps.at[core])
        quarter_weights(pairs, taps.at[core], levels, g_conv.at[core], g_mix.at[core], bias.at[core : core + 1])
        store_columns(store, column, g_conv.at[core], g_mix.at[core], g_conv_out, g_mix_out)
        part = quarter_part(pairs, column, seconds)
        grad_level = part if grad_level is None else grad_level + part
    total[...] = grad_level
    store.wait(*range(len(store.copies)))


def other_columns_kernel(piece, *refs):
    levels, seconds, refs = refs[:4], refs[4:6], refs[6:]
    partial, g_conv_in, g_mix_in, g_conv_out, g_mix_out, bias, total, g_conv, g_mix, out_sems = refs
    store = Fetch(out_sems)
    column = column_of(0, 1)
    pairs = tap_pairs(piece)
    quarter_weights(pairs, piece, levels, g_conv, g_mix, bias)
    store_columns(store, column, g_conv, g_mix, g_conv_out, g_mix_out)
    total[...] = partial[...] + quarter_part(pairs, column, seconds)
    store.wait(*range(len(store.copies)))


def first_layer_kernel(
    far_piece, level_high, level_low, partner_high, partner_low, second_high, second_low,
    piece_00, piece_01, piece_10, piece_11, partial, bias_own, bias_other, embed,
    first_high, first_low, turn_high, turn_low, hidden_high, hidden_low, slopes, hot_in,
    g_conv_in, g_mix_in, g_conv_out, g_mix_out, g_embed_out, g_bias_out, g_out_out,
    quarters, bias_rows, bias_far, far_conv, far_mix, g_conv, g_mix, g_embed, g_bias, g_out, out_sems,
):
    channels = embed.shape[1]
    store = Fetch(out_sems)
    column = column_of(1, 1)
    pairs = tap_pairs(far_piece)
    far_part = quarter_part(pairs, column, (second_high, second_low))
    gather_quarters([(piece,) for piece in (piece_00, piece_01, piece_10, piece_11)], quarters)
    side = channels // 4
    rest = []
    for begin, rows in ((0, INNER // 2), (INNER // 2, EDGE // 2), (INNER // 2 + EDGE // 2, EDGE // 2)):
        begin += 2 * side
        halves = [[quarters[2 * h + i, begin : begin + rows, :] for i in range(2)] for h in range(2)]
        rest.append(jnp.concatenate([jnp.concatenate(x, axis=0) for x in halves], axis=1))
    grad_level = split(partial[...] + far_part + jnp.concatenate(rest, axis=0))
    grad_hidden = dot3_few(grad_level, (turn_high[...], turn_low[...]))
    grad_mixed = slopes[...] * jnp.concatenate([grad_hidden, grad_hidden], axis=1)
    levels = (level_high, level_low, partner_high, partner_low)
    quarter_weights(pairs, far_piece, levels, far_conv, far_mix, bias_far)
    store_columns(store, column, far_conv, far_mix, g_conv_out, g_mix_out)
    hot = hot_in[...]
    by_letter = dot2(hot, split(grad_mixed), 0, 0)
    base = split(padded_base(embed))
    stacked = jnp.concatenate([base[0].astype(F32), base[0].astype(F32), base[1].astype(F32)], axis=0).astype(BF16)
    pieces = []
    for k in range(4):
        piece = split(by_letter[k * 8 : (k + 1) * 8, :])
        pieces.append(piece)
        high, low = piece[0].astype(F32), piece[1].astype(F32)
        value = dot(stacked, jnp.concatenate([high, low, high], axis=0).astype(BF16), 0, 0)
        if k < 3:
            g_conv[k] = value
            store.start(g_conv.at[k], g_conv_out.at[0, k])
        else:
            g_mix[...] = value
            store.start(g_mix, g_mix_out.at[0])
    g_out[0] = dot3((hidden_high[...], hidden_low[...]), grad_level, 0, 0)
    for q in range(4):
        for h in range(2):
            g_out[1, q * side : (q + 1) * side, h * 128 : (h + 1) * 128] = quarters[q, h * side : (h + 1) * side, :]
    store.start(g_out, g_out_out)
    place = lax.axis_index("seq")
    low, high = place & 1, (place >> 1) & 1
    for row, x, y in (
        (bias_own[0:1, :], 0, 0), (bias_own[1:2, :], 1, 0), (bias_other[...], 0, 1), (bias_far[...], 1, 1)
    ):
        bias_rows[(low ^ x) * 2 + (high ^ y)] = row
    g_bias[0:1, :] = jnp.sum(grad_mixed, axis=0, keepdims=True)
    g_bias[1:2, :] = jnp.concatenate([bias_rows[q] for q in range(4)], axis=1)
    store.start(g_bias, g_bias_out)
    grad_base = dot2(hot[:, 8:16], grad_level, 0, 0)
    for k in range(4):
        grad_base = grad_base + dot3_few(pieces[k], (first_high[k], first_low[k]))
    g_embed[...] = grad_base[:4, :]
    store.start(g_embed, g_embed_out)
    store.wait(*range(len(store.copies)))


VMEM, SMEM, HBM = pltpu.VMEM, pltpu.SMEM, pltpu.HBM


def call(kernel, ins, outs, scratch=(), aliases=None, micros=0.001):
    run = pl.pallas_call(
        kernel,
        out_shape=[space(shape, kind) for shape, kind, space in outs],
        in_specs=[pl.BlockSpec(memory_space=space) for space in ins],
        out_specs=[pl.BlockSpec(memory_space=space) for _, _, space in outs],
        scratch_shapes=list(scratch),
        input_output_aliases=aliases or {},
        cost_estimate=pl.CostEstimate(flops=int(micros * 1.1e9), bytes_accessed=int(micros * 3e6), transcendentals=0),
        compiler_params=pltpu.CompilerParams(vmem_limit_bytes=VMEM_LIMIT),
    )

    def placed(*args):
        return run(*[pltpu.with_memory_space_constraint(x, HBM) if space is HBM else x for x, space in zip(args, ins)])

    return placed


def swapped(value, mask):
    pairs = [(source, source ^ mask) for source in range(lax.axis_size("seq"))]
    return lax.ppermute(value, "seq", pairs)


def crossed(piece, count, rest):
    mask = 4
    while mask < count // 2:
        piece = piece + swapped(piece, mask)
        mask *= 2
    return rest(piece, swapped(piece, mask))


def on_device(
    tokens, dilations, embed, conv_weight, mix_weight, gate_bias, out_weight, cot_fwd, cot_rev
):
    channels = embed.shape[1]
    wide = 2 * channels
    length = tokens.shape[0]
    count = lax.axis_size("seq")
    sems = pltpu.SemaphoreType.DMA
    square = (channels, channels)

    row = tokens.reshape(1, length)
    near = [swapped(row, mask) for mask in (1, 2, 3)]
    layer_weights = [(conv_weight.shape[1:], F32, VMEM), (mix_weight.shape[1:], F32, VMEM)]
    own, taps, first_conv, first_mix, turn = call(
        first_tables_kernel,
        [HBM] * 5,
        [(row.shape, row.dtype, VMEM), ((32, wide), F32, VMEM), *layer_weights, (square, F32, VMEM)],
        [VMEM(embed.shape, F32), sems((7,))],
        micros=1.7,
    )(row, embed, conv_weight, mix_weight, out_weight)
    known = call(join_four_kernel, [VMEM] * 5, [((4, length), row.dtype, VMEM)])(own, *near, taps)[0]
    parts = [known, swapped(known, 4)]
    deep = -(-TAPS // 128) * 128
    (table, local, mixed_table, pre_high, pre_low, second_conv, second_mix, last_weight,
     cot_high, cot_low, grad_hidden) = call(
        second_tables_kernel,
        [VMEM] * 4 + [HBM] * 5 + [VMEM],
        [((CONTEXTS, channels), F32, VMEM), ((LOCAL, channels), F32, VMEM), ((CONTEXTS, wide), F32, VMEM)]
        + [((deep, wide), BF16, VMEM)] * 2
        + layer_weights
        + [(square, F32, VMEM)]
        + [((2 * length, channels), BF16, VMEM)] * 2
        + [((2 * length, channels), F32, VMEM)],
        [VMEM((2, length, channels), F32), sems((7,))],
        micros=3.2,
    )(taps, embed, gate_bias, turn, conv_weight, mix_weight, out_weight, cot_fwd, cot_rev, known)
    mask = 8
    while mask < count:
        known = jnp.concatenate([known, parts[-1]], axis=0)
        parts.append(swapped(known, mask))
        mask *= 2

    rows_x, rows_y = TAPS, channels // 2 + LOCAL // 2
    keep_y, send_y, hidden_high, hidden_low, hots, slopes = call(
        lambda *refs: forward_kernel(count, *refs),
        [SMEM] + [VMEM] * (len(parts) + 4),
        [((2, rows_y, 128), F32, VMEM)] * 2
        + [((2 * length, channels), BF16, VMEM)] * 2
        + [((2, deep, length), BF16, VMEM), ((2 * length, wide), F32, VMEM)],
        [VMEM((4, rows_y, 128), F32)],
        micros=2.0,
    )(dilations, *parts, pre_high, pre_low, cot_high, cot_low)
    keep_x, send_x = call(
        taps_kernel,
        [VMEM] * 3,
        [((2, rows_x, 128), F32, VMEM)] * 2,
        [VMEM((4, rows_x, 128), F32)],
        micros=1.5,
    )(hots, slopes, grad_hidden)

    def halved(keep, received, after):
        outs = [(keep.shape[1:], F32, VMEM)] * 2
        return call(halve_after_kernel, [VMEM] * 3, outs)(keep, received, after)

    def added(kept, received, after, space=VMEM):
        return call(add_after_kernel, [VMEM] * 2 + [space], [(kept.shape, F32, VMEM)])(kept, received, after)[0]

    def touched(value, after, cuts=1):
        shape = (value.shape[0] // cuts, value.shape[1])
        return call(touch_kernel, [VMEM] * 2, [(shape, value.dtype, VMEM)] * cuts)(value, after)

    keep_y, send_y = halved(keep_y, swapped(send_y, 1), keep_x)
    keep_x, send_x = halved(keep_x, swapped(send_x, 1), keep_y)
    sum_y = added(keep_y, swapped(send_y, 2), keep_x)
    out_fwd, out_rev = call(
        outputs_kernel,
        [VMEM] * 6,
        [((length, channels), F32, HBM)] * 2,
        [VMEM((2, length, channels), F32), sems((2,))],
        micros=2.0,
    )(hots, hidden_high, hidden_low, local, last_weight, sum_y)
    sum_x = added(keep_x, swapped(send_x, 2), out_rev, HBM)
    first_high, first_low, second_high, second_low, turn_high, turn_low, *tables = call(
        prepare_kernel,
        [VMEM] * 8,
        [((4, wide, channels), BF16, VMEM)] * 4
        + [(square, BF16, VMEM)] * 2
        + [((CONTEXTS, channels), BF16, VMEM)] * 6
        + [((CONTEXTS, wide), F32, VMEM), ((CONTEXTS, 32), BF16, VMEM)],
        micros=1.4,
    )(first_conv, first_mix, second_conv, second_mix, turn, table, mixed_table, sum_x)
    levels, tables = tables[:4], tables[4:]

    def merged(kernel, rows, mine, theirs, after):
        return call(kernel, [VMEM] * 3, [((rows, 128), F32, VMEM)])(mine, theirs, after)[0]

    merged_x, merged_y = 3 * CONTEXTS, rows_y + EDGE // 2
    piece_y = crossed(sum_y, count, lambda x, y: merged(merge_rest_kernel, merged_y, x, y, turn_low))
    piece_x = crossed(sum_x, count, lambda x, y: merged(merge_taps_kernel, merged_x, x, y, piece_y))
    other_y = swapped(piece_y, 2)
    core_x = [swapped(x, 1) for x in touched(piece_x, other_y, 2)]

    core_y, far_y = swapped(piece_y, 1), swapped(other_y, 1)
    shared = (*levels, second_high, second_low)
    large = [(conv_weight.shape, F32, HBM), (mix_weight.shape, F32, HBM)]
    level_out = ((CONTEXTS, channels), F32, VMEM)
    quarter_conv, quarter_mix = (3, channels, 128), (channels, 128)
    g_conv, g_mix, bias_own, partial = call(
        own_columns_kernel,
        [VMEM] * 9,
        [*large, ((2, 128), F32, VMEM), level_out],
        [
            VMEM((2, merged_x, 128), F32),
            VMEM((2, *quarter_conv), F32),
            VMEM((2, *quarter_mix), F32),
            sems((8,)),
        ],
        micros=0.05,
    )(piece_x, *core_x, *shared)
    other_x = swapped(piece_x, 2)
    rest_y = touched(far_y, partial)[0]
    core_y = touched(core_y, rest_y)[0]
    far_x = swapped(touched(other_x, core_y)[0], 1)
    g_conv, g_mix, bias_other, partial = call(
        other_columns_kernel,
        [VMEM] * 8 + [HBM] * 2,
        [*large, ((1, 128), F32, VMEM), level_out],
        [VMEM(quarter_conv, F32), VMEM(quarter_mix, F32), sems((4,))],
        aliases={8: 0, 9: 1},
        micros=0.05,
    )(other_x, *shared, partial, g_conv, g_mix)
    g_conv, g_mix, g_embed, g_bias, g_out = call(
        first_layer_kernel,
        [VMEM] * 23 + [HBM] * 2,
        [*large] + [(shape, F32, HBM) for shape in (embed.shape, gate_bias.shape, out_weight.shape)],
        [
            VMEM((4, merged_y, 128), F32),
            VMEM((4, 1, 128), F32),
            VMEM((1, 128), F32),
            VMEM(quarter_conv, F32),
            VMEM(quarter_mix, F32),
            VMEM(conv_weight.shape[1:], F32),
            VMEM(mix_weight.shape[1:], F32),
            VMEM(embed.shape, F32),
            VMEM(gate_bias.shape, F32),
            VMEM(out_weight.shape, F32),
            sems((11,)),
        ],
        aliases={23: 0, 24: 1},
        micros=2.7,
    )(
        far_x, *shared, piece_y, other_y, core_y, rest_y, partial, bias_own, bias_other, embed,
        first_high, first_low, turn_high, turn_low, *tables, g_conv, g_mix,
    )
    return (out_fwd, out_rev, g_embed, g_conv, g_mix, g_bias, g_out)


def solution(mesh):
    in_specs = (
        P(("dp", "seq")),
        P(),
        P(),
        P(),
        P(),
        P(),
        P(),
        P(("dp", "seq"), None),
        P(("dp", "seq"), None),
    )
    out_specs = (
        P(("dp", "seq"), None),
        P(("dp", "seq"), None),
        P("dp", None),
        P("dp", None, None, None),
        P("dp", None, None),
        P("dp", None),
        P("dp", None, None),
    )
    return jax.shard_map(
        on_device, mesh=mesh, in_specs=in_specs, out_specs=out_specs, check_vma=False
    )
```

```python
import jax
import jax.numpy as jnp
from jax import lax
from jax.experimental import pallas as pl
from jax.experimental.pallas import tpu as pltpu
from jax.sharding import PartitionSpec as P

CONTEXTS = 96
INNER = 64
EDGE = 16
LOCAL = INNER + EDGE
TAPS = 3 * LOCAL
HALO = 128
F32 = jnp.float32
BF16 = jnp.bfloat16
VMEM_LIMIT = 40 * 1024 * 1024


def split(x):
    high = x.astype(BF16)
    return high, (x - high.astype(F32)).astype(BF16)


def dot(a, b, ca=1, cb=0):
    return lax.dot_general(a, b, (((ca,), (cb,)), ((), ())), preferred_element_type=F32)


def dot2(exact, pair, ca=1, cb=0):
    return dot(exact, pair[0], ca, cb) + dot(exact, pair[1], ca, cb)


def dot3(a, b, ca=1, cb=0):
    return dot(a[0], b[0], ca, cb) + (dot(a[0], b[1], ca, cb) + dot(a[1], b[0], ca, cb))


def dot3_few(a, b):
    rows = a[0].shape[0]
    both = dot(jnp.concatenate([a[0].astype(F32), a[1].astype(F32)], axis=0).astype(BF16), b[0])
    return both[:rows] + (both[rows:] + dot(a[0], b[1]))


def letters(index):
    inner = index < 64
    left = (index >= 64) & (index < 80)
    low = index & 3
    mid = (index >> 2) & 3
    l = jnp.where(inner, (index >> 4) & 3, jnp.where(left, -1, mid))
    m = jnp.where(inner | left, mid, low)
    r = jnp.where(inner | left, low, -1)
    return l, m, r


def mirrored(index):
    low = 3 - (index & 3)
    mid = 3 - ((index >> 2) & 3)
    high = 3 - ((index >> 4) & 3)
    inner = low * 16 + mid * 4 + high
    left = 80 + low * 4 + mid
    right = 64 + low * 4 + mid
    return jnp.where(index < 64, inner, jnp.where(index < 80, left, right))


def permutation():
    rows = lax.broadcasted_iota(jnp.int32, (CONTEXTS, CONTEXTS), 0)
    cols = lax.broadcasted_iota(jnp.int32, (CONTEXTS, CONTEXTS), 1)
    return (mirrored(rows) == cols).astype(F32).astype(BF16)


def letter_hot():
    rows = lax.broadcasted_iota(jnp.int32, (CONTEXTS, 32), 0)
    cols = lax.broadcasted_iota(jnp.int32, (CONTEXTS, 32), 1)
    l, m, r = letters(rows)
    kind = cols >> 3
    value = jnp.where(kind == 0, l, jnp.where(kind == 1, m, jnp.where(kind == 2, r, 3 - m)))
    return (value == (cols & 7)).astype(F32).astype(BF16)


def gates(mixed):
    channels = mixed.shape[1] // 2
    tanh_part = jnp.tanh(mixed[:, :channels])
    sig_part = 0.5 + 0.5 * jnp.tanh(0.5 * mixed[:, channels:])
    return tanh_part, sig_part


def gate_grads(grad_hidden, tanh_part, sig_part):
    scaled = grad_hidden * sig_part
    return scaled * (1.0 - tanh_part * tanh_part), scaled * tanh_part * (1.0 - sig_part)


class Fetch:
    def __init__(self, sems):
        self.sems = sems
        self.copies = []

    def start(self, source, target):
        copy = pltpu.make_async_copy(source, target, self.sems.at[len(self.copies)])
        copy.start()
        self.copies.append(copy)
        return len(self.copies) - 1

    def wait(self, *which):
        for at in which:
            self.copies[at].wait()


def padded_base(embed):
    return jnp.concatenate([embed[...], jnp.zeros((4, embed.shape[1]), F32)], axis=0)


def left_side():
    return lax.axis_index("seq") * 2 < lax.axis_size("seq")


def local_rows(rows):
    edge = jnp.where(left_side(), rows[INNER : INNER + EDGE], rows[INNER + EDGE : INNER + 2 * EDGE])
    return jnp.concatenate([rows[:INNER], edge], axis=0)


def join_four_kernel(first, second, third, fourth, after, out):
    for at, part in enumerate((first, second, third, fourth)):
        out[at : at + 1, :] = part[...]


def touch_kernel(value, after, *outs):
    begin = 0
    for out in outs:
        out[...] = value[begin : begin + out.shape[0], :]
        begin += out.shape[0]


def first_tables_kernel(
    tokens_in, embed_in, conv_in, mix_in, out_in, cot_fwd_in, cot_rev_in,
    own, taps, conv, mix, turn, last_weight, cot_high, cot_low, grad_hidden, embed, cots, sems,
):
    length = cots.shape[1]
    fetch = Fetch(sems)
    fetch.start(embed_in, embed)
    first = [fetch.start(conv_in.at[0, k], conv.at[k]) for k in range(3)]
    first += [fetch.start(mix_in.at[0], mix)]
    last = [fetch.start(out_in.at[1], last_weight)]
    last += [fetch.start(cot_in, cots.at[strand]) for strand, cot_in in enumerate((cot_fwd_in, cot_rev_in))]
    rest = [fetch.start(tokens_in, own), fetch.start(out_in.at[0], turn)]
    fetch.wait(0)
    base = split(padded_base(embed))
    for k in range(4):
        fetch.wait(first[k])
        taps[k * 8 : (k + 1) * 8, :] = dot3_few(base, split(conv[k] if k < 3 else mix[...]))
    fetch.wait(last[0])
    weight = split(last_weight[...])
    for strand in range(2):
        rows = slice(strand * length, (strand + 1) * length)
        fetch.wait(last[1 + strand])
        cot = split(cots[strand])
        cot_high[rows, :], cot_low[rows, :] = cot
        grad_hidden[rows, :] = dot3(cot, weight, 1, 1)
    fetch.wait(*rest)


def second_tables_kernel(
    taps, embed, bias, turn, conv_in, mix_in, after, table, local, mixed_table, pre_high, pre_low, conv, mix, sems,
):
    fetch = Fetch(sems)
    second = [fetch.start(conv_in.at[1, k], conv.at[k]) for k in range(3)]
    second += [fetch.start(mix_in.at[1], mix)]
    hot = letter_hot()
    mixed = dot2(hot, split(taps[...])) + bias[0:1, :]
    tanh_part, sig_part = gates(mixed)
    own = dot2(hot[:, 8:16], split(padded_base(embed)))
    level = own + dot3_few(split(tanh_part * sig_part), split(turn[...]))
    table[...] = level
    local[...] = local_rows(level)
    mixed_table[...] = mixed
    level = split(level)
    swap = permutation()
    partner = tuple(dot(swap, piece).astype(BF16) for piece in level)
    pre_high[TAPS:, :] = jnp.zeros((pre_high.shape[0] - TAPS, pre_high.shape[1]), BF16)
    pre_low[TAPS:, :] = jnp.zeros((pre_low.shape[0] - TAPS, pre_low.shape[1]), BF16)
    for k in (0, 2, 1):
        fetch.wait(second[k])
        value = dot3_few(level, split(conv[k]))
        if k == 1:
            fetch.wait(second[3])
            value = value + dot3_few(partner, split(mix[...])) + bias[1:2, :]
        high, low = split(local_rows(value))
        pre_high[k * LOCAL : (k + 1) * LOCAL, :] = high
        pre_low[k * LOCAL : (k + 1) * LOCAL, :] = low


def windows(parts, count):
    length = parts[0].shape[1]
    place = lax.axis_index("seq")
    last = count - 1

    def block(at):
        total, begin = None, 0
        for part in parts:
            rows = lax.broadcasted_iota(jnp.int32, part.shape, 0) + begin
            piece = jnp.sum(jnp.where(rows == (place ^ at), part[...], 0), axis=0, keepdims=True)
            total = piece if total is None else total + piece
            begin += part.shape[0]
        return total

    def window(at):
        before = jnp.where(at == 0, -1, block(jnp.maximum(at - 1, 0))[:, length - HALO :])
        after = jnp.where(at == last, -1, block(jnp.minimum(at + 1, last))[:, :HALO])
        return [before, block(at), after]

    fwd = jnp.concatenate(window(place), axis=1)
    rev = jnp.concatenate(window(last - place), axis=1)
    rev = jnp.where(rev < 0, -1, 3 - rev)
    tiles = rev.shape[1] // 128
    blocks = [rev[:, i * 128 : (i + 1) * 128] for i in reversed(range(tiles))]
    blocks += [jnp.zeros((8 - tiles, 128), jnp.int32)]
    stacked = jnp.concatenate(blocks, axis=0).astype(F32).astype(BF16)
    rows = lax.broadcasted_iota(jnp.int32, (128, 128), 0)
    cols = lax.broadcasted_iota(jnp.int32, (128, 128), 1)
    flip = (rows + cols == 127).astype(F32).astype(BF16)
    turned = dot(stacked, flip).astype(jnp.int32)
    rev = jnp.concatenate([turned[i : i + 1, :] for i in range(tiles)], axis=1)
    return fwd, rev


def local_contexts(window, first, second, length):
    width = window.shape[1]
    base = jnp.broadcast_to(window, (8, width))
    l = pltpu.roll(base, first, 1)
    r = pltpu.roll(base, width - first, 1)
    index = jnp.where(l < 0, INNER + base * 4 + r, jnp.where(r < 0, INNER + l * 4 + base, l * 16 + base * 4 + r))
    index = jnp.where(base < 0, LOCAL, index)
    before = pltpu.roll(index, second, 1)
    after = pltpu.roll(index, width - second, 1)
    return [x[0:1, HALO : HALO + length] for x in (before, index, after)]


def hot_rows(index):
    rows = lax.broadcasted_iota(jnp.int32, (LOCAL, index.shape[1]), 0)
    return (rows == index).astype(F32).astype(BF16)


def deal(quarters, keep, send):
    bit = lax.axis_index("seq") & 1
    keep[...] = quarters[pl.ds(bit * 2, 2)]
    send[...] = quarters[pl.ds((1 - bit) * 2, 2)]


def forward_kernel(count, dil, *refs):
    steps = count.bit_length() - 2
    parts, refs = refs[:steps], refs[steps:]
    (pre_high, pre_low, cot_high, cot_low, keep, send, hidden_high, hidden_low, hots, slopes, quarters) = refs
    length = parts[0].shape[1]
    channels = cot_high.shape[1]
    pre = (pre_high[...], pre_low[...])
    both = windows(parts, count)
    pad = jnp.zeros((pre_high.shape[0] - TAPS, length), BF16)
    total_o = total_c = None
    for strand in range(2):
        index = local_contexts(both[strand], dil[0], dil[1], length)
        hot = jnp.concatenate([hot_rows(x) for x in index] + [pad], axis=0)
        hots[strand] = hot
        mixed = dot2(hot, pre, 0, 0)
        tanh_part, sig_part = gates(mixed)
        product = tanh_part * sig_part
        hidden = split(product)
        rows = slice(strand * length, (strand + 1) * length)
        hidden_high[rows, :] = hidden[0]
        hidden_low[rows, :] = hidden[1]
        slopes[rows, :channels] = sig_part - product * tanh_part
        slopes[rows, channels:] = product - product * sig_part
        cot = (cot_high[rows, :], cot_low[rows, :])
        part_o = dot3(hidden, cot, 0, 0)
        part_c = dot2(hot[LOCAL : 2 * LOCAL], cot)
        total_o = part_o if total_o is None else total_o + part_o
        total_c = part_c if total_c is None else total_c + part_c
    side = channels // 4
    for q in range(4):
        lanes = slice((q >> 1) * 128, (q >> 1) * 128 + 128)
        quarters[q, :side, :] = total_o[q * side : (q + 1) * side, :128]
        quarters[q, side : 2 * side, :] = total_o[q * side : (q + 1) * side, 128:]
        for begin, rows, at in ((0, INNER // 2, 2 * side), (INNER, EDGE // 2, 2 * side + INNER // 2)):
            begin += (q & 1) * rows
            quarters[q, at : at + rows, :] = total_c[begin : begin + rows, lanes]
    deal(quarters, keep, send)


def taps_kernel(hots, slopes, grad_hidden, keep, send, quarters):
    length = hots.shape[2]
    total = None
    for strand in range(2):
        rows = slice(strand * length, (strand + 1) * length)
        grad = grad_hidden[rows, :]
        part = dot2(hots[strand], split(slopes[rows, :] * jnp.concatenate([grad, grad], axis=1)))
        total = part if total is None else total + part
    for q in range(4):
        quarters[q] = total[:TAPS, q * 128 : (q + 1) * 128]
    deal(quarters, keep, send)


def halve_kernel(kept, received, keep, send):
    bit = (lax.axis_index("seq") >> 1) & 1
    send[...] = kept[1 - bit] + received[1 - bit]
    keep[...] = kept[bit] + received[bit]


def add_after_kernel(kept, received, after, out):
    out[...] = kept[...] + received[...]


def halve_after_kernel(kept, received, after, keep, send):
    halve_kernel(kept, received, keep, send)


def outputs_kernel(hots, hidden_high, hidden_low, local, out_w, after, out_fwd, out_rev, values, sems):
    length = hots.shape[2]
    fetch = Fetch(sems)
    weight = split(out_w[...])
    level = split(local[...])
    for strand, out in enumerate((out_fwd, out_rev)):
        rows = slice(strand * length, (strand + 1) * length)
        own = dot2(hots[strand, LOCAL : 2 * LOCAL, :], level, 0, 0)
        values[strand] = own + dot3((hidden_high[rows, :], hidden_low[rows, :]), weight)
        fetch.start(values.at[strand], out)
    fetch.wait(0, 1)


def prepare_kernel(
    first_conv, first_mix, second_conv, second_mix, out_w, table, mixed_table, after,
    first_high, first_low, second_high, second_low, turn_high, turn_low,
    level_high, level_low, partner_high, partner_low, hidden_high, hidden_low, slopes, hot,
):
    level = split(table[...])
    swap = permutation()
    level_high[...], level_low[...] = level
    partner_high[...], partner_low[...] = tuple(dot(swap, piece).astype(BF16) for piece in level)
    for conv, mix, high, low in (
        (second_conv, second_mix, second_high, second_low),
        (first_conv, first_mix, first_high, first_low),
    ):
        for k in range(4):
            high[k], low[k] = split((conv[k] if k < 3 else mix[...]).T)
    turn_high[...], turn_low[...] = split(out_w[...].T)
    tanh_part, sig_part = gates(mixed_table[...])
    product = tanh_part * sig_part
    hidden_high[...], hidden_low[...] = split(product)
    channels = product.shape[1]
    slopes[:, :channels] = sig_part - product * tanh_part
    slopes[:, channels:] = product - product * sig_part
    hot[...] = letter_hot()


def merge(mine, theirs, inner, edge):
    left = left_side()
    both = mine[inner, :] + theirs[inner, :]
    own, other = mine[edge, :], theirs[edge, :]
    return both, jnp.where(left, own, other), jnp.where(left, other, own)


def merge_blocks(mine, theirs, out, sizes):
    at = to = 0
    for inner, edge in sizes:
        pieces = merge(mine, theirs, slice(at, at + inner), slice(at + inner, at + inner + edge))
        out[to : to + inner, :] = pieces[0]
        out[to + inner : to + inner + edge, :] = pieces[1]
        out[to + inner + edge : to + inner + 2 * edge, :] = pieces[2]
        at, to = at + inner + edge, to + inner + 2 * edge


def merge_taps_kernel(mine, theirs, after, out):
    merge_blocks(mine, theirs, out, [(INNER, EDGE)] * 3)


def merge_rest_kernel(mine, theirs, after, out):
    merge_blocks(mine, theirs, out, [(mine.shape[0] - EDGE // 2, EDGE // 2)])


def gather_quarters(pieces, quarters):
    place = lax.axis_index("seq")
    low, high = place & 1, (place >> 1) & 1
    for parts, x, y in zip(pieces, (0, 0, 1, 1), (0, 1, 0, 1)):
        begin = 0
        for part in parts:
            rows = part.shape[0]
            quarters[(low ^ x) * 2 + (high ^ y), begin : begin + rows, :] = part[...]
            begin += rows


def tap_pairs(taps):
    return [split(taps[k * CONTEXTS : (k + 1) * CONTEXTS, :]) for k in range(3)]


def quarter_weights(pairs, taps, levels, g_conv, g_mix, bias):
    level_high, level_low, partner_high, partner_low = levels
    level = (level_high[...], level_low[...])
    partner = (partner_high[...], partner_low[...])
    for k, pair in enumerate(pairs):
        g_conv[k] = dot3(level, pair, 0, 0)
    g_mix[...] = dot3(partner, pairs[1], 0, 0)
    bias[...] = jnp.sum(taps[CONTEXTS : 2 * CONTEXTS, :], axis=0, keepdims=True)


def quarter_part(pairs, column, seconds):
    weights = [tuple(ref[k, pl.ds(column, 128), :] for ref in seconds) for k in range(4)]
    part = dot2(permutation(), split(dot3_few(pairs[1], weights[3])))
    for k, pair in enumerate(pairs):
        part = part + dot3_few(pair, weights[k])
    return part


def column_of(core, chip):
    place = lax.axis_index("seq")
    low, high = place & 1, (place >> 1) & 1
    return pl.multiple_of(((low ^ core) * 2 + (high ^ chip)) * 128, 128)


def store_columns(store, column, g_conv, g_mix, g_conv_out, g_mix_out):
    block = pl.ds(column, 128)
    for k in range(3):
        store.start(g_conv.at[k], g_conv_out.at[1, k, :, block])
    store.start(g_mix, g_mix_out.at[1, :, block])


def own_columns_kernel(own_piece, core_first, core_second, core_third, after, *refs):
    levels, seconds, refs = refs[:4], refs[4:6], refs[6:]
    g_conv_out, g_mix_out, bias, total, taps, g_conv, g_mix, out_sems = refs
    store = Fetch(out_sems)
    taps[0] = own_piece[...]
    fill(taps.at[1], core_first, core_second, core_third)
    grad_level = None
    for core in range(2):
        column = column_of(core, 0)
        pairs = tap_pairs(taps.at[core])
        quarter_weights(pairs, taps.at[core], levels, g_conv.at[core], g_mix.at[core], bias.at[core : core + 1])
        part = quarter_part(pairs, column, seconds)
        store_columns(store, column, g_conv.at[core], g_mix.at[core], g_conv_out, g_mix_out)
        grad_level = part if grad_level is None else grad_level + part
    total[...] = grad_level
    store.wait(*range(len(store.copies)))


def fill(taps, *parts):
    rows = parts[0].shape[0]
    for at, part in enumerate(parts):
        taps[at * rows : (at + 1) * rows, :] = part[...]


def other_columns_kernel(first, second, *refs):
    levels, seconds, refs = refs[:4], refs[4:6], refs[6:]
    partial, g_conv_in, g_mix_in, g_conv_out, g_mix_out, bias, total, taps, g_conv, g_mix, out_sems = refs
    fill(taps, first, second)
    store = Fetch(out_sems)
    column = column_of(0, 1)
    pairs = tap_pairs(taps)
    quarter_weights(pairs, taps, levels, g_conv, g_mix, bias)
    total[...] = partial[...] + quarter_part(pairs, column, seconds)
    store_columns(store, column, g_conv, g_mix, g_conv_out, g_mix_out)
    store.wait(*range(len(store.copies)))


def first_layer_kernel(
    far_first, far_second, level_high, level_low, partner_high, partner_low, second_high, second_low,
    piece_00, piece_01, piece_10, piece_11, partial, bias_own, bias_other, embed,
    first_high, first_low, turn_high, turn_low, hidden_high, hidden_low, slopes, hot_in,
    g_conv_in, g_mix_in, g_conv_out, g_mix_out, g_embed_out, g_bias_out, g_out_out,
    quarters, bias_rows, bias_far, far_piece, far_conv, far_mix, g_conv, g_mix, g_embed, g_bias, g_out, out_sems,
):
    channels = embed.shape[1]
    store = Fetch(out_sems)
    column = column_of(1, 1)
    fill(far_piece, far_first, far_second)
    pairs = tap_pairs(far_piece)
    far_part = quarter_part(pairs, column, (second_high, second_low))
    gather_quarters([(piece,) for piece in (piece_00, piece_01, piece_10, piece_11)], quarters)
    side = channels // 4
    rest = []
    for begin, rows in ((0, INNER // 2), (INNER // 2, EDGE // 2), (INNER // 2 + EDGE // 2, EDGE // 2)):
        begin += 2 * side
        halves = [[quarters[2 * h + i, begin : begin + rows, :] for i in range(2)] for h in range(2)]
        rest.append(jnp.concatenate([jnp.concatenate(x, axis=0) for x in halves], axis=1))
    grad_level = split(partial[...] + far_part + jnp.concatenate(rest, axis=0))
    grad_hidden = dot3_few(grad_level, (turn_high[...], turn_low[...]))
    grad_mixed = slopes[...] * jnp.concatenate([grad_hidden, grad_hidden], axis=1)
    levels = (level_high, level_low, partner_high, partner_low)
    quarter_weights(pairs, far_piece, levels, far_conv, far_mix, bias_far)
    store_columns(store, column, far_conv, far_mix, g_conv_out, g_mix_out)
    hot = hot_in[...]
    by_letter = dot2(hot, split(grad_mixed), 0, 0)
    base = split(padded_base(embed))
    stacked = jnp.concatenate([base[0].astype(F32), base[0].astype(F32), base[1].astype(F32)], axis=0).astype(BF16)
    pieces = []
    for k in range(4):
        piece = split(by_letter[k * 8 : (k + 1) * 8, :])
        pieces.append(piece)
        high, low = piece[0].astype(F32), piece[1].astype(F32)
        value = dot(stacked, jnp.concatenate([high, low, high], axis=0).astype(BF16), 0, 0)
        if k < 3:
            g_conv[k] = value
            store.start(g_conv.at[k], g_conv_out.at[0, k])
        else:
            g_mix[...] = value
            store.start(g_mix, g_mix_out.at[0])
    g_out[0] = dot3((hidden_high[...], hidden_low[...]), grad_level, 0, 0)
    for q in range(4):
        for h in range(2):
            g_out[1, q * side : (q + 1) * side, h * 128 : (h + 1) * 128] = quarters[q, h * side : (h + 1) * side, :]
    store.start(g_out, g_out_out)
    place = lax.axis_index("seq")
    low, high = place & 1, (place >> 1) & 1
    for row, x, y in (
        (bias_own[0:1, :], 0, 0), (bias_own[1:2, :], 1, 0), (bias_other[...], 0, 1), (bias_far[...], 1, 1)
    ):
        bias_rows[(low ^ x) * 2 + (high ^ y)] = row
    g_bias[0:1, :] = jnp.sum(grad_mixed, axis=0, keepdims=True)
    g_bias[1:2, :] = jnp.concatenate([bias_rows[q] for q in range(4)], axis=1)
    store.start(g_bias, g_bias_out)
    grad_base = dot2(hot[:, 8:16], grad_level, 0, 0)
    for k in range(4):
        grad_base = grad_base + dot3_few(pieces[k], (first_high[k], first_low[k]))
    g_embed[...] = grad_base[:4, :]
    store.start(g_embed, g_embed_out)
    store.wait(*range(len(store.copies)))


VMEM, SMEM, HBM = pltpu.VMEM, pltpu.SMEM, pltpu.HBM


def call(kernel, ins, outs, scratch=(), aliases=None, micros=0.001):
    run = pl.pallas_call(
        kernel,
        out_shape=[space(shape, kind) for shape, kind, space in outs],
        in_specs=[pl.BlockSpec(memory_space=space) for space in ins],
        out_specs=[pl.BlockSpec(memory_space=space) for _, _, space in outs],
        scratch_shapes=list(scratch),
        input_output_aliases=aliases or {},
        cost_estimate=pl.CostEstimate(flops=int(micros * 1.1e9), bytes_accessed=int(micros * 3e6), transcendentals=0),
        compiler_params=pltpu.CompilerParams(vmem_limit_bytes=VMEM_LIMIT),
    )

    def placed(*args):
        return run(*[pltpu.with_memory_space_constraint(x, HBM) if space is HBM else x for x, space in zip(args, ins)])

    return placed


def swapped(value, mask):
    pairs = [(source, source ^ mask) for source in range(lax.axis_size("seq"))]
    return lax.ppermute(value, "seq", pairs)


def crossed(piece, count, rest):
    mask = 4
    while mask < count // 2:
        piece = piece + swapped(piece, mask)
        mask *= 2
    return rest(piece, swapped(piece, mask))


def on_device(
    tokens, dilations, embed, conv_weight, mix_weight, gate_bias, out_weight, cot_fwd, cot_rev
):
    channels = embed.shape[1]
    wide = 2 * channels
    length = tokens.shape[0]
    count = lax.axis_size("seq")
    sems = pltpu.SemaphoreType.DMA
    square = (channels, channels)

    row = tokens.reshape(1, length)
    near = [swapped(row, mask) for mask in (1, 2, 3)]
    layer_weights = [(conv_weight.shape[1:], F32, VMEM), (mix_weight.shape[1:], F32, VMEM)]
    own, taps, first_conv, first_mix, turn, last_weight, cot_high, cot_low, grad_hidden = call(
        first_tables_kernel,
        [HBM] * 7,
        [(row.shape, row.dtype, VMEM), ((32, wide), F32, VMEM), *layer_weights]
        + [(square, F32, VMEM)] * 2
        + [((2 * length, channels), BF16, VMEM)] * 2
        + [((2 * length, channels), F32, VMEM)],
        [VMEM(embed.shape, F32), VMEM((2, length, channels), F32), sems((10,))],
        micros=2.7,
    )(row, embed, conv_weight, mix_weight, out_weight, cot_fwd, cot_rev)
    known = call(join_four_kernel, [VMEM] * 5, [((4, length), row.dtype, VMEM)])(own, *near, taps)[0]
    parts = [known, swapped(known, 4)]
    deep = -(-TAPS // 128) * 128
    table, local, mixed_table, pre_high, pre_low, second_conv, second_mix = call(
        second_tables_kernel,
        [VMEM] * 4 + [HBM] * 2 + [VMEM],
        [((CONTEXTS, channels), F32, VMEM), ((LOCAL, channels), F32, VMEM), ((CONTEXTS, wide), F32, VMEM)]
        + [((deep, wide), BF16, VMEM)] * 2
        + layer_weights,
        [sems((4,))],
        micros=2.5,
    )(taps, embed, gate_bias, turn, conv_weight, mix_weight, known)
    mask = 8
    while mask < count:
        known = jnp.concatenate([known, parts[-1]], axis=0)
        parts.append(swapped(known, mask))
        mask *= 2

    rows_x, rows_y = TAPS, channels // 2 + LOCAL // 2
    keep_y, send_y, hidden_high, hidden_low, hots, slopes = call(
        lambda *refs: forward_kernel(count, *refs),
        [SMEM] + [VMEM] * (len(parts) + 4),
        [((2, rows_y, 128), F32, VMEM)] * 2
        + [((2 * length, channels), BF16, VMEM)] * 2
        + [((2, deep, length), BF16, VMEM), ((2 * length, wide), F32, VMEM)],
        [VMEM((4, rows_y, 128), F32)],
        micros=2.0,
    )(dilations, *parts, pre_high, pre_low, cot_high, cot_low)
    keep_x, send_x = call(
        taps_kernel,
        [VMEM] * 3,
        [((2, rows_x, 128), F32, VMEM)] * 2,
        [VMEM((4, rows_x, 128), F32)],
        micros=1.5,
    )(hots, slopes, grad_hidden)

    def halved(keep, received, after):
        outs = [(keep.shape[1:], F32, VMEM)] * 2
        return call(halve_after_kernel, [VMEM] * 3, outs)(keep, received, after)

    def added(kept, received, after, space=VMEM):
        return call(add_after_kernel, [VMEM] * 2 + [space], [(kept.shape, F32, VMEM)])(kept, received, after)[0]

    def touched(value, after, cuts=1):
        shape = (value.shape[0] // cuts, value.shape[1])
        return call(touch_kernel, [VMEM] * 2, [(shape, value.dtype, VMEM)] * cuts)(value, after)

    keep_y, send_y = halved(keep_y, swapped(send_y, 1), keep_x)
    keep_x, send_x = halved(keep_x, swapped(send_x, 1), keep_y)
    sum_y = added(keep_y, swapped(send_y, 2), keep_x)
    out_fwd, out_rev = call(
        outputs_kernel,
        [VMEM] * 6,
        [((length, channels), F32, HBM)] * 2,
        [VMEM((2, length, channels), F32), sems((2,))],
        micros=2.0,
    )(hots, hidden_high, hidden_low, local, last_weight, sum_y)
    sum_x = added(keep_x, swapped(send_x, 2), out_rev, HBM)
    first_high, first_low, second_high, second_low, turn_high, turn_low, *tables = call(
        prepare_kernel,
        [VMEM] * 8,
        [((4, wide, channels), BF16, VMEM)] * 4
        + [(square, BF16, VMEM)] * 2
        + [((CONTEXTS, channels), BF16, VMEM)] * 6
        + [((CONTEXTS, wide), F32, VMEM), ((CONTEXTS, 32), BF16, VMEM)],
        micros=1.4,
    )(first_conv, first_mix, second_conv, second_mix, turn, table, mixed_table, sum_x)
    levels, tables = tables[:4], tables[4:]

    def merged(kernel, rows, mine, theirs, after):
        return call(kernel, [VMEM] * 3, [((rows, 128), F32, VMEM)])(mine, theirs, after)[0]

    merged_x, merged_y = 3 * CONTEXTS, rows_y + EDGE // 2
    piece_y = crossed(sum_y, count, lambda x, y: merged(merge_rest_kernel, merged_y, x, y, turn_low))
    piece_x = crossed(sum_x, count, lambda x, y: merged(merge_taps_kernel, merged_x, x, y, piece_y))
    other_y = swapped(piece_y, 2)
    halves_x = touched(piece_x, sum_x, 2)
    core_x = [swapped(x, 1) for x in touched(piece_x, sum_x, 3)]

    core_y = swapped(piece_y, 1)
    shared = (*levels, second_high, second_low)
    large = [(conv_weight.shape, F32, HBM), (mix_weight.shape, F32, HBM)]
    level_out = ((CONTEXTS, channels), F32, VMEM)
    quarter_conv, quarter_mix = (3, channels, 128), (channels, 128)
    g_conv, g_mix, bias_own, partial = call(
        own_columns_kernel,
        [VMEM] * 11,
        [*large, ((2, 128), F32, VMEM), level_out],
        [
            VMEM((2, merged_x, 128), F32),
            VMEM((2, *quarter_conv), F32),
            VMEM((2, *quarter_mix), F32),
            sems((8,)),
        ],
        micros=0.05,
    )(piece_x, *core_x, other_y, *shared)
    other_x = [swapped(x, 2) for x in halves_x]
    late_y = touched(other_y, partial)[0]
    rest_y = swapped(late_y, 1)
    far_x = [swapped(touched(x, late_y)[0], 1) for x in other_x]
    g_conv, g_mix, bias_other, partial = call(
        other_columns_kernel,
        [VMEM] * 9 + [HBM] * 2,
        [*large, ((1, 128), F32, VMEM), level_out],
        [VMEM((merged_x, 128), F32), VMEM(quarter_conv, F32), VMEM(quarter_mix, F32), sems((4,))],
        aliases={9: 0, 10: 1},
        micros=0.05,
    )(*other_x, *shared, partial, g_conv, g_mix)
    g_conv, g_mix, g_embed, g_bias, g_out = call(
        first_layer_kernel,
        [VMEM] * 24 + [HBM] * 2,
        [*large] + [(shape, F32, HBM) for shape in (embed.shape, gate_bias.shape, out_weight.shape)],
        [
            VMEM((4, merged_y, 128), F32),
            VMEM((4, 1, 128), F32),
            VMEM((1, 128), F32),
            VMEM((merged_x, 128), F32),
            VMEM(quarter_conv, F32),
            VMEM(quarter_mix, F32),
            VMEM(conv_weight.shape[1:], F32),
            VMEM(mix_weight.shape[1:], F32),
            VMEM(embed.shape, F32),
            VMEM(gate_bias.shape, F32),
            VMEM(out_weight.shape, F32),
            sems((11,)),
        ],
        aliases={24: 0, 25: 1},
        micros=2.7,
    )(
        *far_x, *shared, piece_y, other_y, core_y, rest_y, partial, bias_own, bias_other, embed,
        first_high, first_low, turn_high, turn_low, *tables, g_conv, g_mix,
    )
    return (out_fwd, out_rev, g_embed, g_conv, g_mix, g_bias, g_out)


def solution(mesh):
    in_specs = (
        P(("dp", "seq")),
        P(),
        P(),
        P(),
        P(),
        P(),
        P(),
        P(("dp", "seq"), None),
        P(("dp", "seq"), None),
    )
    out_specs = (
        P(("dp", "seq"), None),
        P(("dp", "seq"), None),
        P("dp", None),
        P("dp", None, None, None),
        P("dp", None, None),
        P("dp", None),
        P("dp", None, None),
    )
    return jax.shard_map(
        on_device, mesh=mesh, in_specs=in_specs, out_specs=out_specs, check_vma=False
    )
```

```python
import jax
import jax.numpy as jnp
from jax import lax
from jax.experimental import pallas as pl
from jax.experimental.pallas import tpu as pltpu
from jax.sharding import PartitionSpec as P

CONTEXTS = 96
INNER = 64
EDGE = 16
LOCAL = INNER + EDGE
TAPS = 3 * LOCAL
HALO = 128
F32 = jnp.float32
BF16 = jnp.bfloat16
VMEM_LIMIT = 40 * 1024 * 1024


def split(x):
    high = x.astype(BF16)
    return high, (x - high.astype(F32)).astype(BF16)


def dot(a, b, ca=1, cb=0):
    return lax.dot_general(a, b, (((ca,), (cb,)), ((), ())), preferred_element_type=F32)


def dot2(exact, pair, ca=1, cb=0):
    return dot(exact, pair[0], ca, cb) + dot(exact, pair[1], ca, cb)


def dot3(a, b, ca=1, cb=0):
    return dot(a[0], b[0], ca, cb) + (dot(a[0], b[1], ca, cb) + dot(a[1], b[0], ca, cb))


def dot3_few(a, b):
    rows = a[0].shape[0]
    both = dot(jnp.concatenate([a[0].astype(F32), a[1].astype(F32)], axis=0).astype(BF16), b[0])
    return both[:rows] + (both[rows:] + dot(a[0], b[1]))


def letters(index):
    inner = index < 64
    left = (index >= 64) & (index < 80)
    low = index & 3
    mid = (index >> 2) & 3
    l = jnp.where(inner, (index >> 4) & 3, jnp.where(left, -1, mid))
    m = jnp.where(inner | left, mid, low)
    r = jnp.where(inner | left, low, -1)
    return l, m, r


def mirrored(index):
    low = 3 - (index & 3)
    mid = 3 - ((index >> 2) & 3)
    high = 3 - ((index >> 4) & 3)
    inner = low * 16 + mid * 4 + high
    left = 80 + low * 4 + mid
    right = 64 + low * 4 + mid
    return jnp.where(index < 64, inner, jnp.where(index < 80, left, right))


def permutation():
    rows = lax.broadcasted_iota(jnp.int32, (CONTEXTS, CONTEXTS), 0)
    cols = lax.broadcasted_iota(jnp.int32, (CONTEXTS, CONTEXTS), 1)
    return (mirrored(rows) == cols).astype(F32).astype(BF16)


def letter_hot():
    rows = lax.broadcasted_iota(jnp.int32, (CONTEXTS, 32), 0)
    cols = lax.broadcasted_iota(jnp.int32, (CONTEXTS, 32), 1)
    l, m, r = letters(rows)
    kind = cols >> 3
    value = jnp.where(kind == 0, l, jnp.where(kind == 1, m, jnp.where(kind == 2, r, 3 - m)))
    return (value == (cols & 7)).astype(F32).astype(BF16)


def gates(mixed):
    channels = mixed.shape[1] // 2
    tanh_part = jnp.tanh(mixed[:, :channels])
    sig_part = 0.5 + 0.5 * jnp.tanh(0.5 * mixed[:, channels:])
    return tanh_part, sig_part


def gate_grads(grad_hidden, tanh_part, sig_part):
    scaled = grad_hidden * sig_part
    return scaled * (1.0 - tanh_part * tanh_part), scaled * tanh_part * (1.0 - sig_part)


class Fetch:
    def __init__(self, sems):
        self.sems = sems
        self.copies = []

    def start(self, source, target):
        copy = pltpu.make_async_copy(source, target, self.sems.at[len(self.copies)])
        copy.start()
        self.copies.append(copy)
        return len(self.copies) - 1

    def wait(self, *which):
        for at in which:
            self.copies[at].wait()


def padded_base(embed):
    return jnp.concatenate([embed[...], jnp.zeros((4, embed.shape[1]), F32)], axis=0)


def left_side():
    return lax.axis_index("seq") * 2 < lax.axis_size("seq")


def local_rows(rows):
    edge = jnp.where(left_side(), rows[INNER : INNER + EDGE], rows[INNER + EDGE : INNER + 2 * EDGE])
    return jnp.concatenate([rows[:INNER], edge], axis=0)


def join_four_kernel(first, second, third, fourth, after, out):
    for at, part in enumerate((first, second, third, fourth)):
        out[at : at + 1, :] = part[...]


def touch_kernel(value, after, *outs):
    begin = 0
    for out in outs:
        out[...] = value[begin : begin + out.shape[0], :]
        begin += out.shape[0]


def first_tables_kernel(
    tokens_in, embed_in, conv_in, mix_in, out_in, cot_fwd_in, cot_rev_in,
    own, taps, conv, mix, turn, last_weight, cot_high, cot_low, grad_hidden, embed, cots, sems,
):
    length = cots.shape[1]
    fetch = Fetch(sems)
    fetch.start(embed_in, embed)
    first = [fetch.start(conv_in.at[0, k], conv.at[k]) for k in range(3)]
    first += [fetch.start(mix_in.at[0], mix)]
    last = [fetch.start(out_in.at[1], last_weight)]
    last += [fetch.start(cot_in, cots.at[strand]) for strand, cot_in in enumerate((cot_fwd_in, cot_rev_in))]
    rest = [fetch.start(tokens_in, own), fetch.start(out_in.at[0], turn)]
    fetch.wait(0)
    base = split(padded_base(embed))
    for k in range(4):
        fetch.wait(first[k])
        taps[k * 8 : (k + 1) * 8, :] = dot3_few(base, split(conv[k] if k < 3 else mix[...]))
    fetch.wait(last[0])
    weight = split(last_weight[...])
    for strand in range(2):
        rows = slice(strand * length, (strand + 1) * length)
        fetch.wait(last[1 + strand])
        cot = split(cots[strand])
        cot_high[rows, :], cot_low[rows, :] = cot
        grad_hidden[rows, :] = dot3(cot, weight, 1, 1)
    fetch.wait(*rest)


def second_tables_kernel(
    taps, embed, bias, turn, conv_in, mix_in, after, table, local, mixed_table, pre_high, pre_low, conv, mix, sems,
):
    fetch = Fetch(sems)
    second = [fetch.start(conv_in.at[1, k], conv.at[k]) for k in range(3)]
    second += [fetch.start(mix_in.at[1], mix)]
    hot = letter_hot()
    mixed = dot2(hot, split(taps[...])) + bias[0:1, :]
    tanh_part, sig_part = gates(mixed)
    own = dot2(hot[:, 8:16], split(padded_base(embed)))
    level = own + dot3_few(split(tanh_part * sig_part), split(turn[...]))
    table[...] = level
    local[...] = local_rows(level)
    mixed_table[...] = mixed
    level = split(level)
    swap = permutation()
    partner = tuple(dot(swap, piece).astype(BF16) for piece in level)
    pre_high[TAPS:, :] = jnp.zeros((pre_high.shape[0] - TAPS, pre_high.shape[1]), BF16)
    pre_low[TAPS:, :] = jnp.zeros((pre_low.shape[0] - TAPS, pre_low.shape[1]), BF16)
    for k in (0, 2, 1):
        fetch.wait(second[k])
        value = dot3_few(level, split(conv[k]))
        if k == 1:
            fetch.wait(second[3])
            value = value + dot3_few(partner, split(mix[...])) + bias[1:2, :]
        high, low = split(local_rows(value))
        pre_high[k * LOCAL : (k + 1) * LOCAL, :] = high
        pre_low[k * LOCAL : (k + 1) * LOCAL, :] = low


def windows(parts, count):
    length = parts[0].shape[1]
    place = lax.axis_index("seq")
    last = count - 1

    def block(at):
        total, begin = None, 0
        for part in parts:
            rows = lax.broadcasted_iota(jnp.int32, part.shape, 0) + begin
            piece = jnp.sum(jnp.where(rows == (place ^ at), part[...], 0), axis=0, keepdims=True)
            total = piece if total is None else total + piece
            begin += part.shape[0]
        return total

    def window(at):
        before = jnp.where(at == 0, -1, block(jnp.maximum(at - 1, 0))[:, length - HALO :])
        after = jnp.where(at == last, -1, block(jnp.minimum(at + 1, last))[:, :HALO])
        return [before, block(at), after]

    fwd = jnp.concatenate(window(place), axis=1)
    rev = jnp.concatenate(window(last - place), axis=1)
    rev = jnp.where(rev < 0, -1, 3 - rev)
    tiles = rev.shape[1] // 128
    blocks = [rev[:, i * 128 : (i + 1) * 128] for i in reversed(range(tiles))]
    blocks += [jnp.zeros((8 - tiles, 128), jnp.int32)]
    stacked = jnp.concatenate(blocks, axis=0).astype(F32).astype(BF16)
    rows = lax.broadcasted_iota(jnp.int32, (128, 128), 0)
    cols = lax.broadcasted_iota(jnp.int32, (128, 128), 1)
    flip = (rows + cols == 127).astype(F32).astype(BF16)
    turned = dot(stacked, flip).astype(jnp.int32)
    rev = jnp.concatenate([turned[i : i + 1, :] for i in range(tiles)], axis=1)
    return fwd, rev


def local_contexts(window, first, second, length):
    width = window.shape[1]
    base = jnp.broadcast_to(window, (8, width))
    l = pltpu.roll(base, first, 1)
    r = pltpu.roll(base, width - first, 1)
    index = jnp.where(l < 0, INNER + base * 4 + r, jnp.where(r < 0, INNER + l * 4 + base, l * 16 + base * 4 + r))
    index = jnp.where(base < 0, LOCAL, index)
    before = pltpu.roll(index, second, 1)
    after = pltpu.roll(index, width - second, 1)
    return [x[0:1, HALO : HALO + length] for x in (before, index, after)]


def hot_rows(index):
    rows = lax.broadcasted_iota(jnp.int32, (LOCAL, index.shape[1]), 0)
    return (rows == index).astype(F32).astype(BF16)


def deal(quarters, keep, send):
    bit = lax.axis_index("seq") & 1
    keep[...] = quarters[pl.ds(bit * 2, 2)]
    send[...] = quarters[pl.ds((1 - bit) * 2, 2)]


def forward_kernel(count, dil, *refs):
    steps = count.bit_length() - 2
    parts, refs = refs[:steps], refs[steps:]
    (pre_high, pre_low, cot_high, cot_low, keep, send, hidden_high, hidden_low, hots, slopes, quarters) = refs
    length = parts[0].shape[1]
    channels = cot_high.shape[1]
    pre = (pre_high[...], pre_low[...])
    both = windows(parts, count)
    pad = jnp.zeros((pre_high.shape[0] - TAPS, length), BF16)
    total_o = total_c = None
    for strand in range(2):
        index = local_contexts(both[strand], dil[0], dil[1], length)
        hot = jnp.concatenate([hot_rows(x) for x in index] + [pad], axis=0)
        hots[strand] = hot
        mixed = dot2(hot, pre, 0, 0)
        tanh_part, sig_part = gates(mixed)
        product = tanh_part * sig_part
        hidden = split(product)
        rows = slice(strand * length, (strand + 1) * length)
        hidden_high[rows, :] = hidden[0]
        hidden_low[rows, :] = hidden[1]
        slopes[rows, :channels] = sig_part - product * tanh_part
        slopes[rows, channels:] = product - product * sig_part
        cot = (cot_high[rows, :], cot_low[rows, :])
        part_o = dot3(hidden, cot, 0, 0)
        part_c = dot2(hot[LOCAL : 2 * LOCAL], cot)
        total_o = part_o if total_o is None else total_o + part_o
        total_c = part_c if total_c is None else total_c + part_c
    side = channels // 4
    for q in range(4):
        lanes = slice((q >> 1) * 128, (q >> 1) * 128 + 128)
        quarters[q, :side, :] = total_o[q * side : (q + 1) * side, :128]
        quarters[q, side : 2 * side, :] = total_o[q * side : (q + 1) * side, 128:]
        for begin, rows, at in ((0, INNER // 2, 2 * side), (INNER, EDGE // 2, 2 * side + INNER // 2)):
            begin += (q & 1) * rows
            quarters[q, at : at + rows, :] = total_c[begin : begin + rows, lanes]
    deal(quarters, keep, send)


def taps_kernel(hots, slopes, grad_hidden, keep, send, quarters):
    length = hots.shape[2]
    total = None
    for strand in range(2):
        rows = slice(strand * length, (strand + 1) * length)
        grad = grad_hidden[rows, :]
        part = dot2(hots[strand], split(slopes[rows, :] * jnp.concatenate([grad, grad], axis=1)))
        total = part if total is None else total + part
    for q in range(4):
        quarters[q] = total[:TAPS, q * 128 : (q + 1) * 128]
    deal(quarters, keep, send)


def halve_kernel(kept, received, keep, send):
    bit = (lax.axis_index("seq") >> 1) & 1
    send[...] = kept[1 - bit] + received[1 - bit]
    keep[...] = kept[bit] + received[bit]


def add_after_kernel(kept, received, after, out):
    out[...] = kept[...] + received[...]


def halve_after_kernel(kept, received, after, keep, send):
    halve_kernel(kept, received, keep, send)


def outputs_kernel(hots, hidden_high, hidden_low, local, out_w, after, out_fwd, out_rev, values, sems):
    length = hots.shape[2]
    fetch = Fetch(sems)
    weight = split(out_w[...])
    level = split(local[...])
    for strand, out in enumerate((out_fwd, out_rev)):
        rows = slice(strand * length, (strand + 1) * length)
        own = dot2(hots[strand, LOCAL : 2 * LOCAL, :], level, 0, 0)
        values[strand] = own + dot3((hidden_high[rows, :], hidden_low[rows, :]), weight)
        fetch.start(values.at[strand], out)
    fetch.wait(0, 1)


def prepare_kernel(
    first_conv, first_mix, second_conv, second_mix, out_w, table, mixed_table, after,
    first_high, first_low, second_high, second_low, turn_high, turn_low,
    level_high, level_low, partner_high, partner_low, hidden_high, hidden_low, slopes, hot,
):
    level = split(table[...])
    swap = permutation()
    level_high[...], level_low[...] = level
    partner_high[...], partner_low[...] = tuple(dot(swap, piece).astype(BF16) for piece in level)
    for conv, mix, high, low in (
        (second_conv, second_mix, second_high, second_low),
        (first_conv, first_mix, first_high, first_low),
    ):
        for k in range(4):
            high[k], low[k] = split((conv[k] if k < 3 else mix[...]).T)
    turn_high[...], turn_low[...] = split(out_w[...].T)
    tanh_part, sig_part = gates(mixed_table[...])
    product = tanh_part * sig_part
    hidden_high[...], hidden_low[...] = split(product)
    channels = product.shape[1]
    slopes[:, :channels] = sig_part - product * tanh_part
    slopes[:, channels:] = product - product * sig_part
    hot[...] = letter_hot()


def merge(mine, theirs, inner, edge):
    left = left_side()
    both = mine[inner, :] + theirs[inner, :]
    own, other = mine[edge, :], theirs[edge, :]
    return both, jnp.where(left, own, other), jnp.where(left, other, own)


def merge_blocks(mine, theirs, out, sizes):
    at = to = 0
    for inner, edge in sizes:
        pieces = merge(mine, theirs, slice(at, at + inner), slice(at + inner, at + inner + edge))
        out[to : to + inner, :] = pieces[0]
        out[to + inner : to + inner + edge, :] = pieces[1]
        out[to + inner + edge : to + inner + 2 * edge, :] = pieces[2]
        at, to = at + inner + edge, to + inner + 2 * edge


def merge_taps_kernel(mine, theirs, after, out):
    merge_blocks(mine, theirs, out, [(INNER, EDGE)] * 3)


def merge_rest_kernel(mine, theirs, after, out):
    merge_blocks(mine, theirs, out, [(mine.shape[0] - EDGE // 2, EDGE // 2)])


def gather_quarters(pieces, quarters):
    place = lax.axis_index("seq")
    low, high = place & 1, (place >> 1) & 1
    for parts, x, y in zip(pieces, (0, 0, 1, 1), (0, 1, 0, 1)):
        begin = 0
        for part in parts:
            rows = part.shape[0]
            quarters[(low ^ x) * 2 + (high ^ y), begin : begin + rows, :] = part[...]
            begin += rows


def tap_pairs(taps):
    return [split(taps[k * CONTEXTS : (k + 1) * CONTEXTS, :]) for k in range(3)]


def quarter_weights(pairs, taps, levels, g_conv, g_mix, bias):
    level_high, level_low, partner_high, partner_low = levels
    level = (level_high[...], level_low[...])
    partner = (partner_high[...], partner_low[...])
    for k, pair in enumerate(pairs):
        g_conv[k] = dot3(level, pair, 0, 0)
    g_mix[...] = dot3(partner, pairs[1], 0, 0)
    bias[...] = jnp.sum(taps[CONTEXTS : 2 * CONTEXTS, :], axis=0, keepdims=True)


def quarter_part(pairs, column, seconds):
    weights = [tuple(ref[k, pl.ds(column, 128), :] for ref in seconds) for k in range(4)]
    part = dot2(permutation(), split(dot3_few(pairs[1], weights[3])))
    for k, pair in enumerate(pairs):
        part = part + dot3_few(pair, weights[k])
    return part


def column_of(core, chip):
    place = lax.axis_index("seq")
    low, high = place & 1, (place >> 1) & 1
    return pl.multiple_of(((low ^ core) * 2 + (high ^ chip)) * 128, 128)


def store_columns(store, column, g_conv, g_mix, g_conv_out, g_mix_out):
    block = pl.ds(column, 128)
    for k in range(3):
        store.start(g_conv.at[k], g_conv_out.at[1, k, :, block])
    store.start(g_mix, g_mix_out.at[1, :, block])


def own_columns_kernel(own_piece, core_first, core_second, *refs):
    levels, seconds, refs = refs[:4], refs[4:6], refs[6:]
    g_conv_out, g_mix_out, bias, total, taps, g_conv, g_mix, out_sems = refs
    store = Fetch(out_sems)
    taps[0] = own_piece[...]
    fill(taps.at[1], core_first, core_second)
    grad_level = None
    for core in range(2):
        column = column_of(core, 0)
        pairs = tap_pairs(taps.at[core])
        quarter_weights(pairs, taps.at[core], levels, g_conv.at[core], g_mix.at[core], bias.at[core : core + 1])
        part = quarter_part(pairs, column, seconds)
        store_columns(store, column, g_conv.at[core], g_mix.at[core], g_conv_out, g_mix_out)
        grad_level = part if grad_level is None else grad_level + part
    total[...] = grad_level
    store.wait(*range(len(store.copies)))


def fill(taps, first, second):
    half = first.shape[0]
    taps[:half, :] = first[...]
    taps[half:, :] = second[...]


def other_columns_kernel(taps, *refs):
    levels, seconds, refs = refs[:4], refs[4:6], refs[6:]
    partial, g_conv_in, g_mix_in, g_conv_out, g_mix_out, bias, total, g_conv, g_mix, out_sems = refs
    store = Fetch(out_sems)
    column = column_of(0, 1)
    pairs = tap_pairs(taps)
    quarter_weights(pairs, taps, levels, g_conv, g_mix, bias)
    total[...] = partial[...] + quarter_part(pairs, column, seconds)
    store_columns(store, column, g_conv, g_mix, g_conv_out, g_mix_out)
    store.wait(*range(len(store.copies)))


def first_layer_kernel(
    far_piece, level_high, level_low, partner_high, partner_low, second_high, second_low,
    piece_00, piece_01, piece_10, piece_11, partial, bias_own, bias_other, embed,
    first_high, first_low, turn_high, turn_low, hidden_high, hidden_low, slopes, hot_in,
    g_conv_in, g_mix_in, g_conv_out, g_mix_out, g_embed_out, g_bias_out, g_out_out,
    quarters, bias_rows, bias_far, far_conv, far_mix, g_conv, g_mix, g_embed, g_bias, g_out, out_sems,
):
    channels = embed.shape[1]
    store = Fetch(out_sems)
    column = column_of(1, 1)
    pairs = tap_pairs(far_piece)
    far_part = quarter_part(pairs, column, (second_high, second_low))
    gather_quarters([(piece,) for piece in (piece_00, piece_01, piece_10, piece_11)], quarters)
    side = channels // 4
    rest = []
    for begin, rows in ((0, INNER // 2), (INNER // 2, EDGE // 2), (INNER // 2 + EDGE // 2, EDGE // 2)):
        begin += 2 * side
        halves = [[quarters[2 * h + i, begin : begin + rows, :] for i in range(2)] for h in range(2)]
        rest.append(jnp.concatenate([jnp.concatenate(x, axis=0) for x in halves], axis=1))
    grad_level = split(partial[...] + far_part + jnp.concatenate(rest, axis=0))
    grad_hidden = dot3_few(grad_level, (turn_high[...], turn_low[...]))
    grad_mixed = slopes[...] * jnp.concatenate([grad_hidden, grad_hidden], axis=1)
    levels = (level_high, level_low, partner_high, partner_low)
    quarter_weights(pairs, far_piece, levels, far_conv, far_mix, bias_far)
    store_columns(store, column, far_conv, far_mix, g_conv_out, g_mix_out)
    hot = hot_in[...]
    by_letter = dot2(hot, split(grad_mixed), 0, 0)
    base = split(padded_base(embed))
    stacked = jnp.concatenate([base[0].astype(F32), base[0].astype(F32), base[1].astype(F32)], axis=0).astype(BF16)
    pieces = []
    for k in range(4):
        piece = split(by_letter[k * 8 : (k + 1) * 8, :])
        pieces.append(piece)
        high, low = piece[0].astype(F32), piece[1].astype(F32)
        value = dot(stacked, jnp.concatenate([high, low, high], axis=0).astype(BF16), 0, 0)
        if k < 3:
            g_conv[k] = value
            store.start(g_conv.at[k], g_conv_out.at[0, k])
        else:
            g_mix[...] = value
            store.start(g_mix, g_mix_out.at[0])
    g_out[0] = dot3((hidden_high[...], hidden_low[...]), grad_level, 0, 0)
    for q in range(4):
        for h in range(2):
            g_out[1, q * side : (q + 1) * side, h * 128 : (h + 1) * 128] = quarters[q, h * side : (h + 1) * side, :]
    store.start(g_out, g_out_out)
    place = lax.axis_index("seq")
    low, high = place & 1, (place >> 1) & 1
    for row, x, y in (
        (bias_own[0:1, :], 0, 0), (bias_own[1:2, :], 1, 0), (bias_other[...], 0, 1), (bias_far[...], 1, 1)
    ):
        bias_rows[(low ^ x) * 2 + (high ^ y)] = row
    g_bias[0:1, :] = jnp.sum(grad_mixed, axis=0, keepdims=True)
    g_bias[1:2, :] = jnp.concatenate([bias_rows[q] for q in range(4)], axis=1)
    store.start(g_bias, g_bias_out)
    grad_base = dot2(hot[:, 8:16], grad_level, 0, 0)
    for k in range(4):
        grad_base = grad_base + dot3_few(pieces[k], (first_high[k], first_low[k]))
    g_embed[...] = grad_base[:4, :]
    store.start(g_embed, g_embed_out)
    store.wait(*range(len(store.copies)))


VMEM, SMEM, HBM = pltpu.VMEM, pltpu.SMEM, pltpu.HBM


def call(kernel, ins, outs, scratch=(), aliases=None, micros=0.001):
    run = pl.pallas_call(
        kernel,
        out_shape=[space(shape, kind) for shape, kind, space in outs],
        in_specs=[pl.BlockSpec(memory_space=space) for space in ins],
        out_specs=[pl.BlockSpec(memory_space=space) for _, _, space in outs],
        scratch_shapes=list(scratch),
        input_output_aliases=aliases or {},
        cost_estimate=pl.CostEstimate(flops=int(micros * 1.1e9), bytes_accessed=int(micros * 3e6), transcendentals=0),
        compiler_params=pltpu.CompilerParams(vmem_limit_bytes=VMEM_LIMIT),
    )

    def placed(*args):
        return run(*[pltpu.with_memory_space_constraint(x, HBM) if space is HBM else x for x, space in zip(args, ins)])

    return placed


def swapped(value, mask):
    pairs = [(source, source ^ mask) for source in range(lax.axis_size("seq"))]
    return lax.ppermute(value, "seq", pairs)


def crossed(piece, count, rest):
    mask = 4
    while mask < count // 2:
        piece = piece + swapped(piece, mask)
        mask *= 2
    return rest(piece, swapped(piece, mask))


def on_device(
    tokens, dilations, embed, conv_weight, mix_weight, gate_bias, out_weight, cot_fwd, cot_rev
):
    channels = embed.shape[1]
    wide = 2 * channels
    length = tokens.shape[0]
    count = lax.axis_size("seq")
    sems = pltpu.SemaphoreType.DMA
    square = (channels, channels)

    row = tokens.reshape(1, length)
    near = [swapped(row, mask) for mask in (1, 2, 3)]
    layer_weights = [(conv_weight.shape[1:], F32, VMEM), (mix_weight.shape[1:], F32, VMEM)]
    own, taps, first_conv, first_mix, turn, last_weight, cot_high, cot_low, grad_hidden = call(
        first_tables_kernel,
        [HBM] * 7,
        [(row.shape, row.dtype, VMEM), ((32, wide), F32, VMEM), *layer_weights]
        + [(square, F32, VMEM)] * 2
        + [((2 * length, channels), BF16, VMEM)] * 2
        + [((2 * length, channels), F32, VMEM)],
        [VMEM(embed.shape, F32), VMEM((2, length, channels), F32), sems((10,))],
        micros=2.7,
    )(row, embed, conv_weight, mix_weight, out_weight, cot_fwd, cot_rev)
    known = call(join_four_kernel, [VMEM] * 5, [((4, length), row.dtype, VMEM)])(own, *near, taps)[0]
    parts = [known, swapped(known, 4)]
    deep = -(-TAPS // 128) * 128
    table, local, mixed_table, pre_high, pre_low, second_conv, second_mix = call(
        second_tables_kernel,
        [VMEM] * 4 + [HBM] * 2 + [VMEM],
        [((CONTEXTS, channels), F32, VMEM), ((LOCAL, channels), F32, VMEM), ((CONTEXTS, wide), F32, VMEM)]
        + [((deep, wide), BF16, VMEM)] * 2
        + layer_weights,
        [sems((4,))],
        micros=2.5,
    )(taps, embed, gate_bias, turn, conv_weight, mix_weight, known)
    mask = 8
    while mask < count:
        known = jnp.concatenate([known, parts[-1]], axis=0)
        parts.append(swapped(known, mask))
        mask *= 2

    rows_x, rows_y = TAPS, channels // 2 + LOCAL // 2
    keep_y, send_y, hidden_high, hidden_low, hots, slopes = call(
        lambda *refs: forward_kernel(count, *refs),
        [SMEM] + [VMEM] * (len(parts) + 4),
        [((2, rows_y, 128), F32, VMEM)] * 2
        + [((2 * length, channels), BF16, VMEM)] * 2
        + [((2, deep, length), BF16, VMEM), ((2 * length, wide), F32, VMEM)],
        [VMEM((4, rows_y, 128), F32)],
        micros=2.0,
    )(dilations, *parts, pre_high, pre_low, cot_high, cot_low)
    keep_x, send_x = call(
        taps_kernel,
        [VMEM] * 3,
        [((2, rows_x, 128), F32, VMEM)] * 2,
        [VMEM((4, rows_x, 128), F32)],
        micros=1.5,
    )(hots, slopes, grad_hidden)

    def halved(keep, received, after):
        outs = [(keep.shape[1:], F32, VMEM)] * 2
        return call(halve_after_kernel, [VMEM] * 3, outs)(keep, received, after)

    def added(kept, received, after, space=VMEM):
        return call(add_after_kernel, [VMEM] * 2 + [space], [(kept.shape, F32, VMEM)])(kept, received, after)[0]

    def touched(value, after, cuts=1):
        shape = (value.shape[0] // cuts, value.shape[1])
        return call(touch_kernel, [VMEM] * 2, [(shape, value.dtype, VMEM)] * cuts)(value, after)

    keep_y, send_y = halved(keep_y, swapped(send_y, 1), keep_x)
    keep_x, send_x = halved(keep_x, swapped(send_x, 1), keep_y)
    sum_y = added(keep_y, swapped(send_y, 2), keep_x)
    out_fwd, out_rev = call(
        outputs_kernel,
        [VMEM] * 6,
        [((length, channels), F32, HBM)] * 2,
        [VMEM((2, length, channels), F32), sems((2,))],
        micros=2.0,
    )(hots, hidden_high, hidden_low, local, last_weight, sum_y)
    sum_x = added(keep_x, swapped(send_x, 2), out_rev, HBM)
    first_high, first_low, second_high, second_low, turn_high, turn_low, *tables = call(
        prepare_kernel,
        [VMEM] * 8,
        [((4, wide, channels), BF16, VMEM)] * 4
        + [(square, BF16, VMEM)] * 2
        + [((CONTEXTS, channels), BF16, VMEM)] * 6
        + [((CONTEXTS, wide), F32, VMEM), ((CONTEXTS, 32), BF16, VMEM)],
        micros=1.4,
    )(first_conv, first_mix, second_conv, second_mix, turn, table, mixed_table, sum_x)
    levels, tables = tables[:4], tables[4:]

    def merged(kernel, rows, mine, theirs, after):
        return call(kernel, [VMEM] * 3, [((rows, 128), F32, VMEM)])(mine, theirs, after)[0]

    merged_x, merged_y = 3 * CONTEXTS, rows_y + EDGE // 2
    piece_y = crossed(sum_y, count, lambda x, y: merged(merge_rest_kernel, merged_y, x, y, turn_low))
    core_y = swapped(piece_y, 1)
    piece_x = crossed(sum_x, count, lambda x, y: merged(merge_taps_kernel, merged_x, x, y, core_y))
    other_y = swapped(piece_y, 2)
    core_x = [swapped(x, 1) for x in touched(piece_x, other_y, 2)]

    far_y = swapped(other_y, 1)
    shared = (*levels, second_high, second_low)
    large = [(conv_weight.shape, F32, HBM), (mix_weight.shape, F32, HBM)]
    level_out = ((CONTEXTS, channels), F32, VMEM)
    quarter_conv, quarter_mix = (3, channels, 128), (channels, 128)
    g_conv, g_mix, bias_own, partial = call(
        own_columns_kernel,
        [VMEM] * 9,
        [*large, ((2, 128), F32, VMEM), level_out],
        [
            VMEM((2, merged_x, 128), F32),
            VMEM((2, *quarter_conv), F32),
            VMEM((2, *quarter_mix), F32),
            sems((8,)),
        ],
        micros=0.05,
    )(piece_x, *core_x, *shared)
    other_x = swapped(piece_x, 2)
    rest_y = touched(far_y, partial)[0]
    far_x = swapped(touched(other_x, rest_y)[0], 1)
    g_conv, g_mix, bias_other, partial = call(
        other_columns_kernel,
        [VMEM] * 8 + [HBM] * 2,
        [*large, ((1, 128), F32, VMEM), level_out],
        [VMEM(quarter_conv, F32), VMEM(quarter_mix, F32), sems((4,))],
        aliases={8: 0, 9: 1},
        micros=0.05,
    )(other_x, *shared, partial, g_conv, g_mix)
    g_conv, g_mix, g_embed, g_bias, g_out = call(
        first_layer_kernel,
        [VMEM] * 23 + [HBM] * 2,
        [*large] + [(shape, F32, HBM) for shape in (embed.shape, gate_bias.shape, out_weight.shape)],
        [
            VMEM((4, merged_y, 128), F32),
            VMEM((4, 1, 128), F32),
            VMEM((1, 128), F32),
            VMEM(quarter_conv, F32),
            VMEM(quarter_mix, F32),
            VMEM(conv_weight.shape[1:], F32),
            VMEM(mix_weight.shape[1:], F32),
            VMEM(embed.shape, F32),
            VMEM(gate_bias.shape, F32),
            VMEM(out_weight.shape, F32),
            sems((11,)),
        ],
        aliases={23: 0, 24: 1},
        micros=2.7,
    )(
        far_x, *shared, piece_y, other_y, core_y, rest_y, partial, bias_own, bias_other, embed,
        first_high, first_low, turn_high, turn_low, *tables, g_conv, g_mix,
    )
    return (out_fwd, out_rev, g_embed, g_conv, g_mix, g_bias, g_out)


def solution(mesh):
    in_specs = (
        P(("dp", "seq")),
        P(),
        P(),
        P(),
        P(),
        P(),
        P(),
        P(("dp", "seq"), None),
        P(("dp", "seq"), None),
    )
    out_specs = (
        P(("dp", "seq"), None),
        P(("dp", "seq"), None),
        P("dp", None),
        P("dp", None, None, None),
        P("dp", None, None),
        P("dp", None),
        P("dp", None, None),
    )
    return jax.shard_map(
        on_device, mesh=mesh, in_specs=in_specs, out_specs=out_specs, check_vma=False
    )
```

```python
import jax
import jax.numpy as jnp
from jax import lax
from jax.experimental import pallas as pl
from jax.experimental.pallas import tpu as pltpu
from jax.sharding import PartitionSpec as P

CONTEXTS = 96
INNER = 64
EDGE = 16
LOCAL = INNER + EDGE
TAPS = 3 * LOCAL
HALO = 128
F32 = jnp.float32
BF16 = jnp.bfloat16
VMEM_LIMIT = 40 * 1024 * 1024


def split(x):
    high = x.astype(BF16)
    return high, (x - high.astype(F32)).astype(BF16)


def dot(a, b, ca=1, cb=0):
    return lax.dot_general(a, b, (((ca,), (cb,)), ((), ())), preferred_element_type=F32)


def dot2(exact, pair, ca=1, cb=0):
    return dot(exact, pair[0], ca, cb) + dot(exact, pair[1], ca, cb)


def dot3(a, b, ca=1, cb=0):
    return dot(a[0], b[0], ca, cb) + (dot(a[0], b[1], ca, cb) + dot(a[1], b[0], ca, cb))


def dot3_few(a, b):
    rows = a[0].shape[0]
    both = dot(jnp.concatenate([a[0].astype(F32), a[1].astype(F32)], axis=0).astype(BF16), b[0])
    return both[:rows] + (both[rows:] + dot(a[0], b[1]))


def letters(index):
    inner = index < 64
    left = (index >= 64) & (index < 80)
    low = index & 3
    mid = (index >> 2) & 3
    l = jnp.where(inner, (index >> 4) & 3, jnp.where(left, -1, mid))
    m = jnp.where(inner | left, mid, low)
    r = jnp.where(inner | left, low, -1)
    return l, m, r


def mirrored(index):
    low = 3 - (index & 3)
    mid = 3 - ((index >> 2) & 3)
    high = 3 - ((index >> 4) & 3)
    inner = low * 16 + mid * 4 + high
    left = 80 + low * 4 + mid
    right = 64 + low * 4 + mid
    return jnp.where(index < 64, inner, jnp.where(index < 80, left, right))


def permutation():
    rows = lax.broadcasted_iota(jnp.int32, (CONTEXTS, CONTEXTS), 0)
    cols = lax.broadcasted_iota(jnp.int32, (CONTEXTS, CONTEXTS), 1)
    return (mirrored(rows) == cols).astype(F32).astype(BF16)


def letter_hot():
    rows = lax.broadcasted_iota(jnp.int32, (CONTEXTS, 32), 0)
    cols = lax.broadcasted_iota(jnp.int32, (CONTEXTS, 32), 1)
    l, m, r = letters(rows)
    kind = cols >> 3
    value = jnp.where(kind == 0, l, jnp.where(kind == 1, m, jnp.where(kind == 2, r, 3 - m)))
    return (value == (cols & 7)).astype(F32).astype(BF16)


def gates(mixed):
    channels = mixed.shape[1] // 2
    tanh_part = jnp.tanh(mixed[:, :channels])
    sig_part = 0.5 + 0.5 * jnp.tanh(0.5 * mixed[:, channels:])
    return tanh_part, sig_part


def gate_grads(grad_hidden, tanh_part, sig_part):
    scaled = grad_hidden * sig_part
    return scaled * (1.0 - tanh_part * tanh_part), scaled * tanh_part * (1.0 - sig_part)


class Fetch:
    def __init__(self, sems):
        self.sems = sems
        self.copies = []

    def start(self, source, target):
        copy = pltpu.make_async_copy(source, target, self.sems.at[len(self.copies)])
        copy.start()
        self.copies.append(copy)
        return len(self.copies) - 1

    def wait(self, *which):
        for at in which:
            self.copies[at].wait()


def padded_base(embed):
    return jnp.concatenate([embed[...], jnp.zeros((4, embed.shape[1]), F32)], axis=0)


def left_side():
    return lax.axis_index("seq") * 2 < lax.axis_size("seq")


def local_rows(rows):
    edge = jnp.where(left_side(), rows[INNER : INNER + EDGE], rows[INNER + EDGE : INNER + 2 * EDGE])
    return jnp.concatenate([rows[:INNER], edge], axis=0)


def join_four_kernel(first, second, third, fourth, after, out):
    for at, part in enumerate((first, second, third, fourth)):
        out[at : at + 1, :] = part[...]


def touch_kernel(value, after, *outs):
    begin = 0
    for out in outs:
        out[...] = value[begin : begin + out.shape[0], :]
        begin += out.shape[0]


def first_tables_kernel(
    tokens_in, embed_in, conv_in, mix_in, out_in, cot_fwd_in, cot_rev_in,
    own, taps, conv, mix, turn, last_weight, cot_high, cot_low, grad_hidden, embed, cots, sems,
):
    length = cots.shape[1]
    fetch = Fetch(sems)
    fetch.start(embed_in, embed)
    first = [fetch.start(conv_in.at[0, k], conv.at[k]) for k in range(3)]
    first += [fetch.start(mix_in.at[0], mix)]
    last = [fetch.start(out_in.at[1], last_weight)]
    last += [fetch.start(cot_in, cots.at[strand]) for strand, cot_in in enumerate((cot_fwd_in, cot_rev_in))]
    rest = [fetch.start(tokens_in, own), fetch.start(out_in.at[0], turn)]
    fetch.wait(0)
    base = split(padded_base(embed))
    for k in range(4):
        fetch.wait(first[k])
        taps[k * 8 : (k + 1) * 8, :] = dot3_few(base, split(conv[k] if k < 3 else mix[...]))
    fetch.wait(last[0])
    weight = split(last_weight[...])
    for strand in range(2):
        rows = slice(strand * length, (strand + 1) * length)
        fetch.wait(last[1 + strand])
        cot = split(cots[strand])
        cot_high[rows, :], cot_low[rows, :] = cot
        grad_hidden[rows, :] = dot3(cot, weight, 1, 1)
    fetch.wait(*rest)


def second_tables_kernel(
    taps, embed, bias, turn, conv_in, mix_in, after, table, local, mixed_table, pre_high, pre_low, conv, mix, sems,
):
    fetch = Fetch(sems)
    second = [fetch.start(conv_in.at[1, k], conv.at[k]) for k in range(3)]
    second += [fetch.start(mix_in.at[1], mix)]
    hot = letter_hot()
    mixed = dot2(hot, split(taps[...])) + bias[0:1, :]
    tanh_part, sig_part = gates(mixed)
    own = dot2(hot[:, 8:16], split(padded_base(embed)))
    level = own + dot3_few(split(tanh_part * sig_part), split(turn[...]))
    table[...] = level
    local[...] = local_rows(level)
    mixed_table[...] = mixed
    level = split(level)
    swap = permutation()
    partner = tuple(dot(swap, piece).astype(BF16) for piece in level)
    pre_high[TAPS:, :] = jnp.zeros((pre_high.shape[0] - TAPS, pre_high.shape[1]), BF16)
    pre_low[TAPS:, :] = jnp.zeros((pre_low.shape[0] - TAPS, pre_low.shape[1]), BF16)
    for k in (0, 2, 1):
        fetch.wait(second[k])
        value = dot3_few(level, split(conv[k]))
        if k == 1:
            fetch.wait(second[3])
            value = value + dot3_few(partner, split(mix[...])) + bias[1:2, :]
        high, low = split(local_rows(value))
        pre_high[k * LOCAL : (k + 1) * LOCAL, :] = high
        pre_low[k * LOCAL : (k + 1) * LOCAL, :] = low


def windows(parts, count):
    length = parts[0].shape[1]
    place = lax.axis_index("seq")
    last = count - 1

    def block(at):
        total, begin = None, 0
        for part in parts:
            rows = lax.broadcasted_iota(jnp.int32, part.shape, 0) + begin
            piece = jnp.sum(jnp.where(rows == (place ^ at), part[...], 0), axis=0, keepdims=True)
            total = piece if total is None else total + piece
            begin += part.shape[0]
        return total

    def window(at):
        before = jnp.where(at == 0, -1, block(jnp.maximum(at - 1, 0))[:, length - HALO :])
        after = jnp.where(at == last, -1, block(jnp.minimum(at + 1, last))[:, :HALO])
        return [before, block(at), after]

    fwd = jnp.concatenate(window(place), axis=1)
    rev = jnp.concatenate(window(last - place), axis=1)
    rev = jnp.where(rev < 0, -1, 3 - rev)
    tiles = rev.shape[1] // 128
    blocks = [rev[:, i * 128 : (i + 1) * 128] for i in reversed(range(tiles))]
    blocks += [jnp.zeros((8 - tiles, 128), jnp.int32)]
    stacked = jnp.concatenate(blocks, axis=0).astype(F32).astype(BF16)
    rows = lax.broadcasted_iota(jnp.int32, (128, 128), 0)
    cols = lax.broadcasted_iota(jnp.int32, (128, 128), 1)
    flip = (rows + cols == 127).astype(F32).astype(BF16)
    turned = dot(stacked, flip).astype(jnp.int32)
    rev = jnp.concatenate([turned[i : i + 1, :] for i in range(tiles)], axis=1)
    return fwd, rev


def local_contexts(window, first, second, length):
    width = window.shape[1]
    base = jnp.broadcast_to(window, (8, width))
    l = pltpu.roll(base, first, 1)
    r = pltpu.roll(base, width - first, 1)
    index = jnp.where(l < 0, INNER + base * 4 + r, jnp.where(r < 0, INNER + l * 4 + base, l * 16 + base * 4 + r))
    index = jnp.where(base < 0, LOCAL, index)
    before = pltpu.roll(index, second, 1)
    after = pltpu.roll(index, width - second, 1)
    return [x[0:1, HALO : HALO + length] for x in (before, index, after)]


def hot_rows(index):
    rows = lax.broadcasted_iota(jnp.int32, (LOCAL, index.shape[1]), 0)
    return (rows == index).astype(F32).astype(BF16)


def deal(quarters, keep, send):
    bit = lax.axis_index("seq") & 1
    keep[...] = quarters[pl.ds(bit * 2, 2)]
    send[...] = quarters[pl.ds((1 - bit) * 2, 2)]


def forward_kernel(count, dil, *refs):
    steps = count.bit_length() - 2
    parts, refs = refs[:steps], refs[steps:]
    (pre_high, pre_low, cot_high, cot_low, keep, send, hidden_high, hidden_low, hots, slopes, quarters) = refs
    length = parts[0].shape[1]
    channels = cot_high.shape[1]
    pre = (pre_high[...], pre_low[...])
    both = windows(parts, count)
    pad = jnp.zeros((pre_high.shape[0] - TAPS, length), BF16)
    total_o = total_c = None
    for strand in range(2):
        index = local_contexts(both[strand], dil[0], dil[1], length)
        hot = jnp.concatenate([hot_rows(x) for x in index] + [pad], axis=0)
        hots[strand] = hot
        mixed = dot2(hot, pre, 0, 0)
        tanh_part, sig_part = gates(mixed)
        product = tanh_part * sig_part
        hidden = split(product)
        rows = slice(strand * length, (strand + 1) * length)
        hidden_high[rows, :] = hidden[0]
        hidden_low[rows, :] = hidden[1]
        slopes[rows, :channels] = sig_part - product * tanh_part
        slopes[rows, channels:] = product - product * sig_part
        cot = (cot_high[rows, :], cot_low[rows, :])
        part_o = dot3(hidden, cot, 0, 0)
        part_c = dot2(hot[LOCAL : 2 * LOCAL], cot)
        total_o = part_o if total_o is None else total_o + part_o
        total_c = part_c if total_c is None else total_c + part_c
    side = channels // 4
    for q in range(4):
        lanes = slice((q >> 1) * 128, (q >> 1) * 128 + 128)
        quarters[q, :side, :] = total_o[q * side : (q + 1) * side, :128]
        quarters[q, side : 2 * side, :] = total_o[q * side : (q + 1) * side, 128:]
        for begin, rows, at in ((0, INNER // 2, 2 * side), (INNER, EDGE // 2, 2 * side + INNER // 2)):
            begin += (q & 1) * rows
            quarters[q, at : at + rows, :] = total_c[begin : begin + rows, lanes]
    deal(quarters, keep, send)


def taps_kernel(hots, slopes, grad_hidden, keep, send, quarters):
    length = hots.shape[2]
    total = None
    for strand in range(2):
        rows = slice(strand * length, (strand + 1) * length)
        grad = grad_hidden[rows, :]
        part = dot2(hots[strand], split(slopes[rows, :] * jnp.concatenate([grad, grad], axis=1)))
        total = part if total is None else total + part
    for q in range(4):
        quarters[q] = total[:TAPS, q * 128 : (q + 1) * 128]
    deal(quarters, keep, send)


def halve_kernel(kept, received, keep, send):
    bit = (lax.axis_index("seq") >> 1) & 1
    send[...] = kept[1 - bit] + received[1 - bit]
    keep[...] = kept[bit] + received[bit]


def add_after_kernel(kept, received, after, out):
    out[...] = kept[...] + received[...]


def halve_after_kernel(kept, received, after, keep, send):
    halve_kernel(kept, received, keep, send)


def outputs_kernel(hots, hidden_high, hidden_low, local, out_w, after, out_fwd, out_rev, values, sems):
    length = hots.shape[2]
    fetch = Fetch(sems)
    weight = split(out_w[...])
    level = split(local[...])
    for strand, out in enumerate((out_fwd, out_rev)):
        rows = slice(strand * length, (strand + 1) * length)
        own = dot2(hots[strand, LOCAL : 2 * LOCAL, :], level, 0, 0)
        values[strand] = own + dot3((hidden_high[rows, :], hidden_low[rows, :]), weight)
        fetch.start(values.at[strand], out)
    fetch.wait(0, 1)


def prepare_kernel(
    first_conv, first_mix, second_conv, second_mix, out_w, table, mixed_table, after,
    first_high, first_low, second_high, second_low, turn_high, turn_low,
    level_high, level_low, partner_high, partner_low, hidden_high, hidden_low, slopes, hot,
):
    level = split(table[...])
    swap = permutation()
    level_high[...], level_low[...] = level
    partner_high[...], partner_low[...] = tuple(dot(swap, piece).astype(BF16) for piece in level)
    for conv, mix, high, low in (
        (second_conv, second_mix, second_high, second_low),
        (first_conv, first_mix, first_high, first_low),
    ):
        for k in range(4):
            high[k], low[k] = split((conv[k] if k < 3 else mix[...]).T)
    turn_high[...], turn_low[...] = split(out_w[...].T)
    tanh_part, sig_part = gates(mixed_table[...])
    product = tanh_part * sig_part
    hidden_high[...], hidden_low[...] = split(product)
    channels = product.shape[1]
    slopes[:, :channels] = sig_part - product * tanh_part
    slopes[:, channels:] = product - product * sig_part
    hot[...] = letter_hot()


def merge(mine, theirs, inner, edge):
    left = left_side()
    both = mine[inner, :] + theirs[inner, :]
    own, other = mine[edge, :], theirs[edge, :]
    return both, jnp.where(left, own, other), jnp.where(left, other, own)


def merge_blocks(mine, theirs, out, sizes):
    at = to = 0
    for inner, edge in sizes:
        pieces = merge(mine, theirs, slice(at, at + inner), slice(at + inner, at + inner + edge))
        out[to : to + inner, :] = pieces[0]
        out[to + inner : to + inner + edge, :] = pieces[1]
        out[to + inner + edge : to + inner + 2 * edge, :] = pieces[2]
        at, to = at + inner + edge, to + inner + 2 * edge


def merge_taps_kernel(mine, theirs, after, out):
    merge_blocks(mine, theirs, out, [(INNER, EDGE)] * 3)


def merge_rest_kernel(mine, theirs, after, out):
    merge_blocks(mine, theirs, out, [(mine.shape[0] - EDGE // 2, EDGE // 2)])


def gather_quarters(pieces, quarters):
    place = lax.axis_index("seq")
    low, high = place & 1, (place >> 1) & 1
    for parts, x, y in zip(pieces, (0, 0, 1, 1), (0, 1, 0, 1)):
        begin = 0
        for part in parts:
            rows = part.shape[0]
            quarters[(low ^ x) * 2 + (high ^ y), begin : begin + rows, :] = part[...]
            begin += rows


def tap_pairs(taps):
    return [split(taps[k * CONTEXTS : (k + 1) * CONTEXTS, :]) for k in range(3)]


def quarter_weights(pairs, taps, levels, g_conv, g_mix, bias):
    level_high, level_low, partner_high, partner_low = levels
    level = (level_high[...], level_low[...])
    partner = (partner_high[...], partner_low[...])
    for k, pair in enumerate(pairs):
        g_conv[k] = dot3(level, pair, 0, 0)
    g_mix[...] = dot3(partner, pairs[1], 0, 0)
    bias[...] = jnp.sum(taps[CONTEXTS : 2 * CONTEXTS, :], axis=0, keepdims=True)


def quarter_part(pairs, column, seconds):
    weights = [tuple(ref[k, pl.ds(column, 128), :] for ref in seconds) for k in range(4)]
    part = dot2(permutation(), split(dot3_few(pairs[1], weights[3])))
    for k, pair in enumerate(pairs):
        part = part + dot3_few(pair, weights[k])
    return part


def column_of(core, chip):
    place = lax.axis_index("seq")
    low, high = place & 1, (place >> 1) & 1
    return pl.multiple_of(((low ^ core) * 2 + (high ^ chip)) * 128, 128)


def store_columns(store, column, g_conv, g_mix, g_conv_out, g_mix_out):
    block = pl.ds(column, 128)
    for k in range(3):
        store.start(g_conv.at[k], g_conv_out.at[1, k, :, block])
    store.start(g_mix, g_mix_out.at[1, :, block])


def fill(taps, first, second):
    half = first.shape[0]
    taps[:half, :] = first[...]
    taps[half:, :] = second[...]


def own_columns_kernel(taps, *refs):
    levels, seconds, refs = refs[:4], refs[4:6], refs[6:]
    after, g_conv_out, g_mix_out, bias, total, g_conv, g_mix, out_sems = refs
    store = Fetch(out_sems)
    column = column_of(0, 0)
    pairs = tap_pairs(taps)
    quarter_weights(pairs, taps, levels, g_conv, g_mix, bias)
    total[...] = quarter_part(pairs, column, seconds)
    store_columns(store, column, g_conv, g_mix, g_conv_out, g_mix_out)
    store.wait(*range(len(store.copies)))


def core_columns_kernel(first, second, *refs):
    levels, seconds, refs = refs[:4], refs[4:6], refs[6:]
    partial, g_conv_in, g_mix_in, g_conv_out, g_mix_out, bias, total, taps, g_conv, g_mix, out_sems = refs
    fill(taps, first, second)
    store = Fetch(out_sems)
    column = column_of(1, 0)
    pairs = tap_pairs(taps)
    quarter_weights(pairs, taps, levels, g_conv, g_mix, bias)
    total[...] = partial[...] + quarter_part(pairs, column, seconds)
    store_columns(store, column, g_conv, g_mix, g_conv_out, g_mix_out)
    store.wait(*range(len(store.copies)))


def other_columns_kernel(taps, *refs):
    levels, seconds, refs = refs[:4], refs[4:6], refs[6:]
    partial, g_conv_in, g_mix_in, g_conv_out, g_mix_out, bias, total, g_conv, g_mix, out_sems = refs
    store = Fetch(out_sems)
    column = column_of(0, 1)
    pairs = tap_pairs(taps)
    quarter_weights(pairs, taps, levels, g_conv, g_mix, bias)
    total[...] = partial[...] + quarter_part(pairs, column, seconds)
    store_columns(store, column, g_conv, g_mix, g_conv_out, g_mix_out)
    store.wait(*range(len(store.copies)))


def first_layer_kernel(
    far_piece, level_high, level_low, partner_high, partner_low, second_high, second_low,
    piece_00, piece_01, piece_10, piece_11, partial, bias_own, bias_core, bias_other, embed,
    first_high, first_low, turn_high, turn_low, hidden_high, hidden_low, slopes, hot_in,
    g_conv_in, g_mix_in, g_conv_out, g_mix_out, g_embed_out, g_bias_out, g_out_out,
    quarters, bias_rows, bias_far, far_conv, far_mix, g_conv, g_mix, g_embed, g_bias, g_out, out_sems,
):
    channels = embed.shape[1]
    store = Fetch(out_sems)
    column = column_of(1, 1)
    pairs = tap_pairs(far_piece)
    far_part = quarter_part(pairs, column, (second_high, second_low))
    gather_quarters([(piece,) for piece in (piece_00, piece_01, piece_10, piece_11)], quarters)
    side = channels // 4
    rest = []
    for begin, rows in ((0, INNER // 2), (INNER // 2, EDGE // 2), (INNER // 2 + EDGE // 2, EDGE // 2)):
        begin += 2 * side
        halves = [[quarters[2 * h + i, begin : begin + rows, :] for i in range(2)] for h in range(2)]
        rest.append(jnp.concatenate([jnp.concatenate(x, axis=0) for x in halves], axis=1))
    grad_level = split(partial[...] + far_part + jnp.concatenate(rest, axis=0))
    grad_hidden = dot3_few(grad_level, (turn_high[...], turn_low[...]))
    grad_mixed = slopes[...] * jnp.concatenate([grad_hidden, grad_hidden], axis=1)
    levels = (level_high, level_low, partner_high, partner_low)
    quarter_weights(pairs, far_piece, levels, far_conv, far_mix, bias_far)
    store_columns(store, column, far_conv, far_mix, g_conv_out, g_mix_out)
    hot = hot_in[...]
    by_letter = dot2(hot, split(grad_mixed), 0, 0)
    base = split(padded_base(embed))
    stacked = jnp.concatenate([base[0].astype(F32), base[0].astype(F32), base[1].astype(F32)], axis=0).astype(BF16)
    pieces = []
    for k in range(4):
        piece = split(by_letter[k * 8 : (k + 1) * 8, :])
        pieces.append(piece)
        high, low = piece[0].astype(F32), piece[1].astype(F32)
        value = dot(stacked, jnp.concatenate([high, low, high], axis=0).astype(BF16), 0, 0)
        if k < 3:
            g_conv[k] = value
            store.start(g_conv.at[k], g_conv_out.at[0, k])
        else:
            g_mix[...] = value
            store.start(g_mix, g_mix_out.at[0])
    g_out[0] = dot3((hidden_high[...], hidden_low[...]), grad_level, 0, 0)
    for q in range(4):
        for h in range(2):
            g_out[1, q * side : (q + 1) * side, h * 128 : (h + 1) * 128] = quarters[q, h * side : (h + 1) * side, :]
    store.start(g_out, g_out_out)
    place = lax.axis_index("seq")
    low, high = place & 1, (place >> 1) & 1
    for row, x, y in (
        (bias_own[...], 0, 0), (bias_core[...], 1, 0), (bias_other[...], 0, 1), (bias_far[...], 1, 1)
    ):
        bias_rows[(low ^ x) * 2 + (high ^ y)] = row
    g_bias[0:1, :] = jnp.sum(grad_mixed, axis=0, keepdims=True)
    g_bias[1:2, :] = jnp.concatenate([bias_rows[q] for q in range(4)], axis=1)
    store.start(g_bias, g_bias_out)
    grad_base = dot2(hot[:, 8:16], grad_level, 0, 0)
    for k in range(4):
        grad_base = grad_base + dot3_few(pieces[k], (first_high[k], first_low[k]))
    g_embed[...] = grad_base[:4, :]
    store.start(g_embed, g_embed_out)
    store.wait(*range(len(store.copies)))


VMEM, SMEM, HBM = pltpu.VMEM, pltpu.SMEM, pltpu.HBM


def call(kernel, ins, outs, scratch=(), aliases=None, micros=0.001):
    run = pl.pallas_call(
        kernel,
        out_shape=[space(shape, kind) for shape, kind, space in outs],
        in_specs=[pl.BlockSpec(memory_space=space) for space in ins],
        out_specs=[pl.BlockSpec(memory_space=space) for _, _, space in outs],
        scratch_shapes=list(scratch),
        input_output_aliases=aliases or {},
        cost_estimate=pl.CostEstimate(flops=int(micros * 1.1e9), bytes_accessed=int(micros * 3e6), transcendentals=0),
        compiler_params=pltpu.CompilerParams(vmem_limit_bytes=VMEM_LIMIT),
    )

    def placed(*args):
        return run(*[pltpu.with_memory_space_constraint(x, HBM) if space is HBM else x for x, space in zip(args, ins)])

    return placed


def swapped(value, mask):
    pairs = [(source, source ^ mask) for source in range(lax.axis_size("seq"))]
    return lax.ppermute(value, "seq", pairs)


def crossed(piece, count, rest):
    mask = 4
    while mask < count // 2:
        piece = piece + swapped(piece, mask)
        mask *= 2
    return rest(piece, swapped(piece, mask))


def on_device(
    tokens, dilations, embed, conv_weight, mix_weight, gate_bias, out_weight, cot_fwd, cot_rev
):
    channels = embed.shape[1]
    wide = 2 * channels
    length = tokens.shape[0]
    count = lax.axis_size("seq")
    sems = pltpu.SemaphoreType.DMA
    square = (channels, channels)

    row = tokens.reshape(1, length)
    near = [swapped(row, mask) for mask in (1, 2, 3)]
    layer_weights = [(conv_weight.shape[1:], F32, VMEM), (mix_weight.shape[1:], F32, VMEM)]
    own, taps, first_conv, first_mix, turn, last_weight, cot_high, cot_low, grad_hidden = call(
        first_tables_kernel,
        [HBM] * 7,
        [(row.shape, row.dtype, VMEM), ((32, wide), F32, VMEM), *layer_weights]
        + [(square, F32, VMEM)] * 2
        + [((2 * length, channels), BF16, VMEM)] * 2
        + [((2 * length, channels), F32, VMEM)],
        [VMEM(embed.shape, F32), VMEM((2, length, channels), F32), sems((10,))],
        micros=2.7,
    )(row, embed, conv_weight, mix_weight, out_weight, cot_fwd, cot_rev)
    known = call(join_four_kernel, [VMEM] * 5, [((4, length), row.dtype, VMEM)])(own, *near, taps)[0]
    parts = [known, swapped(known, 4)]
    deep = -(-TAPS // 128) * 128
    table, local, mixed_table, pre_high, pre_low, second_conv, second_mix = call(
        second_tables_kernel,
        [VMEM] * 4 + [HBM] * 2 + [VMEM],
        [((CONTEXTS, channels), F32, VMEM), ((LOCAL, channels), F32, VMEM), ((CONTEXTS, wide), F32, VMEM)]
        + [((deep, wide), BF16, VMEM)] * 2
        + layer_weights,
        [sems((4,))],
        micros=2.5,
    )(taps, embed, gate_bias, turn, conv_weight, mix_weight, known)
    mask = 8
    while mask < count:
        known = jnp.concatenate([known, parts[-1]], axis=0)
        parts.append(swapped(known, mask))
        mask *= 2

    rows_x, rows_y = TAPS, channels // 2 + LOCAL // 2
    keep_y, send_y, hidden_high, hidden_low, hots, slopes = call(
        lambda *refs: forward_kernel(count, *refs),
        [SMEM] + [VMEM] * (len(parts) + 4),
        [((2, rows_y, 128), F32, VMEM)] * 2
        + [((2 * length, channels), BF16, VMEM)] * 2
        + [((2, deep, length), BF16, VMEM), ((2 * length, wide), F32, VMEM)],
        [VMEM((4, rows_y, 128), F32)],
        micros=2.0,
    )(dilations, *parts, pre_high, pre_low, cot_high, cot_low)
    keep_x, send_x = call(
        taps_kernel,
        [VMEM] * 3,
        [((2, rows_x, 128), F32, VMEM)] * 2,
        [VMEM((4, rows_x, 128), F32)],
        micros=1.5,
    )(hots, slopes, grad_hidden)

    def halved(keep, received, after):
        outs = [(keep.shape[1:], F32, VMEM)] * 2
        return call(halve_after_kernel, [VMEM] * 3, outs)(keep, received, after)

    def added(kept, received, after, space=VMEM):
        return call(add_after_kernel, [VMEM] * 2 + [space], [(kept.shape, F32, VMEM)])(kept, received, after)[0]

    def touched(value, after, cuts=1):
        shape = (value.shape[0] // cuts, value.shape[1])
        return call(touch_kernel, [VMEM] * 2, [(shape, value.dtype, VMEM)] * cuts)(value, after)

    keep_y, send_y = halved(keep_y, swapped(send_y, 1), keep_x)
    keep_x, send_x = halved(keep_x, swapped(send_x, 1), keep_y)
    sum_y = added(keep_y, swapped(send_y, 2), keep_x)
    out_fwd, out_rev = call(
        outputs_kernel,
        [VMEM] * 6,
        [((length, channels), F32, HBM)] * 2,
        [VMEM((2, length, channels), F32), sems((2,))],
        micros=2.0,
    )(hots, hidden_high, hidden_low, local, last_weight, sum_y)
    sum_x = added(keep_x, swapped(send_x, 2), out_rev, HBM)
    first_high, first_low, second_high, second_low, turn_high, turn_low, *tables = call(
        prepare_kernel,
        [VMEM] * 8,
        [((4, wide, channels), BF16, VMEM)] * 4
        + [(square, BF16, VMEM)] * 2
        + [((CONTEXTS, channels), BF16, VMEM)] * 6
        + [((CONTEXTS, wide), F32, VMEM), ((CONTEXTS, 32), BF16, VMEM)],
        micros=1.4,
    )(first_conv, first_mix, second_conv, second_mix, turn, table, mixed_table, sum_x)
    levels, tables = tables[:4], tables[4:]

    def merged(kernel, rows, mine, theirs, after):
        return call(kernel, [VMEM] * 3, [((rows, 128), F32, VMEM)])(mine, theirs, after)[0]

    merged_x, merged_y = 3 * CONTEXTS, rows_y + EDGE // 2
    piece_y = crossed(sum_y, count, lambda x, y: merged(merge_rest_kernel, merged_y, x, y, turn_low))
    core_y = swapped(piece_y, 1)
    piece_x = crossed(sum_x, count, lambda x, y: merged(merge_taps_kernel, merged_x, x, y, core_y))
    other_y = swapped(piece_y, 2)
    halves_x = touched(piece_x, other_y, 2)
    core_x = [swapped(x, 1) for x in halves_x]

    shared = (*levels, second_high, second_low)
    large = [(conv_weight.shape, F32, HBM), (mix_weight.shape, F32, HBM)]
    level_out = ((CONTEXTS, channels), F32, VMEM)
    quarter_conv, quarter_mix = (3, channels, 128), (channels, 128)
    bias_out = ((1, 128), F32, VMEM)
    g_conv, g_mix, bias_own, partial = call(
        own_columns_kernel,
        [VMEM] * 8,
        [*large, bias_out, level_out],
        [VMEM(quarter_conv, F32), VMEM(quarter_mix, F32), sems((4,))],
        micros=1.2,
    )(piece_x, *shared, halves_x[0])
    g_conv, g_mix, bias_core, partial = call(
        core_columns_kernel,
        [VMEM] * 9 + [HBM] * 2,
        [*large, bias_out, level_out],
        [VMEM((merged_x, 128), F32), VMEM(quarter_conv, F32), VMEM(quarter_mix, F32), sems((4,))],
        aliases={9: 0, 10: 1},
        micros=0.05,
    )(*core_x, *shared, partial, g_conv, g_mix)
    other_x = swapped(piece_x, 2)
    late_y = touched(other_y, partial)[0]
    rest_y = swapped(late_y, 1)
    far_x = swapped(touched(other_x, late_y)[0], 1)
    g_conv, g_mix, bias_other, partial = call(
        other_columns_kernel,
        [VMEM] * 8 + [HBM] * 2,
        [*large, ((1, 128), F32, VMEM), level_out],
        [VMEM(quarter_conv, F32), VMEM(quarter_mix, F32), sems((4,))],
        aliases={8: 0, 9: 1},
        micros=0.05,
    )(other_x, *shared, partial, g_conv, g_mix)
    g_conv, g_mix, g_embed, g_bias, g_out = call(
        first_layer_kernel,
        [VMEM] * 24 + [HBM] * 2,
        [*large] + [(shape, F32, HBM) for shape in (embed.shape, gate_bias.shape, out_weight.shape)],
        [
            VMEM((4, merged_y, 128), F32),
            VMEM((4, 1, 128), F32),
            VMEM((1, 128), F32),
            VMEM(quarter_conv, F32),
            VMEM(quarter_mix, F32),
            VMEM(conv_weight.shape[1:], F32),
            VMEM(mix_weight.shape[1:], F32),
            VMEM(embed.shape, F32),
            VMEM(gate_bias.shape, F32),
            VMEM(out_weight.shape, F32),
            sems((11,)),
        ],
        aliases={24: 0, 25: 1},
        micros=2.7,
    )(
        far_x, *shared, piece_y, other_y, core_y, rest_y, partial, bias_own, bias_core, bias_other, embed,
        first_high, first_low, turn_high, turn_low, *tables, g_conv, g_mix,
    )
    return (out_fwd, out_rev, g_embed, g_conv, g_mix, g_bias, g_out)


def solution(mesh):
    in_specs = (
        P(("dp", "seq")),
        P(),
        P(),
        P(),
        P(),
        P(),
        P(),
        P(("dp", "seq"), None),
        P(("dp", "seq"), None),
    )
    out_specs = (
        P(("dp", "seq"), None),
        P(("dp", "seq"), None),
        P("dp", None),
        P("dp", None, None, None),
        P("dp", None, None),
        P("dp", None),
        P("dp", None, None),
    )
    return jax.shard_map(
        on_device, mesh=mesh, in_specs=in_specs, out_specs=out_specs, check_vma=False
    )
```

```python
import jax
import jax.numpy as jnp
from jax import lax
from jax.experimental import pallas as pl
from jax.experimental.pallas import tpu as pltpu
from jax.sharding import PartitionSpec as P

CONTEXTS = 96
INNER = 64
EDGE = 16
LOCAL = INNER + EDGE
TAPS = 3 * LOCAL
HALO = 128
F32 = jnp.float32
BF16 = jnp.bfloat16
VMEM_LIMIT = 40 * 1024 * 1024


def split(x):
    high = x.astype(BF16)
    return high, (x - high.astype(F32)).astype(BF16)


def dot(a, b, ca=1, cb=0):
    return lax.dot_general(a, b, (((ca,), (cb,)), ((), ())), preferred_element_type=F32)


def dot2(exact, pair, ca=1, cb=0):
    return dot(exact, pair[0], ca, cb) + dot(exact, pair[1], ca, cb)


def dot3(a, b, ca=1, cb=0):
    return dot(a[0], b[0], ca, cb) + (dot(a[0], b[1], ca, cb) + dot(a[1], b[0], ca, cb))


def dot3_few(a, b):
    rows = a[0].shape[0]
    both = dot(jnp.concatenate([a[0].astype(F32), a[1].astype(F32)], axis=0).astype(BF16), b[0])
    return both[:rows] + (both[rows:] + dot(a[0], b[1]))


def letters(index):
    inner = index < 64
    left = (index >= 64) & (index < 80)
    low = index & 3
    mid = (index >> 2) & 3
    l = jnp.where(inner, (index >> 4) & 3, jnp.where(left, -1, mid))
    m = jnp.where(inner | left, mid, low)
    r = jnp.where(inner | left, low, -1)
    return l, m, r


def mirrored(index):
    low = 3 - (index & 3)
    mid = 3 - ((index >> 2) & 3)
    high = 3 - ((index >> 4) & 3)
    inner = low * 16 + mid * 4 + high
    left = 80 + low * 4 + mid
    right = 64 + low * 4 + mid
    return jnp.where(index < 64, inner, jnp.where(index < 80, left, right))


def permutation():
    rows = lax.broadcasted_iota(jnp.int32, (CONTEXTS, CONTEXTS), 0)
    cols = lax.broadcasted_iota(jnp.int32, (CONTEXTS, CONTEXTS), 1)
    return (mirrored(rows) == cols).astype(F32).astype(BF16)


def letter_hot():
    rows = lax.broadcasted_iota(jnp.int32, (CONTEXTS, 32), 0)
    cols = lax.broadcasted_iota(jnp.int32, (CONTEXTS, 32), 1)
    l, m, r = letters(rows)
    kind = cols >> 3
    value = jnp.where(kind == 0, l, jnp.where(kind == 1, m, jnp.where(kind == 2, r, 3 - m)))
    return (value == (cols & 7)).astype(F32).astype(BF16)


def gates(mixed):
    channels = mixed.shape[1] // 2
    tanh_part = jnp.tanh(mixed[:, :channels])
    sig_part = 0.5 + 0.5 * jnp.tanh(0.5 * mixed[:, channels:])
    return tanh_part, sig_part


def gate_grads(grad_hidden, tanh_part, sig_part):
    scaled = grad_hidden * sig_part
    return scaled * (1.0 - tanh_part * tanh_part), scaled * tanh_part * (1.0 - sig_part)


class Fetch:
    def __init__(self, sems):
        self.sems = sems
        self.copies = []

    def start(self, source, target):
        copy = pltpu.make_async_copy(source, target, self.sems.at[len(self.copies)])
        copy.start()
        self.copies.append(copy)
        return len(self.copies) - 1

    def wait(self, *which):
        for at in which:
            self.copies[at].wait()


def padded_base(embed):
    return jnp.concatenate([embed[...], jnp.zeros((4, embed.shape[1]), F32)], axis=0)


def left_side():
    return lax.axis_index("seq") * 2 < lax.axis_size("seq")


def local_rows(rows):
    edge = jnp.where(left_side(), rows[INNER : INNER + EDGE], rows[INNER + EDGE : INNER + 2 * EDGE])
    return jnp.concatenate([rows[:INNER], edge], axis=0)


def join_four_kernel(first, second, third, fourth, after, out):
    for at, part in enumerate((first, second, third, fourth)):
        out[at : at + 1, :] = part[...]


def touch_kernel(value, after, *outs):
    begin = 0
    for out in outs:
        out[...] = value[begin : begin + out.shape[0], :]
        begin += out.shape[0]


def first_tables_kernel(
    tokens_in, embed_in, conv_in, mix_in, out_in, cot_fwd_in, cot_rev_in,
    own, taps, conv, mix, turn, last_weight, cot_high, cot_low, grad_hidden, embed, cots, sems,
):
    length = cots.shape[1]
    fetch = Fetch(sems)
    fetch.start(embed_in, embed)
    first = [fetch.start(conv_in.at[0, k], conv.at[k]) for k in range(3)]
    first += [fetch.start(mix_in.at[0], mix)]
    last = [fetch.start(out_in.at[1], last_weight)]
    last += [fetch.start(cot_in, cots.at[strand]) for strand, cot_in in enumerate((cot_fwd_in, cot_rev_in))]
    rest = [fetch.start(tokens_in, own), fetch.start(out_in.at[0], turn)]
    fetch.wait(0)
    base = split(padded_base(embed))
    for k in range(4):
        fetch.wait(first[k])
        taps[k * 8 : (k + 1) * 8, :] = dot3_few(base, split(conv[k] if k < 3 else mix[...]))
    fetch.wait(last[0])
    weight = split(last_weight[...])
    for strand in range(2):
        rows = slice(strand * length, (strand + 1) * length)
        fetch.wait(last[1 + strand])
        cot = split(cots[strand])
        cot_high[rows, :], cot_low[rows, :] = cot
        grad_hidden[rows, :] = dot3(cot, weight, 1, 1)
    fetch.wait(*rest)


def second_tables_kernel(
    taps, embed, bias, turn, conv_in, mix_in, after, table, local, mixed_table, pre_high, pre_low, conv, mix, sems,
):
    fetch = Fetch(sems)
    second = [fetch.start(conv_in.at[1, k], conv.at[k]) for k in range(3)]
    second += [fetch.start(mix_in.at[1], mix)]
    hot = letter_hot()
    mixed = dot2(hot, split(taps[...])) + bias[0:1, :]
    tanh_part, sig_part = gates(mixed)
    own = dot2(hot[:, 8:16], split(padded_base(embed)))
    level = own + dot3_few(split(tanh_part * sig_part), split(turn[...]))
    table[...] = level
    local[...] = local_rows(level)
    mixed_table[...] = mixed
    level = split(level)
    swap = permutation()
    partner = tuple(dot(swap, piece).astype(BF16) for piece in level)
    pre_high[TAPS:, :] = jnp.zeros((pre_high.shape[0] - TAPS, pre_high.shape[1]), BF16)
    pre_low[TAPS:, :] = jnp.zeros((pre_low.shape[0] - TAPS, pre_low.shape[1]), BF16)
    for k in (0, 2, 1):
        fetch.wait(second[k])
        value = dot3_few(level, split(conv[k]))
        if k == 1:
            fetch.wait(second[3])
            value = value + dot3_few(partner, split(mix[...])) + bias[1:2, :]
        high, low = split(local_rows(value))
        pre_high[k * LOCAL : (k + 1) * LOCAL, :] = high
        pre_low[k * LOCAL : (k + 1) * LOCAL, :] = low


def windows(parts, count):
    length = parts[0].shape[1]
    place = lax.axis_index("seq")
    last = count - 1

    def block(at):
        total, begin = None, 0
        for part in parts:
            rows = lax.broadcasted_iota(jnp.int32, part.shape, 0) + begin
            piece = jnp.sum(jnp.where(rows == (place ^ at), part[...], 0), axis=0, keepdims=True)
            total = piece if total is None else total + piece
            begin += part.shape[0]
        return total

    def window(at):
        before = jnp.where(at == 0, -1, block(jnp.maximum(at - 1, 0))[:, length - HALO :])
        after = jnp.where(at == last, -1, block(jnp.minimum(at + 1, last))[:, :HALO])
        return [before, block(at), after]

    fwd = jnp.concatenate(window(place), axis=1)
    rev = jnp.concatenate(window(last - place), axis=1)
    rev = jnp.where(rev < 0, -1, 3 - rev)
    tiles = rev.shape[1] // 128
    blocks = [rev[:, i * 128 : (i + 1) * 128] for i in reversed(range(tiles))]
    blocks += [jnp.zeros((8 - tiles, 128), jnp.int32)]
    stacked = jnp.concatenate(blocks, axis=0).astype(F32).astype(BF16)
    rows = lax.broadcasted_iota(jnp.int32, (128, 128), 0)
    cols = lax.broadcasted_iota(jnp.int32, (128, 128), 1)
    flip = (rows + cols == 127).astype(F32).astype(BF16)
    turned = dot(stacked, flip).astype(jnp.int32)
    rev = jnp.concatenate([turned[i : i + 1, :] for i in range(tiles)], axis=1)
    return fwd, rev


def local_contexts(window, first, second, length):
    width = window.shape[1]
    base = jnp.broadcast_to(window, (8, width))
    l = pltpu.roll(base, first, 1)
    r = pltpu.roll(base, width - first, 1)
    index = jnp.where(l < 0, INNER + base * 4 + r, jnp.where(r < 0, INNER + l * 4 + base, l * 16 + base * 4 + r))
    index = jnp.where(base < 0, LOCAL, index)
    before = pltpu.roll(index, second, 1)
    after = pltpu.roll(index, width - second, 1)
    return [x[0:1, HALO : HALO + length] for x in (before, index, after)]


def hot_rows(index):
    rows = lax.broadcasted_iota(jnp.int32, (LOCAL, index.shape[1]), 0)
    return (rows == index).astype(F32).astype(BF16)


def deal(quarters, keep, send):
    bit = lax.axis_index("seq") & 1
    keep[...] = quarters[pl.ds(bit * 2, 2)]
    send[...] = quarters[pl.ds((1 - bit) * 2, 2)]


def forward_kernel(count, dil, *refs):
    steps = count.bit_length() - 2
    parts, refs = refs[:steps], refs[steps:]
    (pre_high, pre_low, cot_high, cot_low, keep, send, hidden_high, hidden_low, hots, slopes, quarters) = refs
    length = parts[0].shape[1]
    channels = cot_high.shape[1]
    pre = (pre_high[...], pre_low[...])
    both = windows(parts, count)
    pad = jnp.zeros((pre_high.shape[0] - TAPS, length), BF16)
    total_o = total_c = None
    for strand in range(2):
        index = local_contexts(both[strand], dil[0], dil[1], length)
        hot = jnp.concatenate([hot_rows(x) for x in index] + [pad], axis=0)
        hots[strand] = hot
        mixed = dot2(hot, pre, 0, 0)
        tanh_part, sig_part = gates(mixed)
        product = tanh_part * sig_part
        hidden = split(product)
        rows = slice(strand * length, (strand + 1) * length)
        hidden_high[rows, :] = hidden[0]
        hidden_low[rows, :] = hidden[1]
        slopes[rows, :channels] = sig_part - product * tanh_part
        slopes[rows, channels:] = product - product * sig_part
        cot = (cot_high[rows, :], cot_low[rows, :])
        part_o = dot3(hidden, cot, 0, 0)
        part_c = dot2(hot[LOCAL : 2 * LOCAL], cot)
        total_o = part_o if total_o is None else total_o + part_o
        total_c = part_c if total_c is None else total_c + part_c
    side = channels // 4
    for q in range(4):
        lanes = slice((q >> 1) * 128, (q >> 1) * 128 + 128)
        quarters[q, :side, :] = total_o[q * side : (q + 1) * side, :128]
        quarters[q, side : 2 * side, :] = total_o[q * side : (q + 1) * side, 128:]
        for begin, rows, at in ((0, INNER // 2, 2 * side), (INNER, EDGE // 2, 2 * side + INNER // 2)):
            begin += (q & 1) * rows
            quarters[q, at : at + rows, :] = total_c[begin : begin + rows, lanes]
    deal(quarters, keep, send)


def taps_kernel(hots, slopes, grad_hidden, keep, send, quarters):
    length = hots.shape[2]
    total = None
    for strand in range(2):
        rows = slice(strand * length, (strand + 1) * length)
        grad = grad_hidden[rows, :]
        part = dot2(hots[strand], split(slopes[rows, :] * jnp.concatenate([grad, grad], axis=1)))
        total = part if total is None else total + part
    for q in range(4):
        quarters[q] = total[:TAPS, q * 128 : (q + 1) * 128]
    deal(quarters, keep, send)


def halve_kernel(kept, received, keep, send):
    bit = (lax.axis_index("seq") >> 1) & 1
    send[...] = kept[1 - bit] + received[1 - bit]
    keep[...] = kept[bit] + received[bit]


def add_after_kernel(kept, received, after, out):
    out[...] = kept[...] + received[...]


def halve_after_kernel(kept, received, after, keep, send):
    halve_kernel(kept, received, keep, send)


def outputs_kernel(hots, hidden_high, hidden_low, local, out_w, after, out_fwd, out_rev, values, sems):
    length = hots.shape[2]
    fetch = Fetch(sems)
    weight = split(out_w[...])
    level = split(local[...])
    for strand, out in enumerate((out_fwd, out_rev)):
        rows = slice(strand * length, (strand + 1) * length)
        own = dot2(hots[strand, LOCAL : 2 * LOCAL, :], level, 0, 0)
        values[strand] = own + dot3((hidden_high[rows, :], hidden_low[rows, :]), weight)
        fetch.start(values.at[strand], out)
    fetch.wait(0, 1)


def prepare_kernel(
    first_conv, first_mix, second_conv, second_mix, out_w, table, mixed_table, after,
    first_high, first_low, second_high, second_low, turn_high, turn_low,
    level_high, level_low, partner_high, partner_low, hidden_high, hidden_low, slopes, hot,
):
    level = split(table[...])
    swap = permutation()
    level_high[...], level_low[...] = level
    partner_high[...], partner_low[...] = tuple(dot(swap, piece).astype(BF16) for piece in level)
    for conv, mix, high, low in (
        (second_conv, second_mix, second_high, second_low),
        (first_conv, first_mix, first_high, first_low),
    ):
        for k in range(4):
            high[k], low[k] = split((conv[k] if k < 3 else mix[...]).T)
    turn_high[...], turn_low[...] = split(out_w[...].T)
    tanh_part, sig_part = gates(mixed_table[...])
    product = tanh_part * sig_part
    hidden_high[...], hidden_low[...] = split(product)
    channels = product.shape[1]
    slopes[:, :channels] = sig_part - product * tanh_part
    slopes[:, channels:] = product - product * sig_part
    hot[...] = letter_hot()


def merge(mine, theirs, inner, edge):
    left = left_side()
    both = mine[inner, :] + theirs[inner, :]
    own, other = mine[edge, :], theirs[edge, :]
    return both, jnp.where(left, own, other), jnp.where(left, other, own)


def merge_blocks(mine, theirs, out, sizes):
    at = to = 0
    for inner, edge in sizes:
        pieces = merge(mine, theirs, slice(at, at + inner), slice(at + inner, at + inner + edge))
        out[to : to + inner, :] = pieces[0]
        out[to + inner : to + inner + edge, :] = pieces[1]
        out[to + inner + edge : to + inner + 2 * edge, :] = pieces[2]
        at, to = at + inner + edge, to + inner + 2 * edge


def merge_taps_kernel(mine, theirs, after, out):
    merge_blocks(mine, theirs, out, [(INNER, EDGE)] * 3)


def merge_rest_kernel(mine, theirs, after, out):
    merge_blocks(mine, theirs, out, [(mine.shape[0] - EDGE // 2, EDGE // 2)])


def gather_quarters(pieces, quarters):
    place = lax.axis_index("seq")
    low, high = place & 1, (place >> 1) & 1
    for parts, x, y in zip(pieces, (0, 0, 1, 1), (0, 1, 0, 1)):
        begin = 0
        for part in parts:
            rows = part.shape[0]
            quarters[(low ^ x) * 2 + (high ^ y), begin : begin + rows, :] = part[...]
            begin += rows


def tap_pairs(taps):
    return [split(taps[k * CONTEXTS : (k + 1) * CONTEXTS, :]) for k in range(3)]


def quarter_weights(pairs, taps, levels, g_conv, g_mix, bias):
    level_high, level_low, partner_high, partner_low = levels
    level = (level_high[...], level_low[...])
    partner = (partner_high[...], partner_low[...])
    for k, pair in enumerate(pairs):
        g_conv[k] = dot3(level, pair, 0, 0)
    g_mix[...] = dot3(partner, pairs[1], 0, 0)
    bias[...] = jnp.sum(taps[CONTEXTS : 2 * CONTEXTS, :], axis=0, keepdims=True)


def quarter_part(pairs, column, seconds):
    weights = [tuple(ref[k, pl.ds(column, 128), :] for ref in seconds) for k in range(4)]
    part = dot2(permutation(), split(dot3_few(pairs[1], weights[3])))
    for k, pair in enumerate(pairs):
        part = part + dot3_few(pair, weights[k])
    return part


def column_of(core, chip):
    place = lax.axis_index("seq")
    low, high = place & 1, (place >> 1) & 1
    return pl.multiple_of(((low ^ core) * 2 + (high ^ chip)) * 128, 128)


def store_columns(store, column, g_conv, g_mix, g_conv_out, g_mix_out):
    block = pl.ds(column, 128)
    for k in range(3):
        store.start(g_conv.at[k], g_conv_out.at[1, k, :, block])
    store.start(g_mix, g_mix_out.at[1, :, block])


def own_columns_kernel(own_piece, core_first, core_second, *refs):
    levels, seconds, refs = refs[:4], refs[4:6], refs[6:]
    g_conv_out, g_mix_out, bias, total, taps, g_conv, g_mix, out_sems = refs
    store = Fetch(out_sems)
    taps[0] = own_piece[...]
    fill(taps.at[1], core_first, core_second)
    grad_level = None
    for core in range(2):
        column = column_of(core, 0)
        pairs = tap_pairs(taps.at[core])
        quarter_weights(pairs, taps.at[core], levels, g_conv.at[core], g_mix.at[core], bias.at[core : core + 1])
        part = quarter_part(pairs, column, seconds)
        store_columns(store, column, g_conv.at[core], g_mix.at[core], g_conv_out, g_mix_out)
        grad_level = part if grad_level is None else grad_level + part
    total[...] = grad_level
    store.wait(*range(len(store.copies)))


def fill(taps, first, second):
    half = first.shape[0]
    taps[:half, :] = first[...]
    taps[half:, :] = second[...]


def other_columns_kernel(taps, *refs):
    levels, seconds, refs = refs[:4], refs[4:6], refs[6:]
    partial, g_conv_in, g_mix_in, g_conv_out, g_mix_out, bias, total, g_conv, g_mix, out_sems = refs
    store = Fetch(out_sems)
    column = column_of(0, 1)
    pairs = tap_pairs(taps)
    quarter_weights(pairs, taps, levels, g_conv, g_mix, bias)
    total[...] = partial[...] + quarter_part(pairs, column, seconds)
    store_columns(store, column, g_conv, g_mix, g_conv_out, g_mix_out)
    store.wait(*range(len(store.copies)))


def first_layer_kernel(
    far_piece, level_high, level_low, partner_high, partner_low, second_high, second_low,
    piece_00, piece_01, piece_10, piece_11, partial, bias_own, bias_other, embed,
    first_high, first_low, turn_high, turn_low, hidden_high, hidden_low, slopes, hot_in,
    g_conv_in, g_mix_in, g_conv_out, g_mix_out, g_embed_out, g_bias_out, g_out_out,
    quarters, bias_rows, bias_far, far_conv, far_mix, g_conv, g_mix, g_embed, g_bias, g_out, out_sems,
):
    channels = embed.shape[1]
    store = Fetch(out_sems)
    column = column_of(1, 1)
    far_pairs = tap_pairs(far_piece)
    far_part = quarter_part(far_pairs, column, (second_high, second_low))
    gather_quarters([(piece,) for piece in (piece_00, piece_01, piece_10, piece_11)], quarters)
    side = channels // 4
    rest = []
    for begin, rows in ((0, INNER // 2), (INNER // 2, EDGE // 2), (INNER // 2 + EDGE // 2, EDGE // 2)):
        begin += 2 * side
        halves = [[quarters[2 * h + i, begin : begin + rows, :] for i in range(2)] for h in range(2)]
        rest.append(jnp.concatenate([jnp.concatenate(x, axis=0) for x in halves], axis=1))
    grad_level = split(partial[...] + far_part + jnp.concatenate(rest, axis=0))
    grad_hidden = dot3_few(grad_level, (turn_high[...], turn_low[...]))
    grad_mixed = slopes[...] * jnp.concatenate([grad_hidden, grad_hidden], axis=1)
    hot = hot_in[...]
    by_letter = dot2(hot, split(grad_mixed), 0, 0)
    base = split(padded_base(embed))
    stacked = jnp.concatenate([base[0].astype(F32), base[0].astype(F32), base[1].astype(F32)], axis=0).astype(BF16)
    pieces = []
    for k in range(4):
        piece = split(by_letter[k * 8 : (k + 1) * 8, :])
        pieces.append(piece)
        high, low = piece[0].astype(F32), piece[1].astype(F32)
        value = dot(stacked, jnp.concatenate([high, low, high], axis=0).astype(BF16), 0, 0)
        if k < 3:
            g_conv[k] = value
            store.start(g_conv.at[k], g_conv_out.at[0, k])
        else:
            g_mix[...] = value
            store.start(g_mix, g_mix_out.at[0])
    levels = (level_high, level_low, partner_high, partner_low)
    quarter_weights(far_pairs, far_piece, levels, far_conv, far_mix, bias_far)
    store_columns(store, column, far_conv, far_mix, g_conv_out, g_mix_out)
    g_out[0] = dot3((hidden_high[...], hidden_low[...]), grad_level, 0, 0)
    for q in range(4):
        for h in range(2):
            g_out[1, q * side : (q + 1) * side, h * 128 : (h + 1) * 128] = quarters[q, h * side : (h + 1) * side, :]
    store.start(g_out, g_out_out)
    place = lax.axis_index("seq")
    low, high = place & 1, (place >> 1) & 1
    for row, x, y in (
        (bias_own[0:1, :], 0, 0), (bias_own[1:2, :], 1, 0), (bias_other[...], 0, 1), (bias_far[...], 1, 1)
    ):
        bias_rows[(low ^ x) * 2 + (high ^ y)] = row
    g_bias[0:1, :] = jnp.sum(grad_mixed, axis=0, keepdims=True)
    g_bias[1:2, :] = jnp.concatenate([bias_rows[q] for q in range(4)], axis=1)
    store.start(g_bias, g_bias_out)
    grad_base = dot2(hot[:, 8:16], grad_level, 0, 0)
    for k in range(4):
        grad_base = grad_base + dot3_few(pieces[k], (first_high[k], first_low[k]))
    g_embed[...] = grad_base[:4, :]
    store.start(g_embed, g_embed_out)
    store.wait(*range(len(store.copies)))


VMEM, SMEM, HBM = pltpu.VMEM, pltpu.SMEM, pltpu.HBM


def call(kernel, ins, outs, scratch=(), aliases=None, micros=0.001):
    run = pl.pallas_call(
        kernel,
        out_shape=[space(shape, kind) for shape, kind, space in outs],
        in_specs=[pl.BlockSpec(memory_space=space) for space in ins],
        out_specs=[pl.BlockSpec(memory_space=space) for _, _, space in outs],
        scratch_shapes=list(scratch),
        input_output_aliases=aliases or {},
        cost_estimate=pl.CostEstimate(flops=int(micros * 1.1e9), bytes_accessed=int(micros * 3e6), transcendentals=0),
        compiler_params=pltpu.CompilerParams(vmem_limit_bytes=VMEM_LIMIT),
    )

    def placed(*args):
        return run(*[pltpu.with_memory_space_constraint(x, HBM) if space is HBM else x for x, space in zip(args, ins)])

    return placed


def swapped(value, mask):
    pairs = [(source, source ^ mask) for source in range(lax.axis_size("seq"))]
    return lax.ppermute(value, "seq", pairs)


def crossed(piece, count, rest):
    mask = 4
    while mask < count // 2:
        piece = piece + swapped(piece, mask)
        mask *= 2
    return rest(piece, swapped(piece, mask))


def on_device(
    tokens, dilations, embed, conv_weight, mix_weight, gate_bias, out_weight, cot_fwd, cot_rev
):
    channels = embed.shape[1]
    wide = 2 * channels
    length = tokens.shape[0]
    count = lax.axis_size("seq")
    sems = pltpu.SemaphoreType.DMA
    square = (channels, channels)

    row = tokens.reshape(1, length)
    near = [swapped(row, mask) for mask in (1, 2, 3)]
    layer_weights = [(conv_weight.shape[1:], F32, VMEM), (mix_weight.shape[1:], F32, VMEM)]
    own, taps, first_conv, first_mix, turn, last_weight, cot_high, cot_low, grad_hidden = call(
        first_tables_kernel,
        [HBM] * 7,
        [(row.shape, row.dtype, VMEM), ((32, wide), F32, VMEM), *layer_weights]
        + [(square, F32, VMEM)] * 2
        + [((2 * length, channels), BF16, VMEM)] * 2
        + [((2 * length, channels), F32, VMEM)],
        [VMEM(embed.shape, F32), VMEM((2, length, channels), F32), sems((10,))],
        micros=2.7,
    )(row, embed, conv_weight, mix_weight, out_weight, cot_fwd, cot_rev)
    known = call(join_four_kernel, [VMEM] * 5, [((4, length), row.dtype, VMEM)])(own, *near, taps)[0]
    parts = [known, swapped(known, 4)]
    deep = -(-TAPS // 128) * 128
    table, local, mixed_table, pre_high, pre_low, second_conv, second_mix = call(
        second_tables_kernel,
        [VMEM] * 4 + [HBM] * 2 + [VMEM],
        [((CONTEXTS, channels), F32, VMEM), ((LOCAL, channels), F32, VMEM), ((CONTEXTS, wide), F32, VMEM)]
        + [((deep, wide), BF16, VMEM)] * 2
        + layer_weights,
        [sems((4,))],
        micros=2.5,
    )(taps, embed, gate_bias, turn, conv_weight, mix_weight, known)
    mask = 8
    while mask < count:
        known = jnp.concatenate([known, parts[-1]], axis=0)
        parts.append(swapped(known, mask))
        mask *= 2

    rows_x, rows_y = TAPS, channels // 2 + LOCAL // 2
    keep_y, send_y, hidden_high, hidden_low, hots, slopes = call(
        lambda *refs: forward_kernel(count, *refs),
        [SMEM] + [VMEM] * (len(parts) + 4),
        [((2, rows_y, 128), F32, VMEM)] * 2
        + [((2 * length, channels), BF16, VMEM)] * 2
        + [((2, deep, length), BF16, VMEM), ((2 * length, wide), F32, VMEM)],
        [VMEM((4, rows_y, 128), F32)],
        micros=2.0,
    )(dilations, *parts, pre_high, pre_low, cot_high, cot_low)
    keep_x, send_x = call(
        taps_kernel,
        [VMEM] * 3,
        [((2, rows_x, 128), F32, VMEM)] * 2,
        [VMEM((4, rows_x, 128), F32)],
        micros=1.5,
    )(hots, slopes, grad_hidden)

    def halved(keep, received, after):
        outs = [(keep.shape[1:], F32, VMEM)] * 2
        return call(halve_after_kernel, [VMEM] * 3, outs)(keep, received, after)

    def added(kept, received, after, space=VMEM):
        return call(add_after_kernel, [VMEM] * 2 + [space], [(kept.shape, F32, VMEM)])(kept, received, after)[0]

    def touched(value, after, cuts=1):
        shape = (value.shape[0] // cuts, value.shape[1])
        return call(touch_kernel, [VMEM] * 2, [(shape, value.dtype, VMEM)] * cuts)(value, after)

    keep_y, send_y = halved(keep_y, swapped(send_y, 1), keep_x)
    keep_x, send_x = halved(keep_x, swapped(send_x, 1), keep_y)
    sum_y = added(keep_y, swapped(send_y, 2), keep_x)
    out_fwd, out_rev = call(
        outputs_kernel,
        [VMEM] * 6,
        [((length, channels), F32, HBM)] * 2,
        [VMEM((2, length, channels), F32), sems((2,))],
        micros=2.0,
    )(hots, hidden_high, hidden_low, local, last_weight, sum_y)
    sum_x = added(keep_x, swapped(send_x, 2), out_rev, HBM)
    first_high, first_low, second_high, second_low, turn_high, turn_low, *tables = call(
        prepare_kernel,
        [VMEM] * 8,
        [((4, wide, channels), BF16, VMEM)] * 4
        + [(square, BF16, VMEM)] * 2
        + [((CONTEXTS, channels), BF16, VMEM)] * 6
        + [((CONTEXTS, wide), F32, VMEM), ((CONTEXTS, 32), BF16, VMEM)],
        micros=1.4,
    )(first_conv, first_mix, second_conv, second_mix, turn, table, mixed_table, sum_x)
    levels, tables = tables[:4], tables[4:]

    def merged(kernel, rows, mine, theirs, after):
        return call(kernel, [VMEM] * 3, [((rows, 128), F32, VMEM)])(mine, theirs, after)[0]

    merged_x, merged_y = 3 * CONTEXTS, rows_y + EDGE // 2
    piece_y = crossed(sum_y, count, lambda x, y: merged(merge_rest_kernel, merged_y, x, y, turn_low))
    core_y = swapped(piece_y, 1)
    piece_x = crossed(sum_x, count, lambda x, y: merged(merge_taps_kernel, merged_x, x, y, core_y))
    other_y = swapped(piece_y, 2)
    core_x = [swapped(x, 1) for x in touched(piece_x, other_y, 2)]

    far_y = swapped(other_y, 1)
    shared = (*levels, second_high, second_low)
    large = [(conv_weight.shape, F32, HBM), (mix_weight.shape, F32, HBM)]
    level_out = ((CONTEXTS, channels), F32, VMEM)
    quarter_conv, quarter_mix = (3, channels, 128), (channels, 128)
    g_conv, g_mix, bias_own, partial = call(
        own_columns_kernel,
        [VMEM] * 9,
        [*large, ((2, 128), F32, VMEM), level_out],
        [
            VMEM((2, merged_x, 128), F32),
            VMEM((2, *quarter_conv), F32),
            VMEM((2, *quarter_mix), F32),
            sems((8,)),
        ],
        micros=0.05,
    )(piece_x, *core_x, *shared)
    other_x = swapped(piece_x, 2)
    rest_y = touched(far_y, partial)[0]
    far_x = swapped(touched(other_x, rest_y)[0], 1)
    g_conv, g_mix, bias_other, partial = call(
        other_columns_kernel,
        [VMEM] * 8 + [HBM] * 2,
        [*large, ((1, 128), F32, VMEM), level_out],
        [VMEM(quarter_conv, F32), VMEM(quarter_mix, F32), sems((4,))],
        aliases={8: 0, 9: 1},
        micros=0.05,
    )(other_x, *shared, partial, g_conv, g_mix)
    g_conv, g_mix, g_embed, g_bias, g_out = call(
        first_layer_kernel,
        [VMEM] * 23 + [HBM] * 2,
        [*large] + [(shape, F32, HBM) for shape in (embed.shape, gate_bias.shape, out_weight.shape)],
        [
            VMEM((4, merged_y, 128), F32),
            VMEM((4, 1, 128), F32),
            VMEM((1, 128), F32),
            VMEM(quarter_conv, F32),
            VMEM(quarter_mix, F32),
            VMEM(conv_weight.shape[1:], F32),
            VMEM(mix_weight.shape[1:], F32),
            VMEM(embed.shape, F32),
            VMEM(gate_bias.shape, F32),
            VMEM(out_weight.shape, F32),
            sems((11,)),
        ],
        aliases={23: 0, 24: 1},
        micros=2.7,
    )(
        far_x, *shared, piece_y, other_y, core_y, rest_y, partial, bias_own, bias_other, embed,
        first_high, first_low, turn_high, turn_low, *tables, g_conv, g_mix,
    )
    return (out_fwd, out_rev, g_embed, g_conv, g_mix, g_bias, g_out)


def solution(mesh):
    in_specs = (
        P(("dp", "seq")),
        P(),
        P(),
        P(),
        P(),
        P(),
        P(),
        P(("dp", "seq"), None),
        P(("dp", "seq"), None),
    )
    out_specs = (
        P(("dp", "seq"), None),
        P(("dp", "seq"), None),
        P("dp", None),
        P("dp", None, None, None),
        P("dp", None, None),
        P("dp", None),
        P("dp", None, None),
    )
    return jax.shard_map(
        on_device, mesh=mesh, in_specs=in_specs, out_specs=out_specs, check_vma=False
    )
```

```python
import jax
import jax.numpy as jnp
from jax import lax
from jax.experimental import pallas as pl
from jax.experimental.pallas import tpu as pltpu
from jax.sharding import PartitionSpec as P

CONTEXTS = 96
INNER = 64
EDGE = 16
LOCAL = INNER + EDGE
TAPS = 3 * LOCAL
HALO = 128
F32 = jnp.float32
BF16 = jnp.bfloat16
VMEM_LIMIT = 40 * 1024 * 1024


def split(x):
    high = x.astype(BF16)
    return high, (x - high.astype(F32)).astype(BF16)


def dot(a, b, ca=1, cb=0):
    return lax.dot_general(a, b, (((ca,), (cb,)), ((), ())), preferred_element_type=F32)


def dot2(exact, pair, ca=1, cb=0):
    return dot(exact, pair[0], ca, cb) + dot(exact, pair[1], ca, cb)


def dot3(a, b, ca=1, cb=0):
    return dot(a[0], b[0], ca, cb) + (dot(a[0], b[1], ca, cb) + dot(a[1], b[0], ca, cb))


def dot3_few(a, b):
    rows = a[0].shape[0]
    both = dot(jnp.concatenate([a[0].astype(F32), a[1].astype(F32)], axis=0).astype(BF16), b[0])
    return both[:rows] + (both[rows:] + dot(a[0], b[1]))


def letters(index):
    inner = index < 64
    left = (index >= 64) & (index < 80)
    low = index & 3
    mid = (index >> 2) & 3
    l = jnp.where(inner, (index >> 4) & 3, jnp.where(left, -1, mid))
    m = jnp.where(inner | left, mid, low)
    r = jnp.where(inner | left, low, -1)
    return l, m, r


def mirrored(index):
    low = 3 - (index & 3)
    mid = 3 - ((index >> 2) & 3)
    high = 3 - ((index >> 4) & 3)
    inner = low * 16 + mid * 4 + high
    left = 80 + low * 4 + mid
    right = 64 + low * 4 + mid
    return jnp.where(index < 64, inner, jnp.where(index < 80, left, right))


def permutation():
    rows = lax.broadcasted_iota(jnp.int32, (CONTEXTS, CONTEXTS), 0)
    cols = lax.broadcasted_iota(jnp.int32, (CONTEXTS, CONTEXTS), 1)
    return (mirrored(rows) == cols).astype(F32).astype(BF16)


def letter_hot():
    rows = lax.broadcasted_iota(jnp.int32, (CONTEXTS, 32), 0)
    cols = lax.broadcasted_iota(jnp.int32, (CONTEXTS, 32), 1)
    l, m, r = letters(rows)
    kind = cols >> 3
    value = jnp.where(kind == 0, l, jnp.where(kind == 1, m, jnp.where(kind == 2, r, 3 - m)))
    return (value == (cols & 7)).astype(F32).astype(BF16)


def gates(mixed):
    channels = mixed.shape[1] // 2
    tanh_part = jnp.tanh(mixed[:, :channels])
    sig_part = 0.5 + 0.5 * jnp.tanh(0.5 * mixed[:, channels:])
    return tanh_part, sig_part


def gate_grads(grad_hidden, tanh_part, sig_part):
    scaled = grad_hidden * sig_part
    return scaled * (1.0 - tanh_part * tanh_part), scaled * tanh_part * (1.0 - sig_part)


class Fetch:
    def __init__(self, sems):
        self.sems = sems
        self.copies = []

    def start(self, source, target):
        copy = pltpu.make_async_copy(source, target, self.sems.at[len(self.copies)])
        copy.start()
        self.copies.append(copy)
        return len(self.copies) - 1

    def wait(self, *which):
        for at in which:
            self.copies[at].wait()


def padded_base(embed):
    return jnp.concatenate([embed[...], jnp.zeros((4, embed.shape[1]), F32)], axis=0)


def left_side():
    return lax.axis_index("seq") * 2 < lax.axis_size("seq")


def local_rows(rows):
    edge = jnp.where(left_side(), rows[INNER : INNER + EDGE], rows[INNER + EDGE : INNER + 2 * EDGE])
    return jnp.concatenate([rows[:INNER], edge], axis=0)


def join_four_kernel(first, second, third, fourth, after, out):
    for at, part in enumerate((first, second, third, fourth)):
        out[at : at + 1, :] = part[...]


def touch_kernel(value, after, *outs):
    begin = 0
    for out in outs:
        out[...] = value[begin : begin + out.shape[0], :]
        begin += out.shape[0]


def first_tables_kernel(
    tokens_in, embed_in, conv_in, mix_in, out_in, cot_fwd_in, cot_rev_in,
    own, taps, conv, mix, turn, last_weight, cot_high, cot_low, grad_hidden, embed, cots, sems,
):
    length = cots.shape[1]
    fetch = Fetch(sems)
    fetch.start(embed_in, embed)
    first = [fetch.start(conv_in.at[0, k], conv.at[k]) for k in range(3)]
    first += [fetch.start(mix_in.at[0], mix)]
    last = [fetch.start(out_in.at[1], last_weight)]
    last += [fetch.start(cot_in, cots.at[strand]) for strand, cot_in in enumerate((cot_fwd_in, cot_rev_in))]
    rest = [fetch.start(tokens_in, own), fetch.start(out_in.at[0], turn)]
    fetch.wait(0)
    base = split(padded_base(embed))
    for k in range(4):
        fetch.wait(first[k])
        taps[k * 8 : (k + 1) * 8, :] = dot3_few(base, split(conv[k] if k < 3 else mix[...]))
    fetch.wait(last[0])
    weight = split(last_weight[...])
    for strand in range(2):
        rows = slice(strand * length, (strand + 1) * length)
        fetch.wait(last[1 + strand])
        cot = split(cots[strand])
        cot_high[rows, :], cot_low[rows, :] = cot
        grad_hidden[rows, :] = dot3(cot, weight, 1, 1)
    fetch.wait(*rest)


def second_tables_kernel(
    taps, embed, bias, turn, conv_in, mix_in, after, table, local, mixed_table, pre_high, pre_low, conv, mix, sems,
):
    fetch = Fetch(sems)
    second = [fetch.start(conv_in.at[1, k], conv.at[k]) for k in range(3)]
    second += [fetch.start(mix_in.at[1], mix)]
    hot = letter_hot()
    mixed = dot2(hot, split(taps[...])) + bias[0:1, :]
    tanh_part, sig_part = gates(mixed)
    own = dot2(hot[:, 8:16], split(padded_base(embed)))
    level = own + dot3_few(split(tanh_part * sig_part), split(turn[...]))
    table[...] = level
    local[...] = local_rows(level)
    mixed_table[...] = mixed
    level = split(level)
    swap = permutation()
    partner = tuple(dot(swap, piece).astype(BF16) for piece in level)
    pre_high[TAPS:, :] = jnp.zeros((pre_high.shape[0] - TAPS, pre_high.shape[1]), BF16)
    pre_low[TAPS:, :] = jnp.zeros((pre_low.shape[0] - TAPS, pre_low.shape[1]), BF16)
    for k in (0, 2, 1):
        fetch.wait(second[k])
        value = dot3_few(level, split(conv[k]))
        if k == 1:
            fetch.wait(second[3])
            value = value + dot3_few(partner, split(mix[...])) + bias[1:2, :]
        high, low = split(local_rows(value))
        pre_high[k * LOCAL : (k + 1) * LOCAL, :] = high
        pre_low[k * LOCAL : (k + 1) * LOCAL, :] = low


def windows(parts, count):
    length = parts[0].shape[1]
    place = lax.axis_index("seq")
    last = count - 1

    def block(at):
        total, begin = None, 0
        for part in parts:
            rows = lax.broadcasted_iota(jnp.int32, part.shape, 0) + begin
            piece = jnp.sum(jnp.where(rows == (place ^ at), part[...], 0), axis=0, keepdims=True)
            total = piece if total is None else total + piece
            begin += part.shape[0]
        return total

    def window(at):
        before = jnp.where(at == 0, -1, block(jnp.maximum(at - 1, 0))[:, length - HALO :])
        after = jnp.where(at == last, -1, block(jnp.minimum(at + 1, last))[:, :HALO])
        return [before, block(at), after]

    fwd = jnp.concatenate(window(place), axis=1)
    rev = jnp.concatenate(window(last - place), axis=1)
    rev = jnp.where(rev < 0, -1, 3 - rev)
    tiles = rev.shape[1] // 128
    blocks = [rev[:, i * 128 : (i + 1) * 128] for i in reversed(range(tiles))]
    blocks += [jnp.zeros((8 - tiles, 128), jnp.int32)]
    stacked = jnp.concatenate(blocks, axis=0).astype(F32).astype(BF16)
    rows = lax.broadcasted_iota(jnp.int32, (128, 128), 0)
    cols = lax.broadcasted_iota(jnp.int32, (128, 128), 1)
    flip = (rows + cols == 127).astype(F32).astype(BF16)
    turned = dot(stacked, flip).astype(jnp.int32)
    rev = jnp.concatenate([turned[i : i + 1, :] for i in range(tiles)], axis=1)
    return fwd, rev


def local_contexts(window, first, second, length):
    width = window.shape[1]
    base = jnp.broadcast_to(window, (8, width))
    l = pltpu.roll(base, first, 1)
    r = pltpu.roll(base, width - first, 1)
    index = jnp.where(l < 0, INNER + base * 4 + r, jnp.where(r < 0, INNER + l * 4 + base, l * 16 + base * 4 + r))
    index = jnp.where(base < 0, LOCAL, index)
    before = pltpu.roll(index, second, 1)
    after = pltpu.roll(index, width - second, 1)
    return [x[0:1, HALO : HALO + length] for x in (before, index, after)]


def hot_rows(index):
    rows = lax.broadcasted_iota(jnp.int32, (LOCAL, index.shape[1]), 0)
    return (rows == index).astype(F32).astype(BF16)


def deal(quarters, keep, send):
    bit = lax.axis_index("seq") & 1
    keep[...] = quarters[pl.ds(bit * 2, 2)]
    send[...] = quarters[pl.ds((1 - bit) * 2, 2)]


def forward_kernel(count, dil, *refs):
    steps = count.bit_length() - 2
    parts, refs = refs[:steps], refs[steps:]
    (pre_high, pre_low, cot_high, cot_low, keep, send, hidden_high, hidden_low, hots, slopes, quarters) = refs
    length = parts[0].shape[1]
    channels = cot_high.shape[1]
    pre = (pre_high[...], pre_low[...])
    both = windows(parts, count)
    pad = jnp.zeros((pre_high.shape[0] - TAPS, length), BF16)
    total_o = total_c = None
    for strand in range(2):
        index = local_contexts(both[strand], dil[0], dil[1], length)
        hot = jnp.concatenate([hot_rows(x) for x in index] + [pad], axis=0)
        hots[strand] = hot
        mixed = dot2(hot, pre, 0, 0)
        tanh_part, sig_part = gates(mixed)
        product = tanh_part * sig_part
        hidden = split(product)
        rows = slice(strand * length, (strand + 1) * length)
        hidden_high[rows, :] = hidden[0]
        hidden_low[rows, :] = hidden[1]
        slopes[rows, :channels] = sig_part - product * tanh_part
        slopes[rows, channels:] = product - product * sig_part
        cot = (cot_high[rows, :], cot_low[rows, :])
        part_o = dot3(hidden, cot, 0, 0)
        part_c = dot2(hot[LOCAL : 2 * LOCAL], cot)
        total_o = part_o if total_o is None else total_o + part_o
        total_c = part_c if total_c is None else total_c + part_c
    side = channels // 4
    for q in range(4):
        lanes = slice((q >> 1) * 128, (q >> 1) * 128 + 128)
        quarters[q, :side, :] = total_o[q * side : (q + 1) * side, :128]
        quarters[q, side : 2 * side, :] = total_o[q * side : (q + 1) * side, 128:]
        for begin, rows, at in ((0, INNER // 2, 2 * side), (INNER, EDGE // 2, 2 * side + INNER // 2)):
            begin += (q & 1) * rows
            quarters[q, at : at + rows, :] = total_c[begin : begin + rows, lanes]
    deal(quarters, keep, send)


def taps_kernel(hots, slopes, grad_hidden, keep, send, quarters):
    length = hots.shape[2]
    total = None
    for strand in range(2):
        rows = slice(strand * length, (strand + 1) * length)
        grad = grad_hidden[rows, :]
        part = dot2(hots[strand], split(slopes[rows, :] * jnp.concatenate([grad, grad], axis=1)))
        total = part if total is None else total + part
    for q in range(4):
        quarters[q] = total[:TAPS, q * 128 : (q + 1) * 128]
    deal(quarters, keep, send)


def halve_kernel(kept, received, keep, send):
    bit = (lax.axis_index("seq") >> 1) & 1
    send[...] = kept[1 - bit] + received[1 - bit]
    keep[...] = kept[bit] + received[bit]


def add_after_kernel(kept, received, after, out):
    out[...] = kept[...] + received[...]


def halve_after_kernel(kept, received, after, keep, send):
    halve_kernel(kept, received, keep, send)


def outputs_kernel(hots, hidden_high, hidden_low, local, out_w, after, out_fwd, out_rev, values, sems):
    length = hots.shape[2]
    fetch = Fetch(sems)
    weight = split(out_w[...])
    level = split(local[...])
    for strand, out in enumerate((out_fwd, out_rev)):
        rows = slice(strand * length, (strand + 1) * length)
        own = dot2(hots[strand, LOCAL : 2 * LOCAL, :], level, 0, 0)
        values[strand] = own + dot3((hidden_high[rows, :], hidden_low[rows, :]), weight)
        fetch.start(values.at[strand], out)
    fetch.wait(0, 1)


def prepare_kernel(
    first_conv, first_mix, second_conv, second_mix, out_w, table, mixed_table, after,
    first_high, first_low, second_high, second_low, turn_high, turn_low,
    level_high, level_low, partner_high, partner_low, hidden_high, hidden_low, slopes, hot,
):
    level = split(table[...])
    swap = permutation()
    level_high[...], level_low[...] = level
    partner_high[...], partner_low[...] = tuple(dot(swap, piece).astype(BF16) for piece in level)
    for conv, mix, high, low in (
        (second_conv, second_mix, second_high, second_low),
        (first_conv, first_mix, first_high, first_low),
    ):
        for k in range(4):
            high[k], low[k] = split((conv[k] if k < 3 else mix[...]).T)
    turn_high[...], turn_low[...] = split(out_w[...].T)
    tanh_part, sig_part = gates(mixed_table[...])
    product = tanh_part * sig_part
    hidden_high[...], hidden_low[...] = split(product)
    channels = product.shape[1]
    slopes[:, :channels] = sig_part - product * tanh_part
    slopes[:, channels:] = product - product * sig_part
    hot[...] = letter_hot()


def merge(mine, theirs, inner, edge):
    left = left_side()
    both = mine[inner, :] + theirs[inner, :]
    own, other = mine[edge, :], theirs[edge, :]
    return both, jnp.where(left, own, other), jnp.where(left, other, own)


def merge_blocks(mine, theirs, out, sizes):
    at = to = 0
    for inner, edge in sizes:
        pieces = merge(mine, theirs, slice(at, at + inner), slice(at + inner, at + inner + edge))
        out[to : to + inner, :] = pieces[0]
        out[to + inner : to + inner + edge, :] = pieces[1]
        out[to + inner + edge : to + inner + 2 * edge, :] = pieces[2]
        at, to = at + inner + edge, to + inner + 2 * edge


def merge_taps_kernel(mine, theirs, after, out):
    merge_blocks(mine, theirs, out, [(INNER, EDGE)] * 3)


def merge_rest_kernel(mine, theirs, after, out):
    merge_blocks(mine, theirs, out, [(mine.shape[0] - EDGE // 2, EDGE // 2)])


def gather_quarters(pieces, quarters):
    place = lax.axis_index("seq")
    low, high = place & 1, (place >> 1) & 1
    for parts, x, y in zip(pieces, (0, 0, 1, 1), (0, 1, 0, 1)):
        begin = 0
        for part in parts:
            rows = part.shape[0]
            quarters[(low ^ x) * 2 + (high ^ y), begin : begin + rows, :] = part[...]
            begin += rows


def tap_pairs(taps):
    return [split(taps[k * CONTEXTS : (k + 1) * CONTEXTS, :]) for k in range(3)]


def quarter_weights(pairs, taps, levels, g_conv, g_mix, bias):
    level_high, level_low, partner_high, partner_low = levels
    level = (level_high[...], level_low[...])
    partner = (partner_high[...], partner_low[...])
    for k, pair in enumerate(pairs):
        g_conv[k] = dot3(level, pair, 0, 0)
    g_mix[...] = dot3(partner, pairs[1], 0, 0)
    bias[...] = jnp.sum(taps[CONTEXTS : 2 * CONTEXTS, :], axis=0, keepdims=True)


def quarter_part(pairs, column, seconds):
    weights = [tuple(ref[k, pl.ds(column, 128), :] for ref in seconds) for k in range(4)]
    part = dot2(permutation(), split(dot3_few(pairs[1], weights[3])))
    for k, pair in enumerate(pairs):
        part = part + dot3_few(pair, weights[k])
    return part


def column_of(core, chip):
    place = lax.axis_index("seq")
    low, high = place & 1, (place >> 1) & 1
    return pl.multiple_of(((low ^ core) * 2 + (high ^ chip)) * 128, 128)


def store_columns(store, column, g_conv, g_mix, g_conv_out, g_mix_out):
    block = pl.ds(column, 128)
    for k in range(3):
        store.start(g_conv.at[k], g_conv_out.at[1, k, :, block])
    store.start(g_mix, g_mix_out.at[1, :, block])


def own_columns_kernel(own_piece, core_first, core_second, *refs):
    levels, seconds, refs = refs[:4], refs[4:6], refs[6:]
    g_conv_out, g_mix_out, bias, total, taps, g_conv, g_mix, out_sems = refs
    store = Fetch(out_sems)
    taps[0] = own_piece[...]
    fill(taps.at[1], core_first, core_second)
    grad_level = None
    for core in range(2):
        column = column_of(core, 0)
        pairs = tap_pairs(taps.at[core])
        quarter_weights(pairs, taps.at[core], levels, g_conv.at[core], g_mix.at[core], bias.at[core : core + 1])
        part = quarter_part(pairs, column, seconds)
        store_columns(store, column, g_conv.at[core], g_mix.at[core], g_conv_out, g_mix_out)
        grad_level = part if grad_level is None else grad_level + part
    total[...] = grad_level
    store.wait(*range(len(store.copies)))


def fill(taps, first, second):
    half = first.shape[0]
    taps[:half, :] = first[...]
    taps[half:, :] = second[...]


def other_columns_kernel(taps, *refs):
    levels, seconds, refs = refs[:4], refs[4:6], refs[6:]
    partial, g_conv_in, g_mix_in, g_conv_out, g_mix_out, bias, total, g_conv, g_mix, out_sems = refs
    store = Fetch(out_sems)
    column = column_of(0, 1)
    pairs = tap_pairs(taps)
    quarter_weights(pairs, taps, levels, g_conv, g_mix, bias)
    total[...] = partial[...] + quarter_part(pairs, column, seconds)
    store_columns(store, column, g_conv, g_mix, g_conv_out, g_mix_out)
    store.wait(*range(len(store.copies)))


def first_layer_kernel(
    far_piece, level_high, level_low, partner_high, partner_low, second_high, second_low,
    piece_00, piece_01, piece_10, piece_11, partial, bias_own, bias_other, embed,
    first_high, first_low, turn_high, turn_low, hidden_high, hidden_low, slopes, hot_in,
    g_conv_in, g_mix_in, g_conv_out, g_mix_out, g_embed_out, g_bias_out, g_out_out,
    quarters, bias_rows, bias_far, far_conv, far_mix, g_conv, g_mix, g_embed, g_bias, g_out, out_sems,
):
    channels = embed.shape[1]
    store = Fetch(out_sems)
    column = column_of(1, 1)
    pairs = tap_pairs(far_piece)
    far_part = quarter_part(pairs, column, (second_high, second_low))
    gather_quarters([(piece,) for piece in (piece_00, piece_01, piece_10, piece_11)], quarters)
    side = channels // 4
    rest = []
    for begin, rows in ((0, INNER // 2), (INNER // 2, EDGE // 2), (INNER // 2 + EDGE // 2, EDGE // 2)):
        begin += 2 * side
        halves = [[quarters[2 * h + i, begin : begin + rows, :] for i in range(2)] for h in range(2)]
        rest.append(jnp.concatenate([jnp.concatenate(x, axis=0) for x in halves], axis=1))
    grad_level = split(partial[...] + far_part + jnp.concatenate(rest, axis=0))
    grad_hidden = dot3_few(grad_level, (turn_high[...], turn_low[...]))
    grad_mixed = slopes[...] * jnp.concatenate([grad_hidden, grad_hidden], axis=1)
    levels = (level_high, level_low, partner_high, partner_low)
    quarter_weights(pairs, far_piece, levels, far_conv, far_mix, bias_far)
    store_columns(store, column, far_conv, far_mix, g_conv_out, g_mix_out)
    hot = hot_in[...]
    by_letter = dot2(hot, split(grad_mixed), 0, 0)
    base = split(padded_base(embed))
    stacked = jnp.concatenate([base[0].astype(F32), base[0].astype(F32), base[1].astype(F32)], axis=0).astype(BF16)
    pieces = []
    for k in range(4):
        piece = split(by_letter[k * 8 : (k + 1) * 8, :])
        pieces.append(piece)
        high, low = piece[0].astype(F32), piece[1].astype(F32)
        value = dot(stacked, jnp.concatenate([high, low, high], axis=0).astype(BF16), 0, 0)
        if k < 3:
            g_conv[k] = value
            store.start(g_conv.at[k], g_conv_out.at[0, k])
        else:
            g_mix[...] = value
            store.start(g_mix, g_mix_out.at[0])
    g_out[0] = dot3((hidden_high[...], hidden_low[...]), grad_level, 0, 0)
    for q in range(4):
        for h in range(2):
            g_out[1, q * side : (q + 1) * side, h * 128 : (h + 1) * 128] = quarters[q, h * side : (h + 1) * side, :]
    store.start(g_out, g_out_out)
    place = lax.axis_index("seq")
    low, high = place & 1, (place >> 1) & 1
    for row, x, y in (
        (bias_own[0:1, :], 0, 0), (bias_own[1:2, :], 1, 0), (bias_other[...], 0, 1), (bias_far[...], 1, 1)
    ):
        bias_rows[(low ^ x) * 2 + (high ^ y)] = row
    g_bias[0:1, :] = jnp.sum(grad_mixed, axis=0, keepdims=True)
    g_bias[1:2, :] = jnp.concatenate([bias_rows[q] for q in range(4)], axis=1)
    store.start(g_bias, g_bias_out)
    grad_base = dot2(hot[:, 8:16], grad_level, 0, 0)
    for k in range(4):
        grad_base = grad_base + dot3_few(pieces[k], (first_high[k], first_low[k]))
    g_embed[...] = grad_base[:4, :]
    store.start(g_embed, g_embed_out)
    store.wait(*range(len(store.copies)))


VMEM, SMEM, HBM = pltpu.VMEM, pltpu.SMEM, pltpu.HBM


def call(kernel, ins, outs, scratch=(), aliases=None, micros=0.001):
    run = pl.pallas_call(
        kernel,
        out_shape=[space(shape, kind) for shape, kind, space in outs],
        in_specs=[pl.BlockSpec(memory_space=space) for space in ins],
        out_specs=[pl.BlockSpec(memory_space=space) for _, _, space in outs],
        scratch_shapes=list(scratch),
        input_output_aliases=aliases or {},
        cost_estimate=pl.CostEstimate(flops=int(micros * 1.1e9), bytes_accessed=int(micros * 3e6), transcendentals=0),
        compiler_params=pltpu.CompilerParams(vmem_limit_bytes=VMEM_LIMIT),
    )

    def placed(*args):
        return run(*[pltpu.with_memory_space_constraint(x, HBM) if space is HBM else x for x, space in zip(args, ins)])

    return placed


def swapped(value, mask):
    pairs = [(source, source ^ mask) for source in range(lax.axis_size("seq"))]
    return lax.ppermute(value, "seq", pairs)


def crossed(piece, count, rest):
    mask = 4
    while mask < count // 2:
        piece = piece + swapped(piece, mask)
        mask *= 2
    return rest(piece, swapped(piece, mask))


def on_device(
    tokens, dilations, embed, conv_weight, mix_weight, gate_bias, out_weight, cot_fwd, cot_rev
):
    channels = embed.shape[1]
    wide = 2 * channels
    length = tokens.shape[0]
    count = lax.axis_size("seq")
    sems = pltpu.SemaphoreType.DMA
    square = (channels, channels)

    row = tokens.reshape(1, length)
    near = [swapped(row, mask) for mask in (1, 2, 3)]
    layer_weights = [(conv_weight.shape[1:], F32, VMEM), (mix_weight.shape[1:], F32, VMEM)]
    own, taps, first_conv, first_mix, turn, last_weight, cot_high, cot_low, grad_hidden = call(
        first_tables_kernel,
        [HBM] * 7,
        [(row.shape, row.dtype, VMEM), ((32, wide), F32, VMEM), *layer_weights]
        + [(square, F32, VMEM)] * 2
        + [((2 * length, channels), BF16, VMEM)] * 2
        + [((2 * length, channels), F32, VMEM)],
        [VMEM(embed.shape, F32), VMEM((2, length, channels), F32), sems((10,))],
        micros=2.7,
    )(row, embed, conv_weight, mix_weight, out_weight, cot_fwd, cot_rev)
    known = call(join_four_kernel, [VMEM] * 5, [((4, length), row.dtype, VMEM)])(own, *near, taps)[0]
    parts = [known, swapped(known, 4)]
    deep = -(-TAPS // 128) * 128
    table, local, mixed_table, pre_high, pre_low, second_conv, second_mix = call(
        second_tables_kernel,
        [VMEM] * 4 + [HBM] * 2 + [VMEM],
        [((CONTEXTS, channels), F32, VMEM), ((LOCAL, channels), F32, VMEM), ((CONTEXTS, wide), F32, VMEM)]
        + [((deep, wide), BF16, VMEM)] * 2
        + layer_weights,
        [sems((4,))],
        micros=2.5,
    )(taps, embed, gate_bias, turn, conv_weight, mix_weight, known)
    mask = 8
    while mask < count:
        known = jnp.concatenate([known, parts[-1]], axis=0)
        parts.append(swapped(known, mask))
        mask *= 2

    rows_x, rows_y = TAPS, channels // 2 + LOCAL // 2
    keep_y, send_y, hidden_high, hidden_low, hots, slopes = call(
        lambda *refs: forward_kernel(count, *refs),
        [SMEM] + [VMEM] * (len(parts) + 4),
        [((2, rows_y, 128), F32, VMEM)] * 2
        + [((2 * length, channels), BF16, VMEM)] * 2
        + [((2, deep, length), BF16, VMEM), ((2 * length, wide), F32, VMEM)],
        [VMEM((4, rows_y, 128), F32)],
        micros=2.0,
    )(dilations, *parts, pre_high, pre_low, cot_high, cot_low)
    keep_x, send_x = call(
        taps_kernel,
        [VMEM] * 3,
        [((2, rows_x, 128), F32, VMEM)] * 2,
        [VMEM((4, rows_x, 128), F32)],
        micros=1.5,
    )(hots, slopes, grad_hidden)

    def halved(keep, received, after):
        outs = [(keep.shape[1:], F32, VMEM)] * 2
        return call(halve_after_kernel, [VMEM] * 3, outs)(keep, received, after)

    def added(kept, received, after, space=VMEM):
        return call(add_after_kernel, [VMEM] * 2 + [space], [(kept.shape, F32, VMEM)])(kept, received, after)[0]

    def touched(value, after, cuts=1):
        shape = (value.shape[0] // cuts, value.shape[1])
        return call(touch_kernel, [VMEM] * 2, [(shape, value.dtype, VMEM)] * cuts)(value, after)

    keep_y, send_y = halved(keep_y, swapped(send_y, 1), keep_x)
    keep_x, send_x = halved(keep_x, swapped(send_x, 1), keep_y)
    sum_y = added(keep_y, swapped(send_y, 2), keep_x)
    out_fwd, out_rev = call(
        outputs_kernel,
        [VMEM] * 6,
        [((length, channels), F32, HBM)] * 2,
        [VMEM((2, length, channels), F32), sems((2,))],
        micros=2.0,
    )(hots, hidden_high, hidden_low, local, last_weight, sum_y)
    sum_x = added(keep_x, swapped(send_x, 2), out_rev, HBM)
    first_high, first_low, second_high, second_low, turn_high, turn_low, *tables = call(
        prepare_kernel,
        [VMEM] * 8,
        [((4, wide, channels), BF16, VMEM)] * 4
        + [(square, BF16, VMEM)] * 2
        + [((CONTEXTS, channels), BF16, VMEM)] * 6
        + [((CONTEXTS, wide), F32, VMEM), ((CONTEXTS, 32), BF16, VMEM)],
        micros=1.4,
    )(first_conv, first_mix, second_conv, second_mix, turn, table, mixed_table, sum_x)
    levels, tables = tables[:4], tables[4:]

    def merged(kernel, rows, mine, theirs, after):
        return call(kernel, [VMEM] * 3, [((rows, 128), F32, VMEM)])(mine, theirs, after)[0]

    merged_x, merged_y = 3 * CONTEXTS, rows_y + EDGE // 2
    piece_y = crossed(sum_y, count, lambda x, y: merged(merge_rest_kernel, merged_y, x, y, turn_low))
    core_y = swapped(piece_y, 1)
    piece_x = crossed(sum_x, count, lambda x, y: merged(merge_taps_kernel, merged_x, x, y, core_y))
    other_y = swapped(piece_y, 2)
    core_x = [swapped(x, 1) for x in touched(piece_x, other_y, 2)]

    shared = (*levels, second_high, second_low)
    large = [(conv_weight.shape, F32, HBM), (mix_weight.shape, F32, HBM)]
    level_out = ((CONTEXTS, channels), F32, VMEM)
    quarter_conv, quarter_mix = (3, channels, 128), (channels, 128)
    g_conv, g_mix, bias_own, partial = call(
        own_columns_kernel,
        [VMEM] * 9,
        [*large, ((2, 128), F32, VMEM), level_out],
        [
            VMEM((2, merged_x, 128), F32),
            VMEM((2, *quarter_conv), F32),
            VMEM((2, *quarter_mix), F32),
            sems((8,)),
        ],
        micros=0.05,
    )(piece_x, *core_x, *shared)
    other_x = swapped(piece_x, 2)
    late_y = touched(other_y, partial)[0]
    rest_y = swapped(late_y, 1)
    far_x = swapped(touched(other_x, late_y)[0], 1)
    g_conv, g_mix, bias_other, partial = call(
        other_columns_kernel,
        [VMEM] * 8 + [HBM] * 2,
        [*large, ((1, 128), F32, VMEM), level_out],
        [VMEM(quarter_conv, F32), VMEM(quarter_mix, F32), sems((4,))],
        aliases={8: 0, 9: 1},
        micros=0.05,
    )(other_x, *shared, partial, g_conv, g_mix)
    g_conv, g_mix, g_embed, g_bias, g_out = call(
        first_layer_kernel,
        [VMEM] * 23 + [HBM] * 2,
        [*large] + [(shape, F32, HBM) for shape in (embed.shape, gate_bias.shape, out_weight.shape)],
        [
            VMEM((4, merged_y, 128), F32),
            VMEM((4, 1, 128), F32),
            VMEM((1, 128), F32),
            VMEM(quarter_conv, F32),
            VMEM(quarter_mix, F32),
            VMEM(conv_weight.shape[1:], F32),
            VMEM(mix_weight.shape[1:], F32),
            VMEM(embed.shape, F32),
            VMEM(gate_bias.shape, F32),
            VMEM(out_weight.shape, F32),
            sems((11,)),
        ],
        aliases={23: 0, 24: 1},
        micros=2.7,
    )(
        far_x, *shared, piece_y, other_y, core_y, rest_y, partial, bias_own, bias_other, embed,
        first_high, first_low, turn_high, turn_low, *tables, g_conv, g_mix,
    )
    return (out_fwd, out_rev, g_embed, g_conv, g_mix, g_bias, g_out)


def solution(mesh):
    in_specs = (
        P(("dp", "seq")),
        P(),
        P(),
        P(),
        P(),
        P(),
        P(),
        P(("dp", "seq"), None),
        P(("dp", "seq"), None),
    )
    out_specs = (
        P(("dp", "seq"), None),
        P(("dp", "seq"), None),
        P("dp", None),
        P("dp", None, None, None),
        P("dp", None, None),
        P("dp", None),
        P("dp", None, None),
    )
    return jax.shard_map(
        on_device, mesh=mesh, in_specs=in_specs, out_specs=out_specs, check_vma=False
    )
```

```python
import jax
import jax.numpy as jnp
from jax import lax
from jax.experimental import pallas as pl
from jax.experimental.pallas import tpu as pltpu
from jax.sharding import PartitionSpec as P

CONTEXTS = 96
INNER = 64
EDGE = 16
LOCAL = INNER + EDGE
TAPS = 3 * LOCAL
HALO = 128
F32 = jnp.float32
BF16 = jnp.bfloat16
VMEM_LIMIT = 40 * 1024 * 1024


def split(x):
    high = x.astype(BF16)
    return high, (x - high.astype(F32)).astype(BF16)


def dot(a, b, ca=1, cb=0):
    return lax.dot_general(a, b, (((ca,), (cb,)), ((), ())), preferred_element_type=F32)


def dot2(exact, pair, ca=1, cb=0):
    return dot(exact, pair[0], ca, cb) + dot(exact, pair[1], ca, cb)


def dot3(a, b, ca=1, cb=0):
    return dot(a[0], b[0], ca, cb) + (dot(a[0], b[1], ca, cb) + dot(a[1], b[0], ca, cb))


def dot3_few(a, b):
    rows = a[0].shape[0]
    both = dot(jnp.concatenate([a[0].astype(F32), a[1].astype(F32)], axis=0).astype(BF16), b[0])
    return both[:rows] + (both[rows:] + dot(a[0], b[1]))


def letters(index):
    inner = index < 64
    left = (index >= 64) & (index < 80)
    low = index & 3
    mid = (index >> 2) & 3
    l = jnp.where(inner, (index >> 4) & 3, jnp.where(left, -1, mid))
    m = jnp.where(inner | left, mid, low)
    r = jnp.where(inner | left, low, -1)
    return l, m, r


def mirrored(index):
    low = 3 - (index & 3)
    mid = 3 - ((index >> 2) & 3)
    high = 3 - ((index >> 4) & 3)
    inner = low * 16 + mid * 4 + high
    left = 80 + low * 4 + mid
    right = 64 + low * 4 + mid
    return jnp.where(index < 64, inner, jnp.where(index < 80, left, right))


def permutation():
    rows = lax.broadcasted_iota(jnp.int32, (CONTEXTS, CONTEXTS), 0)
    cols = lax.broadcasted_iota(jnp.int32, (CONTEXTS, CONTEXTS), 1)
    return (mirrored(rows) == cols).astype(F32).astype(BF16)


def letter_hot():
    rows = lax.broadcasted_iota(jnp.int32, (CONTEXTS, 32), 0)
    cols = lax.broadcasted_iota(jnp.int32, (CONTEXTS, 32), 1)
    l, m, r = letters(rows)
    kind = cols >> 3
    value = jnp.where(kind == 0, l, jnp.where(kind == 1, m, jnp.where(kind == 2, r, 3 - m)))
    return (value == (cols & 7)).astype(F32).astype(BF16)


def gates(mixed):
    channels = mixed.shape[1] // 2
    tanh_part = jnp.tanh(mixed[:, :channels])
    sig_part = 0.5 + 0.5 * jnp.tanh(0.5 * mixed[:, channels:])
    return tanh_part, sig_part


def gate_grads(grad_hidden, tanh_part, sig_part):
    scaled = grad_hidden * sig_part
    return scaled * (1.0 - tanh_part * tanh_part), scaled * tanh_part * (1.0 - sig_part)


class Fetch:
    def __init__(self, sems):
        self.sems = sems
        self.copies = []

    def start(self, source, target):
        copy = pltpu.make_async_copy(source, target, self.sems.at[len(self.copies)])
        copy.start()
        self.copies.append(copy)
        return len(self.copies) - 1

    def wait(self, *which):
        for at in which:
            self.copies[at].wait()


def padded_base(embed):
    return jnp.concatenate([embed[...], jnp.zeros((4, embed.shape[1]), F32)], axis=0)


def left_side():
    return lax.axis_index("seq") * 2 < lax.axis_size("seq")


def local_rows(rows):
    edge = jnp.where(left_side(), rows[INNER : INNER + EDGE], rows[INNER + EDGE : INNER + 2 * EDGE])
    return jnp.concatenate([rows[:INNER], edge], axis=0)


def join_four_kernel(first, second, third, fourth, after, out):
    for at, part in enumerate((first, second, third, fourth)):
        out[at : at + 1, :] = part[...]


def touch_kernel(value, after, *outs):
    begin = 0
    for out in outs:
        out[...] = value[begin : begin + out.shape[0], :]
        begin += out.shape[0]


def first_tables_kernel(
    tokens_in, embed_in, conv_in, mix_in, out_in, cot_fwd_in, cot_rev_in,
    own, taps, conv, mix, turn, last_weight, cot_high, cot_low, grad_hidden, embed, cots, sems,
):
    length = cots.shape[1]
    fetch = Fetch(sems)
    fetch.start(embed_in, embed)
    first = [fetch.start(conv_in.at[0, k], conv.at[k]) for k in range(3)]
    first += [fetch.start(mix_in.at[0], mix)]
    last = [fetch.start(out_in.at[1], last_weight)]
    last += [fetch.start(cot_in, cots.at[strand]) for strand, cot_in in enumerate((cot_fwd_in, cot_rev_in))]
    rest = [fetch.start(tokens_in, own), fetch.start(out_in.at[0], turn)]
    fetch.wait(0)
    base = split(padded_base(embed))
    for k in range(4):
        fetch.wait(first[k])
        taps[k * 8 : (k + 1) * 8, :] = dot3_few(base, split(conv[k] if k < 3 else mix[...]))
    fetch.wait(last[0])
    weight = split(last_weight[...])
    for strand in range(2):
        rows = slice(strand * length, (strand + 1) * length)
        fetch.wait(last[1 + strand])
        cot = split(cots[strand])
        cot_high[rows, :], cot_low[rows, :] = cot
        grad_hidden[rows, :] = dot3(cot, weight, 1, 1)
    fetch.wait(*rest)


def second_tables_kernel(
    taps, embed, bias, turn, conv_in, mix_in, after, table, local, mixed_table, pre_high, pre_low, conv, mix, sems,
):
    fetch = Fetch(sems)
    second = [fetch.start(conv_in.at[1, k], conv.at[k]) for k in range(3)]
    second += [fetch.start(mix_in.at[1], mix)]
    hot = letter_hot()
    mixed = dot2(hot, split(taps[...])) + bias[0:1, :]
    tanh_part, sig_part = gates(mixed)
    own = dot2(hot[:, 8:16], split(padded_base(embed)))
    level = own + dot3_few(split(tanh_part * sig_part), split(turn[...]))
    table[...] = level
    local[...] = local_rows(level)
    mixed_table[...] = mixed
    level = split(level)
    swap = permutation()
    partner = tuple(dot(swap, piece).astype(BF16) for piece in level)
    pre_high[TAPS:, :] = jnp.zeros((pre_high.shape[0] - TAPS, pre_high.shape[1]), BF16)
    pre_low[TAPS:, :] = jnp.zeros((pre_low.shape[0] - TAPS, pre_low.shape[1]), BF16)
    for k in (0, 2, 1):
        fetch.wait(second[k])
        value = dot3_few(level, split(conv[k]))
        if k == 1:
            fetch.wait(second[3])
            value = value + dot3_few(partner, split(mix[...])) + bias[1:2, :]
        high, low = split(local_rows(value))
        pre_high[k * LOCAL : (k + 1) * LOCAL, :] = high
        pre_low[k * LOCAL : (k + 1) * LOCAL, :] = low


def windows(parts, count):
    length = parts[0].shape[1]
    place = lax.axis_index("seq")
    last = count - 1

    def block(at):
        total, begin = None, 0
        for part in parts:
            rows = lax.broadcasted_iota(jnp.int32, part.shape, 0) + begin
            piece = jnp.sum(jnp.where(rows == (place ^ at), part[...], 0), axis=0, keepdims=True)
            total = piece if total is None else total + piece
            begin += part.shape[0]
        return total

    def window(at):
        before = jnp.where(at == 0, -1, block(jnp.maximum(at - 1, 0))[:, length - HALO :])
        after = jnp.where(at == last, -1, block(jnp.minimum(at + 1, last))[:, :HALO])
        return [before, block(at), after]

    fwd = jnp.concatenate(window(place), axis=1)
    rev = jnp.concatenate(window(last - place), axis=1)
    rev = jnp.where(rev < 0, -1, 3 - rev)
    tiles = rev.shape[1] // 128
    blocks = [rev[:, i * 128 : (i + 1) * 128] for i in reversed(range(tiles))]
    blocks += [jnp.zeros((8 - tiles, 128), jnp.int32)]
    stacked = jnp.concatenate(blocks, axis=0).astype(F32).astype(BF16)
    rows = lax.broadcasted_iota(jnp.int32, (128, 128), 0)
    cols = lax.broadcasted_iota(jnp.int32, (128, 128), 1)
    flip = (rows + cols == 127).astype(F32).astype(BF16)
    turned = dot(stacked, flip).astype(jnp.int32)
    rev = jnp.concatenate([turned[i : i + 1, :] for i in range(tiles)], axis=1)
    return fwd, rev


def local_contexts(window, first, second, length):
    width = window.shape[1]
    base = jnp.broadcast_to(window, (8, width))
    l = pltpu.roll(base, first, 1)
    r = pltpu.roll(base, width - first, 1)
    index = jnp.where(l < 0, INNER + base * 4 + r, jnp.where(r < 0, INNER + l * 4 + base, l * 16 + base * 4 + r))
    index = jnp.where(base < 0, LOCAL, index)
    before = pltpu.roll(index, second, 1)
    after = pltpu.roll(index, width - second, 1)
    return [x[0:1, HALO : HALO + length] for x in (before, index, after)]


def hot_rows(index):
    rows = lax.broadcasted_iota(jnp.int32, (LOCAL, index.shape[1]), 0)
    return (rows == index).astype(F32).astype(BF16)


def deal(quarters, keep, send):
    bit = lax.axis_index("seq") & 1
    keep[...] = quarters[pl.ds(bit * 2, 2)]
    send[...] = quarters[pl.ds((1 - bit) * 2, 2)]


def forward_kernel(count, dil, *refs):
    steps = count.bit_length() - 2
    parts, refs = refs[:steps], refs[steps:]
    (pre_high, pre_low, cot_high, cot_low, keep, send, hidden_high, hidden_low, hots, slopes, quarters) = refs
    length = parts[0].shape[1]
    channels = cot_high.shape[1]
    pre = (pre_high[...], pre_low[...])
    both = windows(parts, count)
    pad = jnp.zeros((pre_high.shape[0] - TAPS, length), BF16)
    total_o = total_c = None
    for strand in range(2):
        index = local_contexts(both[strand], dil[0], dil[1], length)
        hot = jnp.concatenate([hot_rows(x) for x in index] + [pad], axis=0)
        hots[strand] = hot
        mixed = dot2(hot, pre, 0, 0)
        tanh_part, sig_part = gates(mixed)
        product = tanh_part * sig_part
        hidden = split(product)
        rows = slice(strand * length, (strand + 1) * length)
        hidden_high[rows, :] = hidden[0]
        hidden_low[rows, :] = hidden[1]
        slopes[rows, :channels] = sig_part - product * tanh_part
        slopes[rows, channels:] = product - product * sig_part
        cot = (cot_high[rows, :], cot_low[rows, :])
        part_o = dot3(hidden, cot, 0, 0)
        part_c = dot2(hot[LOCAL : 2 * LOCAL], cot)
        total_o = part_o if total_o is None else total_o + part_o
        total_c = part_c if total_c is None else total_c + part_c
    side = channels // 4
    for q in range(4):
        lanes = slice((q >> 1) * 128, (q >> 1) * 128 + 128)
        quarters[q, :side, :] = total_o[q * side : (q + 1) * side, :128]
        quarters[q, side : 2 * side, :] = total_o[q * side : (q + 1) * side, 128:]
        for begin, rows, at in ((0, INNER // 2, 2 * side), (INNER, EDGE // 2, 2 * side + INNER // 2)):
            begin += (q & 1) * rows
            quarters[q, at : at + rows, :] = total_c[begin : begin + rows, lanes]
    deal(quarters, keep, send)


def taps_kernel(hots, slopes, grad_hidden, keep, send, quarters):
    length = hots.shape[2]
    total = None
    for strand in range(2):
        rows = slice(strand * length, (strand + 1) * length)
        grad = grad_hidden[rows, :]
        part = dot2(hots[strand], split(slopes[rows, :] * jnp.concatenate([grad, grad], axis=1)))
        total = part if total is None else total + part
    for q in range(4):
        quarters[q] = total[:TAPS, q * 128 : (q + 1) * 128]
    deal(quarters, keep, send)


def halve_kernel(kept, received, keep, send):
    bit = (lax.axis_index("seq") >> 1) & 1
    send[...] = kept[1 - bit] + received[1 - bit]
    keep[...] = kept[bit] + received[bit]


def add_after_kernel(kept, received, after, out):
    out[...] = kept[...] + received[...]


def halve_after_kernel(kept, received, after, keep, send):
    halve_kernel(kept, received, keep, send)


def outputs_kernel(hots, hidden_high, hidden_low, local, out_w, after, out_fwd, out_rev, values, sems):
    length = hots.shape[2]
    fetch = Fetch(sems)
    weight = split(out_w[...])
    level = split(local[...])
    for strand, out in enumerate((out_fwd, out_rev)):
        rows = slice(strand * length, (strand + 1) * length)
        own = dot2(hots[strand, LOCAL : 2 * LOCAL, :], level, 0, 0)
        values[strand] = own + dot3((hidden_high[rows, :], hidden_low[rows, :]), weight)
        fetch.start(values.at[strand], out)
    fetch.wait(0, 1)


def prepare_kernel(
    first_conv, first_mix, second_conv, second_mix, out_w, table, mixed_table, after,
    first_high, first_low, second_high, second_low, turn_high, turn_low,
    level_high, level_low, partner_high, partner_low, hidden_high, hidden_low, slopes, hot,
):
    level = split(table[...])
    swap = permutation()
    level_high[...], level_low[...] = level
    partner_high[...], partner_low[...] = tuple(dot(swap, piece).astype(BF16) for piece in level)
    for conv, mix, high, low in (
        (second_conv, second_mix, second_high, second_low),
        (first_conv, first_mix, first_high, first_low),
    ):
        for k in range(4):
            high[k], low[k] = split((conv[k] if k < 3 else mix[...]).T)
    turn_high[...], turn_low[...] = split(out_w[...].T)
    tanh_part, sig_part = gates(mixed_table[...])
    product = tanh_part * sig_part
    hidden_high[...], hidden_low[...] = split(product)
    channels = product.shape[1]
    slopes[:, :channels] = sig_part - product * tanh_part
    slopes[:, channels:] = product - product * sig_part
    hot[...] = letter_hot()


def merge(mine, theirs, inner, edge):
    left = left_side()
    both = mine[inner, :] + theirs[inner, :]
    own, other = mine[edge, :], theirs[edge, :]
    return both, jnp.where(left, own, other), jnp.where(left, other, own)


def merge_blocks(mine, theirs, out, sizes):
    at = to = 0
    for inner, edge in sizes:
        pieces = merge(mine, theirs, slice(at, at + inner), slice(at + inner, at + inner + edge))
        out[to : to + inner, :] = pieces[0]
        out[to + inner : to + inner + edge, :] = pieces[1]
        out[to + inner + edge : to + inner + 2 * edge, :] = pieces[2]
        at, to = at + inner + edge, to + inner + 2 * edge


def merge_taps_kernel(mine, theirs, after, out):
    merge_blocks(mine, theirs, out, [(INNER, EDGE)] * 3)


def merge_rest_kernel(mine, theirs, after, out):
    merge_blocks(mine, theirs, out, [(mine.shape[0] - EDGE // 2, EDGE // 2)])


def gather_quarters(pieces, quarters):
    place = lax.axis_index("seq")
    low, high = place & 1, (place >> 1) & 1
    for parts, x, y in zip(pieces, (0, 0, 1, 1), (0, 1, 0, 1)):
        begin = 0
        for part in parts:
            rows = part.shape[0]
            quarters[(low ^ x) * 2 + (high ^ y), begin : begin + rows, :] = part[...]
            begin += rows


def tap_pairs(taps):
    return [split(taps[k * CONTEXTS : (k + 1) * CONTEXTS, :]) for k in range(3)]


def quarter_weights(pairs, taps, levels, g_conv, g_mix, bias):
    level_high, level_low, partner_high, partner_low = levels
    level = (level_high[...], level_low[...])
    partner = (partner_high[...], partner_low[...])
    for k, pair in enumerate(pairs):
        g_conv[k] = dot3(level, pair, 0, 0)
    g_mix[...] = dot3(partner, pairs[1], 0, 0)
    bias[...] = jnp.sum(taps[CONTEXTS : 2 * CONTEXTS, :], axis=0, keepdims=True)


def quarter_part(pairs, column, seconds):
    weights = [tuple(ref[k, pl.ds(column, 128), :] for ref in seconds) for k in range(4)]
    part = dot2(permutation(), split(dot3_few(pairs[1], weights[3])))
    for k, pair in enumerate(pairs):
        part = part + dot3_few(pair, weights[k])
    return part


def column_of(core, chip):
    place = lax.axis_index("seq")
    low, high = place & 1, (place >> 1) & 1
    return pl.multiple_of(((low ^ core) * 2 + (high ^ chip)) * 128, 128)


def store_columns(store, column, g_conv, g_mix, g_conv_out, g_mix_out):
    block = pl.ds(column, 128)
    for k in range(3):
        store.start(g_conv.at[k], g_conv_out.at[1, k, :, block])
    store.start(g_mix, g_mix_out.at[1, :, block])


def fill(taps, first, second):
    half = first.shape[0]
    taps[:half, :] = first[...]
    taps[half:, :] = second[...]


def own_columns_kernel(taps, *refs):
    levels, seconds, refs = refs[:4], refs[4:6], refs[6:]
    after, g_conv_out, g_mix_out, bias, total, g_conv, g_mix, out_sems = refs
    store = Fetch(out_sems)
    column = column_of(0, 0)
    pairs = tap_pairs(taps)
    quarter_weights(pairs, taps, levels, g_conv, g_mix, bias)
    total[...] = quarter_part(pairs, column, seconds)
    store_columns(store, column, g_conv, g_mix, g_conv_out, g_mix_out)
    store.wait(*range(len(store.copies)))


def core_columns_kernel(first, second, *refs):
    levels, seconds, refs = refs[:4], refs[4:6], refs[6:]
    partial, g_conv_in, g_mix_in, g_conv_out, g_mix_out, bias, total, taps, g_conv, g_mix, out_sems = refs
    fill(taps, first, second)
    store = Fetch(out_sems)
    column = column_of(1, 0)
    pairs = tap_pairs(taps)
    quarter_weights(pairs, taps, levels, g_conv, g_mix, bias)
    total[...] = partial[...] + quarter_part(pairs, column, seconds)
    store_columns(store, column, g_conv, g_mix, g_conv_out, g_mix_out)
    store.wait(*range(len(store.copies)))


def other_columns_kernel(taps, *refs):
    levels, seconds, refs = refs[:4], refs[4:6], refs[6:]
    partial, g_conv_in, g_mix_in, g_conv_out, g_mix_out, bias, total, g_conv, g_mix, out_sems = refs
    store = Fetch(out_sems)
    column = column_of(0, 1)
    pairs = tap_pairs(taps)
    quarter_weights(pairs, taps, levels, g_conv, g_mix, bias)
    total[...] = partial[...] + quarter_part(pairs, column, seconds)
    store_columns(store, column, g_conv, g_mix, g_conv_out, g_mix_out)
    store.wait(*range(len(store.copies)))


def first_layer_kernel(
    far_piece, level_high, level_low, partner_high, partner_low, second_high, second_low,
    piece_00, piece_01, piece_10, piece_11, partial, bias_own, bias_core, bias_other, embed,
    first_high, first_low, turn_high, turn_low, hidden_high, hidden_low, slopes, hot_in,
    g_conv_in, g_mix_in, g_conv_out, g_mix_out, g_embed_out, g_bias_out, g_out_out,
    quarters, bias_rows, bias_far, far_conv, far_mix, g_conv, g_mix, g_embed, g_bias, g_out, out_sems,
):
    channels = embed.shape[1]
    store = Fetch(out_sems)
    column = column_of(1, 1)
    pairs = tap_pairs(far_piece)
    far_part = quarter_part(pairs, column, (second_high, second_low))
    gather_quarters([(piece,) for piece in (piece_00, piece_01, piece_10, piece_11)], quarters)
    side = channels // 4
    rest = []
    for begin, rows in ((0, INNER // 2), (INNER // 2, EDGE // 2), (INNER // 2 + EDGE // 2, EDGE // 2)):
        begin += 2 * side
        halves = [[quarters[2 * h + i, begin : begin + rows, :] for i in range(2)] for h in range(2)]
        rest.append(jnp.concatenate([jnp.concatenate(x, axis=0) for x in halves], axis=1))
    grad_level = split(partial[...] + far_part + jnp.concatenate(rest, axis=0))
    grad_hidden = dot3_few(grad_level, (turn_high[...], turn_low[...]))
    grad_mixed = slopes[...] * jnp.concatenate([grad_hidden, grad_hidden], axis=1)
    levels = (level_high, level_low, partner_high, partner_low)
    quarter_weights(pairs, far_piece, levels, far_conv, far_mix, bias_far)
    store_columns(store, column, far_conv, far_mix, g_conv_out, g_mix_out)
    hot = hot_in[...]
    by_letter = dot2(hot, split(grad_mixed), 0, 0)
    base = split(padded_base(embed))
    stacked = jnp.concatenate([base[0].astype(F32), base[0].astype(F32), base[1].astype(F32)], axis=0).astype(BF16)
    pieces = []
    for k in range(4):
        piece = split(by_letter[k * 8 : (k + 1) * 8, :])
        pieces.append(piece)
        high, low = piece[0].astype(F32), piece[1].astype(F32)
        value = dot(stacked, jnp.concatenate([high, low, high], axis=0).astype(BF16), 0, 0)
        if k < 3:
            g_conv[k] = value
            store.start(g_conv.at[k], g_conv_out.at[0, k])
        else:
            g_mix[...] = value
            store.start(g_mix, g_mix_out.at[0])
    g_out[0] = dot3((hidden_high[...], hidden_low[...]), grad_level, 0, 0)
    for q in range(4):
        for h in range(2):
            g_out[1, q * side : (q + 1) * side, h * 128 : (h + 1) * 128] = quarters[q, h * side : (h + 1) * side, :]
    store.start(g_out, g_out_out)
    place = lax.axis_index("seq")
    low, high = place & 1, (place >> 1) & 1
    for row, x, y in (
        (bias_own[...], 0, 0), (bias_core[...], 1, 0), (bias_other[...], 0, 1), (bias_far[...], 1, 1)
    ):
        bias_rows[(low ^ x) * 2 + (high ^ y)] = row
    g_bias[0:1, :] = jnp.sum(grad_mixed, axis=0, keepdims=True)
    g_bias[1:2, :] = jnp.concatenate([bias_rows[q] for q in range(4)], axis=1)
    store.start(g_bias, g_bias_out)
    grad_base = dot2(hot[:, 8:16], grad_level, 0, 0)
    for k in range(4):
        grad_base = grad_base + dot3_few(pieces[k], (first_high[k], first_low[k]))
    g_embed[...] = grad_base[:4, :]
    store.start(g_embed, g_embed_out)
    store.wait(*range(len(store.copies)))


VMEM, SMEM, HBM = pltpu.VMEM, pltpu.SMEM, pltpu.HBM


def call(kernel, ins, outs, scratch=(), aliases=None, micros=0.001):
    run = pl.pallas_call(
        kernel,
        out_shape=[space(shape, kind) for shape, kind, space in outs],
        in_specs=[pl.BlockSpec(memory_space=space) for space in ins],
        out_specs=[pl.BlockSpec(memory_space=space) for _, _, space in outs],
        scratch_shapes=list(scratch),
        input_output_aliases=aliases or {},
        cost_estimate=pl.CostEstimate(flops=int(micros * 1.1e9), bytes_accessed=int(micros * 3e6), transcendentals=0),
        compiler_params=pltpu.CompilerParams(vmem_limit_bytes=VMEM_LIMIT),
    )

    def placed(*args):
        return run(*[pltpu.with_memory_space_constraint(x, HBM) if space is HBM else x for x, space in zip(args, ins)])

    return placed


def swapped(value, mask):
    pairs = [(source, source ^ mask) for source in range(lax.axis_size("seq"))]
    return lax.ppermute(value, "seq", pairs)


def crossed(piece, count, rest):
    mask = 4
    while mask < count // 2:
        piece = piece + swapped(piece, mask)
        mask *= 2
    return rest(piece, swapped(piece, mask))


def on_device(
    tokens, dilations, embed, conv_weight, mix_weight, gate_bias, out_weight, cot_fwd, cot_rev
):
    channels = embed.shape[1]
    wide = 2 * channels
    length = tokens.shape[0]
    count = lax.axis_size("seq")
    sems = pltpu.SemaphoreType.DMA
    square = (channels, channels)

    row = tokens.reshape(1, length)
    near = [swapped(row, mask) for mask in (1, 2, 3)]
    layer_weights = [(conv_weight.shape[1:], F32, VMEM), (mix_weight.shape[1:], F32, VMEM)]
    own, taps, first_conv, first_mix, turn, last_weight, cot_high, cot_low, grad_hidden = call(
        first_tables_kernel,
        [HBM] * 7,
        [(row.shape, row.dtype, VMEM), ((32, wide), F32, VMEM), *layer_weights]
        + [(square, F32, VMEM)] * 2
        + [((2 * length, channels), BF16, VMEM)] * 2
        + [((2 * length, channels), F32, VMEM)],
        [VMEM(embed.shape, F32), VMEM((2, length, channels), F32), sems((10,))],
        micros=2.7,
    )(row, embed, conv_weight, mix_weight, out_weight, cot_fwd, cot_rev)
    known = call(join_four_kernel, [VMEM] * 5, [((4, length), row.dtype, VMEM)])(own, *near, taps)[0]
    parts = [known, swapped(known, 4)]
    deep = -(-TAPS // 128) * 128
    table, local, mixed_table, pre_high, pre_low, second_conv, second_mix = call(
        second_tables_kernel,
        [VMEM] * 4 + [HBM] * 2 + [VMEM],
        [((CONTEXTS, channels), F32, VMEM), ((LOCAL, channels), F32, VMEM), ((CONTEXTS, wide), F32, VMEM)]
        + [((deep, wide), BF16, VMEM)] * 2
        + layer_weights,
        [sems((4,))],
        micros=2.5,
    )(taps, embed, gate_bias, turn, conv_weight, mix_weight, known)
    mask = 8
    while mask < count:
        known = jnp.concatenate([known, parts[-1]], axis=0)
        parts.append(swapped(known, mask))
        mask *= 2

    rows_x, rows_y = TAPS, channels // 2 + LOCAL // 2
    keep_y, send_y, hidden_high, hidden_low, hots, slopes = call(
        lambda *refs: forward_kernel(count, *refs),
        [SMEM] + [VMEM] * (len(parts) + 4),
        [((2, rows_y, 128), F32, VMEM)] * 2
        + [((2 * length, channels), BF16, VMEM)] * 2
        + [((2, deep, length), BF16, VMEM), ((2 * length, wide), F32, VMEM)],
        [VMEM((4, rows_y, 128), F32)],
        micros=2.0,
    )(dilations, *parts, pre_high, pre_low, cot_high, cot_low)
    keep_x, send_x = call(
        taps_kernel,
        [VMEM] * 3,
        [((2, rows_x, 128), F32, VMEM)] * 2,
        [VMEM((4, rows_x, 128), F32)],
        micros=1.5,
    )(hots, slopes, grad_hidden)

    def halved(keep, received, after):
        outs = [(keep.shape[1:], F32, VMEM)] * 2
        return call(halve_after_kernel, [VMEM] * 3, outs)(keep, received, after)

    def added(kept, received, after, space=VMEM):
        return call(add_after_kernel, [VMEM] * 2 + [space], [(kept.shape, F32, VMEM)])(kept, received, after)[0]

    def touched(value, after, cuts=1):
        shape = (value.shape[0] // cuts, value.shape[1])
        return call(touch_kernel, [VMEM] * 2, [(shape, value.dtype, VMEM)] * cuts)(value, after)

    keep_y, send_y = halved(keep_y, swapped(send_y, 1), keep_x)
    keep_x, send_x = halved(keep_x, swapped(send_x, 1), keep_y)
    sum_y = added(keep_y, swapped(send_y, 2), keep_x)
    out_fwd, out_rev = call(
        outputs_kernel,
        [VMEM] * 6,
        [((length, channels), F32, HBM)] * 2,
        [VMEM((2, length, channels), F32), sems((2,))],
        micros=2.0,
    )(hots, hidden_high, hidden_low, local, last_weight, sum_y)
    sum_x = added(keep_x, swapped(send_x, 2), out_rev, HBM)
    first_high, first_low, second_high, second_low, turn_high, turn_low, *tables = call(
        prepare_kernel,
        [VMEM] * 8,
        [((4, wide, channels), BF16, VMEM)] * 4
        + [(square, BF16, VMEM)] * 2
        + [((CONTEXTS, channels), BF16, VMEM)] * 6
        + [((CONTEXTS, wide), F32, VMEM), ((CONTEXTS, 32), BF16, VMEM)],
        micros=1.4,
    )(first_conv, first_mix, second_conv, second_mix, turn, table, mixed_table, sum_x)
    levels, tables = tables[:4], tables[4:]

    def merged(kernel, rows, mine, theirs, after):
        return call(kernel, [VMEM] * 3, [((rows, 128), F32, VMEM)])(mine, theirs, after)[0]

    merged_x, merged_y = 3 * CONTEXTS, rows_y + EDGE // 2
    piece_y = crossed(sum_y, count, lambda x, y: merged(merge_rest_kernel, merged_y, x, y, turn_low))
    core_y = swapped(piece_y, 1)
    piece_x = crossed(sum_x, count, lambda x, y: merged(merge_taps_kernel, merged_x, x, y, core_y))
    other_y = swapped(piece_y, 2)
    halves_x = touched(piece_x, other_y, 2)
    core_x = [swapped(x, 1) for x in halves_x]

    shared = (*levels, second_high, second_low)
    large = [(conv_weight.shape, F32, HBM), (mix_weight.shape, F32, HBM)]
    level_out = ((CONTEXTS, channels), F32, VMEM)
    quarter_conv, quarter_mix = (3, channels, 128), (channels, 128)
    bias_out = ((1, 128), F32, VMEM)
    g_conv, g_mix, bias_own, partial = call(
        own_columns_kernel,
        [VMEM] * 8,
        [*large, bias_out, level_out],
        [VMEM(quarter_conv, F32), VMEM(quarter_mix, F32), sems((4,))],
        micros=1.2,
    )(piece_x, *shared, halves_x[0])
    g_conv, g_mix, bias_core, partial = call(
        core_columns_kernel,
        [VMEM] * 9 + [HBM] * 2,
        [*large, bias_out, level_out],
        [VMEM((merged_x, 128), F32), VMEM(quarter_conv, F32), VMEM(quarter_mix, F32), sems((4,))],
        aliases={9: 0, 10: 1},
        micros=0.05,
    )(*core_x, *shared, partial, g_conv, g_mix)
    other_x = swapped(piece_x, 2)
    late_y = touched(other_y, partial)[0]
    rest_y = swapped(other_y, 1)
    far_x = swapped(touched(other_x, late_y)[0], 1)
    g_conv, g_mix, bias_other, partial = call(
        other_columns_kernel,
        [VMEM] * 8 + [HBM] * 2,
        [*large, ((1, 128), F32, VMEM), level_out],
        [VMEM(quarter_conv, F32), VMEM(quarter_mix, F32), sems((4,))],
        aliases={8: 0, 9: 1},
        micros=0.05,
    )(other_x, *shared, partial, g_conv, g_mix)
    g_conv, g_mix, g_embed, g_bias, g_out = call(
        first_layer_kernel,
        [VMEM] * 24 + [HBM] * 2,
        [*large] + [(shape, F32, HBM) for shape in (embed.shape, gate_bias.shape, out_weight.shape)],
        [
            VMEM((4, merged_y, 128), F32),
            VMEM((4, 1, 128), F32),
            VMEM((1, 128), F32),
            VMEM(quarter_conv, F32),
            VMEM(quarter_mix, F32),
            VMEM(conv_weight.shape[1:], F32),
            VMEM(mix_weight.shape[1:], F32),
            VMEM(embed.shape, F32),
            VMEM(gate_bias.shape, F32),
            VMEM(out_weight.shape, F32),
            sems((11,)),
        ],
        aliases={24: 0, 25: 1},
        micros=2.7,
    )(
        far_x, *shared, piece_y, other_y, core_y, rest_y, partial, bias_own, bias_core, bias_other, embed,
        first_high, first_low, turn_high, turn_low, *tables, g_conv, g_mix,
    )
    return (out_fwd, out_rev, g_embed, g_conv, g_mix, g_bias, g_out)


def solution(mesh):
    in_specs = (
        P(("dp", "seq")),
        P(),
        P(),
        P(),
        P(),
        P(),
        P(),
        P(("dp", "seq"), None),
        P(("dp", "seq"), None),
    )
    out_specs = (
        P(("dp", "seq"), None),
        P(("dp", "seq"), None),
        P("dp", None),
        P("dp", None, None, None),
        P("dp", None, None),
        P("dp", None),
        P("dp", None, None),
    )
    return jax.shard_map(
        on_device, mesh=mesh, in_specs=in_specs, out_specs=out_specs, check_vma=False
    )
```
